32 devices in a mesh: rows: 8 (over y, x, core), heads: 4 (over z).
Axes of the slice: x: 2, y: 2, z: 4, core: 2. Of those that a mesh axis runs over, the one named last changes fastest.
Arguments:
- images: bfloat16 [16, 64, 64, 512], P('heads', 'rows'), may hold values from -6 to 6
- image_sides: int32 [16], replicated, may hold values from 32 to 64, as said below
- labels: int32 [16], replicated, may hold values from 0 to 999
- timesteps: int32 [16], replicated, may hold values from 0 to 999
- cotangent: bfloat16 [16, 64, 64, 512], P('heads', 'rows'), may hold values from -6 to 6
- first_gain: bfloat16 [512], replicated, may hold values from 0.25 to 1.75
- first_bias: bfloat16 [512], replicated, may hold values from -3 to 3
- conv_one: bfloat16 [4608, 512], replicated, may hold values from -0.09375 to 0.09375
- time_proj: bfloat16 [1024, 512], replicated, may hold values from -0.5 to 0.5
- time_bias: bfloat16 [512], replicated, may hold values from -3 to 3
- second_gain: bfloat16 [512], replicated, may hold values from 0.25 to 1.75
- second_bias: bfloat16 [512], replicated, may hold values from -3 to 3
- conv_two: bfloat16 [4608, 512], replicated, may hold values from -0.09375 to 0.09375
- conv_bias: bfloat16 [512], replicated, may hold values from -3 to 3
- third_gain: bfloat16 [512], replicated, may hold values from 0.25 to 1.75
- third_bias: bfloat16 [512], replicated, may hold values from -3 to 3
- proj_in: bfloat16 [512, 512], replicated, may hold values from -0.25 to 0.25
- proj_in_bias: bfloat16 [512], replicated, may hold values from -3 to 3
- attn_gain: bfloat16 [512], replicated, may hold values from 0.25 to 1.75
- attn_bias: bfloat16 [512], replicated, may hold values from -3 to 3
- qkv_proj: bfloat16 [512, 1536], replicated, may hold values from -0.25 to 0.25
- attn_out: bfloat16 [512, 512], replicated, may hold values from -16 to 16
- attn_out_bias: bfloat16 [512], replicated, may hold values from -6 to 6
- class_table: bfloat16 [1000, 512], replicated, may hold values from -6 to 6
- cross_value: bfloat16 [512, 512], replicated, may hold values from -0.25 to 0.25
- cross_out: bfloat16 [512, 512], replicated, may hold values from -0.25 to 0.25
- feed_gain: bfloat16 [512], replicated, may hold values from 0.25 to 1.75
- feed_bias: bfloat16 [512], replicated, may hold values from -3 to 3
- geglu_proj: bfloat16 [512, 4096], replicated, may hold values from -0.25 to 0.25
- geglu_bias: bfloat16 [4096], replicated, may hold values from -3 to 3
- feed_out: bfloat16 [2048, 512], replicated, may hold values from -0.1875 to 0.1875
- feed_out_bias: bfloat16 [512], replicated, may hold values from -7 to 7
- proj_out: bfloat16 [512, 512], replicated, may hold values from -0.25 to 0.25
- proj_out_bias: bfloat16 [512], replicated, may hold values from -6 to 6
Outputs:
- output: bfloat16 [16, 64, 64, 512], P('heads', 'rows')
- grad_images: float32 [16, 64, 64, 512], P('heads', 'rows')
- grad_first_gain: float32 [512], P('rows')
- grad_first_bias: float32 [512], P('rows')
- grad_conv_one: float32 [4608, 512], P('rows')
- grad_time_proj: float32 [1024, 512], P('rows')
- grad_time_bias: float32 [512], P('rows')
- grad_second_gain: float32 [512], P('rows')
- grad_second_bias: float32 [512], P('rows')
- grad_conv_two: float32 [4608, 512], P('rows')
- grad_conv_bias: float32 [512], P('rows')
- grad_third_gain: float32 [512], P('rows')
- grad_third_bias: float32 [512], P('rows')
- grad_proj_in: float32 [512, 512], P('rows')
- grad_proj_in_bias: float32 [512], P('rows')
- grad_attn_gain: float32 [512], P('rows')
- grad_attn_bias: float32 [512], P('rows')
- grad_qkv_proj: float32 [512, 1536], P('rows')
- grad_attn_out: float32 [512, 512], P('rows')
- grad_attn_out_bias: float32 [512], P('rows')
- grad_class_table: float32 [1000, 512], P(None, 'rows')
- grad_cross_value: float32 [512, 512], P('rows')
- grad_cross_out: float32 [512, 512], P('rows')
- grad_feed_gain: float32 [512], P('rows')
- grad_feed_bias: float32 [512], P('rows')
- grad_geglu_proj: float32 [512, 4096], P('rows')
- grad_geglu_bias: float32 [4096], P('rows')
- grad_feed_out: float32 [2048, 512], P('rows')
- grad_feed_out_bias: float32 [512], P('rows')
- grad_proj_out: float32 [512, 512], P('rows')
- grad_proj_out_bias: float32 [512], P('rows')
The draws below stay inside these ranges and needn't reach their ends.
Inputs may be any that keep to these rules, and one draw needn't show every extreme that they name: `image_sides`: each side is 64, 48 or 32; each block of 4 consecutive images holds at least one of side 64.
All inputs are finite; a program needn't handle non-finite values.
Results may differ from the reference program's by a relative error of at most 0.018.
Values may be sent and summed in bfloat16 or wider, within the bound.
A program may use at most 640 MiB of HBM per device.

```python
import math
import jax
import jax.numpy as jnp
from jax import lax

CHANNELS = 512
HEADS = 8
GROUPS = 32
FFN = 2048
TIME_DIM = 1024
CLASSES = 1000
CANVAS = 64
IMG_DEV = 4
IMAGES = 16


def draw_image_sides(key, part):
    key = jax.random.fold_in(key, 7)
    level_key, full_key = jax.random.split(key)
    level = jax.random.randint(level_key, (IMAGES,), 0, 3)
    sides = CANVAS - level * (CANVAS // 4)
    full_slot = jax.random.randint(full_key, (IMAGES // IMG_DEV,), 0, IMG_DEV)
    position = jnp.arange(IMAGES, dtype=jnp.int32)
    is_full = position % IMG_DEV == full_slot[position // IMG_DEV]
    return jnp.where(is_full, CANVAS, sides).astype(jnp.int32)


def place_ends(entries, key, smallest, largest):
    dims = entries.shape
    index_at = [jax.random.randint(jax.random.fold_in(key, axis), (), 0, dims[axis]) for axis in range(len(dims))]
    entries = entries.at[tuple(index_at)].set(smallest)
    longest = dims.index(max(dims))
    index_at[longest] = (index_at[longest] + 1) % dims[longest]
    return entries.at[tuple(index_at)].set(largest)


def levels(key, shape, cuts, least, high):
    def one(axis_at, parts):
        steps = jax.random.uniform(jax.random.fold_in(jax.random.fold_in(key, 6), axis_at), (parts,), jnp.float32, least / len(cuts), high / len(cuts))
        return jnp.repeat(jnp.exp(steps), shape[axis_at] // parts).reshape((-1,) + (1,) * (len(shape) - axis_at - 1))

    loudness = one(*cuts[0])
    for cut in cuts[1:]:
        loudness = loudness * one(*cut)
    return loudness


def noise(own_key, shape, deviation, most, shards=(), kind=jnp.bfloat16):
    entries = deviation * jax.random.normal(own_key, shape, jnp.float32)
    if shards:
        entries = entries * levels(own_key, shape, shards, -0.22, 0.18)
    return jnp.clip(entries, -most, most).astype(kind)


def setup_inputs(seed: int = 0) -> dict:
    key_list = jax.random.split(jax.random.key(seed), 35)
    return {
        "images": noise(key_list[0], (IMAGES, CANVAS, CANVAS, CHANNELS), 1.0, 6.0, ((0, 4), (1, 8))),
        "image_sides": draw_image_sides(jax.random.fold_in(key_list[34], 71), 0),
        "labels": place_ends(jax.random.randint(key_list[2], (IMAGES,), 0, CLASSES), jax.random.fold_in(key_list[2], 1), 0, CLASSES - 1).astype(jnp.int32),
        "timesteps": place_ends(jax.random.randint(key_list[3], (IMAGES,), 0, 1000), jax.random.fold_in(key_list[3], 1), 0, 999).astype(jnp.int32),
        "cotangent": noise(key_list[4], (IMAGES, CANVAS, CANVAS, CHANNELS), 1.0, 6.0, ((0, 4), (1, 8))),
        "first_gain": jnp.clip(1.0 + 0.15 * jax.random.normal(key_list[5], (CHANNELS,), jnp.float32), 0.25, 1.75).astype(jnp.bfloat16),
        "first_bias": noise(key_list[6], (CHANNELS,), 0.5, 3.0),
        "conv_one": noise(key_list[7], (9 * CHANNELS, CHANNELS), (9 * CHANNELS) ** -0.5, 0.09375),
        "time_proj": noise(key_list[8], (TIME_DIM, CHANNELS), (TIME_DIM // 8) ** -0.5, 0.5),
        "time_bias": noise(key_list[9], (CHANNELS,), 0.5, 3.0),
        "second_gain": jnp.clip(1.0 + 0.15 * jax.random.normal(key_list[10], (CHANNELS,), jnp.float32), 0.25, 1.75).astype(jnp.bfloat16),
        "second_bias": noise(key_list[11], (CHANNELS,), 0.5, 3.0),
        "conv_two": noise(key_list[12], (9 * CHANNELS, CHANNELS), (9 * CHANNELS) ** -0.5, 0.09375),
        "conv_bias": noise(key_list[13], (CHANNELS,), 0.5, 3.0),
        "third_gain": jnp.clip(1.0 + 0.15 * jax.random.normal(key_list[14], (CHANNELS,), jnp.float32), 0.25, 1.75).astype(jnp.bfloat16),
        "third_bias": noise(key_list[15], (CHANNELS,), 0.5, 3.0),
        "proj_in": noise(key_list[16], (CHANNELS, CHANNELS), CHANNELS ** -0.5, 0.25),
        "proj_in_bias": noise(key_list[17], (CHANNELS,), 0.5, 3.0),
        "attn_gain": jnp.clip(1.0 + 0.15 * jax.random.normal(key_list[18], (CHANNELS,), jnp.float32), 0.25, 1.75).astype(jnp.bfloat16),
        "attn_bias": noise(key_list[19], (CHANNELS,), 0.5, 3.0),
        "qkv_proj": noise(key_list[20], (CHANNELS, 3 * CHANNELS), CHANNELS ** -0.5, 0.25),
        "attn_out": noise(key_list[21], (CHANNELS, CHANNELS), (CANVAS * CHANNELS ** -0.5), 16.0),
        "attn_out_bias": noise(key_list[22], (CHANNELS,), 1.0, 6.0),
        "class_table": noise(key_list[23], (CLASSES, CHANNELS), 1.0, 6.0),
        "cross_value": noise(key_list[24], (CHANNELS, CHANNELS), CHANNELS ** -0.5, 0.25),
        "cross_out": noise(key_list[25], (CHANNELS, CHANNELS), CHANNELS ** -0.5, 0.25),
        "feed_gain": jnp.clip(1.0 + 0.15 * jax.random.normal(key_list[26], (CHANNELS,), jnp.float32), 0.25, 1.75).astype(jnp.bfloat16),
        "feed_bias": noise(key_list[27], (CHANNELS,), 0.5, 3.0),
        "geglu_proj": noise(key_list[28], (CHANNELS, 2 * FFN), CHANNELS ** -0.5, 0.25),
        "geglu_bias": noise(key_list[29], (2 * FFN,), 0.5, 3.0),
        "feed_out": noise(key_list[30], (FFN, CHANNELS), (FFN // 2) ** -0.5, 0.1875),
        "feed_out_bias": noise(key_list[31], (CHANNELS,), 1.2, 7.0),
        "proj_out": noise(key_list[32], (CHANNELS, CHANNELS), CHANNELS ** -0.5, 0.25),
        "proj_out_bias": noise(key_list[33], (CHANNELS,), 1.0, 6.0),
    }


@jax.custom_vjp
def low(v):
    return lax.optimization_barrier(v.astype(jnp.bfloat16)).astype(jnp.float32)

@jax.custom_vjp
def low_back(v):
    return v

def low_keep(v):
    return (low(v), None)

def low_pass(kept, grad):
    return (grad,)

def back_keep(v):
    return (v, None)

def back_low(kept, grad):
    return (low(grad),)
low.defvjp(low_keep, low_pass)
low_back.defvjp(back_keep, back_low)
HIGH = lax.Precision.HIGHEST
GN_EPS = 1e-06
LN_EPS = 1e-05
NEG_FILL = -1e+30

def product(lhs_rows, rhs_cols):
    return jnp.matmul(lhs_rows, rhs_cols, precision=HIGH)

def group_norm(field, inside, pixel_count, norm_gain, norm_bias):
    channels = field.shape[-1]
    masked = field * inside
    shaped = (field.shape[0] * field.shape[1], GROUPS, channels // GROUPS)
    row_total = lax.optimization_barrier(jnp.sum(masked.reshape(shaped), axis=(0, 2)))
    square = lax.optimization_barrier(jnp.sum((masked * field).reshape(shaped), axis=(0, 2)))
    group_mean = row_total / pixel_count
    inv_std = lax.rsqrt(square / pixel_count - group_mean * group_mean + GN_EPS)
    mean_full = jnp.repeat(group_mean, channels // GROUPS)
    std_full = jnp.repeat(inv_std, channels // GROUPS)
    return (field - mean_full) * std_full * norm_gain + norm_bias

def layer_norm(field, norm_gain, norm_bias):
    centre = lax.optimization_barrier(jnp.mean(field, axis=-1, keepdims=True))
    centred = field - centre
    spread = lax.optimization_barrier(jnp.mean(centred * centred, axis=-1, keepdims=True))
    return centred * lax.rsqrt(spread + LN_EPS) * norm_gain + norm_bias

def convolve(field, weight):
    padded = jnp.pad(low(field), ((1, 1), (1, 1), (0, 0)))
    tap_stack = jnp.concatenate([padded[row_off:row_off + CANVAS, col_off:col_off + CANVAS] for row_off in range(3) for col_off in range(3)], axis=-1)
    return low_back(product(tap_stack, weight))

def time_features(time_step):
    half_dim = TIME_DIM // 2
    frequency = jnp.exp(-math.log(10000.0) * jnp.arange(half_dim, dtype=jnp.float32) / half_dim)
    angles = time_step.astype(jnp.float32) * frequency
    return jnp.concatenate([jnp.cos(angles), jnp.sin(angles)])

def geglu_act(gate_pair):
    return gate_pair[:, :FFN] * jax.nn.gelu(gate_pair[:, FFN:], approximate=False)

def attention(qkv_rows, key_valid):
    tokens = qkv_rows.shape[0]
    shaped = qkv_rows.reshape(tokens, 3, HEADS, CHANNELS // HEADS)
    queries, keys_all, values_all = (shaped[:, 0], shaped[:, 1], shaped[:, 2])
    score_scale = (CHANNELS // HEADS) ** (-0.5)
    block_rows = min(512, tokens)

    def score_block(query_rows):
        scores = low_back(jnp.einsum('qhd,khd->hqk', query_rows, keys_all, precision=HIGH) * score_scale)
        scores = jnp.where(key_valid[None, None, :], scores, NEG_FILL)
        row_max = lax.optimization_barrier(jnp.max(scores, axis=-1, keepdims=True))
        raw_weights = jnp.exp(scores - row_max)
        probs = raw_weights / lax.optimization_barrier(jnp.sum(raw_weights, axis=-1, keepdims=True))
        return jnp.einsum('hqk,khd->qhd', low(probs), values_all, precision=HIGH)
    blocks = queries.reshape(tokens // block_rows, block_rows, HEADS, CHANNELS // HEADS)
    mixed_out = lax.map(jax.checkpoint(score_block), blocks)
    return mixed_out.reshape(tokens, CHANNELS)

def image_pass(params, picture, image_side, image_label, time_step):
    first_gain, first_bias, conv_one, time_proj, time_bias, second_gain, second_bias, conv_two, conv_bias, third_gain, third_bias, proj_in, proj_in_bias, attn_gain, attn_bias, qkv_proj, attn_out, attn_out_bias, class_table, cross_value, cross_out, feed_gain, feed_bias, geglu_proj, geglu_bias, feed_out, feed_out_bias, proj_out, proj_out_bias = params
    positions = jnp.arange(CANVAS, dtype=jnp.int32)
    within = (positions[:, None] < image_side) & (positions[None, :] < image_side)
    inside = within.astype(jnp.float32)[:, :, None]
    pixel_count = (image_side * image_side * (CHANNELS // GROUPS)).astype(jnp.float32)
    start = picture * inside
    act_one = jax.nn.silu(group_norm(start, inside, pixel_count, first_gain, first_bias)) * inside
    time_embed = jax.nn.silu(time_features(time_step))
    time_shift = product(low(time_embed), time_proj)
    hidden_one = convolve(act_one, conv_one) + time_shift + time_bias
    act_two = jax.nn.silu(group_norm(hidden_one, inside, pixel_count, second_gain, second_bias)) * inside
    residual = start + convolve(act_two, conv_two) + conv_bias
    normed = group_norm(residual, inside, pixel_count, third_gain, third_bias)
    flat_in = normed.reshape(CANVAS * CANVAS, CHANNELS)
    stream = low_back(product(low(flat_in), proj_in)) + proj_in_bias
    qkv_rows = low(low_back(product(low(layer_norm(stream, attn_gain, attn_bias)), qkv_proj)))
    mixed_out = low(low_back(attention(qkv_rows, within.reshape(-1))))
    stream = stream + low_back(product(mixed_out, attn_out)) + attn_out_bias
    context = class_table[image_label]
    value_vec = product(context, cross_value)
    stream = stream + product(low(value_vec), cross_out)
    gate_pair = low_back(product(low(layer_norm(stream, feed_gain, feed_bias)), geglu_proj)) + geglu_bias
    gated_hidden = geglu_act(gate_pair)
    stream = stream + low_back(product(low(gated_hidden), feed_out)) + feed_out_bias
    branch = low_back(product(low(stream), proj_out)) + proj_out_bias
    return (residual + branch.reshape(CANVAS, CANVAS, CHANNELS)) * inside

def reference(images, image_sides, labels, timesteps, cotangent, first_gain, first_bias, conv_one, time_proj, time_bias, second_gain, second_bias, conv_two, conv_bias, third_gain, third_bias, proj_in, proj_in_bias, attn_gain, attn_bias, qkv_proj, attn_out, attn_out_bias, class_table, cross_value, cross_out, feed_gain, feed_bias, geglu_proj, geglu_bias, feed_out, feed_out_bias, proj_out, proj_out_bias):
    params = tuple((weight.astype(jnp.float32) for weight in (first_gain, first_bias, conv_one, time_proj, time_bias, second_gain, second_bias, conv_two, conv_bias, third_gain, third_bias, proj_in, proj_in_bias, attn_gain, attn_bias, qkv_proj, attn_out, attn_out_bias, class_table, cross_value, cross_out, feed_gain, feed_bias, geglu_proj, geglu_bias, feed_out, feed_out_bias, proj_out, proj_out_bias)))

    def forward(weights, inputs):

        def per_image(record):
            picture, image_side, image_label, time_step = record
            return image_pass(weights, picture, image_side, image_label, time_step)
        return lax.map(jax.checkpoint(per_image), (inputs, image_sides, labels, timesteps))
    output, pullback = jax.vjp(forward, params, images.astype(jnp.float32))
    weight_grads, grad_images = pullback(cotangent.astype(jnp.float32))
    g01, g02, g03, g04, g05, g06, g07, g08, g09, g10, g11, g12, g13, g14, g15, g16, g17, g18, g19, g20, g21, g22, g23, g24, g25, g26, g27, g28, g29 = weight_grads
    return (output.astype(jnp.bfloat16), grad_images, g01, g02, g03, g04, g05, g06, g07, g08, g09, g10, g11, g12, g13, g14, g15, g16, g17, g18, g19, g20, g21, g22, g23, g24, g25, g26, g27, g28, g29)
```

```python
from functools import partial
import math

import jax
import jax.numpy as jnp
from jax import lax
from jax.experimental import pallas as pl
from jax.experimental.pallas import tpu as pltpu
from jax.sharding import PartitionSpec as P

HEADS = 8
GROUPS = 32


GN_EPS = 1e-06
LN_EPS = 1e-05
HIGH = lax.Precision.HIGHEST


LOG2E = math.log2(math.e)
BF = jnp.bfloat16
F32 = jnp.float32

def dot_nt(lhs, rhs):
    return lax.dot_general(lhs, rhs, (((1,), (1,)), ((), ())), preferred_element_type=F32)


def dot_nn(lhs, rhs):
    return lax.dot_general(lhs, rhs, (((1,), (0,)), ((), ())), preferred_element_type=F32)


def lane_ids(rows):
    return lax.broadcasted_iota(jnp.int32, (rows, 128), 1)


def swap_halves(field):
    return pltpu.roll(field, 64, 1)


def pieces_of(column):
    top = column.astype(BF).astype(F32)
    rest = column - top
    mid = rest.astype(BF).astype(F32)
    return (top, mid, rest - mid)


def extras(column, lanes, first):
    top, mid, low = pieces_of(column)
    return jnp.where(
        lanes == first, top, jnp.where(lanes == first + 1, mid, jnp.where(lanes == first + 2, low, 0.0))
    )


def block_of(count, pref):
    for size in pref:
        if count % size == 0:
            return size
    return count


def crop(field, width, side):
    rows = field.shape[0] // width
    if side == width:
        return field
    return field.reshape(rows, width, 128)[:, :side].reshape(rows * side, 128)


def uncrop(field, width, side):
    if side == width:
        return field
    rows = field.shape[0] // side
    spread = field.reshape(rows, side, 128)
    return jnp.concatenate(
        [spread, jnp.zeros((rows, width - side, 128), field.dtype)], axis=1
    ).reshape(rows * width, 128)


def unpack_pairs(pairs):
    return jnp.concatenate([pairs, swap_halves(pairs)], axis=0)


def pack_pairs(field, lanes):
    half = field.shape[0] // 2
    return jnp.where(lanes[:half] < 64, field[:half], swap_halves(field[half:]))


def attend_kernel(width, scale, side_ref, qkv_ref, out_ref, norm_ref, q_s, k_s, v_s, vt_s, top_s, safe_s):
    bands, packed, _ = qkv_ref.shape
    band_tokens = packed * 2 // 3
    band_rows = band_tokens // width
    side_now = side_ref[0]

    def variant(side):
        tokens = side * side
        used = side // band_rows
        own = band_rows * side
        lanes = lane_ids(own)
        low = lanes < 64
        row_ids = lax.broadcasted_iota(jnp.int32, (128, 128), 0)
        col_ids = lax.broadcasted_iota(jnp.int32, (128, 128), 1)
        picks = jnp.where((row_ids < 64) == (col_ids < 64), 1.0, 0.0).astype(BF)

        def gather_band(band, norms):
            pairs = crop(qkv_ref[band, band_tokens:, :].astype(F32), width, side)
            keys = crop(qkv_ref[band, :band_tokens, :].astype(F32), width, side)
            queries = unpack_pairs(pairs) * (scale * LOG2E)
            head = queries.astype(BF).astype(F32)
            turned = swap_halves(keys)
            rows = pl.ds(pl.multiple_of(band * own, 16), own)
            q_s[rows, :] = jnp.where(low, head, swap_halves(queries - head)).astype(BF)
            k_s[rows, :] = jnp.where(low, keys, turned).astype(BF)
            v_s[rows, :] = jnp.where(low, turned, jnp.where(lanes == 64, 1.0, 0.0)).astype(BF)
            joint = jnp.where(low, queries, turned)
            sums = dot_nn((joint * joint).astype(BF), picks)
            return jnp.maximum(norms, jnp.max(sums, axis=0, keepdims=True))

        norms = lax.fori_loop(0, used, gather_band, jnp.zeros((1, 128), F32))
        step = block_of(tokens, (512, 256))
        for first in range(0, tokens, step):
            vt_s[:, first : first + step] = v_s[first : first + step, :].T
        first_lanes = lane_ids(1) < 64
        query_top = jnp.max(jnp.where(first_lanes, norms, 0.0))
        key_top = jnp.max(jnp.where(first_lanes, 0.0, norms))
        safe = query_top * key_top * 1.05 <= 100.0 * 100.0
        bq = block_of(tokens, (512, 768, 256))
        bk = block_of(tokens, (512, 768, 256))

        @pl.when(safe)
        def _():
            top_s[...] = jnp.zeros_like(top_s)

        @pl.when(jnp.logical_not(safe))
        def _():
            def tops(qi, _):
                cols = pl.ds(pl.multiple_of(qi * bq, 256), bq)
                queries = q_s[cols, :]

                def more(ki, top):
                    scores = dot_nt(k_s[pl.ds(pl.multiple_of(ki * bk, 256), bk), :], queries)
                    return jnp.maximum(top, jnp.max(scores, axis=0, keepdims=True))

                top = lax.fori_loop(0, tokens // bk, more, jnp.full((1, bq), -jnp.inf, F32))
                top_s[:, cols] = jnp.broadcast_to(top, (8, bq))
                return 0

            lax.fori_loop(0, tokens // bq, tops, 0)

        def main(qi, _):
            cols = pl.ds(pl.multiple_of(qi * bq, 256), bq)
            queries = q_s[cols, :]
            top = top_s[0:1, cols]
            total = jnp.zeros((80, bq), F32)
            for first in range(0, tokens, bk):
                scores = dot_nt(k_s[first : first + bk, :], queries)
                weights = jnp.exp2(scores - top).astype(BF)
                total = total + dot_nn(vt_s[0:80, first : first + bk], weights)
            row_total = total[64:65]
            mixed = total[:64] / row_total
            log_total = jnp.broadcast_to(top + jnp.log2(row_total), (64, bq))
            norm_ref[cols, :] = jnp.concatenate([mixed, log_total], axis=0).T
            return 0

        lax.fori_loop(0, tokens // bq, main, 0)

        def spread_band(band, _):
            rows = pl.ds(pl.multiple_of(band * own, 16), own)
            pairs = pack_pairs(norm_ref[rows, :], lanes)
            out_ref[band] = uncrop(pairs, width, side).astype(BF)
            return 0

        lax.fori_loop(0, used, spread_band, 0)
        if used < bands:
            out_ref[used:] = jnp.zeros((bands - used,) + out_ref.shape[1:], BF)

    for side in (width, width * 3 // 4, width // 2):
        pl.when(side_now == side)(partial(variant, side))


def attend(side, qkv, width, scale):
    bands, packed, _ = qkv.shape
    tokens = bands * packed * 2 // 3
    vm = pl.BlockSpec(memory_space=pltpu.VMEM)
    return pl.pallas_call(
        partial(attend_kernel, width, scale),
        out_shape=(
            jax.ShapeDtypeStruct((bands, packed // 3, 128), BF),
            jax.ShapeDtypeStruct((tokens, 128), F32),
        ),
        in_specs=[pl.BlockSpec(memory_space=pltpu.SMEM), vm],
        out_specs=(vm, vm),
        scratch_shapes=[
            pltpu.VMEM((tokens, 128), BF),
            pltpu.VMEM((tokens, 128), BF),
            pltpu.VMEM((tokens, 128), BF),
            pltpu.VMEM((128, tokens), BF),
            pltpu.VMEM((8, tokens), F32),
            pltpu.SMEM((1,), jnp.int32),
        ],
        compiler_params=pltpu.CompilerParams(vmem_limit_bytes=48 << 20),
        cost_estimate=pl.CostEstimate(
            flops=4 * 256 * tokens * tokens, bytes_accessed=8 << 20, transcendentals=tokens * tokens
        ),
        name="attend",
    )(side, qkv)


def attend_back_kernel(width, scale, side_ref, qkv_ref, grad_ref, norm_ref, out_ref,
                       q_s, k_s, kn_s, g_s, v_s, qt_s, gt_s, dq_s, dkv_s):
    bands, packed, _ = qkv_ref.shape
    band_tokens = packed * 2 // 3
    band_rows = band_tokens // width
    side_now = side_ref[0]

    def variant(side):
        tokens = side * side
        used = side // band_rows
        own = band_rows * side
        lanes = lane_ids(own)
        low = lanes < 64
        ones_high = jnp.where((lanes >= 64) & (lanes < 67), 1.0, 0.0)
        ones_low = jnp.where(lanes < 3, 1.0, 0.0).astype(BF)

        def gather_band(band, _):
            queries = unpack_pairs(crop(qkv_ref[band, band_tokens:, :].astype(F32), width, side))
            keys = crop(qkv_ref[band, :band_tokens, :].astype(F32), width, side)
            grads = unpack_pairs(crop(grad_ref[band].astype(F32), width, side))
            rows = pl.ds(pl.multiple_of(band * own, 16), own)
            mixed = norm_ref[rows, :]
            delta = jnp.sum(jnp.where(low, grads * mixed, 0.0), axis=1, keepdims=True)
            log_total = mixed[:, 64:65]
            scaled = queries * (scale * LOG2E)
            head = scaled.astype(BF).astype(F32)
            turned = swap_halves(keys)
            q_s[rows, :128] = jnp.where(low, head, swap_halves(scaled - head)).astype(BF)
            q_s[rows, 128:] = extras(-log_total, lanes, 0).astype(BF)
            k_s[rows, :128] = jnp.where(low, keys, turned).astype(BF)
            k_s[rows, 128:] = ones_low
            kn_s[rows, :] = jnp.where(low, keys, 0.0).astype(BF)
            g_s[rows, :] = jnp.where(low, grads, extras(-delta, lanes, 64)).astype(BF)
            v_s[rows, :] = jnp.where(low, turned, ones_high).astype(BF)
            dq_s[rows, :] = jnp.where(low, queries, swap_halves(grads))
            return 0

        lax.fori_loop(0, used, gather_band, 0)
        step = block_of(tokens, (512, 256))
        for first in range(0, tokens, step):
            turned = dq_s[first : first + step, :].T.astype(BF)
            qt_s[:, first : first + step] = turned[:64]
            gt_s[:, first : first + step] = turned[64:]
        dkv_s[...] = jnp.zeros_like(dkv_s)
        bq = block_of(tokens, (512, 768, 256))
        bk = block_of(tokens, (512, 768, 256))

        def main(qi, _):
            rows = pl.ds(pl.multiple_of(qi * bq, 256), bq)
            queries = q_s[rows, :]
            grads = g_s[rows, :]
            grads_t = gt_s[:, rows]
            queries_t = qt_s[:, rows]
            total = jnp.zeros((bq, 128), F32)
            for first in range(0, tokens, bk):
                probs = jnp.exp2(dot_nt(queries, k_s[first : first + bk, :]))
                slopes = dot_nt(grads, v_s[first : first + bk, :])
                grad_scores = (probs * slopes).astype(BF)
                dkv_s[64:, first : first + bk] += dot_nn(grads_t, probs.astype(BF))
                dkv_s[:64, first : first + bk] += dot_nn(queries_t, grad_scores)
                total = total + dot_nn(grad_scores, kn_s[first : first + bk, :])
            dq_s[rows, :] = total
            return 0

        lax.fori_loop(0, tokens // bq, main, 0)
        for first in range(0, tokens, step):
            turned = dkv_s[:, first : first + step].T
            k_s[first : first + step, :128] = jnp.where(
                lane_ids(step) < 64, turned * scale, turned
            ).astype(BF)

        def spread_band(band, _):
            rows = pl.ds(pl.multiple_of(band * own, 16), own)
            out_ref[band, :band_tokens] = uncrop(k_s[rows, :128], width, side)
            pairs = pack_pairs(dq_s[rows, :] * scale, lanes)
            out_ref[band, band_tokens:] = uncrop(pairs, width, side).astype(BF)
            return 0

        lax.fori_loop(0, used, spread_band, 0)
        if used < bands:
            out_ref[used:] = jnp.zeros((bands - used,) + out_ref.shape[1:], BF)

    for side in (width, width * 3 // 4, width // 2):
        pl.when(side_now == side)(partial(variant, side))


def attend_back(side, qkv, grads, norms, width, scale):
    bands, packed, _ = qkv.shape
    tokens = bands * packed * 2 // 3
    vm = pl.BlockSpec(memory_space=pltpu.VMEM)
    return pl.pallas_call(
        partial(attend_back_kernel, width, scale),
        out_shape=jax.ShapeDtypeStruct((bands, packed, 128), BF),
        in_specs=[pl.BlockSpec(memory_space=pltpu.SMEM), vm, vm, vm],
        out_specs=vm,
        scratch_shapes=[
            pltpu.VMEM((tokens, 256), BF),
            pltpu.VMEM((tokens, 256), BF),
            pltpu.VMEM((tokens, 128), BF),
            pltpu.VMEM((tokens, 128), BF),
            pltpu.VMEM((tokens, 128), BF),
            pltpu.VMEM((64, tokens), BF),
            pltpu.VMEM((64, tokens), BF),
            pltpu.VMEM((tokens, 128), F32),
            pltpu.VMEM((128, tokens), F32),
        ],
        compiler_params=pltpu.CompilerParams(vmem_limit_bytes=56 << 20),
        cost_estimate=pl.CostEstimate(
            flops=10 * 256 * tokens * tokens, bytes_accessed=10 << 20, transcendentals=tokens * tokens
        ),
        name="attend_back",
    )(side, qkv, grads, norms)


def extended(block, sides, width):
    for axis, dim in sides:
        count = lax.axis_size(axis)
        forward = [(i, i + 1) for i in range(count - 1)]
        backward = [(target, source) for source, target in forward]
        low = lax.ppermute(
            lax.slice_in_dim(block, block.shape[dim] - width, None, axis=dim), axis, forward
        )
        high = lax.ppermute(lax.slice_in_dim(block, 0, width, axis=dim), axis, backward)
        block = jnp.concatenate([low, block, high], axis=dim)
    return block


def rounded(field):
    return field.astype(jnp.bfloat16)


def pixel_mask(sides, row_first, row_count, row_width):
    row_ids = row_first + jnp.arange(row_count, dtype=jnp.int32)
    col_ids = jnp.arange(row_width, dtype=jnp.int32)
    limit = sides[:, None, None]
    within = (row_ids[None, :, None] < limit) & (col_ids[None, None, :] < limit)
    return within.astype(jnp.float32)[..., None]


def group_sums(first_term, second_term):
    shaped = (
        first_term.shape[0],
        first_term.shape[1] * first_term.shape[2],
        GROUPS,
        first_term.shape[3] // GROUPS,
    )
    return lax.psum(
        (
            jnp.sum(first_term.reshape(shaped), axis=(1, 3)),
            jnp.sum(second_term.reshape(shaped), axis=(1, 3)),
        ),
        "rows",
    )


def spread_groups(stat, channels):
    return jnp.repeat(stat, channels // GROUPS, axis=1)[:, None, None, :]


def norm_forward(field, inside, pixel_count, norm_gain, norm_bias):
    channels = field.shape[-1]
    masked = field * inside
    row_total, square = group_sums(masked, masked * field)
    group_mean = row_total / pixel_count
    inv_std = spread_groups(
        lax.rsqrt(square / pixel_count - group_mean * group_mean + GN_EPS), channels
    )
    normed = (field - spread_groups(group_mean, channels)) * inv_std
    return (normed * norm_gain + norm_bias, normed, inv_std)


def norm_backward(grad_norm, normed, inv_std, inside, pixel_count, norm_gain):
    channels = normed.shape[-1]
    grad_norm = grad_norm * inside
    scaled = grad_norm * norm_gain
    row_total, crossed = group_sums(scaled, scaled * normed)
    grad_field = (
        inside
        * inv_std
        * (
            scaled
            - spread_groups(row_total / pixel_count, channels)
            - normed * spread_groups(crossed / pixel_count, channels)
        )
    )
    return (
        grad_field,
        jnp.sum(grad_norm * normed, axis=(0, 1, 2)),
        jnp.sum(grad_norm, axis=(0, 1, 2)),
    )


def layer_norm(field, norm_gain, norm_bias):
    centre = jnp.mean(field, axis=-1, keepdims=True)
    centred = field - centre
    spread = jnp.mean(centred * centred, axis=-1, keepdims=True)
    return centred * lax.rsqrt(spread + LN_EPS) * norm_gain + norm_bias


def geglu_act(gate_pair):
    half_dim = gate_pair.shape[-1] // 2
    return gate_pair[..., :half_dim] * jax.nn.gelu(gate_pair[..., half_dim:], approximate=False)


def conv_taps(field, flipped):
    padded = extended(field, (("rows", 1),), 1)
    padded = jnp.pad(padded, ((0, 0), (0, 0), (1, 1), (0, 0)))
    band_rows, row_width = (field.shape[1], field.shape[2])
    offsets = [
        (2 - row_off, 2 - col_off) if flipped else (row_off, col_off)
        for row_off in range(3)
        for col_off in range(3)
    ]
    return jnp.stack(
        [
            padded[:, top_row : top_row + band_rows, left_col : left_col + row_width, :]
            for top_row, left_col in offsets
        ],
        axis=3,
    )


def conv_apply(tap_stack, weight):
    channels = tap_stack.shape[-1]
    return jnp.einsum(
        "brwtc,tco->brwo",
        tap_stack,
        weight.reshape(9, channels, -1),
        preferred_element_type=jnp.float32,
    )


def conv_weight_grad(tap_stack, grads_low):
    channels = tap_stack.shape[-1]
    return jnp.einsum(
        "brwtc,brwo->tco", tap_stack, grads_low, preferred_element_type=jnp.float32
    ).reshape(9 * channels, -1)


def conv_back(grads_low, weight):
    channels = grads_low.shape[-1]
    return jnp.einsum(
        "brwtc,tic->brwi",
        conv_taps(grads_low, True),
        weight.reshape(9, channels, channels),
        preferred_element_type=jnp.float32,
    )


def tokens_dot(inputs_low, weight):
    return jnp.einsum("blc,co->blo", inputs_low, weight, preferred_element_type=jnp.float32)


def weight_grad(inputs_low, grads_low):
    return jnp.einsum("blc,blo->co", inputs_low, grads_low, preferred_element_type=jnp.float32)


def back_dot(grads_low, weight):
    return jnp.einsum("blo,co->blc", grads_low, weight, preferred_element_type=jnp.float32)


def time_features(time_steps, dims):
    half_dim = dims // 2
    frequency = jnp.exp(-math.log(10000.0) * jnp.arange(half_dim, dtype=jnp.float32) / half_dim)
    angles = time_steps.astype(jnp.float32)[:, None] * frequency[None, :]
    return jnp.concatenate([jnp.cos(angles), jnp.sin(angles)], axis=-1)


def pack_tokens(field):
    turned = jnp.transpose(field, (2, 0, 1, 3))
    half = turned.shape[2] // 2
    return jnp.concatenate([turned[:, :, :half], turned[:, :, half:]], axis=-1)


def pack_rows(queries, keys, values):
    joint = jnp.transpose(jnp.concatenate([keys, values], axis=-1), (2, 0, 1, 3))
    return jnp.concatenate([joint, pack_tokens(queries)], axis=2)


def unpack_tokens(pairs):
    heads, images, half, _ = pairs.shape
    joint = jnp.concatenate([pairs[..., :64], pairs[..., 64:]], axis=2)
    return jnp.transpose(joint, (1, 2, 0, 3)).reshape(images, 2 * half, heads * 64)


def to_items(sent, bands):
    heads, images, packed, lanes = sent.shape
    per_band = heads * images // bands
    items = sent.reshape(bands, per_band, packed, lanes)
    chunks = [
        lax.all_to_all(items[:, at], "rows", split_axis=0, concat_axis=0, tiled=True)
        for at in range(per_band)
    ]
    return chunks, lax.axis_index("rows") * per_band


def from_items(results, images):
    bands = results[0].shape[0]
    back = [
        lax.all_to_all(result, "rows", split_axis=0, concat_axis=0, tiled=True)
        for result in results
    ]
    joint = jnp.stack(back, axis=1)
    return joint.reshape((HEADS, images) + joint.shape[2:])


def per_device(
    images,
    image_sides,
    labels,
    timesteps,
    cotangent,
    first_gain,
    first_bias,
    conv_one,
    time_proj,
    time_bias,
    second_gain,
    second_bias,
    conv_two,
    conv_bias,
    third_gain,
    third_bias,
    proj_in,
    proj_in_bias,
    attn_gain,
    attn_bias,
    qkv_proj,
    attn_out,
    attn_out_bias,
    class_table,
    cross_value,
    cross_out,
    feed_gain,
    feed_bias,
    geglu_proj,
    geglu_bias,
    feed_out,
    feed_out_bias,
    proj_out,
    proj_out_bias,
):
    image_count, band_rows, row_width, channels = images.shape
    tokens = band_rows * row_width
    head_dim = channels // HEADS
    score_scale = head_dim ** (-0.5)
    first_image = lax.axis_index("heads") * image_count
    first_row = lax.axis_index("rows") * band_rows
    own_sides = lax.dynamic_slice_in_dim(image_sides, first_image, image_count)
    own_labels = lax.dynamic_slice_in_dim(labels, first_image, image_count)
    own_steps = lax.dynamic_slice_in_dim(timesteps, first_image, image_count)
    inside = pixel_mask(own_sides, first_row, band_rows, row_width)
    pixel_count = (own_sides * own_sides * (channels // GROUPS)).astype(jnp.float32)[:, None]
    start = images.astype(jnp.float32) * inside
    norm_one, normed_one, std_one = norm_forward(start, inside, pixel_count, first_gain, first_bias)
    act_one = rounded(jax.nn.silu(norm_one) * inside)
    taps_one = conv_taps(act_one, False)
    time_embed = rounded(jax.nn.silu(time_features(own_steps, time_proj.shape[0])))
    time_shift = jnp.dot(time_embed, time_proj, preferred_element_type=jnp.float32)
    hidden_one = conv_apply(taps_one, conv_one) + time_shift[:, None, None, :] + time_bias
    norm_two, normed_two, std_two = norm_forward(
        hidden_one, inside, pixel_count, second_gain, second_bias
    )
    act_two = rounded(jax.nn.silu(norm_two) * inside)
    taps_two = conv_taps(act_two, False)
    residual = start + conv_apply(taps_two, conv_two) + conv_bias
    norm_three, normed_three, std_three = norm_forward(
        residual, inside, pixel_count, third_gain, third_bias
    )
    flat_in = rounded(norm_three.reshape(image_count, tokens, channels))
    stream = tokens_dot(flat_in, proj_in) + proj_in_bias
    attn_in = rounded(layer_norm(stream, attn_gain, attn_bias))
    bands = lax.axis_size("rows")
    qkv_rows = rounded(tokens_dot(attn_in, qkv_proj)).reshape(
        image_count, tokens, 3, HEADS, head_dim
    )
    sent = pack_rows(qkv_rows[:, :, 0], qkv_rows[:, :, 1], qkv_rows[:, :, 2])
    chunks, first_item = to_items(sent, bands)
    item_sides = [
        lax.dynamic_slice_in_dim(own_sides, lax.rem(first_item + at, image_count), 1)
        for at in range(len(chunks))
    ]
    attended = [
        attend(side, chunk, row_width, score_scale) for side, chunk in zip(item_sides, chunks)
    ]
    mixed_out = from_items([pairs for pairs, _ in attended], image_count)
    mixed_out = unpack_tokens(mixed_out)
    stream_two = stream + tokens_dot(mixed_out, attn_out) + attn_out_bias
    one_hot = rounded(
        (own_labels[:, None] == jnp.arange(class_table.shape[0], dtype=jnp.int32)[None, :]).astype(
            jnp.float32
        )
    )
    context = jnp.dot(one_hot, class_table, preferred_element_type=jnp.float32)
    value_vec = jnp.dot(rounded(context), cross_value, preferred_element_type=jnp.float32)
    value_low = rounded(value_vec)
    cross_term = jnp.dot(value_low, cross_out, preferred_element_type=jnp.float32)
    stream_three = stream_two + cross_term[:, None, :]
    feed_in = rounded(layer_norm(stream_three, feed_gain, feed_bias))
    gate_pair = tokens_dot(feed_in, geglu_proj) + geglu_bias
    gated_hidden = rounded(geglu_act(gate_pair))
    stream_four = stream_three + tokens_dot(gated_hidden, feed_out) + feed_out_bias
    last_in = rounded(stream_four)
    branch = tokens_dot(last_in, proj_out) + proj_out_bias
    output = (residual + branch.reshape(images.shape)) * inside
    grad_out = cotangent.astype(jnp.float32) * inside
    grad_branch = grad_out.reshape(image_count, tokens, channels)
    grad_proj_out_bias = jnp.sum(grad_branch, axis=(0, 1))
    low_branch = rounded(grad_branch)
    grad_proj_out = weight_grad(last_in, low_branch)
    grad_four = back_dot(low_branch, proj_out)
    grad_feed_out_bias = jnp.sum(grad_four, axis=(0, 1))
    low_feed = rounded(grad_four)
    grad_feed_out = weight_grad(gated_hidden, low_feed)
    grad_gated = back_dot(low_feed, feed_out)
    geglu_value, geglu_pull = jax.vjp(geglu_act, gate_pair)
    grad_pair = geglu_pull(grad_gated)[0]
    grad_geglu_bias = jnp.sum(grad_pair, axis=(0, 1))
    low_pair = rounded(grad_pair)
    grad_geglu_proj = weight_grad(feed_in, low_pair)
    feed_value, feed_pull = jax.vjp(
        layer_norm, stream_three, feed_gain.astype(jnp.float32), feed_bias.astype(jnp.float32)
    )
    norm_part, grad_feed_gain, grad_feed_bias = feed_pull(back_dot(low_pair, geglu_proj))
    grad_three = grad_four + norm_part
    grad_cross = jnp.sum(grad_three, axis=1)
    grad_attn_out_bias = jnp.sum(grad_three, axis=(0, 1))
    low_attn = rounded(grad_three)
    grad_attn_out = weight_grad(mixed_out, low_attn)
    grad_mixed = rounded(back_dot(low_attn, attn_out)).reshape(
        image_count, tokens, HEADS, head_dim
    )
    grad_chunks, _ = to_items(pack_tokens(grad_mixed), bands)
    grad_qkv = from_items(
        [
            attend_back(side, chunk, grad_chunk, norms, row_width, score_scale)
            for side, chunk, grad_chunk, (_, norms) in zip(
                item_sides, chunks, grad_chunks, attended
            )
        ],
        image_count,
    )
    grad_queries = unpack_tokens(grad_qkv[:, :, tokens:])
    grad_keys = jnp.transpose(grad_qkv[:, :, :tokens, :64], (1, 2, 0, 3)).reshape(
        image_count, tokens, channels
    )
    grad_values = jnp.transpose(grad_qkv[:, :, :tokens, 64:], (1, 2, 0, 3)).reshape(
        image_count, tokens, channels
    )
    grad_qkv = jnp.concatenate([grad_queries, grad_keys, grad_values], axis=-1)
    grad_qkv_proj = weight_grad(attn_in, grad_qkv)
    attn_value, attn_pull = jax.vjp(
        layer_norm, stream, attn_gain.astype(jnp.float32), attn_bias.astype(jnp.float32)
    )
    norm_part, grad_attn_gain, grad_attn_bias = attn_pull(back_dot(grad_qkv, qkv_proj))
    grad_stream = grad_three + norm_part
    grad_proj_in_bias = jnp.sum(grad_stream, axis=(0, 1))
    low_in = rounded(grad_stream)
    grad_proj_in = weight_grad(flat_in, low_in)
    grad_norm_three = back_dot(low_in, proj_in).reshape(images.shape)
    resid_part, grad_third_gain, grad_third_bias = norm_backward(
        grad_norm_three, normed_three, std_three, inside, pixel_count, third_gain
    )
    grad_residual = grad_out + resid_part
    grad_conv_bias = jnp.sum(grad_residual, axis=(0, 1, 2))
    low_two = rounded(grad_residual)
    grad_conv_two = conv_weight_grad(taps_two, low_two)
    grad_act_two = conv_back(low_two, conv_two)
    silu_two, silu_pull_two = jax.vjp(jax.nn.silu, norm_two)
    grad_norm_two = silu_pull_two(grad_act_two * inside)[0]
    grad_hidden, grad_second_gain, grad_second_bias = norm_backward(
        grad_norm_two, normed_two, std_two, inside, pixel_count, second_gain
    )
    grad_shift = jnp.sum(grad_hidden, axis=(1, 2))
    low_one = rounded(grad_hidden)
    grad_conv_one = conv_weight_grad(taps_one, low_one)
    grad_act_one = conv_back(low_one, conv_one)
    silu_one, silu_pull_one = jax.vjp(jax.nn.silu, norm_one)
    grad_norm_one = silu_pull_one(grad_act_one * inside)[0]
    start_part, grad_first_gain, grad_first_bias = norm_backward(
        grad_norm_one, normed_one, std_one, inside, pixel_count, first_gain
    )
    grad_images = (grad_residual + start_part) * inside
    me = lax.axis_index("rows")

    def own(field, axis=0):
        size = field.shape[axis] // bands
        return lax.dynamic_slice_in_dim(field, me * size, size, axis)

    per_image = lax.psum(jnp.stack([grad_cross, grad_shift]), "rows")
    per_image = lax.all_gather(per_image, "heads", axis=1, tiled=True)
    all_cross, all_shift = per_image[0], per_image[1]
    all_hot = rounded(
        (labels[:, None] == jnp.arange(class_table.shape[0], dtype=jnp.int32)[None, :]).astype(
            jnp.float32
        )
    )
    all_context = jnp.dot(all_hot, class_table, preferred_element_type=jnp.float32)
    all_value = rounded(
        jnp.dot(rounded(all_context), cross_value, preferred_element_type=jnp.float32)
    ).astype(jnp.float32)
    all_embed = rounded(jax.nn.silu(time_features(timesteps, time_proj.shape[0])))
    grad_cross_out = jnp.dot(own(all_value, 1).T, all_cross, precision=HIGH)
    grad_value = jnp.dot(all_cross, cross_out.astype(jnp.float32).T, precision=HIGH)
    grad_cross_value = jnp.dot(own(all_context, 1).T, grad_value, precision=HIGH)
    grad_context = jnp.dot(grad_value, own(cross_value).astype(jnp.float32).T, precision=HIGH)
    grad_class_table = jnp.dot(all_hot.astype(jnp.float32).T, grad_context, precision=HIGH)
    grad_time_proj = jnp.dot(
        own(all_embed.astype(jnp.float32), 1).T, all_shift, precision=HIGH
    )
    vectors = [
        grad_first_gain,
        grad_first_bias,
        grad_second_gain,
        grad_second_bias,
        grad_conv_bias,
        grad_third_gain,
        grad_third_bias,
        grad_proj_in_bias,
        grad_attn_gain,
        grad_attn_bias,
        grad_attn_out_bias,
        grad_feed_gain,
        grad_feed_bias,
        grad_feed_out_bias,
        grad_proj_out_bias,
    ]
    joint = lax.psum(
        jnp.concatenate([v.reshape(-1, channels) for v in vectors + [grad_geglu_bias]]),
        ("rows", "heads"),
    )
    (
        grad_first_gain,
        grad_first_bias,
        grad_second_gain,
        grad_second_bias,
        grad_conv_bias,
        grad_third_gain,
        grad_third_bias,
        grad_proj_in_bias,
        grad_attn_gain,
        grad_attn_bias,
        grad_attn_out_bias,
        grad_feed_gain,
        grad_feed_bias,
        grad_feed_out_bias,
        grad_proj_out_bias,
    ) = [own(joint[at]) for at in range(len(vectors))]
    grad_geglu_bias = own(joint[len(vectors) :].reshape(-1))

    def reduced(field):
        part = lax.psum_scatter(rounded(field), "rows", scatter_dimension=0, tiled=True)
        return lax.psum(part, "heads").astype(jnp.float32)

    return (
        rounded(output),
        grad_images,
        grad_first_gain,
        grad_first_bias,
        reduced(grad_conv_one),
        grad_time_proj,
        own(jnp.sum(all_shift, axis=0)),
        grad_second_gain,
        grad_second_bias,
        reduced(grad_conv_two),
        grad_conv_bias,
        grad_third_gain,
        grad_third_bias,
        reduced(grad_proj_in),
        grad_proj_in_bias,
        grad_attn_gain,
        grad_attn_bias,
        reduced(grad_qkv_proj),
        reduced(grad_attn_out),
        grad_attn_out_bias,
        grad_class_table,
        grad_cross_value,
        grad_cross_out,
        grad_feed_gain,
        grad_feed_bias,
        reduced(grad_geglu_proj),
        grad_geglu_bias,
        reduced(grad_feed_out),
        grad_feed_out_bias,
        reduced(grad_proj_out),
        grad_proj_out_bias,
    )


def solution(mesh):
    return jax.shard_map(
        per_device,
        mesh=mesh,
        in_specs=(
            P("heads", "rows", None, None),
            P(),
            P(),
            P(),
            P("heads", "rows", None, None),
            P(),
            P(),
            P(),
            P(),
            P(),
            P(),
            P(),
            P(),
            P(),
            P(),
            P(),
            P(),
            P(),
            P(),
            P(),
            P(),
            P(),
            P(),
            P(),
            P(),
            P(),
            P(),
            P(),
            P(),
            P(),
            P(),
            P(),
            P(),
            P(),
        ),
        out_specs=(
            P("heads", "rows", None, None),
            P("heads", "rows", None, None),
            P("rows"),
            P("rows"),
            P("rows", None),
            P("rows", None),
            P("rows"),
            P("rows"),
            P("rows"),
            P("rows", None),
            P("rows"),
            P("rows"),
            P("rows"),
            P("rows", None),
            P("rows"),
            P("rows"),
            P("rows"),
            P("rows", None),
            P("rows", None),
            P("rows"),
            P(None, "rows"),
            P("rows", None),
            P("rows", None),
            P("rows"),
            P("rows"),
            P("rows", None),
            P("rows"),
            P("rows", None),
            P("rows"),
            P("rows", None),
            P("rows"),
        ),
        check_vma=False,
    )
```

```python
from functools import partial
import math

import jax
import jax.numpy as jnp
from jax import lax
from jax.experimental import pallas as pl
from jax.experimental.pallas import tpu as pltpu
from jax.sharding import PartitionSpec as P

HEADS = 8
GROUPS = 32
GN_EPS = 1e-06
LN_EPS = 1e-05
HIGH = lax.Precision.HIGHEST
LOG2E = math.log2(math.e)
BF = jnp.bfloat16
F32 = jnp.float32

def dot_nt(lhs, rhs):
    return lax.dot_general(lhs, rhs, (((1,), (1,)), ((), ())), preferred_element_type=F32)


def dot_nn(lhs, rhs):
    return lax.dot_general(lhs, rhs, (((1,), (0,)), ((), ())), preferred_element_type=F32)


def lane_ids(rows):
    return lax.broadcasted_iota(jnp.int32, (rows, 128), 1)


def swap_halves(field):
    return pltpu.roll(field, 64, 1)


def pieces_of(column):
    top = column.astype(BF).astype(F32)
    rest = column - top
    mid = rest.astype(BF).astype(F32)
    return (top, mid, rest - mid)


def extras(column, lanes, first):
    top, mid, low = pieces_of(column)
    return jnp.where(
        lanes == first, top, jnp.where(lanes == first + 1, mid, jnp.where(lanes == first + 2, low, 0.0))
    )


def block_of(count, pref):
    for size in pref:
        if count % size == 0:
            return size
    return count


def crop(field, width, side):
    rows = field.shape[0] // width
    if side == width:
        return field
    return field.reshape(rows, width, 128)[:, :side].reshape(rows * side, 128)


def uncrop(field, width, side):
    if side == width:
        return field
    rows = field.shape[0] // side
    spread = field.reshape(rows, side, 128)
    return jnp.concatenate(
        [spread, jnp.zeros((rows, width - side, 128), field.dtype)], axis=1
    ).reshape(rows * width, 128)


def unpack_pairs(pairs):
    return jnp.concatenate([pairs, swap_halves(pairs)], axis=0)


def pack_pairs(field, lanes):
    half = field.shape[0] // 2
    return jnp.where(lanes[:half] < 64, field[:half], swap_halves(field[half:]))


def attend_kernel(width, scale, side_ref, qkv_ref, out_ref, norm_ref, q_s, k_s, v_s, vt_s, top_s, safe_s):
    bands, packed, _ = qkv_ref.shape
    band_tokens = packed * 2 // 3
    band_rows = band_tokens // width
    side_now = side_ref[0]

    def variant(side):
        tokens = side * side
        used = side // band_rows
        own = band_rows * side
        lanes = lane_ids(own)
        low = lanes < 64
        row_ids = lax.broadcasted_iota(jnp.int32, (128, 128), 0)
        col_ids = lax.broadcasted_iota(jnp.int32, (128, 128), 1)
        picks = jnp.where((row_ids < 64) == (col_ids < 64), 1.0, 0.0).astype(BF)

        def gather_band(band, norms):
            pairs = crop(qkv_ref[band, band_tokens:, :].astype(F32), width, side)
            keys = crop(qkv_ref[band, :band_tokens, :].astype(F32), width, side)
            queries = unpack_pairs(pairs) * (scale * LOG2E)
            head = queries.astype(BF).astype(F32)
            turned = swap_halves(keys)
            rows = pl.ds(pl.multiple_of(band * own, 16), own)
            q_s[rows, :] = jnp.where(low, head, swap_halves(queries - head)).astype(BF)
            k_s[rows, :] = jnp.where(low, keys, turned).astype(BF)
            v_s[rows, :] = jnp.where(low, turned, jnp.where(lanes == 64, 1.0, 0.0)).astype(BF)
            joint = jnp.where(low, queries, turned)
            sums = dot_nn((joint * joint).astype(BF), picks)
            return jnp.maximum(norms, jnp.max(sums, axis=0, keepdims=True))

        norms = lax.fori_loop(0, used, gather_band, jnp.zeros((1, 128), F32))
        step = block_of(tokens, (512, 256))
        for first in range(0, tokens, step):
            vt_s[:, first : first + step] = v_s[first : first + step, :].T
        first_lanes = lane_ids(1) < 64
        query_top = jnp.max(jnp.where(first_lanes, norms, 0.0))
        key_top = jnp.max(jnp.where(first_lanes, 0.0, norms))
        safe = query_top * key_top * 1.05 <= 100.0 * 100.0
        bq = block_of(tokens, (512, 768, 256))
        bk = block_of(tokens, (512, 768, 256))

        @pl.when(safe)
        def _():
            top_s[...] = jnp.zeros_like(top_s)

        @pl.when(jnp.logical_not(safe))
        def _():
            def tops(qi, _):
                cols = pl.ds(pl.multiple_of(qi * bq, 256), bq)
                queries = q_s[cols, :]

                def more(ki, top):
                    scores = dot_nt(k_s[pl.ds(pl.multiple_of(ki * bk, 256), bk), :], queries)
                    return jnp.maximum(top, jnp.max(scores, axis=0, keepdims=True))

                top = lax.fori_loop(0, tokens // bk, more, jnp.full((1, bq), -jnp.inf, F32))
                top_s[:, cols] = jnp.broadcast_to(top, (8, bq))
                return 0

            lax.fori_loop(0, tokens // bq, tops, 0)

        def main(qi, _):
            cols = pl.ds(pl.multiple_of(qi * bq, 256), bq)
            queries = q_s[cols, :]
            top = top_s[0:1, cols]
            total = jnp.zeros((80, bq), F32)
            for first in range(0, tokens, bk):
                scores = dot_nt(k_s[first : first + bk, :], queries)
                weights = jnp.exp2(scores - top).astype(BF)
                total = total + dot_nn(vt_s[0:80, first : first + bk], weights)
            row_total = total[64:65]
            mixed = total[:64] / row_total
            log_total = jnp.broadcast_to(top + jnp.log2(row_total), (64, bq))
            norm_ref[cols, :] = jnp.concatenate([mixed, log_total], axis=0).T
            return 0

        lax.fori_loop(0, tokens // bq, main, 0)

        def spread_band(band, _):
            rows = pl.ds(pl.multiple_of(band * own, 16), own)
            pairs = pack_pairs(norm_ref[rows, :], lanes)
            out_ref[band] = uncrop(pairs, width, side).astype(BF)
            return 0

        lax.fori_loop(0, used, spread_band, 0)
        if used < bands:
            out_ref[used:] = jnp.zeros((bands - used,) + out_ref.shape[1:], BF)

    for side in (width, width * 3 // 4, width // 2):
        pl.when(side_now == side)(partial(variant, side))


def attend(side, qkv, width, scale):
    bands, packed, _ = qkv.shape
    tokens = bands * packed * 2 // 3
    vm = pl.BlockSpec(memory_space=pltpu.VMEM)
    return pl.pallas_call(
        partial(attend_kernel, width, scale),
        out_shape=(
            jax.ShapeDtypeStruct((bands, packed // 3, 128), BF),
            jax.ShapeDtypeStruct((tokens, 128), F32),
        ),
        in_specs=[pl.BlockSpec(memory_space=pltpu.SMEM), vm],
        out_specs=(vm, vm),
        scratch_shapes=[
            pltpu.VMEM((tokens, 128), BF),
            pltpu.VMEM((tokens, 128), BF),
            pltpu.VMEM((tokens, 128), BF),
            pltpu.VMEM((128, tokens), BF),
            pltpu.VMEM((8, tokens), F32),
            pltpu.SMEM((1,), jnp.int32),
        ],
        compiler_params=pltpu.CompilerParams(vmem_limit_bytes=48 << 20),
        cost_estimate=pl.CostEstimate(
            flops=4 * 256 * tokens * tokens, bytes_accessed=8 << 20, transcendentals=tokens * tokens
        ),
        name="attend",
    )(side, qkv)


def attend_back_kernel(width, scale, side_ref, qkv_ref, grad_ref, norm_ref, out_ref,
                       q_s, k_s, kn_s, g_s, v_s, qt_s, gt_s, dq_s, dkv_s):
    bands, packed, _ = qkv_ref.shape
    band_tokens = packed * 2 // 3
    band_rows = band_tokens // width
    side_now = side_ref[0]

    def variant(side):
        tokens = side * side
        used = side // band_rows
        own = band_rows * side
        lanes = lane_ids(own)
        low = lanes < 64
        ones_high = jnp.where((lanes >= 64) & (lanes < 67), 1.0, 0.0)
        ones_low = jnp.where(lanes < 3, 1.0, 0.0).astype(BF)

        def gather_band(band, _):
            queries = unpack_pairs(crop(qkv_ref[band, band_tokens:, :].astype(F32), width, side))
            keys = crop(qkv_ref[band, :band_tokens, :].astype(F32), width, side)
            grads = unpack_pairs(crop(grad_ref[0, band].astype(F32), width, side))
            rows = pl.ds(pl.multiple_of(band * own, 16), own)
            mixed = norm_ref[rows, :]
            delta = jnp.sum(jnp.where(low, grads * mixed, 0.0), axis=1, keepdims=True)
            log_total = mixed[:, 64:65]
            scaled = queries * (scale * LOG2E)
            head = scaled.astype(BF).astype(F32)
            turned = swap_halves(keys)
            q_s[rows, :128] = jnp.where(low, head, swap_halves(scaled - head)).astype(BF)
            q_s[rows, 128:] = extras(-log_total, lanes, 0).astype(BF)
            k_s[rows, :128] = jnp.where(low, keys, turned).astype(BF)
            k_s[rows, 128:] = ones_low
            kn_s[rows, :] = jnp.where(low, keys, 0.0).astype(BF)
            g_s[rows, :] = jnp.where(low, grads, extras(-delta, lanes, 64)).astype(BF)
            v_s[rows, :] = jnp.where(low, turned, ones_high).astype(BF)
            dq_s[rows, :] = jnp.where(low, queries, swap_halves(grads))
            return 0

        lax.fori_loop(0, used, gather_band, 0)
        step = block_of(tokens, (512, 256))
        for first in range(0, tokens, step):
            turned = dq_s[first : first + step, :].T.astype(BF)
            qt_s[:, first : first + step] = turned[:64]
            gt_s[:, first : first + step] = turned[64:]
        dkv_s[...] = jnp.zeros_like(dkv_s)
        bq = block_of(tokens, (512, 768, 256))
        bk = block_of(tokens, (512, 768, 256))

        def main(qi, _):
            rows = pl.ds(pl.multiple_of(qi * bq, 256), bq)
            queries = q_s[rows, :]
            grads = g_s[rows, :]
            grads_t = gt_s[:, rows]
            queries_t = qt_s[:, rows]
            total = jnp.zeros((bq, 128), F32)
            for first in range(0, tokens, bk):
                probs = jnp.exp2(dot_nt(queries, k_s[first : first + bk, :]))
                slopes = dot_nt(grads, v_s[first : first + bk, :])
                grad_scores = (probs * slopes).astype(BF)
                dkv_s[64:, first : first + bk] += dot_nn(grads_t, probs.astype(BF))
                dkv_s[:64, first : first + bk] += dot_nn(queries_t, grad_scores)
                total = total + dot_nn(grad_scores, kn_s[first : first + bk, :])
            dq_s[rows, :] = total
            return 0

        lax.fori_loop(0, tokens // bq, main, 0)
        for first in range(0, tokens, step):
            turned = dkv_s[:, first : first + step].T
            k_s[first : first + step, :128] = jnp.where(
                lane_ids(step) < 64, turned * scale, turned
            ).astype(BF)

        def spread_band(band, _):
            rows = pl.ds(pl.multiple_of(band * own, 16), own)
            out_ref[band, :band_tokens] = uncrop(k_s[rows, :128], width, side)
            pairs = pack_pairs(dq_s[rows, :] * scale, lanes)
            out_ref[band, band_tokens:] = uncrop(pairs, width, side).astype(BF)
            return 0

        lax.fori_loop(0, used, spread_band, 0)
        if used < bands:
            out_ref[used:] = jnp.zeros((bands - used,) + out_ref.shape[1:], BF)

    for side in (width, width * 3 // 4, width // 2):
        pl.when(side_now == side)(partial(variant, side))


def attend_back(side, qkv, grads, spot, norms, width, scale):
    bands, packed, _ = qkv.shape
    tokens = bands * packed * 2 // 3
    vm = pl.BlockSpec(memory_space=pltpu.VMEM)
    return pl.pallas_call(
        partial(attend_back_kernel, width, scale),
        out_shape=jax.ShapeDtypeStruct((bands, packed, 128), BF),
        grid=(1,),
        in_specs=[
            pl.BlockSpec(memory_space=pltpu.SMEM),
            vm,
            pl.BlockSpec((1,) + grads.shape[1:], lambda at: (spot, 0, 0, 0)),
            vm,
        ],
        out_specs=vm,
        scratch_shapes=[
            pltpu.VMEM((tokens, 256), BF),
            pltpu.VMEM((tokens, 256), BF),
            pltpu.VMEM((tokens, 128), BF),
            pltpu.VMEM((tokens, 128), BF),
            pltpu.VMEM((tokens, 128), BF),
            pltpu.VMEM((64, tokens), BF),
            pltpu.VMEM((64, tokens), BF),
            pltpu.VMEM((tokens, 128), F32),
            pltpu.VMEM((128, tokens), F32),
        ],
        compiler_params=pltpu.CompilerParams(vmem_limit_bytes=56 << 20),
        cost_estimate=pl.CostEstimate(
            flops=10 * 256 * tokens * tokens, bytes_accessed=10 << 20, transcendentals=tokens * tokens
        ),
        name="attend_back",
    )(side, qkv, grads, norms)


def dot_tn(lhs, rhs):
    return lax.dot_general(lhs, rhs, (((0,), (0,)), ((), ())), preferred_element_type=F32)


def row_of(table, at):
    ids = lax.broadcasted_iota(jnp.int32, table.shape, 0)
    return jnp.sum(jnp.where(ids == at, table, 0.0), axis=0, keepdims=True)


def put_row(table_ref, at, row):
    ids = lax.broadcasted_iota(jnp.int32, table_ref.shape, 0)
    table_ref[...] = jnp.where(ids == at, row, table_ref[...])


def col_sum(field):
    return jnp.sum(field, axis=0, keepdims=True)


def pixel_inside(shape, first_row, side, width):
    token = lax.broadcasted_iota(jnp.int32, shape, 0)
    row = first_row + lax.shift_right_logical(token, int(math.log2(width)))
    return (row >= 0) & (row < side) & ((token & (width - 1)) < side)


def moments(avg_ref, at):
    table = avg_ref[...]
    mean = row_of(table, 2 * at)
    return mean, lax.rsqrt(row_of(table, 2 * at + 1) - mean * mean + GN_EPS)


def put_taps(taps_s, first, field, width, flipped):
    channels = field.shape[1]
    column = lax.broadcasted_iota(jnp.int32, field.shape, 0) & (width - 1)
    count = field.shape[0]
    left = jnp.where(column == 0, 0.0, pltpu.roll(field, 1, 0))
    right = jnp.where(column == width - 1, 0.0, pltpu.roll(field, count - 1, 0))
    order = (right, field, left) if flipped else (left, field, right)
    for at, part in enumerate(order):
        taps_s[first : first + count, at * channels : (at + 1) * channels] = part.astype(BF)


VMEM_WHOLE = pl.BlockSpec(memory_space=pltpu.VMEM)
SMEM_WHOLE = pl.BlockSpec(memory_space=pltpu.SMEM)


def image_block(tokens, channels):
    return pl.BlockSpec((1, tokens, channels), lambda at: (at, 0, 0))


def edge_block(width, channels):
    return pl.BlockSpec((2, 1, width, channels), lambda at: (0, at, 0, 0))


def table_block(channels, rows=8):
    return pl.BlockSpec((rows, channels), lambda at: (0, 0))


def fixed_block(shape):
    return pl.BlockSpec(shape, lambda at: (0,) * len(shape), pipeline_mode=pl.Buffered(1))


def conv_forward_kernel(width, base_given, *refs):
    if base_given:
        (place, sides, field_ref, halo_ref, avg_ref, gain_ref, bias_ref, weight_ref, shift_ref,
         base_ref, out_ref, edge_ref, stats_ref, taps_s) = refs
    else:
        (place, sides, field_ref, halo_ref, avg_ref, gain_ref, bias_ref, weight_ref, shift_ref,
         out_ref, edge_ref, stats_ref, taps_s) = refs
    at = pl.program_id(0)
    _, tokens, channels = field_ref.shape
    first_row = place[0]
    side = sides[at]
    mean, inv_std = moments(avg_ref, at)
    slope = inv_std * gain_ref[...]
    offset = bias_ref[...] - mean * slope

    def active(field, row):
        normed = field.astype(F32) * slope + offset
        inside = pixel_inside(normed.shape, row, side, width)
        return jnp.where(inside, normed * jax.nn.sigmoid(normed), 0.0)

    rows = tokens // width
    put_taps(taps_s, 0, active(halo_ref[0, 0], first_row - 1), width, False)
    put_taps(taps_s, width, active(field_ref[0], first_row), width, False)
    put_taps(taps_s, width + tokens, active(halo_ref[1, 0], first_row + rows), width, False)
    deep = 3 * channels
    total = dot_nn(taps_s[:tokens], weight_ref[:deep])
    for tap in (1, 2):
        total = total + dot_nn(
            taps_s[tap * width : tap * width + tokens], weight_ref[tap * deep : (tap + 1) * deep]
        )
    total = total + row_of(shift_ref[...], at)
    inside = pixel_inside(total.shape, first_row, side, width)
    if base_given:
        total = total + jnp.where(inside, base_ref[0].astype(F32), 0.0)
    out_ref[0] = total
    edge_ref[0, 0] = total[:width].astype(BF)
    edge_ref[1, 0] = total[tokens - width :].astype(BF)
    masked = jnp.where(inside, total, 0.0)

    @pl.when(at == 0)
    def _():
        stats_ref[...] = jnp.zeros_like(stats_ref)

    put_row(stats_ref, 2 * at, col_sum(masked))
    put_row(stats_ref, 2 * at + 1, col_sum(masked * masked))


def conv_forward(place, sides, field, halo, avg, gain, bias, weight, shift, base, width):
    images, tokens, channels = field.shape
    ins = [place, sides, field, halo, avg, gain, bias, weight, shift]
    specs = [
        SMEM_WHOLE,
        SMEM_WHOLE,
        image_block(tokens, channels),
        edge_block(width, channels),
        table_block(channels),
        table_block(channels, 1),
        table_block(channels, 1),
        fixed_block(weight.shape),
        table_block(channels),
    ]
    if base is not None:
        ins.append(base)
        specs.append(image_block(tokens, channels))
    return pl.pallas_call(
        partial(conv_forward_kernel, width, base is not None),
        grid=(images,),
        out_shape=(
            jax.ShapeDtypeStruct(field.shape, F32),
            jax.ShapeDtypeStruct((2, images, width, channels), BF),
            jax.ShapeDtypeStruct((8, channels), F32),
        ),
        in_specs=specs,
        out_specs=(
            image_block(tokens, channels),
            edge_block(width, channels),
            table_block(channels),
        ),
        scratch_shapes=[pltpu.VMEM((tokens + 2 * width, 3 * channels), BF)],
        compiler_params=pltpu.CompilerParams(vmem_limit_bytes=56 << 20),
        name="conv_forward",
    )(*ins)


def conv_backward_kernel(width, added, *refs):
    refs = list(refs)
    (place, sides, grad_ref, grad_halo, field_ref, field_halo, avg_ref, back_avg, gain_ref) = refs[:9]
    refs = refs[9:]
    if added:
        add_ref, add_halo = refs[:2]
        refs = refs[2:]
    (weight_ref, prior_ref, prior_avg, prior_gain, prior_bias) = refs[:5]
    refs = refs[5:]
    if added:
        kept_ref = refs[0]
        refs = refs[1:]
    (out_ref, edge_ref, stats_ref, sums_ref, weight_grad, taps_s, act_s, total_s) = refs
    at = pl.program_id(0)
    last = pl.num_programs(0) - 1
    _, tokens, channels = grad_ref.shape
    first_row = place[0]
    side = sides[at]
    mean, inv_std = moments(avg_ref, at)
    back = back_avg[...]
    back_mean, back_cross = row_of(back, 2 * at), row_of(back, 2 * at + 1)
    gain = gain_ref[...]
    grad_slope = inv_std * gain
    field_slope = inv_std * inv_std * back_cross
    offset = inv_std * back_mean - mean * field_slope

    def through(grads, field, extra, row):
        moved = grads.astype(F32) * grad_slope - field.astype(F32) * field_slope - offset
        if extra is not None:
            moved = moved + extra.astype(F32)
        return jnp.where(pixel_inside(moved.shape, row, side, width), moved, 0.0)

    rows = tokens // width
    own = through(grad_ref[0], field_ref[0], add_ref[0] if added else None, first_row)
    put_taps(taps_s, width, own, width, True)
    for end, row, first in ((0, first_row - 1, 0), (1, first_row + rows, width + tokens)):
        put_taps(
            taps_s,
            first,
            through(grad_halo[end, 0], field_halo[end, 0], add_halo[end, 0] if added else None, row),
            width,
            True,
        )
    if added:
        kept_ref[0] = own

    @pl.when(at == 0)
    def _():
        stats_ref[...] = jnp.zeros_like(stats_ref)
        sums_ref[...] = jnp.zeros_like(sums_ref)
        total_s[...] = jnp.zeros_like(total_s)

    put_row(sums_ref, at, col_sum(own))
    prior_mean, prior_std = moments(prior_avg, at)
    centred = (prior_ref[0].astype(F32) - prior_mean) * prior_std
    normed = centred * prior_gain[...] + prior_bias[...]
    gate = jax.nn.sigmoid(normed)
    inside = pixel_inside(normed.shape, first_row, side, width)
    act_s[...] = jnp.where(inside, normed * gate, 0.0).T.astype(BF)
    act_t = act_s[...]
    moved = None
    for down in range(3):
        lines = pl.ds((2 - down) * width, tokens)
        for across in range(3):
            tap = 3 * down + across
            low = taps_s[lines, across * channels : (across + 1) * channels]
            part = slice(tap * channels, (tap + 1) * channels)
            term = dot_nt(low, weight_ref[part])
            moved = term if moved is None else moved + term
            total_s[part] += dot_nn(act_t, low)
    grads = jnp.where(inside, moved * (gate + normed * gate * (1.0 - gate)), 0.0)
    out_ref[0] = grads
    edge_ref[0, 0] = grads[:width].astype(BF)
    edge_ref[1, 0] = grads[tokens - width :].astype(BF)
    put_row(stats_ref, 2 * at, col_sum(grads))
    put_row(stats_ref, 2 * at + 1, col_sum(grads * centred))

    @pl.when(at == last)
    def _():
        weight_grad[...] = total_s[...].astype(BF)


def conv_backward(place, sides, grads, grad_halo, field, field_halo, avg, back_avg, gain, extra,
                  extra_halo, weight, prior, prior_avg, prior_gain, prior_bias, width):
    images, tokens, channels = grads.shape
    added = extra is not None
    tok = image_block(tokens, channels)
    edge = edge_block(width, channels)
    table = table_block(channels)
    vector = table_block(channels, 1)
    ins = [place, sides, grads, grad_halo, field, field_halo, avg, back_avg, gain]
    specs = [SMEM_WHOLE, SMEM_WHOLE, tok, edge, tok, edge, table, table, vector]
    if added:
        ins += [extra, extra_halo]
        specs += [tok, edge]
    ins += [weight, prior, prior_avg, prior_gain, prior_bias]
    specs += [fixed_block(weight.shape), tok, table, vector, vector]
    outs = [
        jax.ShapeDtypeStruct(grads.shape, F32),
        jax.ShapeDtypeStruct((2, images, width, channels), BF),
        jax.ShapeDtypeStruct((8, channels), F32),
        jax.ShapeDtypeStruct((8, channels), F32),
        jax.ShapeDtypeStruct(weight.shape, BF),
    ]
    out_specs = [tok, edge, table, table, fixed_block(weight.shape)]
    if added:
        outs.insert(0, jax.ShapeDtypeStruct(grads.shape, F32))
        out_specs.insert(0, tok)
    return pl.pallas_call(
        partial(conv_backward_kernel, width, added),
        grid=(images,),
        out_shape=outs,
        in_specs=specs,
        out_specs=out_specs,
        scratch_shapes=[
            pltpu.VMEM((tokens + 2 * width, 3 * channels), BF),
            pltpu.VMEM((channels, tokens), BF),
            pltpu.VMEM(weight.shape, F32),
        ],
        compiler_params=pltpu.CompilerParams(vmem_limit_bytes=60 << 20),
        name="conv_backward",
    )(*ins)


def layer_stats(field):
    centre = jnp.mean(field, axis=-1, keepdims=True)
    centred = field - centre
    inv_std = lax.rsqrt(jnp.mean(centred * centred, axis=-1, keepdims=True) + LN_EPS)
    return centred * inv_std, inv_std


def layer_back(grads, gain, centred, inv_std):
    scaled = grads * gain
    return inv_std * (
        scaled
        - jnp.mean(scaled, axis=-1, keepdims=True)
        - centred * jnp.mean(scaled * centred, axis=-1, keepdims=True)
    )


def entry_kernel(field_ref, avg_ref, gain_ref, bias_ref, proj_ref, proj_bias, ln_gain, ln_bias, qkv_ref,
                 stream_ref, sent_ref):
    at = pl.program_id(0)
    _, tokens, channels = field_ref.shape
    half = tokens // 2
    mean, inv_std = moments(avg_ref, at)
    slope = inv_std * gain_ref[...]
    flat = (field_ref[0] * slope + (bias_ref[...] - mean * slope)).astype(BF)
    stream = dot_nn(flat, proj_ref[...]) + proj_bias[...]
    stream_ref[0] = stream
    centred, _ = layer_stats(stream)
    joint = dot_nn((centred * ln_gain[...] + ln_bias[...]).astype(BF), qkv_ref[...])
    low = lane_ids(half) < 64
    for head in range(HEADS):
        sent_ref[0, head, :tokens] = joint[:, head * 128 : head * 128 + 128].astype(BF)
        first = 2 * channels + (head // 2) * 128
        upper, lower = joint[:half, first : first + 128], joint[half:, first : first + 128]
        if head % 2 == 0:
            pairs = jnp.where(low, upper, swap_halves(lower))
        else:
            pairs = jnp.where(low, swap_halves(upper), lower)
        sent_ref[0, head, tokens:] = pairs.astype(BF)


def entry(field, avg, gain, bias, proj, proj_bias, ln_gain, ln_bias, qkv):
    images, tokens, channels = field.shape
    vector = table_block(channels, 1)
    return pl.pallas_call(
        entry_kernel,
        grid=(images,),
        out_shape=(
            jax.ShapeDtypeStruct(field.shape, F32),
            jax.ShapeDtypeStruct((images, HEADS, tokens * 3 // 2, 128), BF),
        ),
        in_specs=[
            image_block(tokens, channels),
            table_block(channels),
            vector,
            vector,
            fixed_block(proj.shape),
            vector,
            vector,
            vector,
            fixed_block(qkv.shape),
        ],
        out_specs=(
            image_block(tokens, channels),
            pl.BlockSpec((1, HEADS, tokens * 3 // 2, 128), lambda at: (at, 0, 0, 0)),
        ),
        compiler_params=pltpu.CompilerParams(vmem_limit_bytes=48 << 20),
        name="entry",
    )(field, avg, gain, bias, proj, proj_bias, ln_gain, ln_bias, qkv)


def join_heads(pairs_ref, at):
    half = pairs_ref.shape[-2]
    low = lane_ids(half) < 64
    upper, lower = [], []
    for head in range(0, HEADS, 2):
        one, two = pairs_ref[at, head].astype(F32), pairs_ref[at, head + 1].astype(F32)
        upper.append(jnp.where(low, one, swap_halves(two)))
        lower.append(jnp.where(low, swap_halves(one), two))
    return jnp.concatenate(
        [jnp.concatenate(upper, axis=1), jnp.concatenate(lower, axis=1)], axis=0
    ).astype(BF)


def split_heads(field, out_ref, at):
    half = field.shape[0] // 2
    low = lane_ids(half) < 64
    for head in range(HEADS):
        first = (head // 2) * 128
        upper, lower = field[:half, first : first + 128], field[half:, first : first + 128]
        if head % 2 == 0:
            pairs = jnp.where(low, upper, swap_halves(lower))
        else:
            pairs = jnp.where(low, swap_halves(upper), lower)
        out_ref[at, head] = pairs.astype(BF)


def feed_pieces(channels, wide, hidden, bands):
    size = channels // bands
    geglu = [(at * size, size) for at in range(wide // channels)]
    first = wide // bands
    return (
        geglu,
        [(first, hidden // bands)],
        [(first + hidden // bands, size)],
        [(first + hidden // bands + size, size)],
    )


def feed_kernel(width, bands, per_band, place, sides, *refs):
    given = refs[:per_band]
    (stream_ref, residual_ref, cot_ref, cross_ref, attn_ref, attn_bias, ln_gain, ln_bias,
     geglu_ref, geglu_bias, feed_ref, feed_bias, proj_ref, proj_bias,
     out_ref, three_ref, back_ref, grads_ref, sums_ref, cross_sum, pair_sums, geglu_s, feed_s, proj_s, attn_s,
     mixed_s, sent_s, out_send, out_recv, back_send, back_recv) = refs[per_band:]
    at = pl.program_id(0)
    images = pl.num_programs(0)
    last = images - 1
    me = lax.axis_index("rows")

    def move(src, dst, send, recv, target):
        @pl.when(target != me)
        def _():
            pltpu.make_async_remote_copy(
                src_ref=src, dst_ref=dst, send_sem=send, recv_sem=recv, device_id={"rows": target},
                device_id_type=pl.DeviceIdType.MESH,
            ).start()

        @pl.when(target == me)
        def _():
            pltpu.make_async_copy(src, dst, recv).start()

    def arrived(dst, send, recv, source):
        @pl.when(source != me)
        def _():
            pltpu.make_async_remote_copy(
                src_ref=dst, dst_ref=dst, send_sem=send, recv_sem=recv, device_id={"rows": source},
                device_id_type=pl.DeviceIdType.MESH,
            ).wait_recv()

        @pl.when(source == me)
        def _():
            pltpu.make_async_copy(dst, dst, recv).wait()

    def left(src, send, recv, target):
        @pl.when(target != me)
        def _():
            pltpu.make_async_remote_copy(
                src_ref=src, dst_ref=src, send_sem=send, recv_sem=recv, device_id={"rows": target},
                device_id_type=pl.DeviceIdType.MESH,
            ).wait_send()

    @pl.when(at == 0)
    def _():
        barrier = pltpu.get_barrier_semaphore()
        for away in range(1, bands):
            pl.semaphore_signal(
                barrier, inc=1, device_id={"rows": lax.rem(me + away, bands)},
                device_id_type=pl.DeviceIdType.MESH,
            )
        pl.semaphore_wait(barrier, bands - 1)
        for spot in range(per_band):
            item = me * per_band + spot
            head, image = item // images, lax.rem(item, images)
            for away in range(bands):
                band = lax.rem(me + away, bands)
                move(
                    given[spot].at[band], mixed_s.at[image, head], out_send.at[spot, away],
                    out_recv.at[image, head], band,
                )

    for head in range(HEADS):
        arrived(
            mixed_s.at[at, head], out_send.at[0, 0], out_recv.at[at, head], (head * images + at) // per_band
        )
    _, tokens, channels = stream_ref.shape
    hidden = feed_ref.shape[0]
    side = sides[at]
    inside = pixel_inside((tokens, channels), place[0], side, width)

    @pl.when(at == 0)
    def _():
        for ref in (sums_ref, cross_sum, pair_sums, geglu_s, feed_s, proj_s, attn_s):
            ref[...] = jnp.zeros_like(ref)

    mixed = join_heads(mixed_s, at)
    three = stream_ref[0] + dot_nn(mixed, attn_ref[...]) + (attn_bias[...] + row_of(cross_ref[...], at))
    centred, inv_std = layer_stats(three)
    feed_in = (centred * ln_gain[...] + ln_bias[...]).astype(BF)
    grad_out = jnp.where(inside, cot_ref[0].astype(F32), 0.0)
    branch = grad_out.astype(BF)
    grad_four = dot_nt(branch, proj_ref[...])
    low_feed = grad_four.astype(BF)
    four = three + feed_bias[...]
    grad_in = jnp.zeros((tokens, channels), F32)
    step = 512
    for first in range(0, hidden, step):
        own = slice(first, first + step)
        gates = slice(hidden + first, hidden + first + step)
        value = dot_nn(feed_in, geglu_ref[:, own]) + geglu_bias[:, own]
        gate = dot_nn(feed_in, geglu_ref[:, gates]) + geglu_bias[:, gates]
        back = dot_nt(low_feed, feed_ref[own])
        below = 0.5 + 0.5 * lax.erf(gate * math.sqrt(0.5))
        bell = jnp.exp(gate * gate * -0.5) * (1.0 / math.sqrt(2.0 * math.pi))
        act = gate * below
        gated = (value * act).astype(BF)
        four = four + dot_nn(gated, feed_ref[own])
        feed_s[own] += dot_tn(gated, low_feed)
        grad_value = back * act
        grad_gate = back * value * (below + gate * bell)
        pair_sums[:, own] += col_sum(grad_value)
        pair_sums[:, gates] += col_sum(grad_gate)
        low_value, low_gate = grad_value.astype(BF), grad_gate.astype(BF)
        geglu_s[:, own] += dot_tn(feed_in, low_value)
        geglu_s[:, gates] += dot_tn(feed_in, low_gate)
        grad_in = grad_in + dot_nt(low_value, geglu_ref[:, own]) + dot_nt(low_gate, geglu_ref[:, gates])
    last_in = four.astype(BF)
    proj_s[...] += dot_tn(last_in, branch)
    output = residual_ref[0] + dot_nn(last_in, proj_ref[...]) + proj_bias[...]
    out_ref[0] = jnp.where(inside, output, 0.0).astype(BF)
    grad_three = grad_four + layer_back(grad_in, ln_gain[...], centred, inv_std)
    three_ref[0] = grad_three
    low_attn = grad_three.astype(BF)
    attn_s[...] += dot_tn(mixed, low_attn)
    split_heads(dot_nt(low_attn, attn_ref[...]), sent_s, at)
    for head in range(HEADS):
        item = head * images + at
        move(
            sent_s.at[at, head], back_ref.at[lax.rem(item, per_band), me], back_send.at[at, head],
            back_recv.at[lax.rem(item, per_band), me], item // per_band,
        )
    put_row(cross_sum, at, col_sum(grad_three))
    ids = lax.broadcasted_iota(jnp.int32, sums_ref.shape, 0)
    for row, total in enumerate(
        (col_sum(grad_out), col_sum(grad_four), col_sum(grad_in * centred), col_sum(grad_in))
    ):
        sums_ref[...] += jnp.where(ids == row, total, 0.0)

    @pl.when(at == last)
    def _():
        for spot in range(per_band):
            for away in range(bands):
                band = lax.rem(me + away, bands)
                left(given[spot].at[band], out_send.at[spot, away], out_recv.at[0, 0], band)
                arrived(back_ref.at[spot, band], back_send.at[0, 0], back_recv.at[spot, band], band)
        for image in range(sent_s.shape[0]):
            for head in range(HEADS):
                left(
                    sent_s.at[image, head], back_send.at[image, head], back_recv.at[0, 0],
                    (head * sent_s.shape[0] + image) // per_band,
                )
        halving = len(grads_ref.shape) == 5
        for band in range(bands):
            if halving:
                apart = jnp.bitwise_xor(me, band)
                own = (apart & 1, (apart >> 1) & 1, apart >> 2)
            else:
                own = (band,)
            pieces = feed_pieces(channels, 2 * hidden, hidden, bands)
            for total, parts in zip((geglu_s, feed_s, proj_s, attn_s), pieces):
                for at_col, (first, size) in enumerate(parts):
                    grads_ref[own + (pl.ds(first, size),)] = total[
                        band * size : (band + 1) * size, at_col * channels : (at_col + 1) * channels
                    ].astype(BF)


def feed(place, sides, mixed, stream, residual, cot, cross, attn, attn_bias, ln_gain, ln_bias, geglu,
         geglu_bias, feed_out, feed_bias, proj, proj_bias, width, bands, halving):
    images, tokens, channels = stream.shape
    tok = image_block(tokens, channels)
    vector = table_block(channels, 1)
    table = table_block(channels)
    half = tokens // 2
    per_band = len(mixed)
    anywhere = pl.BlockSpec(memory_space=pl.ANY)
    wide = geglu.shape[1]
    weights = (geglu, feed_out, proj, attn)
    rows = sum(w.size for w in weights) // channels // bands
    lead = (2, 2, 2) if halving else (bands,)
    grads = lead + (rows, channels)
    return pl.pallas_call(
        partial(feed_kernel, width, bands, per_band),
        grid=(images,),
        out_shape=(
            jax.ShapeDtypeStruct(stream.shape, BF),
            jax.ShapeDtypeStruct(stream.shape, F32),
            jax.ShapeDtypeStruct((per_band, bands, half, 128), BF),
        )
        + (
            jax.ShapeDtypeStruct(grads, BF),
            jax.ShapeDtypeStruct((8, channels), F32),
            jax.ShapeDtypeStruct((8, channels), F32),
            jax.ShapeDtypeStruct((1, wide), F32),
        ),
        in_specs=[
            SMEM_WHOLE,
            SMEM_WHOLE,
        ]
        + [anywhere] * per_band
        + [
            tok,
            tok,
            tok,
            table,
            fixed_block(attn.shape),
            vector,
            vector,
            vector,
            fixed_block(geglu.shape),
            table_block(wide, 1),
            fixed_block(feed_out.shape),
            vector,
            fixed_block(proj.shape),
            vector,
        ],
        out_specs=(tok, tok, anywhere)
        + (fixed_block(grads), table, table, table_block(wide, 1)),
        scratch_shapes=[pltpu.VMEM(w.shape, F32) for w in weights]
        + [pltpu.VMEM((images, HEADS, half, 128), BF)] * 2
        + [
            pltpu.SemaphoreType.DMA((per_band, bands)),
            pltpu.SemaphoreType.DMA((images, HEADS)),
            pltpu.SemaphoreType.DMA((images, HEADS)),
            pltpu.SemaphoreType.DMA((per_band, bands)),
        ],
        compiler_params=pltpu.CompilerParams(
            vmem_limit_bytes=62 << 20, collective_id=5, has_side_effects=True
        ),
        name="feed",
    )(place, sides, *mixed, stream, residual, cot, cross, attn, attn_bias, ln_gain, ln_bias, geglu,
      geglu_bias, feed_out, feed_bias, proj, proj_bias)


def leave_kernel(width, place, sides, *refs):
    (packed_ref, stream_ref, three_ref, field_ref, avg_ref, gain_ref, bias_ref, proj_ref, ln_gain, ln_bias,
     qkv_ref, out_ref, edge_ref, stats_ref, sums_ref, grad_qkv, grad_proj, qkv_s, proj_s) = refs
    at = pl.program_id(0)
    last = pl.num_programs(0) - 1
    _, tokens, channels = stream_ref.shape
    inside = pixel_inside((tokens, channels), place[0], sides[at], width)

    @pl.when(at == 0)
    def _():
        for ref in (stats_ref, sums_ref, qkv_s, proj_s):
            ref[...] = jnp.zeros_like(ref)

    queries = join_heads(packed_ref.at[:, :, tokens:, :], 0)
    joint = jnp.concatenate([packed_ref[0, head, :tokens] for head in range(HEADS)] + [queries], axis=1)
    centred, inv_std = layer_stats(stream_ref[0])
    attn_in = (centred * ln_gain[...] + ln_bias[...]).astype(BF)
    qkv_s[...] += dot_tn(attn_in, joint)
    grads = dot_nt(joint, qkv_ref[...])
    grad_stream = three_ref[0] + layer_back(grads, ln_gain[...], centred, inv_std)
    low_in = grad_stream.astype(BF)
    mean, deviation = moments(avg_ref, at)
    normed = (field_ref[0] - mean) * deviation
    flat = (normed * gain_ref[...] + bias_ref[...]).astype(BF)
    proj_s[...] += dot_tn(flat, low_in)
    moved = jnp.where(inside, dot_nt(low_in, proj_ref[...]), 0.0)
    out_ref[0] = moved
    edge_ref[0, 0] = moved[:width].astype(BF)
    edge_ref[1, 0] = moved[tokens - width :].astype(BF)
    put_row(stats_ref, 2 * at, col_sum(moved))
    put_row(stats_ref, 2 * at + 1, col_sum(moved * normed))
    ids = lax.broadcasted_iota(jnp.int32, sums_ref.shape, 0)
    for row, total in enumerate((col_sum(grads * centred), col_sum(grads), col_sum(grad_stream))):
        sums_ref[...] += jnp.where(ids == row, total, 0.0)

    @pl.when(at == last)
    def _():
        grad_qkv[...] = qkv_s[...].astype(BF)
        grad_proj[...] = proj_s[...].astype(BF)


def leave(place, sides, packed, stream, three, field, avg, gain, bias, proj, ln_gain, ln_bias, qkv, width):
    images, tokens, channels = stream.shape
    tok = image_block(tokens, channels)
    vector = table_block(channels, 1)
    table = table_block(channels)
    return pl.pallas_call(
        partial(leave_kernel, width),
        grid=(images,),
        out_shape=(
            jax.ShapeDtypeStruct(stream.shape, F32),
            jax.ShapeDtypeStruct((2, images, width, channels), BF),
            jax.ShapeDtypeStruct((8, channels), F32),
            jax.ShapeDtypeStruct((8, channels), F32),
            jax.ShapeDtypeStruct(qkv.shape, BF),
            jax.ShapeDtypeStruct(proj.shape, BF),
        ),
        in_specs=[
            SMEM_WHOLE,
            SMEM_WHOLE,
            pl.BlockSpec((1,) + packed.shape[1:], lambda at: (at, 0, 0, 0)),
            tok,
            tok,
            tok,
            table,
            vector,
            vector,
            fixed_block(proj.shape),
            vector,
            vector,
            fixed_block(qkv.shape),
        ],
        out_specs=(
            tok,
            edge_block(width, channels),
            table,
            table,
            fixed_block(qkv.shape),
            fixed_block(proj.shape),
        ),
        scratch_shapes=[pltpu.VMEM(qkv.shape, F32), pltpu.VMEM(proj.shape, F32)],
        compiler_params=pltpu.CompilerParams(vmem_limit_bytes=56 << 20),
        name="leave",
    )(place, sides, packed, stream, three, field, avg, gain, bias, proj, ln_gain, ln_bias, qkv)


def exchange_kernel(count, bands, sent_ref, weight_ref, scale_ref, *refs):
    edges, avg_ref, halos = refs[:count], refs[count], refs[count + 1 : 2 * count + 1]
    slots, send_sem, recv_sem, edge_send, edge_recv = refs[2 * count + 1 :]
    me = lax.axis_index("rows")
    barrier = pltpu.get_barrier_semaphore()
    for away in range(1, bands):
        pl.semaphore_signal(
            barrier,
            inc=1,
            device_id={"rows": lax.rem(me + away, bands)},
            device_id_type=pl.DeviceIdType.MESH,
        )
    slots[me] = sent_ref[...]
    pl.semaphore_wait(barrier, bands - 1)
    copies = []
    for at in range(count):
        for end, away in ((0, bands - 1), (1, 1)):
            copies.append(
                pltpu.make_async_remote_copy(
                    src_ref=edges[at].at[end],
                    dst_ref=halos[at].at[1 - end],
                    send_sem=edge_send.at[at, end],
                    recv_sem=edge_recv.at[at, 1 - end],
                    device_id={"rows": lax.rem(me + away, bands)},
                    device_id_type=pl.DeviceIdType.MESH,
                )
            )
    for away in range(1, bands):
        copies.append(
            pltpu.make_async_remote_copy(
                src_ref=sent_ref,
                dst_ref=slots.at[me],
                send_sem=send_sem.at[away],
                recv_sem=recv_sem.at[me],
                device_id={"rows": lax.rem(me + away, bands)},
                device_id_type=pl.DeviceIdType.MESH,
            )
        )
    for copy in copies[2 * count :] + copies[: 2 * count]:
        copy.start()
    for copy in copies:
        copy.wait_send()
    for away in range(1, bands):
        source = lax.rem(me + away, bands)
        pltpu.make_async_remote_copy(
            src_ref=sent_ref,
            dst_ref=slots.at[source],
            send_sem=send_sem.at[away],
            recv_sem=recv_sem.at[source],
            device_id={"rows": source},
            device_id_type=pl.DeviceIdType.MESH,
        ).wait_recv()
    total = slots[0]
    for at in range(1, bands):
        total = total + slots[at]
    channels = total.shape[1]
    size = channels // GROUPS
    rows = lax.broadcasted_iota(jnp.int32, (channels, channels), 0) // size
    cols = lax.broadcasted_iota(jnp.int32, (channels, channels), 1) // size
    same = jnp.where(rows == cols, 1.0, 0.0)
    avg_ref[...] = jnp.dot(
        total * weight_ref[...], same, precision=HIGH, preferred_element_type=F32
    ) * scale_ref[...]
    for copy in copies[: 2 * count]:
        copy.wait_recv()


def exchange(sums, weight, scale, edges, bands):
    count = len(edges)
    hbm = pl.BlockSpec(memory_space=pl.ANY)
    return pl.pallas_call(
        partial(exchange_kernel, count, bands),
        out_shape=(jax.ShapeDtypeStruct(sums.shape, F32),)
        + tuple(jax.ShapeDtypeStruct(edge.shape, edge.dtype) for edge in edges),
        in_specs=[VMEM_WHOLE] * 3 + [hbm] * count,
        out_specs=(VMEM_WHOLE,) + (hbm,) * count,
        scratch_shapes=[
            pltpu.VMEM((bands,) + sums.shape, F32),
            pltpu.SemaphoreType.DMA((bands,)),
            pltpu.SemaphoreType.DMA((bands,)),
            pltpu.SemaphoreType.DMA((max(count, 1), 2)),
            pltpu.SemaphoreType.DMA((max(count, 1), 2)),
        ],
        compiler_params=pltpu.CompilerParams(collective_id=count, has_side_effects=True),
        name="exchange",
    )(sums, weight, scale, *edges)

def rounded(field):
    return field.astype(BF)


def reduce_kernel(chunks, shapes, bands, groups, *refs):
    count = len(shapes)
    parts, table_ref = refs[:count], refs[count]
    outs, gathered = refs[count + 1 : 2 * count + 1], refs[2 * count + 1]
    refs = refs[2 * count + 2 :]
    pairs, crossed, summed, pieces = (refs[at * count : (at + 1) * count] for at in range(4))
    (slots, pair_send, pair_recv, cross_send, cross_recv, piece_send, piece_recv, back_send, back_recv,
     table_send, table_recv, far_send, far_recv) = refs[4 * count :]
    chips = bands // 2
    me = lax.axis_index("rows")
    group = lax.axis_index("heads")
    core, chip = lax.rem(me, 2), me // 2
    row_peers = [lax.rem(me + away, bands) for away in range(1, bands)]
    far_peers = [lax.rem(group + away, groups) for away in range(1, groups)]
    barrier = pltpu.get_barrier_semaphore()
    for axis, peers in (("rows", row_peers), ("heads", far_peers)):
        for peer in peers:
            pl.semaphore_signal(
                barrier, inc=1, device_id={axis: peer}, device_id_type=pl.DeviceIdType.MESH
            )
    pl.semaphore_wait(barrier, bands + groups - 2)

    def copy(src, dst, send, recv, axis, peer):
        return pltpu.make_async_remote_copy(
            src_ref=src,
            dst_ref=dst,
            send_sem=send,
            recv_sem=recv,
            device_id={axis: peer},
            device_id_type=pl.DeviceIdType.MESH,
        )

    def rows_of(band, size):
        return pl.ds(pl.multiple_of(band * size, 16), size)

    near = [
        copy(table_ref, slots.at[away], table_send.at[away], table_recv.at[away], "rows", peer)
        for away, peer in enumerate(row_peers)
    ]
    for item in near:
        item.start()
    stage_one = []
    for at, (which, first, wide) in enumerate(chunks):
        size = shapes[which][0] // bands
        cols = pl.ds(first, wide)
        own = []
        for spot in range(chips):
            own.append(
                copy(
                    parts[which].at[rows_of(2 * spot + 1 - core, size), cols],
                    pairs[which].at[spot, :, cols],
                    pair_send.at[at, spot],
                    pair_recv.at[at, spot],
                    "rows",
                    me + 1 - 2 * core,
                )
            )
        for item in own:
            item.start()
        stage_one.append(own)
    for item in near:
        item.wait_recv()
    total = table_ref[...]
    for away in range(bands - 1):
        total = total + slots[away]
    gathered[group] = total
    far = [
        copy(gathered.at[group], gathered.at[group], far_send.at[away], far_recv.at[away], "heads", peer)
        for away, peer in enumerate(far_peers)
    ]
    for item in far:
        item.start()
    def to_owner(at):
        which, first, wide = chunks[at]
        size = shapes[which][0] // bands
        cols = pl.ds(first, wide)
        for item in stage_one[at]:
            item.wait_recv()
        own = []
        for away in range(1, chips):
            spot = lax.rem(chip + away, chips)
            pairs[which][spot, :, cols] = (
                pairs[which][spot, :, cols].astype(F32)
                + parts[which][rows_of(2 * spot + core, size), cols].astype(F32)
            ).astype(BF)
            item = copy(
                pairs[which].at[spot, :, cols],
                crossed[which].at[away - 1, :, cols],
                cross_send.at[at, away - 1],
                cross_recv.at[at, away - 1],
                "rows",
                2 * spot + core,
            )
            item.start()
            own.append(item)
        stage_two.append(own)

    def to_groups(at):
        which, first, wide = chunks[at]
        size = shapes[which][0] // bands
        piece = size // groups
        cols = pl.ds(first, wide)
        for item in stage_two[at]:
            item.wait_recv()
        total = pairs[which][chip, :, cols].astype(F32) + parts[which][rows_of(me, size), cols].astype(F32)
        for away in range(chips - 1):
            total = total + crossed[which][away, :, cols].astype(F32)
        summed[which][:, cols] = total.astype(BF)
        own = []
        for away, peer in enumerate(far_peers):
            item = copy(
                summed[which].at[rows_of(peer, piece), cols],
                pieces[which].at[away, :, cols],
                piece_send.at[at, away],
                piece_recv.at[at, away],
                "heads",
                peer,
            )
            item.start()
            own.append(item)
        stage_three.append(own)

    def back_round(at):
        which, first, wide = chunks[at]
        piece = shapes[which][0] // bands // groups
        cols = pl.ds(first, wide)
        for item in stage_three[at]:
            item.wait_recv()
        mine = rows_of(group, piece)
        total = summed[which][mine, cols].astype(F32)
        for away in range(groups - 1):
            total = total + pieces[which][away, :, cols].astype(F32)
        outs[which][mine, cols] = total.astype(BF)
        own = []
        for away, peer in enumerate(far_peers):
            item = copy(
                outs[which].at[mine, cols],
                outs[which].at[mine, cols],
                back_send.at[at, away],
                back_recv.at[at, away],
                "heads",
                peer,
            )
            item.start()
            own.append(item)
        stage_four.append(own)

    stage_two, stage_three, stage_four = [], [], []
    steps = len(chunks)
    for at in range(steps + 3):
        if at < steps:
            to_owner(at)
        if 2 <= at + 1 and 0 <= at - 1 < steps:
            to_groups(at - 1)
        if 0 <= at - 3 < steps:
            back_round(at - 3)
    for away in range(groups - 1):
        source = lax.rem(group - (away + 1) + groups, groups)
        copy(
            gathered.at[source], gathered.at[source], far_send.at[away], far_recv.at[away], "heads", source
        ).wait_recv()
        for at, (which, first, wide) in enumerate(chunks):
            piece = shapes[which][0] // bands // groups
            theirs = outs[which].at[rows_of(source, piece), pl.ds(first, wide)]
            copy(theirs, theirs, back_send.at[at, away], back_recv.at[at, away], "heads", source).wait_recv()
    for item in near + far + sum(stage_one + stage_two + stage_three + stage_four, []):
        item.wait_send()


def reduce_fits(shapes, bands, groups):
    return bands % 2 == 0 and all(rows % (16 * bands * groups) == 0 for rows, _ in shapes)


def reduce_parts(parts, table, bands, groups):
    shapes = [part.shape for part in parts]
    chunks = []
    for which, (rows, cols) in enumerate(shapes):
        wide = cols if rows * cols < 1 << 19 else 512 if cols > 512 else 128
        chunks += [(which, first, wide) for first in range(0, cols, wide)]
    chips = bands // 2

    def scratch(lead, split):
        return [
            pltpu.VMEM(lead + (rows // bands // split, cols), BF) for rows, cols in shapes
        ]

    def sems(count):
        return [pltpu.SemaphoreType.DMA((len(chunks), count))] * 2

    return pl.pallas_call(
        partial(reduce_kernel, chunks, shapes, bands, groups),
        out_shape=tuple(jax.ShapeDtypeStruct((rows // bands, cols), BF) for rows, cols in shapes)
        + (jax.ShapeDtypeStruct((groups,) + table.shape, F32),),
        in_specs=[VMEM_WHOLE] * (len(parts) + 1),
        out_specs=(VMEM_WHOLE,) * (len(parts) + 1),
        scratch_shapes=scratch((chips,), 1)
        + scratch((chips - 1,), 1)
        + scratch((), 1)
        + scratch((groups - 1,), groups)
        + [pltpu.VMEM((bands - 1,) + table.shape, F32)]
        + sems(chips)
        + sems(chips - 1)
        + sems(groups - 1)
        + sems(groups - 1)
        + [pltpu.SemaphoreType.DMA((bands - 1,))] * 2
        + [pltpu.SemaphoreType.DMA((groups - 1,))] * 2,
        compiler_params=pltpu.CompilerParams(
            vmem_limit_bytes=56 << 20, collective_id=8, has_side_effects=True
        ),
        name="reduce_parts",
    )(*parts, table)


def halve_rows(packed, step):
    pairs = [(band, band ^ (1 << step)) for band in range(8)]
    return rounded(packed[0].astype(F32) + lax.ppermute(packed[1], "rows", pairs).astype(F32))


def sum_groups(part, step, groups):
    odd = lax.rem(lax.axis_index("heads"), 2)
    near = [(at, at ^ 1) for at in range(groups)]
    far = [(at, at ^ 2) for at in range(groups)]
    if step == 0:
        half = part.shape[0] // 2
        kept = lax.dynamic_slice_in_dim(part, odd * half, half, 0)
        sent = lax.dynamic_slice_in_dim(part, (1 - odd) * half, half, 0)
        return rounded(kept.astype(F32) + lax.ppermute(sent, "heads", near).astype(F32))
    if step == 1:
        return rounded(part.astype(F32) + lax.ppermute(part, "heads", far).astype(F32))
    other = lax.ppermute(part, "heads", near)
    return jnp.where(odd == 0, jnp.concatenate([part, other]), jnp.concatenate([other, part]))


def finish_kernel(width, place, sides, kept_ref, grad_ref, field_ref, avg_ref, back_avg, gain_ref, out_ref):
    at = pl.program_id(0)
    mean, inv_std = moments(avg_ref, at)
    back = back_avg[...]
    field_slope = inv_std * inv_std * row_of(back, 2 * at + 1)
    offset = inv_std * row_of(back, 2 * at) - mean * field_slope
    moved = grad_ref[0] * (inv_std * gain_ref[...]) - field_ref[0].astype(F32) * field_slope - offset
    inside = pixel_inside(moved.shape, place[0], sides[at], width)
    out_ref[0] = jnp.where(inside, kept_ref[0] + moved, 0.0)


def finish(place, sides, kept, grads, field, avg, back_avg, gain, width):
    images, tokens, channels = kept.shape
    tok = image_block(tokens, channels)
    table = table_block(channels)
    return pl.pallas_call(
        partial(finish_kernel, width),
        grid=(images,),
        out_shape=jax.ShapeDtypeStruct(kept.shape, F32),
        in_specs=[SMEM_WHOLE, SMEM_WHOLE, tok, tok, tok, table, table, table_block(channels, 1)],
        out_specs=tok,
        compiler_params=pltpu.CompilerParams(vmem_limit_bytes=32 << 20),
        name="finish",
    )(place, sides, kept, grads, field, avg, back_avg, gain)


def time_features(time_steps, dims):
    half_dim = dims // 2
    frequency = jnp.exp(-math.log(10000.0) * jnp.arange(half_dim, dtype=jnp.float32) / half_dim)
    angles = time_steps.astype(jnp.float32)[:, None] * frequency[None, :]
    return jnp.concatenate([jnp.cos(angles), jnp.sin(angles)], axis=-1)


def pad_rows(table):
    return jnp.pad(table, ((0, 8 - table.shape[0]), (0, 0)))


def to_items(sent, bands):
    images, heads = sent.shape[:2]
    per_band = heads * images // bands
    if bands == heads:
        parts = [sent[at] for at in range(images)]
    else:
        items = jnp.swapaxes(sent, 0, 1).reshape((bands, per_band) + sent.shape[2:])
        parts = [items[:, at] for at in range(per_band)]
    return [lax.all_to_all(part, "rows", split_axis=0, concat_axis=0, tiled=True) for part in parts]


def from_items(results, images, bands):
    back = [
        lax.all_to_all(result, "rows", split_axis=0, concat_axis=0, tiled=True)
        for result in results
    ]
    if bands == HEADS:
        return jnp.stack(back)
    joint = jnp.stack(back, axis=1)
    return jnp.swapaxes(joint.reshape((HEADS, images) + joint.shape[2:]), 0, 1)


def per_device(
    images,
    image_sides,
    labels,
    timesteps,
    cotangent,
    first_gain,
    first_bias,
    conv_one,
    time_proj,
    time_bias,
    second_gain,
    second_bias,
    conv_two,
    conv_bias,
    third_gain,
    third_bias,
    proj_in,
    proj_in_bias,
    attn_gain,
    attn_bias,
    qkv_proj,
    attn_out,
    attn_out_bias,
    class_table,
    cross_value,
    cross_out,
    feed_gain,
    feed_bias,
    geglu_proj,
    geglu_bias,
    feed_out,
    feed_out_bias,
    proj_out,
    proj_out_bias,
):
    image_count, band_rows, width, channels = images.shape
    tokens = band_rows * width
    head_dim = channels // HEADS
    score_scale = head_dim ** (-0.5)
    bands = lax.axis_size("rows")
    groups = lax.axis_size("heads")
    halving = bands == 8 and groups == 4
    me = lax.axis_index("rows")
    first_image = lax.axis_index("heads") * image_count
    sides = lax.dynamic_slice_in_dim(image_sides, first_image, image_count)
    place = jnp.stack([me * band_rows, me]).astype(jnp.int32)

    def vector(entries):
        return entries.astype(F32).reshape(1, -1)

    counts = 1.0 / (sides * sides * (channels // GROUPS)).astype(F32)
    scale = jnp.broadcast_to(pad_rows(jnp.repeat(counts, 2)[:, None]), (8, channels))
    ones = jnp.ones((1, channels), F32)
    field = images.reshape(image_count, tokens, channels)
    cot = cotangent.reshape(image_count, tokens, channels)

    def edges_of(whole):
        return jnp.stack([whole[:, 0], whole[:, -1]])

    hot = rounded(
        (labels[:, None] == jnp.arange(class_table.shape[0], dtype=jnp.int32)[None, :]).astype(F32)
    )
    context = jnp.dot(hot, class_table, preferred_element_type=F32)
    value = rounded(jnp.dot(rounded(context), cross_value, preferred_element_type=F32))
    cross = jnp.dot(value, cross_out, preferred_element_type=F32)
    cross = pad_rows(lax.dynamic_slice_in_dim(cross, first_image, image_count))
    embed = rounded(jax.nn.silu(time_features(timesteps, time_proj.shape[0])))
    shift = jnp.dot(embed, time_proj, preferred_element_type=F32) + time_bias.astype(F32)
    shift = pad_rows(lax.dynamic_slice_in_dim(shift, first_image, image_count))

    row_ids = me * band_rows + jnp.arange(band_rows, dtype=jnp.int32)
    col_ids = jnp.arange(width, dtype=jnp.int32)
    limit = sides[:, None, None]
    inside = ((row_ids[None, :, None] < limit) & (col_ids[None, None, :] < limit))[..., None]
    start = jnp.where(inside, images.astype(F32), 0.0)
    sums = jnp.stack([jnp.sum(start, axis=(1, 2)), jnp.sum(start * start, axis=(1, 2))], axis=1)
    sums = pad_rows(sums.reshape(2 * image_count, channels))

    avg_one, halo_images, halo_cot = exchange(
        sums, ones, scale, (edges_of(images), edges_of(cotangent)), bands
    )
    hidden, edge, sums = conv_forward(
        place, sides, field, halo_images, avg_one, vector(first_gain), vector(first_bias), conv_one,
        shift, None, width,
    )
    avg_two, halo_hidden = exchange(sums, ones, scale, (edge,), bands)
    residual, edge, sums = conv_forward(
        place, sides, hidden, halo_hidden, avg_two, vector(second_gain), vector(second_bias), conv_two,
        jnp.broadcast_to(vector(conv_bias), (8, channels)), field, width,
    )
    avg_three, halo_residual = exchange(sums, ones, scale, (edge,), bands)
    split = qkv_proj.reshape(channels, 3, HEADS, head_dim)
    turned_qkv = jnp.concatenate(
        [
            jnp.stack([split[:, 1], split[:, 2]], axis=2).reshape(channels, 2 * channels),
            qkv_proj[:, :channels],
        ],
        axis=1,
    )
    stream, sent = entry(
        residual, avg_three, vector(third_gain), vector(third_bias), proj_in, vector(proj_in_bias),
        vector(attn_gain), vector(attn_bias), turned_qkv,
    )
    chunks = to_items(sent, bands)
    first_item = me * len(chunks)
    item_sides = [
        lax.dynamic_slice_in_dim(sides, lax.rem(first_item + at, image_count), 1)
        for at in range(len(chunks))
    ]
    attended = [attend(side, chunk, width, score_scale) for side, chunk in zip(item_sides, chunks)]
    mixed = [pairs for pairs, _ in attended]
    (
        output, three, grad_chunks, feed_grads, feed_sums, cross_sum, pair_sums,
    ) = feed(
        place, sides, mixed, stream, residual, cot, cross, attn_out, vector(attn_out_bias),
        vector(feed_gain), vector(feed_bias), geglu_proj, vector(geglu_bias), feed_out,
        vector(feed_out_bias), proj_out, vector(proj_out_bias), width, bands, halving,
    )
    halved = feed_grads
    results = []
    for spot, (side, chunk, (_, norms)) in enumerate(zip(item_sides, chunks, attended)):
        if halving and spot in (1, 3):
            halved, norms = lax.optimization_barrier((halve_rows(halved, spot // 2), norms))
        results.append(attend_back(side, chunk, grad_chunks, spot, norms, width, score_scale))
    grad_qkv = from_items(results, image_count, bands)
    if halving:
        halved, grad_qkv = lax.optimization_barrier((halve_rows(halved, 2), grad_qkv))
        early = halved
    else:
        early = feed_grads.reshape((bands,) + feed_grads.shape[-2:])
        early = lax.psum_scatter(early, "rows", scatter_dimension=0, tiled=True)[0]
        early = lax.psum(early, "heads")
    moved, edge, third_sums, leave_sums, grad_qkv_proj, grad_proj_in = leave(
        place, sides, grad_qkv, stream, three, residual, avg_three, vector(third_gain),
        vector(third_bias), proj_in, vector(attn_gain), vector(attn_bias), turned_qkv, width,
    )
    if halving:
        early, third_sums = lax.optimization_barrier((sum_groups(early, 0, groups), third_sums))
    back_three, halo_moved = exchange(third_sums, vector(third_gain), scale, (edge,), bands)
    grad_residual, moved, edge, second_sums, residual_sums, grad_conv_two = conv_backward(
        place, sides, moved, halo_moved, residual, halo_residual, avg_three, back_three,
        vector(third_gain), cot, halo_cot, conv_two, hidden, avg_two, vector(second_gain),
        vector(second_bias), width,
    )
    if halving:
        early, second_sums = lax.optimization_barrier((sum_groups(early, 1, groups), second_sums))
    back_two, halo_moved = exchange(second_sums, vector(second_gain), scale, (edge,), bands)
    moved, _, first_sums, hidden_sums, grad_conv_one = conv_backward(
        place, sides, moved, halo_moved, hidden, halo_hidden, avg_two, back_two, vector(second_gain),
        None, None, conv_one, field, avg_one, vector(first_gain), vector(first_bias), width,
    )
    if halving:
        early, first_sums = lax.optimization_barrier((sum_groups(early, 2, groups), first_sums))
    (back_one,) = exchange(first_sums, vector(first_gain), scale, (), bands)
    grad_images = finish(
        place, sides, grad_residual, moved, field, avg_one, back_one, vector(first_gain), width
    ).reshape(images.shape)

    def own(whole, axis=0):
        size = whole.shape[axis] // bands
        return lax.dynamic_slice_in_dim(whole, me * size, size, axis)

    def reduced(part):
        part = lax.psum_scatter(part, "rows", scatter_dimension=0, tiled=True)
        return lax.psum(part, "heads").astype(F32)

    used = 2 * image_count
    table = jnp.concatenate(
        [
            cross_sum[:image_count],
            hidden_sums[:image_count],
            jnp.stack(
                [
                    jnp.sum(first_sums[1:used:2], axis=0),
                    jnp.sum(first_sums[0:used:2], axis=0),
                    jnp.sum(second_sums[1:used:2], axis=0),
                    jnp.sum(second_sums[0:used:2], axis=0),
                    jnp.sum(third_sums[1:used:2], axis=0),
                    jnp.sum(third_sums[0:used:2], axis=0),
                    jnp.sum(residual_sums[:image_count], axis=0),
                ]
            ),
            leave_sums[:3],
            feed_sums[:4],
            pair_sums.reshape(-1, channels),
        ]
    )
    table = jnp.pad(table, ((0, -table.shape[0] % 8), (0, 0)))
    late = (grad_conv_two, grad_conv_one, grad_qkv_proj, grad_proj_in)
    if reduce_fits([part.shape for part in late], bands, groups):
        grad_images, table = lax.optimization_barrier((grad_images, table))
        *late, table = reduce_parts(late, table, bands, groups)
        late = [part.astype(F32) for part in late]
    else:
        table = lax.all_gather(lax.psum(table, "rows"), "heads")
        late = [reduced(part) for part in late]
    rows_conv_two, rows_conv_one, rows_qkv, rows_proj_in = late
    rows_early = early.astype(F32)
    pieces = feed_pieces(channels, geglu_proj.shape[1], feed_out.shape[0], bands)
    rows_geglu = jnp.concatenate(
        [rows_early[first : first + size] for first, size in pieces[0]], axis=1
    )
    rows_feed, rows_proj_out, rows_attn_out = (
        rows_early[first : first + size] for ((first, size),) in pieces[1:]
    )
    all_cross = table[:, :image_count].reshape(-1, channels)
    all_shift = table[:, image_count : 2 * image_count].reshape(-1, channels)
    joint = jnp.sum(table[:, 2 * image_count :], axis=0)
    grad_cross_out = jnp.dot(own(value.astype(F32), 1).T, all_cross, precision=HIGH)
    grad_value = jnp.dot(all_cross, cross_out.astype(F32).T, precision=HIGH)
    grad_cross_value = jnp.dot(own(context, 1).T, grad_value, precision=HIGH)
    grad_context = jnp.dot(grad_value, own(cross_value).astype(F32).T, precision=HIGH)
    grad_class_table = jnp.dot(hot.astype(F32).T, grad_context, precision=HIGH)
    grad_time_proj = jnp.dot(own(embed.astype(F32), 1).T, all_shift, precision=HIGH)
    singles = [own(joint[at]) for at in range(14)]
    grad_geglu_bias = own(joint[14 : 14 + geglu_bias.shape[0] // channels].reshape(-1))
    keys_values = rows_qkv[:, : 2 * channels].reshape(-1, HEADS, 2, head_dim)
    rows_qkv = jnp.concatenate(
        [
            rows_qkv[:, 2 * channels :],
            keys_values[:, :, 0].reshape(-1, channels),
            keys_values[:, :, 1].reshape(-1, channels),
        ],
        axis=1,
    )
    return (
        output.reshape(images.shape),
        grad_images,
        singles[0],
        singles[1],
        rows_conv_one,
        grad_time_proj,
        own(jnp.sum(all_shift, axis=0)),
        singles[2],
        singles[3],
        rows_conv_two,
        singles[6],
        singles[4],
        singles[5],
        rows_proj_in,
        singles[9],
        singles[7],
        singles[8],
        rows_qkv,
        rows_attn_out,
        own(jnp.sum(all_cross, axis=0)),
        grad_class_table,
        grad_cross_value,
        grad_cross_out,
        singles[12],
        singles[13],
        rows_geglu,
        grad_geglu_bias,
        rows_feed,
        singles[11],
        rows_proj_out,
        singles[10],
    )


def solution(mesh):
    return jax.shard_map(
        per_device,
        mesh=mesh,
        in_specs=(
            P("heads", "rows", None, None),
            P(),
            P(),
            P(),
            P("heads", "rows", None, None),
            P(),
            P(),
            P(),
            P(),
            P(),
            P(),
            P(),
            P(),
            P(),
            P(),
            P(),
            P(),
            P(),
            P(),
            P(),
            P(),
            P(),
            P(),
            P(),
            P(),
            P(),
            P(),
            P(),
            P(),
            P(),
            P(),
            P(),
            P(),
            P(),
        ),
        out_specs=(
            P("heads", "rows", None, None),
            P("heads", "rows", None, None),
            P("rows"),
            P("rows"),
            P("rows", None),
            P("rows", None),
            P("rows"),
            P("rows"),
            P("rows"),
            P("rows", None),
            P("rows"),
            P("rows"),
            P("rows"),
            P("rows", None),
            P("rows"),
            P("rows"),
            P("rows"),
            P("rows", None),
            P("rows", None),
            P("rows"),
            P(None, "rows"),
            P("rows", None),
            P("rows", None),
            P("rows"),
            P("rows"),
            P("rows", None),
            P("rows"),
            P("rows", None),
            P("rows"),
            P("rows", None),
            P("rows"),
        ),
        check_vma=False,
    )
```

```python
from functools import partial
import math

import jax
import jax.numpy as jnp
from jax import lax
from jax.experimental import pallas as pl
from jax.experimental.pallas import tpu as pltpu
from jax.sharding import PartitionSpec as P

HEADS = 8
GROUPS = 32
GN_EPS = 1e-06
LN_EPS = 1e-05
HIGH = lax.Precision.HIGHEST
LOG2E = math.log2(math.e)
BF = jnp.bfloat16
F32 = jnp.float32
KEPT = 256

def dot_nt(lhs, rhs):
    return lax.dot_general(lhs, rhs, (((1,), (1,)), ((), ())), preferred_element_type=F32)


def dot_nn(lhs, rhs):
    return lax.dot_general(lhs, rhs, (((1,), (0,)), ((), ())), preferred_element_type=F32)


def lane_ids(rows):
    return lax.broadcasted_iota(jnp.int32, (rows, 128), 1)


def swap_halves(field):
    return pltpu.roll(field, 64, 1)


def pieces_of(column):
    top = column.astype(BF).astype(F32)
    rest = column - top
    mid = rest.astype(BF).astype(F32)
    return (top, mid, rest - mid)


def extras(column, lanes, first):
    top, mid, low = pieces_of(column)
    return jnp.where(
        lanes == first, top, jnp.where(lanes == first + 1, mid, jnp.where(lanes == first + 2, low, 0.0))
    )


def block_of(count, pref):
    for size in pref:
        if count % size == 0:
            return size
    return count


def crop(field, width, side):
    rows = field.shape[0] // width
    if side == width:
        return field
    return field.reshape(rows, width, 128)[:, :side].reshape(rows * side, 128)


def uncrop(field, width, side):
    if side == width:
        return field
    rows = field.shape[0] // side
    spread = field.reshape(rows, side, 128)
    return jnp.concatenate(
        [spread, jnp.zeros((rows, width - side, 128), field.dtype)], axis=1
    ).reshape(rows * width, 128)


def unpack_pairs(pairs):
    return jnp.concatenate([pairs, swap_halves(pairs)], axis=0)


def pack_pairs(field, lanes):
    half = field.shape[0] // 2
    return jnp.where(lanes[:half] < 64, field[:half], swap_halves(field[half:]))


def attend_kernel(width, scale, side_ref, qkv_ref, out_ref, norm_ref, kept_ref, q_s, k_s, v_s, vt_s, top_s, stage_s, sems):
    bands, packed, _ = qkv_ref.shape
    band_tokens = packed * 2 // 3
    band_rows = band_tokens // width
    side_now = side_ref[0]

    def variant(side):
        tokens = side * side
        used = side // band_rows
        own = band_rows * side
        lanes = lane_ids(own)
        low = lanes < 64
        row_ids = lax.broadcasted_iota(jnp.int32, (128, 128), 0)
        col_ids = lax.broadcasted_iota(jnp.int32, (128, 128), 1)
        picks = jnp.where((row_ids < 64) == (col_ids < 64), 1.0, 0.0).astype(BF)

        def gather_band(band, norms):
            pairs = crop(qkv_ref[band, band_tokens:, :].astype(F32), width, side)
            keys = crop(qkv_ref[band, :band_tokens, :].astype(F32), width, side)
            queries = unpack_pairs(pairs) * (scale * LOG2E)
            head = queries.astype(BF).astype(F32)
            turned = swap_halves(keys)
            rows = pl.ds(pl.multiple_of(band * own, 16), own)
            q_s[rows, :] = jnp.where(low, head, swap_halves(queries - head)).astype(BF)
            k_s[rows, :] = jnp.where(low, keys, turned).astype(BF)
            v_s[rows, :] = jnp.where(low, turned, jnp.where(lanes == 64, 1.0, 0.0)).astype(BF)
            joint = jnp.where(low, queries, turned)
            sums = dot_nn((joint * joint).astype(BF), picks)
            return jnp.maximum(norms, jnp.max(sums, axis=0, keepdims=True))

        norms = lax.fori_loop(0, used, gather_band, jnp.zeros((1, 128), F32))
        step = block_of(tokens, (512, 256))
        for first in range(0, tokens, step):
            vt_s[:, first : first + step] = v_s[first : first + step, :].T
        first_lanes = lane_ids(1) < 64
        query_top = jnp.max(jnp.where(first_lanes, norms, 0.0))
        key_top = jnp.max(jnp.where(first_lanes, 0.0, norms))
        safe = query_top * key_top * 1.05 <= 100.0 * 100.0
        bq = block_of(tokens, (1024, 768, 256))
        bk = block_of(tokens, (1024, 768, 256))

        @pl.when(safe)
        def _():
            top_s[...] = jnp.zeros_like(top_s)

        @pl.when(jnp.logical_not(safe))
        def _():
            def tops(qi, _):
                cols = pl.ds(pl.multiple_of(qi * bq, 256), bq)
                queries = q_s[cols, :]

                def more(ki, top):
                    scores = dot_nt(k_s[pl.ds(pl.multiple_of(ki * bk, 256), bk), :], queries)
                    return jnp.maximum(top, jnp.max(scores, axis=0, keepdims=True))

                top = lax.fori_loop(0, tokens // bk, more, jnp.full((1, bq), -jnp.inf, F32))
                top_s[:, cols] = jnp.broadcast_to(top, (8, bq))
                return 0

            lax.fori_loop(0, tokens // bq, tops, 0)

        parts = bq // KEPT
        steps = tokens // bq

        def stores(qi, first=0, rows=tokens):
            slot = lax.rem(qi, 2)
            return [
                pltpu.make_async_copy(
                    stage_s.at[slot, pl.ds(first, rows), pl.ds(part * KEPT, KEPT)],
                    kept_ref.at[pl.ds(pl.multiple_of((qi * parts + part) * tokens + first, 256), rows)],
                    sems.at[slot, part],
                )
                for part in range(parts)
            ]

        def main(qi, _):
            cols = pl.ds(pl.multiple_of(qi * bq, 256), bq)
            queries = q_s[cols, :]
            top = top_s[0:1, cols]
            slot = lax.rem(qi, 2)

            @pl.when(qi >= 2)
            def _():
                for item in stores(qi - 2):
                    item.wait()

            total = jnp.zeros((80, bq), F32)
            for first in range(0, tokens, bk):
                scores = dot_nt(k_s[first : first + bk, :], queries)
                weights = jnp.exp2(scores - top).astype(BF)
                stage_s[slot, first : first + bk, :bq] = weights
                total = total + dot_nn(vt_s[0:80, first : first + bk], weights)
                for item in stores(qi, first, bk):
                    item.start()
            row_total = total[64:65]
            mixed = total[:64] / row_total
            extra = jnp.broadcast_to(1.0 / row_total, (64, bq))
            norm_ref[cols, :] = jnp.concatenate([mixed, extra], axis=0).T
            return 0

        lax.fori_loop(0, steps, main, 0)
        for qi in range(max(steps - 2, 0), steps):
            for item in stores(qi):
                item.wait()

        def spread_band(band, _):
            rows = pl.ds(pl.multiple_of(band * own, 16), own)
            pairs = pack_pairs(norm_ref[rows, :], lanes)
            out_ref[band] = uncrop(pairs, width, side).astype(BF)
            return 0

        lax.fori_loop(0, used, spread_band, 0)
        if used < bands:
            out_ref[used:] = jnp.zeros((bands - used,) + out_ref.shape[1:], BF)

    for side in (width, width * 3 // 4, width // 2):
        pl.when(side_now == side)(partial(variant, side))


def attend(side, qkv, width, scale):
    bands, packed, _ = qkv.shape
    tokens = bands * packed * 2 // 3
    vm = pl.BlockSpec(memory_space=pltpu.VMEM)
    return pl.pallas_call(
        partial(attend_kernel, width, scale),
        out_shape=(
            jax.ShapeDtypeStruct((bands, packed // 3, 128), BF),
            jax.ShapeDtypeStruct((tokens, 128), F32),
            jax.ShapeDtypeStruct((tokens // KEPT * tokens, KEPT), BF),
        ),
        in_specs=[pl.BlockSpec(memory_space=pltpu.SMEM), vm],
        out_specs=(vm, vm, pl.BlockSpec(memory_space=pl.ANY)),
        scratch_shapes=[
            pltpu.VMEM((tokens, 128), BF),
            pltpu.VMEM((tokens, 128), BF),
            pltpu.VMEM((tokens, 128), BF),
            pltpu.VMEM((128, tokens), BF),
            pltpu.VMEM((8, tokens), F32),
            pltpu.VMEM((2, tokens, 1024), BF),
            pltpu.SemaphoreType.DMA((2, 4)),
        ],
        compiler_params=pltpu.CompilerParams(vmem_limit_bytes=48 << 20),
        cost_estimate=pl.CostEstimate(
            flops=4 * 256 * tokens * tokens, bytes_accessed=8 << 20, transcendentals=tokens * tokens
        ),
        name="attend",
    )(side, qkv)


def attend_back_kernel(width, scale, side_ref, qkv_ref, grad_ref, norm_ref, kept_ref, out_ref,
                       k_s, g_s, gn_s, v_s, q_s, kt_s, dq_s, dkv_s, recip_s, stage_s, sems):
    bands, packed, _ = qkv_ref.shape
    band_tokens = packed * 2 // 3
    band_rows = band_tokens // width
    side_now = side_ref[0]

    def variant(side):
        tokens = side * side
        used = side // band_rows
        own = band_rows * side
        lanes = lane_ids(own)
        low = lanes < 64
        ones_high = jnp.where((lanes >= 64) & (lanes < 67), 1.0, 0.0)
        bq = block_of(tokens, (1024, 768, 256))
        bk = block_of(tokens, (512, 768, 256))
        parts = bq // KEPT
        steps = tokens // bq

        def loads(qi):
            slot = lax.rem(qi, 2)
            return [
                pltpu.make_async_copy(
                    kept_ref.at[pl.ds(pl.multiple_of((qi * parts + part) * tokens, 256), tokens)],
                    stage_s.at[slot, pl.ds(0, tokens), pl.ds(part * KEPT, KEPT)],
                    sems.at[slot, part],
                )
                for part in range(parts)
            ]

        for item in loads(0):
            item.start()

        def gather_band(band, _):
            queries = unpack_pairs(crop(qkv_ref[band, band_tokens:, :].astype(F32), width, side))
            keys = crop(qkv_ref[band, :band_tokens, :].astype(F32), width, side)
            grads = unpack_pairs(crop(grad_ref[0, band].astype(F32), width, side))
            rows = pl.ds(pl.multiple_of(band * own, 16), own)
            mixed = norm_ref[rows, :]
            delta = jnp.sum(jnp.where(low, grads * mixed, 0.0), axis=1, keepdims=True)
            turned = swap_halves(keys)
            q_s[rows, :] = jnp.where(low, 0.0, swap_halves(queries)).astype(BF)
            gn_s[rows, :] = jnp.where(low, grads, 0.0).astype(BF)
            g_s[rows, :] = jnp.where(low, grads, extras(-delta, lanes, 64)).astype(BF)
            v_s[rows, :] = jnp.where(low, turned, ones_high).astype(BF)
            k_s[rows, :] = jnp.where(low, keys, 0.0).astype(BF)
            return 0

        lax.fori_loop(0, used, gather_band, 0)
        step = block_of(tokens, (512, 256))
        for first in range(0, tokens, step):
            kt_s[:, first : first + step] = k_s[first : first + step, :].T[:64]
            recip_s[:, first : first + step] = norm_ref[first : first + step, :].T[64:72]
        dkv_s[...] = jnp.zeros_like(dkv_s)

        def main(qi, _):
            cols = pl.ds(pl.multiple_of(qi * bq, 256), bq)
            slot = lax.rem(qi, 2)
            for item in loads(qi):
                item.wait()

            @pl.when(qi + 1 < steps)
            def _():
                for item in loads(qi + 1):
                    item.start()

            grads = g_s[cols, :]
            plain = gn_s[cols, :]
            queries = q_s[cols, :]
            recip = recip_s[0:1, cols]
            total = jnp.zeros((64, bq), F32)
            for first in range(0, tokens, bk):
                probs = stage_s[slot, first : first + bk, :bq].astype(F32) * recip
                slopes = dot_nt(v_s[first : first + bk, :], grads)
                grad_scores = (probs * slopes).astype(BF)
                dkv_s[first : first + bk, :] += dot_nn(probs.astype(BF), plain) + dot_nn(grad_scores, queries)
                total = total + dot_nn(kt_s[:, first : first + bk], grad_scores)
            dq_s[:, cols] = total
            return 0

        lax.fori_loop(0, steps, main, 0)
        for first in range(0, tokens, step):
            turned = dq_s[:, first : first + step]
            v_s[first : first + step, :] = (
                jnp.concatenate([turned, turned], axis=0).T * scale
            ).astype(BF)

        def spread_band(band, _):
            rows = pl.ds(pl.multiple_of(band * own, 16), own)
            joint = swap_halves(dkv_s[rows, :])
            out_ref[band, :band_tokens] = uncrop(jnp.where(low, joint * scale, joint), width, side).astype(BF)
            pairs = pack_pairs(v_s[rows, :].astype(F32), lanes)
            out_ref[band, band_tokens:] = uncrop(pairs, width, side).astype(BF)
            return 0

        lax.fori_loop(0, used, spread_band, 0)
        if used < bands:
            out_ref[used:] = jnp.zeros((bands - used,) + out_ref.shape[1:], BF)

    for side in (width, width * 3 // 4, width // 2):
        pl.when(side_now == side)(partial(variant, side))


def attend_back(side, qkv, grads, spot, norms, kept, width, scale):
    bands, packed, _ = qkv.shape
    tokens = bands * packed * 2 // 3
    vm = pl.BlockSpec(memory_space=pltpu.VMEM)
    rows = pltpu.VMEM((tokens, 128), BF)
    return pl.pallas_call(
        partial(attend_back_kernel, width, scale),
        out_shape=jax.ShapeDtypeStruct((bands, packed, 128), BF),
        grid=(1,),
        in_specs=[
            pl.BlockSpec(memory_space=pltpu.SMEM),
            vm,
            pl.BlockSpec((1,) + grads.shape[1:], lambda at: (spot, 0, 0, 0)),
            vm,
            pl.BlockSpec(memory_space=pl.ANY),
        ],
        out_specs=vm,
        scratch_shapes=[rows] * 5
        + [
            pltpu.VMEM((64, tokens), BF),
            pltpu.VMEM((64, tokens), F32),
            pltpu.VMEM((tokens, 128), F32),
            pltpu.VMEM((8, tokens), F32),
            pltpu.VMEM((2, tokens, 1024), BF),
            pltpu.SemaphoreType.DMA((2, 4)),
        ],
        compiler_params=pltpu.CompilerParams(vmem_limit_bytes=56 << 20),
        cost_estimate=pl.CostEstimate(
            flops=8 * 256 * tokens * tokens, bytes_accessed=40 << 20, transcendentals=0
        ),
        name="attend_back",
    )(side, qkv, grads, norms, kept)


def dot_tn(lhs, rhs):
    return lax.dot_general(lhs, rhs, (((0,), (0,)), ((), ())), preferred_element_type=F32)


def row_of(table, at):
    ids = lax.broadcasted_iota(jnp.int32, table.shape, 0)
    return jnp.sum(jnp.where(ids == at, table, 0.0), axis=0, keepdims=True)


def put_row(table_ref, at, row):
    ids = lax.broadcasted_iota(jnp.int32, table_ref.shape, 0)
    table_ref[...] = jnp.where(ids == at, row, table_ref[...])


def col_sum(field):
    return jnp.sum(field, axis=0, keepdims=True)


def spread_lanes(tile, channels):
    return jnp.concatenate([tile] * (channels // 128), axis=1)


def token_ids(shape):
    return lax.broadcasted_iota(jnp.int32, (shape[0], 128), 0)


def pixel_inside(shape, first_row, side, width):
    token = token_ids(shape)
    row = first_row + lax.shift_right_logical(token, int(math.log2(width)))
    return spread_lanes((row >= 0) & (row < side) & ((token & (width - 1)) < side), shape[1])


def sigmoid(field):
    return 0.5 * jnp.tanh(0.5 * field) + 0.5


def moments(avg_ref, at):
    table = avg_ref[...]
    mean = row_of(table, 2 * at)
    return mean, lax.rsqrt(row_of(table, 2 * at + 1) - mean * mean + GN_EPS)


def put_taps(taps_s, first, field, width, flipped):
    channels = field.shape[1]
    column = token_ids(field.shape) & (width - 1)
    count = field.shape[0]
    left = jnp.where(spread_lanes(column == 0, channels), 0.0, pltpu.roll(field, 1, 0))
    right = jnp.where(spread_lanes(column == width - 1, channels), 0.0, pltpu.roll(field, count - 1, 0))
    order = (right, field, left) if flipped else (left, field, right)
    for at, part in enumerate(order):
        taps_s[first : first + count, at * channels : (at + 1) * channels] = part.astype(BF)


VMEM_WHOLE = pl.BlockSpec(memory_space=pltpu.VMEM)
SMEM_WHOLE = pl.BlockSpec(memory_space=pltpu.SMEM)


def image_block(tokens, channels):
    return pl.BlockSpec((1, tokens, channels), lambda at: (at, 0, 0))


def edge_block(width, channels):
    return pl.BlockSpec((2, 1, width, channels), lambda at: (0, at, 0, 0))


def table_block(channels, rows=8):
    return pl.BlockSpec((rows, channels), lambda at: (0, 0))


def fixed_block(shape):
    return pl.BlockSpec(shape, lambda at: (0,) * len(shape), pipeline_mode=pl.Buffered(1))


def greet_rows(me, bands):
    barrier = pltpu.get_barrier_semaphore()
    for away in range(1, bands):
        pl.semaphore_signal(
            barrier, inc=1, device_id={"rows": lax.rem(me + away, bands)},
            device_id_type=pl.DeviceIdType.MESH,
        )


def meet_rows(bands):
    pl.semaphore_wait(pltpu.get_barrier_semaphore(), bands - 1)


def row_copy(src, dst, send, recv, target):
    return pltpu.make_async_remote_copy(
        src_ref=src, dst_ref=dst, send_sem=send, recv_sem=recv, device_id={"rows": target},
        device_id_type=pl.DeviceIdType.MESH,
    )


def edge_copies(top, bottom, halo, at, send, recv, me, bands):
    return [
        row_copy(top, halo.at[1, at], send.at[0, at], recv.at[1, at], lax.rem(me + bands - 1, bands)),
        row_copy(bottom, halo.at[0, at], send.at[1, at], recv.at[0, at], lax.rem(me + 1, bands)),
    ]


def group_average(sums, weight_ref, scale_ref, slots, send, recv, me, bands):
    slots[me] = sums
    copies = [
        row_copy(slots.at[me], slots.at[me], send.at[away], recv.at[me], lax.rem(me + away, bands))
        for away in range(1, bands)
    ]
    for item in copies:
        item.start()
    channels = sums.shape[1]
    size = channels // GROUPS
    rows = lax.broadcasted_iota(jnp.int32, (channels, channels), 0) // size
    cols = lax.broadcasted_iota(jnp.int32, (channels, channels), 1) // size
    same = jnp.where(rows == cols, 1.0, 0.0)
    for away in range(1, bands):
        source = lax.rem(me + away, bands)
        row_copy(slots.at[source], slots.at[source], send.at[away], recv.at[source], source).wait_recv()
    total = slots[0]
    for at in range(1, bands):
        total = total + slots[at]
    for item in copies:
        item.wait_send()
    return jnp.dot(
        total * weight_ref[...], same, precision=HIGH, preferred_element_type=F32
    ) * scale_ref[...]


def exchange_scratch(images, width, channels, bands):
    return [
        pltpu.VMEM((2, images, width, channels), BF),
        pltpu.VMEM((bands, 8, channels), F32),
        pltpu.SemaphoreType.DMA((2, images)),
        pltpu.SemaphoreType.DMA((2, images)),
        pltpu.SemaphoreType.DMA((bands,)),
        pltpu.SemaphoreType.DMA((bands,)),
    ]


def share_edges(grads, at, width, halo_ref, scratch, me, bands, met=False):
    edge_s, _, send, recv = scratch[:4]
    tokens = grads.shape[0]
    edge_s[0, at] = grads[:width].astype(BF)
    edge_s[1, at] = grads[tokens - width :].astype(BF)
    if not met:
        pl.when(at == 0)(partial(meet_rows, bands))
    for item in edge_copies(edge_s.at[0, at], edge_s.at[1, at], halo_ref, at, send, recv, me, bands):
        item.start()


def close_exchange(sums, weight_ref, scale_ref, avg_ref, halo_ref, scratch, me, bands):
    edge_s, slots, send, recv, sum_send, sum_recv = scratch
    avg_ref[...] = group_average(sums, weight_ref, scale_ref, slots, sum_send, sum_recv, me, bands)
    for at in range(edge_s.shape[1]):
        for item in edge_copies(
            edge_s.at[0, at], edge_s.at[1, at], halo_ref, at, send, recv, me, bands
        ):
            item.wait_send()
        for end in range(2):
            edge = halo_ref.at[end, at]
            row_copy(
                edge, edge, send.at[end, at], recv.at[end, at], lax.rem(me + 1, bands)
            ).wait_recv()


def begin_kernel(width, bands, place, sides, field_ref, whole_ref, weight_ref, scale_ref,
                 avg_ref, halo_ref, sums_s, slots, send, recv, sum_send, sum_recv):
    at = pl.program_id(0)
    last = pl.num_programs(0) - 1
    me = lax.axis_index("rows")
    images, tokens, _ = whole_ref.shape

    def edges():
        return [
            edge_copies(
                whole_ref.at[image, pl.ds(0, width)], whole_ref.at[image, pl.ds(tokens - width, width)],
                halo_ref, image, send, recv, me, bands,
            )
            for image in range(images)
        ]

    @pl.when(at == 0)
    def _():
        greet_rows(me, bands)
        sums_s[...] = jnp.zeros_like(sums_s)
        meet_rows(bands)
        for pair in edges():
            for item in pair:
                item.start()

    field = field_ref[0].astype(F32)
    field = jnp.where(pixel_inside(field.shape, place[0], sides[at], width), field, 0.0)
    put_row(sums_s, 2 * at, col_sum(field))
    put_row(sums_s, 2 * at + 1, col_sum(field * field))

    @pl.when(at == last)
    def _():
        avg_ref[...] = group_average(
            sums_s[...], weight_ref, scale_ref, slots, sum_send, sum_recv, me, bands
        )
        for image, pair in enumerate(edges()):
            for item in pair:
                item.wait_send()
            for end in range(2):
                edge = halo_ref.at[end, image]
                row_copy(
                    edge, edge, send.at[end, image], recv.at[end, image], lax.rem(me + 1, bands)
                ).wait_recv()


def begin(place, sides, field, weight, scale, width, bands):
    images, tokens, channels = field.shape
    anywhere = pl.BlockSpec(memory_space=pl.ANY)
    return pl.pallas_call(
        partial(begin_kernel, width, bands),
        grid=(images,),
        out_shape=(
            jax.ShapeDtypeStruct((8, channels), F32),
            jax.ShapeDtypeStruct((2, images, width, channels), BF),
        ),
        in_specs=[
            SMEM_WHOLE,
            SMEM_WHOLE,
            image_block(tokens, channels),
            anywhere,
            table_block(channels, 1),
            table_block(channels),
        ],
        out_specs=(table_block(channels), anywhere),
        scratch_shapes=[pltpu.VMEM((8, channels), F32)]
        + exchange_scratch(images, width, channels, bands)[1:],
        compiler_params=pltpu.CompilerParams(collective_id=1, has_side_effects=True),
        name="begin",
    )(place, sides, field, field, weight, scale)


def conv_forward_kernel(width, bands, base_given, *refs):
    (place, sides, field_ref, halo_ref, avg_ref, gain_ref, bias_ref, weight_ref, shift_ref, ones_ref,
     scale_ref, base_ref, out_ref, next_avg, next_halo) = refs[:15]
    refs = refs[15:]
    if not base_given:
        ride_halo, ride_send, ride_recv = refs[0], refs[-2], refs[-1]
        refs = refs[1:-2]
    taps_s, stats_ref = refs[:2]
    scratch = refs[2:]
    me = lax.axis_index("rows")
    at = pl.program_id(0)
    last = pl.num_programs(0) - 1

    @pl.when(at == 0)
    def _():
        greet_rows(me, bands)
        stats_ref[...] = jnp.zeros_like(stats_ref)

    _, tokens, channels = field_ref.shape
    first_row = place[0]
    side = sides[at]
    mean, inv_std = moments(avg_ref, at)
    slope = inv_std * gain_ref[...]
    offset = bias_ref[...] - mean * slope

    def active(field, row):
        normed = field.astype(F32) * slope + offset
        inside = pixel_inside(normed.shape, row, side, width)
        return jnp.where(inside, normed * sigmoid(normed), 0.0)

    rows = tokens // width
    put_taps(taps_s, 0, active(halo_ref[0, 0], first_row - 1), width, False)
    put_taps(taps_s, width, active(field_ref[0], first_row), width, False)
    put_taps(taps_s, width + tokens, active(halo_ref[1, 0], first_row + rows), width, False)
    deep = 3 * channels
    total = dot_nn(taps_s[:tokens], weight_ref[:deep])
    for tap in (1, 2):
        total = total + dot_nn(
            taps_s[tap * width : tap * width + tokens], weight_ref[tap * deep : (tap + 1) * deep]
        )
    total = total + row_of(shift_ref[...], at)
    inside = pixel_inside(total.shape, first_row, side, width)
    if base_given:
        total = total + jnp.where(inside, base_ref[0].astype(F32), 0.0)
    out_ref[0] = total
    share_edges(total, at, width, next_halo, scratch, me, bands)
    if not base_given:
        ride = edge_copies(
            base_ref.at[at, pl.ds(0, width)], base_ref.at[at, pl.ds(tokens - width, width)], ride_halo,
            at, ride_send, ride_recv, me, bands,
        )
        for item in ride:
            item.start()
    masked = jnp.where(inside, total, 0.0)
    put_row(stats_ref, 2 * at, col_sum(masked))
    put_row(stats_ref, 2 * at + 1, col_sum(masked * masked))

    @pl.when(at == last)
    def _():
        close_exchange(stats_ref[...], ones_ref, scale_ref, next_avg, next_halo, scratch, me, bands)
        if not base_given:
            for image in range(base_ref.shape[0]):
                for item in edge_copies(
                    base_ref.at[image, pl.ds(0, width)], base_ref.at[image, pl.ds(tokens - width, width)],
                    ride_halo, image, ride_send, ride_recv, me, bands,
                ):
                    item.wait_send()
                for end in range(2):
                    edge = ride_halo.at[end, image]
                    row_copy(
                        edge, edge, ride_send.at[end, image], ride_recv.at[end, image], lax.rem(me + 1, bands)
                    ).wait_recv()


def conv_forward(place, sides, field, halo, avg, gain, bias, weight, shift, ones, scale, base, added, width,
                 bands):
    images, tokens, channels = field.shape
    anywhere = pl.BlockSpec(memory_space=pl.ANY)
    halos = jax.ShapeDtypeStruct((2, images, width, channels), BF)
    return pl.pallas_call(
        partial(conv_forward_kernel, width, bands, added),
        grid=(images,),
        out_shape=(
            jax.ShapeDtypeStruct(field.shape, F32),
            jax.ShapeDtypeStruct((8, channels), F32),
            halos,
        )
        + (() if added else (halos,)),
        in_specs=[
            SMEM_WHOLE,
            SMEM_WHOLE,
            image_block(tokens, channels),
            edge_block(width, channels),
            table_block(channels),
            table_block(channels, 1),
            table_block(channels, 1),
            fixed_block(weight.shape),
            table_block(channels),
            table_block(channels, 1),
            table_block(channels),
            image_block(tokens, channels) if added else anywhere,
        ],
        out_specs=(image_block(tokens, channels), table_block(channels), anywhere)
        + (() if added else (anywhere,)),
        scratch_shapes=[
            pltpu.VMEM((tokens + 2 * width, 3 * channels), BF),
            pltpu.VMEM((8, channels), F32),
        ]
        + exchange_scratch(images, width, channels, bands)
        + ([] if added else [pltpu.SemaphoreType.DMA((2, images))] * 2),
        compiler_params=pltpu.CompilerParams(
            vmem_limit_bytes=56 << 20, collective_id=2 if added else 3, has_side_effects=True
        ),
        name="conv_forward",
    )(place, sides, field, halo, avg, gain, bias, weight, shift, ones, scale, base)


def conv_backward_kernel(width, bands, added, *refs):
    refs = list(refs)
    me = lax.axis_index("rows")
    (place, sides, grad_ref, grad_halo, field_ref, field_halo, avg_ref, back_avg, gain_ref) = refs[:9]
    refs = refs[9:]
    if added:
        add_ref, add_halo = refs[:2]
        refs = refs[2:]
    (weight_ref, prior_ref, prior_avg, prior_gain, prior_bias, scale_ref) = refs[:6]
    refs = refs[6:]
    if added:
        kept_ref = refs[0]
        refs = refs[1:]
    out_ref, next_avg, stats_ref, sums_ref, weight_grad = refs[:5]
    next_halo = None
    if added:
        next_halo = refs[5]
        refs = refs[1:]
    taps_s, act_s, total_s = refs[5:8]
    scratch = refs[8:]
    at = pl.program_id(0)
    last = pl.num_programs(0) - 1
    _, tokens, channels = grad_ref.shape
    first_row = place[0]
    side = sides[at]
    mean, inv_std = moments(avg_ref, at)
    back = back_avg[...]
    back_mean, back_cross = row_of(back, 2 * at), row_of(back, 2 * at + 1)
    gain = gain_ref[...]
    grad_slope = inv_std * gain
    field_slope = inv_std * inv_std * back_cross
    offset = inv_std * back_mean - mean * field_slope

    def through(grads, field, extra, row):
        moved = grads.astype(F32) * grad_slope - field.astype(F32) * field_slope - offset
        if extra is not None:
            moved = moved + extra.astype(F32)
        return jnp.where(pixel_inside(moved.shape, row, side, width), moved, 0.0)

    rows = tokens // width
    own = through(grad_ref[0], field_ref[0], add_ref[0] if added else None, first_row)
    put_taps(taps_s, width, own, width, True)
    for end, row, first in ((0, first_row - 1, 0), (1, first_row + rows, width + tokens)):
        put_taps(
            taps_s,
            first,
            through(grad_halo[end, 0], field_halo[end, 0], add_halo[end, 0] if added else None, row),
            width,
            True,
        )
    if added:
        kept_ref[0] = own

    @pl.when(at == 0)
    def _():
        greet_rows(me, bands)
        stats_ref[...] = jnp.zeros_like(stats_ref)
        sums_ref[...] = jnp.zeros_like(sums_ref)
        total_s[...] = jnp.zeros_like(total_s)

    put_row(sums_ref, at, col_sum(own))
    prior_mean, prior_std = moments(prior_avg, at)
    centred = (prior_ref[0].astype(F32) - prior_mean) * prior_std
    normed = centred * prior_gain[...] + prior_bias[...]
    gate = sigmoid(normed)
    inside = pixel_inside(normed.shape, first_row, side, width)
    act_s[...] = jnp.where(inside, normed * gate, 0.0).T.astype(BF)
    act_t = act_s[...]
    moved = None
    for down in range(3):
        lines = pl.ds((2 - down) * width, tokens)
        for across in range(3):
            tap = 3 * down + across
            low = taps_s[lines, across * channels : (across + 1) * channels]
            part = slice(tap * channels, (tap + 1) * channels)
            term = dot_nt(low, weight_ref[part])
            moved = term if moved is None else moved + term
            total_s[part] += dot_nn(act_t, low)
    grads = jnp.where(inside, moved * (gate + normed * gate * (1.0 - gate)), 0.0)
    out_ref[0] = grads
    if added:
        share_edges(grads, at, width, next_halo, scratch, me, bands)
    put_row(stats_ref, 2 * at, col_sum(grads))
    put_row(stats_ref, 2 * at + 1, col_sum(grads * centred))

    @pl.when(at == last)
    def _():
        if added:
            close_exchange(stats_ref[...], prior_gain, scale_ref, next_avg, next_halo, scratch, me, bands)
        else:
            meet_rows(bands)
            next_avg[...] = group_average(stats_ref[...], prior_gain, scale_ref, *scratch, me, bands)
        weight_grad[...] = total_s[...].astype(BF)


def conv_backward(place, sides, grads, grad_halo, field, field_halo, avg, back_avg, gain, extra,
                  extra_halo, weight, prior, prior_avg, prior_gain, prior_bias, scale, width, bands):
    images, tokens, channels = grads.shape
    added = extra is not None
    tok = image_block(tokens, channels)
    edge = edge_block(width, channels)
    table = table_block(channels)
    vector = table_block(channels, 1)
    ins = [place, sides, grads, grad_halo, field, field_halo, avg, back_avg, gain]
    specs = [SMEM_WHOLE, SMEM_WHOLE, tok, edge, tok, edge, table, table, vector]
    if added:
        ins += [extra, extra_halo]
        specs += [tok, edge]
    ins += [weight, prior, prior_avg, prior_gain, prior_bias, scale]
    specs += [fixed_block(weight.shape), tok, table, vector, vector, table]
    outs = [
        jax.ShapeDtypeStruct(grads.shape, F32),
        jax.ShapeDtypeStruct((8, channels), F32),
        jax.ShapeDtypeStruct((8, channels), F32),
        jax.ShapeDtypeStruct((8, channels), F32),
        jax.ShapeDtypeStruct(weight.shape, BF),
    ]
    out_specs = [tok, table, table, table, fixed_block(weight.shape)]
    if added:
        outs.append(jax.ShapeDtypeStruct((2, images, width, channels), BF))
        out_specs.append(pl.BlockSpec(memory_space=pl.ANY))
        outs.insert(0, jax.ShapeDtypeStruct(grads.shape, F32))
        out_specs.insert(0, tok)
    return pl.pallas_call(
        partial(conv_backward_kernel, width, bands, added),
        grid=(images,),
        out_shape=outs,
        in_specs=specs,
        out_specs=out_specs,
        scratch_shapes=[
            pltpu.VMEM((tokens + 2 * width, 3 * channels), BF),
            pltpu.VMEM((channels, tokens), BF),
            pltpu.VMEM(weight.shape, F32),
        ]
        + (
            exchange_scratch(images, width, channels, bands)
            if added
            else [
                pltpu.VMEM((bands, 8, channels), F32),
                pltpu.SemaphoreType.DMA((bands,)),
                pltpu.SemaphoreType.DMA((bands,)),
            ]
        ),
        compiler_params=pltpu.CompilerParams(
            vmem_limit_bytes=60 << 20, collective_id=4 if added else 6, has_side_effects=True
        ),
        name="conv_backward",
    )(*ins)


def layer_stats(field):
    centre = jnp.mean(field, axis=-1, keepdims=True)
    centred = field - centre
    inv_std = lax.rsqrt(jnp.mean(centred * centred, axis=-1, keepdims=True) + LN_EPS)
    return centred * inv_std, inv_std


def layer_back(grads, gain, centred, inv_std):
    scaled = grads * gain
    return inv_std * (
        scaled
        - jnp.mean(scaled, axis=-1, keepdims=True)
        - centred * jnp.mean(scaled * centred, axis=-1, keepdims=True)
    )


def turn_qkv(weight_ref, turned_s):
    rows, channels = weight_ref.shape[0], weight_ref.shape[1] // 3
    low = lane_ids(rows) < 64
    for head in range(HEADS):
        first = (head // 2) * 128
        keys = weight_ref[:, channels + first : channels + first + 128].astype(F32)
        values = weight_ref[:, 2 * channels + first : 2 * channels + first + 128].astype(F32)
        if head % 2 == 0:
            joint = jnp.where(low, keys, swap_halves(values))
        else:
            joint = jnp.where(low, swap_halves(keys), values)
        turned_s[:, head * 128 : head * 128 + 128] = joint.astype(BF)
    turned_s[:, 2 * channels :] = weight_ref[:, :channels]


def entry_kernel(bands, direct, field_ref, avg_ref, gain_ref, bias_ref, proj_ref, proj_bias, ln_gain,
                 ln_bias, qkv_ref, stream_ref, *refs):
    images = pl.num_programs(0)
    at = pl.program_id(0)
    if direct:
        count = len(refs) - 4
        sent_refs, (turned_s, first_s, send, recv) = refs[:count], refs[count:]
        me = lax.axis_index("rows")
    else:
        sent_refs, turned_s = refs[:-1], refs[-1]
    _, tokens, channels = field_ref.shape
    half = tokens // 2

    @pl.when(at == 0)
    def _():
        if direct:
            greet_rows(me, bands)
        turn_qkv(qkv_ref, turned_s)

    mean, inv_std = moments(avg_ref, at)
    slope = inv_std * gain_ref[...]
    flat = (field_ref[0] * slope + (bias_ref[...] - mean * slope)).astype(BF)
    stream = dot_nn(flat, proj_ref[...]) + proj_bias[...]
    stream_ref[0] = stream
    centred, _ = layer_stats(stream)
    joint = dot_nn((centred * ln_gain[...] + ln_bias[...]).astype(BF), turned_s[...])
    low = lane_ids(half) < 64

    def put(out):
        for head in range(HEADS):
            out[head, :tokens] = joint[:, head * 128 : head * 128 + 128].astype(BF)
            first = 2 * channels + (head // 2) * 128
            upper, lower = joint[:half, first : first + 128], joint[half:, first : first + 128]
            if head % 2 == 0:
                pairs = jnp.where(low, upper, swap_halves(lower))
            else:
                pairs = jnp.where(low, swap_halves(upper), lower)
            out[head, tokens:] = pairs.astype(BF)

    for image, out in enumerate(sent_refs):
        pl.when(at == image)(partial(put, first_s if direct and image == 0 else out))
    if not direct:
        return
    copies = [
        row_copy(
            first_s.at[lax.rem(me + away, bands)], sent_refs[0].at[me], send.at[away], recv.at[me],
            lax.rem(me + away, bands),
        )
        for away in range(1, bands)
    ]
    own = pltpu.make_async_copy(first_s.at[me], sent_refs[0].at[me], recv.at[me])

    @pl.when(at == 0)
    def _():
        meet_rows(bands)
        for item in copies:
            item.start()
        own.start()

    @pl.when(at == images - 1)
    def _():
        own.wait()
        for away, item in enumerate(copies):
            item.wait_send()
            source = lax.rem(me + away + 1, bands)
            row_copy(
                sent_refs[0].at[source], sent_refs[0].at[source], send.at[away + 1], recv.at[source], source
            ).wait_recv()


def entry(field, avg, gain, bias, proj, proj_bias, ln_gain, ln_bias, qkv, bands):
    images, tokens, channels = field.shape
    vector = table_block(channels, 1)
    direct = bands == HEADS
    packed = (HEADS, tokens * 3 // 2, 128)
    anywhere = pl.BlockSpec(memory_space=pl.ANY)
    params = {"collective_id": 9, "has_side_effects": True} if direct else {}
    return pl.pallas_call(
        partial(entry_kernel, bands, direct),
        grid=(images,),
        out_shape=(jax.ShapeDtypeStruct(field.shape, F32),)
        + (jax.ShapeDtypeStruct(packed, BF),) * images,
        in_specs=[
            image_block(tokens, channels),
            table_block(channels),
            vector,
            vector,
            fixed_block(proj.shape),
            vector,
            vector,
            vector,
            fixed_block(qkv.shape),
        ],
        out_specs=(image_block(tokens, channels),)
        + ((anywhere,) if direct else (fixed_block(packed),))
        + (fixed_block(packed),) * (images - 1),
        scratch_shapes=[pltpu.VMEM(qkv.shape, BF)]
        + (
            [
                pltpu.VMEM(packed, BF),
                pltpu.SemaphoreType.DMA((bands,)),
                pltpu.SemaphoreType.DMA((bands,)),
            ]
            if direct
            else []
        ),
        compiler_params=pltpu.CompilerParams(vmem_limit_bytes=48 << 20, **params),
        name="entry",
    )(field, avg, gain, bias, proj, proj_bias, ln_gain, ln_bias, qkv)


def join_heads(pairs_ref, at):
    half = pairs_ref.shape[-2]
    low = lane_ids(half) < 64
    upper, lower = [], []
    for head in range(0, HEADS, 2):
        one, two = pairs_ref[at, head].astype(F32), pairs_ref[at, head + 1].astype(F32)
        upper.append(jnp.where(low, one, swap_halves(two)))
        lower.append(jnp.where(low, swap_halves(one), two))
    return jnp.concatenate(
        [jnp.concatenate(upper, axis=1), jnp.concatenate(lower, axis=1)], axis=0
    ).astype(BF)


def split_heads(field, out_ref, at):
    half = field.shape[0] // 2
    low = lane_ids(half) < 64
    for head in range(HEADS):
        first = (head // 2) * 128
        upper, lower = field[:half, first : first + 128], field[half:, first : first + 128]
        if head % 2 == 0:
            pairs = jnp.where(low, upper, swap_halves(lower))
        else:
            pairs = jnp.where(low, swap_halves(upper), lower)
        out_ref[at, head] = pairs.astype(BF)


def feed_pieces(channels, wide, hidden, bands):
    size = channels // bands
    geglu = [(at * size, size) for at in range(wide // channels)]
    first = wide // bands
    return (
        geglu,
        [(first, hidden // bands)],
        [(first + hidden // bands, size)],
        [(first + hidden // bands + size, size)],
    )


def feed_kernel(width, bands, per_band, halving, place, sides, *refs):
    given = refs[:per_band]
    (stream_ref, residual_ref, cot_ref, cross_ref, attn_ref, attn_bias, ln_gain, ln_bias,
     geglu_ref, geglu_bias, feed_ref, feed_bias, proj_ref, proj_bias,
     out_ref, three_ref, back_ref, grads_ref, sums_ref, cross_sum, pair_sums, geglu_s, feed_s, proj_s, attn_s,
     turned_s, mixed_s, sent_s, out_send, out_recv, back_send, back_recv, *more) = refs[per_band:]
    if halving:
        given_s, taken_s, pair_sems = more
    at = pl.program_id(0)
    images = pl.num_programs(0)
    last = images - 1
    me = lax.axis_index("rows")

    def move(src, dst, send, recv, target):
        @pl.when(target != me)
        def _():
            pltpu.make_async_remote_copy(
                src_ref=src, dst_ref=dst, send_sem=send, recv_sem=recv, device_id={"rows": target},
                device_id_type=pl.DeviceIdType.MESH,
            ).start()

        @pl.when(target == me)
        def _():
            pltpu.make_async_copy(src, dst, recv).start()

    def arrived(dst, send, recv, source):
        @pl.when(source != me)
        def _():
            pltpu.make_async_remote_copy(
                src_ref=dst, dst_ref=dst, send_sem=send, recv_sem=recv, device_id={"rows": source},
                device_id_type=pl.DeviceIdType.MESH,
            ).wait_recv()

        @pl.when(source == me)
        def _():
            pltpu.make_async_copy(dst, dst, recv).wait()

    def left(src, send, recv, target):
        @pl.when(target != me)
        def _():
            pltpu.make_async_remote_copy(
                src_ref=src, dst_ref=src, send_sem=send, recv_sem=recv, device_id={"rows": target},
                device_id_type=pl.DeviceIdType.MESH,
            ).wait_send()

    def send_spot(spot):
        item = me * per_band + spot
        head, image = item // images, lax.rem(item, images)
        for away in range(bands):
            band = lax.rem(me + away, bands)
            move(
                given[spot].at[band], mixed_s.at[image, head], out_send.at[spot, away],
                out_recv.at[image, head], band,
            )

    @pl.when(at == 0)
    def _():
        greet_rows(me, bands)
        meet_rows(bands)
        send_spot(0)

    for head in range(HEADS):
        arrived(
            mixed_s.at[at, head], out_send.at[0, 0], out_recv.at[at, head], (head * images + at) // per_band
        )
    for spot in range(1, per_band):
        pl.when(at == spot - 1)(partial(send_spot, spot))
    _, tokens, channels = stream_ref.shape
    hidden = feed_ref.shape[0]
    side = sides[at]
    inside = pixel_inside((tokens, channels), place[0], side, width)

    @pl.when(at == 0)
    def _():
        for ref in (sums_ref, cross_sum, pair_sums, geglu_s, feed_s, proj_s, attn_s):
            ref[...] = jnp.zeros_like(ref)

    mixed = join_heads(mixed_s, at)
    three = stream_ref[0] + dot_nn(mixed, attn_ref[...]) + (attn_bias[...] + row_of(cross_ref[...], at))
    centred, inv_std = layer_stats(three)
    feed_in = (centred * ln_gain[...] + ln_bias[...]).astype(BF)
    grad_out = jnp.where(inside, cot_ref[0].astype(F32), 0.0)
    branch = grad_out.astype(BF)
    grad_four = dot_nt(branch, proj_ref[...])
    low_feed = grad_four.astype(BF)
    low_feed_t = grad_four.T.astype(BF)
    feed_in_t = (centred * ln_gain[...] + ln_bias[...]).T.astype(BF)
    four = three + feed_bias[...]
    grad_in = jnp.zeros((tokens, channels), F32)
    step = 512

    def products(first):
        own = slice(first, first + step)
        gates = slice(hidden + first, hidden + first + step)
        value = dot_nn(feed_in, geglu_ref[:, own]) + geglu_bias[:, own]
        gate = dot_nn(feed_in, geglu_ref[:, gates]) + geglu_bias[:, gates]
        return value, gate, dot_nt(low_feed, feed_ref[own])

    ahead = products(0)
    for first in range(0, hidden, step):
        own = slice(first, first + step)
        gates = slice(hidden + first, hidden + first + step)
        value, gate, back = ahead
        if first + step < hidden:
            ahead = products(first + step)
        below = 0.5 + 0.5 * lax.erf(gate * math.sqrt(0.5))
        bell = jnp.exp(gate * gate * -0.5) * (1.0 / math.sqrt(2.0 * math.pi))
        act = gate * below
        gated = (value * act).astype(BF)
        four = four + dot_nn(gated, feed_ref[own])
        feed_s[:, own] += dot_nn(low_feed_t, gated)
        grad_value = back * act
        grad_gate = back * value * (below + gate * bell)
        pair_sums[:, own] += col_sum(grad_value)
        pair_sums[:, gates] += col_sum(grad_gate)
        low_value, low_gate = grad_value.astype(BF), grad_gate.astype(BF)
        geglu_s[:, own] += dot_nn(feed_in_t, low_value)
        geglu_s[:, gates] += dot_nn(feed_in_t, low_gate)
        grad_in = grad_in + dot_nt(low_value, geglu_ref[:, own]) + dot_nt(low_gate, geglu_ref[:, gates])
    last_in = four.astype(BF)
    proj_s[...] += dot_tn(last_in, branch)
    output = residual_ref[0] + dot_nn(last_in, proj_ref[...]) + proj_bias[...]
    out_ref[0] = jnp.where(inside, output, 0.0).astype(BF)
    grad_three = grad_four + layer_back(grad_in, ln_gain[...], centred, inv_std)
    three_ref[0] = grad_three
    low_attn = grad_three.astype(BF)
    attn_s[...] += dot_tn(mixed, low_attn)
    split_heads(dot_nt(low_attn, attn_ref[...]), sent_s, at)
    for head in range(HEADS):
        item = head * images + at
        move(
            sent_s.at[at, head], back_ref.at[lax.rem(item, per_band), me], back_send.at[at, head],
            back_recv.at[lax.rem(item, per_band), me], item // per_band,
        )
    put_row(cross_sum, at, col_sum(grad_three))
    ids = lax.broadcasted_iota(jnp.int32, sums_ref.shape, 0)
    for row, total in enumerate(
        (col_sum(grad_out), col_sum(grad_four), col_sum(grad_in * centred), col_sum(grad_in))
    ):
        sums_ref[...] += jnp.where(ids == row, total, 0.0)

    @pl.when(at == last)
    def _():
        def settle():
            for spot in range(per_band):
                for away in range(bands):
                    band = lax.rem(me + away, bands)
                    left(given[spot].at[band], out_send.at[spot, away], out_recv.at[0, 0], band)
                    arrived(back_ref.at[spot, band], back_send.at[0, 0], back_recv.at[spot, band], band)
            for image in range(sent_s.shape[0]):
                for head in range(HEADS):
                    left(
                        sent_s.at[image, head], back_send.at[image, head], back_recv.at[0, 0],
                        (head * sent_s.shape[0] + image) // per_band,
                    )

        pieces = feed_pieces(channels, 2 * hidden, hidden, bands)

        def put(ref, own, band):
            for total, parts in zip((geglu_s, feed_s, proj_s, attn_s), pieces):
                for at_col, (first, size) in enumerate(parts):
                    if total is feed_s:
                        part = turned_s[pl.ds(pl.multiple_of(band * size, 16), size)]
                    else:
                        part = total[
                            pl.ds(pl.multiple_of(band * size, 16), size),
                            at_col * channels : (at_col + 1) * channels,
                        ]
                    ref[own + (pl.ds(first, size),)] = part.astype(BF)

        for first in range(0, hidden, step):
            turned_s[first : first + step, :] = feed_s[:, first : first + step].T.astype(BF)

        if not halving:
            for band in range(bands):
                put(grads_ref, (band,), band)
            settle()
            return
        for apart in range(bands // 2):
            put(given_s, (apart & 1, apart >> 1), jnp.bitwise_xor(me, 2 * apart + 1))
        item = row_copy(given_s, taken_s, pair_sems.at[0], pair_sems.at[1], jnp.bitwise_xor(me, 1))
        item.start()
        for apart in range(bands // 2):
            put(grads_ref, (apart & 1, apart >> 1), jnp.bitwise_xor(me, 2 * apart))
        item.wait()
        for apart in range(bands // 2):
            own = (apart & 1, apart >> 1)
            grads_ref[own] = (grads_ref[own].astype(F32) + taken_s[own].astype(F32)).astype(BF)
        settle()


def feed(place, sides, mixed, stream, residual, cot, cross, attn, attn_bias, ln_gain, ln_bias, geglu,
         geglu_bias, feed_out, feed_bias, proj, proj_bias, width, bands, halving):
    images, tokens, channels = stream.shape
    tok = image_block(tokens, channels)
    vector = table_block(channels, 1)
    table = table_block(channels)
    half = tokens // 2
    per_band = len(mixed)
    anywhere = pl.BlockSpec(memory_space=pl.ANY)
    wide = geglu.shape[1]
    weights = (geglu, feed_out, proj, attn)
    rows = sum(w.size for w in weights) // channels // bands
    lead = (2, 2) if halving else (bands,)
    grads = lead + (rows, channels)
    return pl.pallas_call(
        partial(feed_kernel, width, bands, per_band, halving),
        grid=(images,),
        out_shape=(
            jax.ShapeDtypeStruct(stream.shape, BF),
            jax.ShapeDtypeStruct(stream.shape, F32),
            jax.ShapeDtypeStruct((per_band, bands, half, 128), BF),
        )
        + (
            jax.ShapeDtypeStruct(grads, BF),
            jax.ShapeDtypeStruct((8, channels), F32),
            jax.ShapeDtypeStruct((8, channels), F32),
            jax.ShapeDtypeStruct((1, wide), F32),
        ),
        in_specs=[
            SMEM_WHOLE,
            SMEM_WHOLE,
        ]
        + [anywhere] * per_band
        + [
            tok,
            tok,
            tok,
            table,
            fixed_block(attn.shape),
            vector,
            vector,
            vector,
            fixed_block(geglu.shape),
            table_block(wide, 1),
            fixed_block(feed_out.shape),
            vector,
            fixed_block(proj.shape),
            vector,
        ],
        out_specs=(tok, tok, anywhere)
        + (fixed_block(grads), table, table, table_block(wide, 1)),
        scratch_shapes=[
            pltpu.VMEM(geglu.shape, F32),
            pltpu.VMEM(feed_out.shape[::-1], F32),
            pltpu.VMEM(proj.shape, F32),
            pltpu.VMEM(attn.shape, F32),
            pltpu.VMEM(feed_out.shape, BF),
        ]
        + [pltpu.VMEM((images, HEADS, half, 128), BF)] * 2
        + [
            pltpu.SemaphoreType.DMA((per_band, bands)),
            pltpu.SemaphoreType.DMA((images, HEADS)),
            pltpu.SemaphoreType.DMA((images, HEADS)),
            pltpu.SemaphoreType.DMA((per_band, bands)),
        ]
        + ([pltpu.VMEM(grads, BF)] * 2 + [pltpu.SemaphoreType.DMA((2,))] if halving else []),
        compiler_params=pltpu.CompilerParams(
            vmem_limit_bytes=62 << 20, collective_id=5, has_side_effects=True
        ),
        name="feed",
    )(place, sides, *mixed, stream, residual, cot, cross, attn, attn_bias, ln_gain, ln_bias, geglu,
      geglu_bias, feed_out, feed_bias, proj, proj_bias)


def leave_kernel(width, bands, images, place, sides, *refs):
    direct = bands == HEADS
    if direct:
        *arrays, raw_ref = refs[:images]
        refs = refs[images:]
    else:
        packed_ref, refs = refs[0], refs[1:]
    (stream_ref, three_ref, field_ref, avg_ref, gain_ref, bias_ref, proj_ref, ln_gain, ln_bias,
     qkv_ref, scale_ref, out_ref, next_avg, next_halo, stats_ref, sums_ref, grad_qkv, grad_proj, qkv_s,
     proj_s, turned_s) = refs[:21]
    scratch = refs[21:27]
    me = lax.axis_index("rows")
    at = pl.program_id(0)
    last = pl.num_programs(0) - 1
    _, tokens, channels = stream_ref.shape
    inside = pixel_inside((tokens, channels), place[0], sides[at], width)

    @pl.when(at == 0)
    def _():
        greet_rows(me, bands)
        for ref in (stats_ref, sums_ref, qkv_s, proj_s):
            ref[...] = jnp.zeros_like(ref)
        turn_qkv(qkv_ref, turned_s)

    if direct:
        item_s, last_s, item_sems, last_send, last_recv = refs[27:]
        fetch = [
            pltpu.make_async_copy(array, item_s.at[image % 2], item_sems.at[image % 2])
            for image, array in enumerate(arrays)
        ]
        send_last = [
            row_copy(
                raw_ref.at[lax.rem(me + away, bands)], last_s.at[me], last_send.at[away], last_recv.at[me],
                lax.rem(me + away, bands),
            )
            for away in range(1, bands)
        ]
        keep_last = pltpu.make_async_copy(raw_ref.at[me], last_s.at[me], last_recv.at[me])

        @pl.when(at == 0)
        def _():
            fetch[0].start()
            meet_rows(bands)
            for item in send_last:
                item.start()
            keep_last.start()

        for image in range(len(fetch)):

            @pl.when(at == image)
            def _(image=image):
                if image + 1 < len(fetch):
                    fetch[image + 1].start()
                fetch[image].wait()

        @pl.when(at == last)
        def _():
            keep_last.wait()
            for away in range(1, bands):
                source = lax.rem(me + away, bands)
                row_copy(
                    last_s.at[source], last_s.at[source], last_send.at[away], last_recv.at[source], source
                ).wait_recv()
            item_s[(images - 1) % 2] = last_s[...]
            for item in send_last:
                item.wait_send()

        packed_ref, spot = item_s, lax.rem(at, 2)
    else:
        spot = 0
    queries = join_heads(packed_ref.at[:, :, tokens:, :], spot)
    joint = jnp.concatenate([packed_ref[spot, head, :tokens] for head in range(HEADS)] + [queries], axis=1)
    centred, inv_std = layer_stats(stream_ref[0])
    attn_in = (centred * ln_gain[...] + ln_bias[...]).astype(BF)
    qkv_s[...] += dot_tn(attn_in, joint)
    grads = dot_nt(joint, turned_s[...])
    grad_stream = three_ref[0] + layer_back(grads, ln_gain[...], centred, inv_std)
    low_in = grad_stream.astype(BF)
    mean, deviation = moments(avg_ref, at)
    normed = (field_ref[0] - mean) * deviation
    flat = (normed * gain_ref[...] + bias_ref[...]).astype(BF)
    proj_s[...] += dot_tn(flat, low_in)
    moved = jnp.where(inside, dot_nt(low_in, proj_ref[...]), 0.0)
    out_ref[0] = moved
    share_edges(moved, at, width, next_halo, scratch, me, bands, direct)
    put_row(stats_ref, 2 * at, col_sum(moved))
    put_row(stats_ref, 2 * at + 1, col_sum(moved * normed))
    ids = lax.broadcasted_iota(jnp.int32, sums_ref.shape, 0)
    for row, total in enumerate((col_sum(grads * centred), col_sum(grads), col_sum(grad_stream))):
        sums_ref[...] += jnp.where(ids == row, total, 0.0)

    @pl.when(at == last)
    def _():
        close_exchange(stats_ref[...], gain_ref, scale_ref, next_avg, next_halo, scratch, me, bands)
        grad_qkv[...] = qkv_s[...].astype(BF)
        grad_proj[...] = proj_s[...].astype(BF)


def leave(place, sides, packed, stream, three, field, avg, gain, bias, proj, ln_gain, ln_bias, qkv, scale, width,
          bands):
    images, tokens, channels = stream.shape
    direct = bands == HEADS
    tok = image_block(tokens, channels)
    vector = table_block(channels, 1)
    table = table_block(channels)
    return pl.pallas_call(
        partial(leave_kernel, width, bands, images),
        grid=(images,),
        out_shape=(
            jax.ShapeDtypeStruct(stream.shape, F32),
            jax.ShapeDtypeStruct((8, channels), F32),
            jax.ShapeDtypeStruct((2, images, width, channels), BF),
            jax.ShapeDtypeStruct((8, channels), F32),
            jax.ShapeDtypeStruct((8, channels), F32),
            jax.ShapeDtypeStruct(qkv.shape, BF),
            jax.ShapeDtypeStruct(proj.shape, BF),
        ),
        in_specs=[
            SMEM_WHOLE,
            SMEM_WHOLE,
        ]
        + (
            [pl.BlockSpec(memory_space=pl.ANY)] * images
            if direct
            else [pl.BlockSpec((1,) + packed[0].shape[1:], lambda at: (at, 0, 0, 0))]
        )
        + [
            tok,
            tok,
            tok,
            table,
            vector,
            vector,
            fixed_block(proj.shape),
            vector,
            vector,
            fixed_block(qkv.shape),
            table,
        ],
        out_specs=(
            tok,
            table,
            pl.BlockSpec(memory_space=pl.ANY),
            table,
            table,
            fixed_block(qkv.shape),
            fixed_block(proj.shape),
        ),
        scratch_shapes=[
            pltpu.VMEM(qkv.shape, F32), pltpu.VMEM(proj.shape, F32), pltpu.VMEM(qkv.shape, BF)
        ]
        + exchange_scratch(images, width, channels, bands)
        + (
            [
                pltpu.VMEM((2,) + packed[0].shape, BF),
                pltpu.VMEM(packed[0].shape, BF),
                pltpu.SemaphoreType.DMA((2,)),
                pltpu.SemaphoreType.DMA((bands,)),
                pltpu.SemaphoreType.DMA((bands,)),
            ]
            if direct
            else []
        ),
        compiler_params=pltpu.CompilerParams(
            vmem_limit_bytes=56 << 20, collective_id=7, has_side_effects=True
        ),
        name="leave",
    )(place, sides, *packed, stream, three, field, avg, gain, bias, proj, ln_gain, ln_bias, qkv, scale)

def rounded(field):
    return field.astype(BF)


def reduce_kernel(chunks, shapes, bands, groups, *refs):
    count = len(shapes)
    parts, (table_ref, half_ref) = refs[:count], refs[count : count + 2]
    outs, (gathered, other_ref) = refs[count + 2 : 2 * count + 2], refs[2 * count + 2 : 2 * count + 4]
    refs = refs[2 * count + 4 :]
    pairs, crossed, summed, pieces = (refs[at * count : (at + 1) * count] for at in range(4))
    (slots, pair_send, pair_recv, cross_send, cross_recv, piece_send, piece_recv, back_send, back_recv,
     table_send, table_recv, far_send, far_recv, half_sems) = refs[4 * count :]
    chips = bands // 2
    me = lax.axis_index("rows")
    group = lax.axis_index("heads")
    core, chip = lax.rem(me, 2), me // 2
    row_peers = [lax.rem(me + away, bands) for away in range(1, bands)]
    far_peers = [lax.rem(group + away, groups) for away in range(1, groups)]
    barrier = pltpu.get_barrier_semaphore()
    for axis, peers in (("rows", row_peers), ("heads", far_peers)):
        for peer in peers:
            pl.semaphore_signal(
                barrier, inc=1, device_id={axis: peer}, device_id_type=pl.DeviceIdType.MESH
            )
    pl.semaphore_wait(barrier, bands + groups - 2)

    def copy(src, dst, send, recv, axis, peer):
        return pltpu.make_async_remote_copy(
            src_ref=src,
            dst_ref=dst,
            send_sem=send,
            recv_sem=recv,
            device_id={axis: peer},
            device_id_type=pl.DeviceIdType.MESH,
        )

    def rows_of(band, size):
        return pl.ds(pl.multiple_of(band * size, 16), size)

    near = [
        copy(table_ref, slots.at[away], table_send.at[away], table_recv.at[away], "rows", peer)
        for away, peer in enumerate(row_peers)
    ]
    for item in near:
        item.start()
    half = copy(half_ref, other_ref, half_sems.at[0], half_sems.at[1], "heads", jnp.bitwise_xor(group, 1))
    half.start()
    stage_one = []
    for at, (which, first, wide) in enumerate(chunks):
        size = shapes[which][0] // bands
        cols = pl.ds(first, wide)
        own = []
        for spot in range(chips):
            own.append(
                copy(
                    parts[which].at[rows_of(2 * spot + 1 - core, size), cols],
                    pairs[which].at[spot, :, cols],
                    pair_send.at[at, spot],
                    pair_recv.at[at, spot],
                    "rows",
                    me + 1 - 2 * core,
                )
            )
        for item in own:
            item.start()
        stage_one.append(own)
    for item in near:
        item.wait_recv()
    total = table_ref[...]
    for away in range(bands - 1):
        total = total + slots[away]
    gathered[group] = total
    far = [
        copy(gathered.at[group], gathered.at[group], far_send.at[away], far_recv.at[away], "heads", peer)
        for away, peer in enumerate(far_peers)
    ]
    for item in far:
        item.start()
    def to_owner(at):
        which, first, wide = chunks[at]
        size = shapes[which][0] // bands
        cols = pl.ds(first, wide)
        for item in stage_one[at]:
            item.wait_recv()
        own = []
        for away in range(1, chips):
            spot = lax.rem(chip + away, chips)
            pairs[which][spot, :, cols] = (
                pairs[which][spot, :, cols].astype(F32)
                + parts[which][rows_of(2 * spot + core, size), cols].astype(F32)
            ).astype(BF)
            item = copy(
                pairs[which].at[spot, :, cols],
                crossed[which].at[away - 1, :, cols],
                cross_send.at[at, away - 1],
                cross_recv.at[at, away - 1],
                "rows",
                2 * spot + core,
            )
            item.start()
            own.append(item)
        stage_two.append(own)

    def to_groups(at):
        which, first, wide = chunks[at]
        size = shapes[which][0] // bands
        piece = size // groups
        cols = pl.ds(first, wide)
        for item in stage_two[at]:
            item.wait_recv()
        total = pairs[which][chip, :, cols].astype(F32) + parts[which][rows_of(me, size), cols].astype(F32)
        for away in range(chips - 1):
            total = total + crossed[which][away, :, cols].astype(F32)
        summed[which][:, cols] = total.astype(BF)
        own = []
        for away, peer in enumerate(far_peers):
            item = copy(
                summed[which].at[rows_of(peer, piece), cols],
                pieces[which].at[away, :, cols],
                piece_send.at[at, away],
                piece_recv.at[at, away],
                "heads",
                peer,
            )
            item.start()
            own.append(item)
        stage_three.append(own)

    def back_round(at):
        which, first, wide = chunks[at]
        piece = shapes[which][0] // bands // groups
        cols = pl.ds(first, wide)
        for item in stage_three[at]:
            item.wait_recv()
        mine = rows_of(group, piece)
        total = summed[which][mine, cols].astype(F32)
        for away in range(groups - 1):
            total = total + pieces[which][away, :, cols].astype(F32)
        outs[which][mine, cols] = total.astype(BF)
        own = []
        for away, peer in enumerate(far_peers):
            item = copy(
                outs[which].at[mine, cols],
                outs[which].at[mine, cols],
                back_send.at[at, away],
                back_recv.at[at, away],
                "heads",
                peer,
            )
            item.start()
            own.append(item)
        stage_four.append(own)

    stage_two, stage_three, stage_four = [], [], []
    steps = len(chunks)
    for at in range(steps + 3):
        if at < steps:
            to_owner(at)
        if 2 <= at + 1 and 0 <= at - 1 < steps:
            to_groups(at - 1)
        if 0 <= at - 3 < steps:
            back_round(at - 3)
    for away in range(groups - 1):
        source = lax.rem(group - (away + 1) + groups, groups)
        copy(
            gathered.at[source], gathered.at[source], far_send.at[away], far_recv.at[away], "heads", source
        ).wait_recv()
        for at, (which, first, wide) in enumerate(chunks):
            piece = shapes[which][0] // bands // groups
            theirs = outs[which].at[rows_of(source, piece), pl.ds(first, wide)]
            copy(theirs, theirs, back_send.at[at, away], back_recv.at[at, away], "heads", source).wait_recv()
    half.wait_recv()
    for item in [half] + near + far + sum(stage_one + stage_two + stage_three + stage_four, []):
        item.wait_send()


def reduce_fits(shapes, bands, groups):
    return bands % 2 == 0 and all(rows % (16 * bands * groups) == 0 for rows, _ in shapes)


def reduce_parts(parts, table, half, bands, groups):
    shapes = [part.shape for part in parts]
    chunks = []
    for which, (rows, cols) in enumerate(shapes):
        wide = cols if rows * cols < 1 << 19 else 512 if cols > 512 else 128
        chunks += [(which, first, wide) for first in range(0, cols, wide)]
    chips = bands // 2

    def scratch(lead, split):
        return [
            pltpu.VMEM(lead + (rows // bands // split, cols), BF) for rows, cols in shapes
        ]

    def sems(count):
        return [pltpu.SemaphoreType.DMA((len(chunks), count))] * 2

    return pl.pallas_call(
        partial(reduce_kernel, chunks, shapes, bands, groups),
        out_shape=tuple(jax.ShapeDtypeStruct((rows // bands, cols), BF) for rows, cols in shapes)
        + (
            jax.ShapeDtypeStruct((groups,) + table.shape, F32),
            jax.ShapeDtypeStruct(half.shape, BF),
        ),
        in_specs=[VMEM_WHOLE] * (len(parts) + 2),
        out_specs=(VMEM_WHOLE,) * (len(parts) + 2),
        scratch_shapes=scratch((chips,), 1)
        + scratch((chips - 1,), 1)
        + scratch((), 1)
        + scratch((groups - 1,), groups)
        + [pltpu.VMEM((bands - 1,) + table.shape, F32)]
        + sems(chips)
        + sems(chips - 1)
        + sems(groups - 1)
        + sems(groups - 1)
        + [pltpu.SemaphoreType.DMA((bands - 1,))] * 2
        + [pltpu.SemaphoreType.DMA((groups - 1,))] * 2
        + [pltpu.SemaphoreType.DMA((2,))],
        compiler_params=pltpu.CompilerParams(
            vmem_limit_bytes=56 << 20, collective_id=8, has_side_effects=True
        ),
        name="reduce_parts",
    )(*parts, table, half)


def halve_rows(packed, step):
    pairs = [(band, band ^ (1 << step)) for band in range(8)]
    return rounded(packed[0].astype(F32) + lax.ppermute(packed[1], "rows", pairs).astype(F32))


def sum_groups(part, step, groups):
    odd = lax.rem(lax.axis_index("heads"), 2)
    near = [(at, at ^ 1) for at in range(groups)]
    far = [(at, at ^ 2) for at in range(groups)]
    if step == 0:
        half = part.shape[0] // 2
        kept = lax.dynamic_slice_in_dim(part, odd * half, half, 0)
        sent = lax.dynamic_slice_in_dim(part, (1 - odd) * half, half, 0)
        return rounded(kept.astype(F32) + lax.ppermute(sent, "heads", near).astype(F32))
    if step == 1:
        return rounded(part.astype(F32) + lax.ppermute(part, "heads", far).astype(F32))
    other = lax.ppermute(part, "heads", near)
    return jnp.where(odd == 0, jnp.concatenate([part, other]), jnp.concatenate([other, part]))


def finals_kernel(pieces, *refs):
    (odd, conv_two, conv_one, qkv, proj_in, kept, other, table, value, context, hot, embed, cross_out,
     cross_value, out_conv_two, out_conv_one, out_qkv, out_proj_in, out_geglu, out_feed, out_proj_out,
     out_attn_out, out_class, out_cross_value, out_cross_out, out_time) = refs
    out_conv_two[...] = conv_two[...].astype(F32)
    out_conv_one[...] = conv_one[...].astype(F32)
    out_proj_in[...] = proj_in[...].astype(F32)
    rows, channels = out_proj_in.shape
    low = lane_ids(rows) < 64
    out_qkv[:, :channels] = qkv[:, 2 * channels :].astype(F32)
    for first in range(0, channels, 128):
        one = qkv[:, 2 * first : 2 * first + 128].astype(F32)
        two = qkv[:, 2 * first + 128 : 2 * first + 256].astype(F32)
        out_qkv[:, channels + first : channels + first + 128] = jnp.where(low, one, swap_halves(two))
        out_qkv[:, 2 * channels + first : 2 * channels + first + 128] = jnp.where(
            low, swap_halves(one), two
        )
    flag = jnp.full((1, channels), odd[0], jnp.int32) == 0
    one, two = kept[...].astype(F32), other[...].astype(F32)
    early = jnp.concatenate([jnp.where(flag, one, two), jnp.where(flag, two, one)], axis=0)
    for at, (first, size) in enumerate(pieces[0]):
        out_geglu[:, at * channels : (at + 1) * channels] = early[first : first + size]
    for out, ((first, size),) in zip((out_feed, out_proj_out, out_attn_out), pieces[1:]):
        out[...] = early[first : first + size]
    per_group = value.shape[0] // table.shape[0]

    def joined(first):
        return jnp.concatenate(
            [table[group, first : first + per_group] for group in range(table.shape[0])], axis=0
        )

    def exact(lhs, rhs, dims):
        return lax.dot_general(lhs, rhs, (dims, ((), ())), precision=HIGH, preferred_element_type=F32)

    crossed, shifted = joined(0), joined(per_group)
    out_cross_out[...] = exact(value[...], crossed, ((0,), (0,)))
    grad_value = exact(crossed, cross_out[...].astype(F32), ((1,), (1,)))
    out_cross_value[...] = exact(context[...], grad_value, ((0,), (0,)))
    grad_context = exact(grad_value, cross_value[...].astype(F32), ((1,), (1,)))
    out_class[...] = exact(hot[...], grad_context, ((0,), (0,)))
    out_time[...] = exact(embed[...], shifted, ((0,), (0,)))


def finals(odd, parts, kept, other, table, value, context, hot, embed, cross_out, cross_value, pieces):
    conv_two, conv_one, qkv, proj_in = parts
    rows, channels = proj_in.shape
    shapes = [part.shape for part in parts] + [
        (rows, len(pieces[0]) * channels),
        (pieces[1][0][1], channels),
        (rows, channels),
        (rows, channels),
        (hot.shape[1], rows),
        (rows, channels),
        (rows, channels),
        (embed.shape[1], channels),
    ]
    return pl.pallas_call(
        partial(finals_kernel, pieces),
        out_shape=tuple(jax.ShapeDtypeStruct(shape, F32) for shape in shapes),
        in_specs=[SMEM_WHOLE] + [VMEM_WHOLE] * 13,
        out_specs=(VMEM_WHOLE,) * len(shapes),
        compiler_params=pltpu.CompilerParams(vmem_limit_bytes=48 << 20),
        name="finals",
    )(odd, *parts, kept, other, table, value, context, hot, embed, cross_out, cross_value)


def finish_kernel(width, place, sides, kept_ref, grad_ref, field_ref, avg_ref, back_avg, gain_ref, out_ref):
    at = pl.program_id(0)
    mean, inv_std = moments(avg_ref, at)
    back = back_avg[...]
    field_slope = inv_std * inv_std * row_of(back, 2 * at + 1)
    offset = inv_std * row_of(back, 2 * at) - mean * field_slope
    moved = grad_ref[0] * (inv_std * gain_ref[...]) - field_ref[0].astype(F32) * field_slope - offset
    inside = pixel_inside(moved.shape, place[0], sides[at], width)
    out_ref[0] = jnp.where(inside, kept_ref[0] + moved, 0.0)


def finish(place, sides, kept, grads, field, avg, back_avg, gain, width):
    images, tokens, channels = kept.shape
    tok = image_block(tokens, channels)
    table = table_block(channels)
    return pl.pallas_call(
        partial(finish_kernel, width),
        grid=(images,),
        out_shape=jax.ShapeDtypeStruct(kept.shape, F32),
        in_specs=[SMEM_WHOLE, SMEM_WHOLE, tok, tok, tok, table, table, table_block(channels, 1)],
        out_specs=tok,
        compiler_params=pltpu.CompilerParams(vmem_limit_bytes=32 << 20),
        name="finish",
    )(place, sides, kept, grads, field, avg, back_avg, gain)


def time_features(time_steps, dims):
    half_dim = dims // 2
    frequency = jnp.exp(-math.log(10000.0) * jnp.arange(half_dim, dtype=jnp.float32) / half_dim)
    angles = time_steps.astype(jnp.float32)[:, None] * frequency[None, :]
    return jnp.concatenate([jnp.cos(angles), jnp.sin(angles)], axis=-1)


def pad_rows(table):
    return jnp.pad(table, ((0, 8 - table.shape[0]), (0, 0)))


def to_items(sent, bands):
    images, heads = len(sent), sent[0].shape[0]
    per_band = heads * images // bands
    if bands == heads:
        first, *parts = sent
    else:
        items = jnp.stack(sent, axis=1).reshape((bands, per_band) + sent[0].shape[1:])
        parts = [items[:, at] for at in range(per_band)]
    parts = [lax.all_to_all(part, "rows", split_axis=0, concat_axis=0, tiled=True) for part in parts]
    return [first] + parts if bands == heads else parts


def from_items(results, images, bands):
    if bands == HEADS:
        return [
            lax.all_to_all(result, "rows", split_axis=0, concat_axis=0, tiled=True)
            for result in results[:-1]
        ] + results[-1:]
    back = [
        lax.all_to_all(result, "rows", split_axis=0, concat_axis=0, tiled=True)
        for result in results
    ]
    joint = jnp.stack(back, axis=1)
    return [jnp.swapaxes(joint.reshape((HEADS, images) + joint.shape[2:]), 0, 1)]


def per_device(
    images,
    image_sides,
    labels,
    timesteps,
    cotangent,
    first_gain,
    first_bias,
    conv_one,
    time_proj,
    time_bias,
    second_gain,
    second_bias,
    conv_two,
    conv_bias,
    third_gain,
    third_bias,
    proj_in,
    proj_in_bias,
    attn_gain,
    attn_bias,
    qkv_proj,
    attn_out,
    attn_out_bias,
    class_table,
    cross_value,
    cross_out,
    feed_gain,
    feed_bias,
    geglu_proj,
    geglu_bias,
    feed_out,
    feed_out_bias,
    proj_out,
    proj_out_bias,
):
    image_count, band_rows, width, channels = images.shape
    tokens = band_rows * width
    head_dim = channels // HEADS
    score_scale = head_dim ** (-0.5)
    bands = lax.axis_size("rows")
    groups = lax.axis_size("heads")
    halving = bands == 8 and groups == 4 and channels == 512
    me = lax.axis_index("rows")
    first_image = lax.axis_index("heads") * image_count
    sides = lax.dynamic_slice_in_dim(image_sides, first_image, image_count)
    place = jnp.stack([me * band_rows, me]).astype(jnp.int32)

    def vector(entries):
        return entries.astype(F32).reshape(1, -1)

    counts = 1.0 / (sides * sides * (channels // GROUPS)).astype(F32)
    scale = jnp.broadcast_to(pad_rows(jnp.repeat(counts, 2)[:, None]), (8, channels))
    ones = jnp.ones((1, channels), F32)
    field = images.reshape(image_count, tokens, channels)
    cot = cotangent.reshape(image_count, tokens, channels)

    hot = rounded(
        (labels[:, None] == jnp.arange(class_table.shape[0], dtype=jnp.int32)[None, :]).astype(F32)
    )
    context = jnp.dot(hot, class_table, preferred_element_type=F32)
    value = rounded(jnp.dot(rounded(context), cross_value, preferred_element_type=F32))
    cross = jnp.dot(value, cross_out, preferred_element_type=F32)
    cross = pad_rows(lax.dynamic_slice_in_dim(cross, first_image, image_count))
    embed = rounded(jax.nn.silu(time_features(timesteps, time_proj.shape[0])))
    shift = jnp.dot(embed, time_proj, preferred_element_type=F32) + time_bias.astype(F32)
    shift = pad_rows(lax.dynamic_slice_in_dim(shift, first_image, image_count))

    avg_one, halo_images = begin(place, sides, field, ones, scale, width, bands)
    hidden, avg_two, halo_hidden, halo_cot = conv_forward(
        place, sides, field, halo_images, avg_one, vector(first_gain), vector(first_bias), conv_one,
        shift, ones, scale, cot, False, width, bands,
    )
    residual, avg_three, halo_residual = conv_forward(
        place, sides, hidden, halo_hidden, avg_two, vector(second_gain), vector(second_bias), conv_two,
        jnp.broadcast_to(vector(conv_bias), (8, channels)), ones, scale, field, True, width, bands,
    )
    stream, *sent = entry(
        residual, avg_three, vector(third_gain), vector(third_bias), proj_in, vector(proj_in_bias),
        vector(attn_gain), vector(attn_bias), qkv_proj, bands,
    )
    chunks = to_items(sent, bands)
    first_item = me * len(chunks)
    item_sides = [
        lax.dynamic_slice_in_dim(sides, lax.rem(first_item + at, image_count), 1)
        for at in range(len(chunks))
    ]
    attended = [attend(side, chunk, width, score_scale) for side, chunk in zip(item_sides, chunks)]
    mixed = [pairs for pairs, _, _ in attended]
    (
        output, three, grad_chunks, feed_grads, feed_sums, cross_sum, pair_sums,
    ) = feed(
        place, sides, mixed, stream, residual, cot, cross, attn_out, vector(attn_out_bias),
        vector(feed_gain), vector(feed_bias), geglu_proj, vector(geglu_bias), feed_out,
        vector(feed_out_bias), proj_out, vector(proj_out_bias), width, bands, halving,
    )
    halved = feed_grads
    results = []
    for spot, (side, chunk, (_, norms, kept)) in enumerate(zip(item_sides, chunks, attended)):
        if halving and spot in (1, 2):
            halved, norms = lax.optimization_barrier((halve_rows(halved, spot), norms))
        results.append(attend_back(side, chunk, grad_chunks, spot, norms, kept, width, score_scale))
    grad_qkv = from_items(results, image_count, bands)
    if halving:
        early = halved
    else:
        early = feed_grads.reshape((bands,) + feed_grads.shape[-2:])
        early = lax.psum_scatter(early, "rows", scatter_dimension=0, tiled=True)[0]
        early = lax.psum(early, "heads")
    moved, back_three, halo_moved, third_sums, leave_sums, grad_qkv_proj, grad_proj_in = leave(
        place, sides, grad_qkv, stream, three, residual, avg_three, vector(third_gain),
        vector(third_bias), proj_in, vector(attn_gain), vector(attn_bias), qkv_proj, scale, width, bands,
    )
    if halving:
        early, back_three = lax.optimization_barrier((early, back_three))
        early = sum_groups(early, 0, groups)
    grad_residual, moved, back_two, second_sums, residual_sums, grad_conv_two, halo_moved = conv_backward(
        place, sides, moved, halo_moved, residual, halo_residual, avg_three, back_three,
        vector(third_gain), cot, halo_cot, conv_two, hidden, avg_two, vector(second_gain),
        vector(second_bias), scale, width, bands,
    )
    if halving:
        early, back_two = lax.optimization_barrier((early, back_two))
        early = sum_groups(early, 1, groups)
    moved, back_one, first_sums, hidden_sums, grad_conv_one = conv_backward(
        place, sides, moved, halo_moved, hidden, halo_hidden, avg_two, back_two, vector(second_gain),
        None, None, conv_one, field, avg_one, vector(first_gain), vector(first_bias), scale, width, bands,
    )
    if halving:
        early, back_one = lax.optimization_barrier((early, back_one))
    grad_images = finish(
        place, sides, grad_residual, moved, field, avg_one, back_one, vector(first_gain), width
    ).reshape(images.shape)

    def own(whole, axis=0):
        size = whole.shape[axis] // bands
        return lax.dynamic_slice_in_dim(whole, me * size, size, axis)

    def reduced(part):
        part = lax.psum_scatter(part, "rows", scatter_dimension=0, tiled=True)
        return lax.psum(part, "heads").astype(F32)

    used = 2 * image_count
    table = jnp.concatenate(
        [
            cross_sum[:image_count],
            hidden_sums[:image_count],
            jnp.stack(
                [
                    jnp.sum(first_sums[1:used:2], axis=0),
                    jnp.sum(first_sums[0:used:2], axis=0),
                    jnp.sum(second_sums[1:used:2], axis=0),
                    jnp.sum(second_sums[0:used:2], axis=0),
                    jnp.sum(third_sums[1:used:2], axis=0),
                    jnp.sum(third_sums[0:used:2], axis=0),
                    jnp.sum(residual_sums[:image_count], axis=0),
                ]
            ),
            leave_sums[:3],
            feed_sums[:4],
            pair_sums.reshape(-1, channels),
        ]
    )
    table = jnp.pad(table, ((0, -table.shape[0] % 8), (0, 0)))
    late = (grad_conv_two, grad_conv_one, grad_qkv_proj, grad_proj_in)
    pieces = feed_pieces(channels, geglu_proj.shape[1], feed_out.shape[0], bands)
    own_value, own_context = own(value.astype(F32), 1), own(context, 1)
    own_embed, own_cross = own(embed.astype(F32), 1), own(cross_value)
    hot = hot.astype(F32)
    if halving:
        grad_images, table = lax.optimization_barrier((grad_images, table))
        *late, table, other = reduce_parts(late, table, early, bands, groups)
        odd = lax.rem(lax.axis_index("heads"), 2).astype(jnp.int32).reshape(1)
        (
            rows_conv_two, rows_conv_one, rows_qkv, rows_proj_in, rows_geglu, rows_feed, rows_proj_out,
            rows_attn_out, grad_class_table, grad_cross_value, grad_cross_out, grad_time_proj,
        ) = finals(
            odd, late, early, other, table, own_value, own_context, hot, own_embed, cross_out, own_cross,
            pieces,
        )
    else:
        table = lax.all_gather(lax.psum(table, "rows"), "heads")
        rows_conv_two, rows_conv_one, rows_qkv, rows_proj_in = (reduced(part) for part in late)
        keys_values = rows_qkv[:, : 2 * channels].reshape(-1, HEADS, 2, head_dim)
        rows_qkv = jnp.concatenate(
            [
                rows_qkv[:, 2 * channels :],
                keys_values[:, :, 0].reshape(-1, channels),
                keys_values[:, :, 1].reshape(-1, channels),
            ],
            axis=1,
        )
        early = early.astype(F32)
        rows_geglu = jnp.concatenate([early[first : first + size] for first, size in pieces[0]], axis=1)
        rows_feed, rows_proj_out, rows_attn_out = (
            early[first : first + size] for ((first, size),) in pieces[1:]
        )
    all_cross = table[:, :image_count].reshape(-1, channels)
    all_shift = table[:, image_count : 2 * image_count].reshape(-1, channels)
    if not halving:
        grad_cross_out = jnp.dot(own_value.T, all_cross, precision=HIGH)
        grad_value = jnp.dot(all_cross, cross_out.astype(F32).T, precision=HIGH)
        grad_cross_value = jnp.dot(own_context.T, grad_value, precision=HIGH)
        grad_context = jnp.dot(grad_value, own_cross.astype(F32).T, precision=HIGH)
        grad_class_table = jnp.dot(hot.T, grad_context, precision=HIGH)
        grad_time_proj = jnp.dot(own_embed.T, all_shift, precision=HIGH)
    joint = jnp.concatenate(
        [jnp.sum(table[:, 2 * image_count :], axis=0), jnp.sum(all_cross, axis=0)[None],
         jnp.sum(all_shift, axis=0)[None]]
    )
    mine = own(joint, 1)
    singles = [mine[at] for at in range(14)]
    grad_geglu_bias = own(joint[14 : 14 + geglu_bias.shape[0] // channels].reshape(-1))
    return (
        output.reshape(images.shape),
        grad_images,
        singles[0],
        singles[1],
        rows_conv_one,
        grad_time_proj,
        mine[-1],
        singles[2],
        singles[3],
        rows_conv_two,
        singles[6],
        singles[4],
        singles[5],
        rows_proj_in,
        singles[9],
        singles[7],
        singles[8],
        rows_qkv,
        rows_attn_out,
        mine[-2],
        grad_class_table,
        grad_cross_value,
        grad_cross_out,
        singles[12],
        singles[13],
        rows_geglu,
        grad_geglu_bias,
        rows_feed,
        singles[11],
        rows_proj_out,
        singles[10],
    )


def solution(mesh):
    return jax.shard_map(
        per_device,
        mesh=mesh,
        in_specs=(
            P("heads", "rows", None, None),
            P(),
            P(),
            P(),
            P("heads", "rows", None, None),
            P(),
            P(),
            P(),
            P(),
            P(),
            P(),
            P(),
            P(),
            P(),
            P(),
            P(),
            P(),
            P(),
            P(),
            P(),
            P(),
            P(),
            P(),
            P(),
            P(),
            P(),
            P(),
            P(),
            P(),
            P(),
            P(),
            P(),
            P(),
            P(),
        ),
        out_specs=(
            P("heads", "rows", None, None),
            P("heads", "rows", None, None),
            P("rows"),
            P("rows"),
            P("rows", None),
            P("rows", None),
            P("rows"),
            P("rows"),
            P("rows"),
            P("rows", None),
            P("rows"),
            P("rows"),
            P("rows"),
            P("rows", None),
            P("rows"),
            P("rows"),
            P("rows"),
            P("rows", None),
            P("rows", None),
            P("rows"),
            P(None, "rows"),
            P("rows", None),
            P("rows", None),
            P("rows"),
            P("rows"),
            P("rows", None),
            P("rows"),
            P("rows", None),
            P("rows"),
            P("rows", None),
            P("rows"),
        ),
        check_vma=False,
    )
```

```python
from functools import partial
import math

import jax
import jax.numpy as jnp
from jax import lax
from jax.experimental import pallas as pl
from jax.experimental.pallas import tpu as pltpu
from jax.sharding import PartitionSpec as P

HEADS = 8
GROUPS = 32
GN_EPS = 1e-06
LN_EPS = 1e-05
HIGH = lax.Precision.HIGHEST
LOG2E = math.log2(math.e)
BF = jnp.bfloat16
F32 = jnp.float32
KEPT = 256

def dot_nt(lhs, rhs):
    return lax.dot_general(lhs, rhs, (((1,), (1,)), ((), ())), preferred_element_type=F32)


def dot_nn(lhs, rhs):
    return lax.dot_general(lhs, rhs, (((1,), (0,)), ((), ())), preferred_element_type=F32)


def lane_ids(rows):
    return lax.broadcasted_iota(jnp.int32, (rows, 128), 1)


def swap_halves(field):
    return pltpu.roll(field, 64, 1)


def pieces_of(column):
    top = column.astype(BF).astype(F32)
    rest = column - top
    mid = rest.astype(BF).astype(F32)
    return (top, mid, rest - mid)


def extras(column, lanes, first):
    top, mid, low = pieces_of(column)
    return jnp.where(
        lanes == first, top, jnp.where(lanes == first + 1, mid, jnp.where(lanes == first + 2, low, 0.0))
    )


def block_of(count, pref):
    for size in pref:
        if count % size == 0:
            return size
    return count


def crop(field, width, side):
    rows = field.shape[0] // width
    if side == width:
        return field
    return field.reshape(rows, width, 128)[:, :side].reshape(rows * side, 128)


def uncrop(field, width, side):
    if side == width:
        return field
    rows = field.shape[0] // side
    spread = field.reshape(rows, side, 128)
    return jnp.concatenate(
        [spread, jnp.zeros((rows, width - side, 128), field.dtype)], axis=1
    ).reshape(rows * width, 128)


def unpack_pairs(pairs):
    return jnp.concatenate([pairs, swap_halves(pairs)], axis=0)


def pack_pairs(field, lanes):
    half = field.shape[0] // 2
    return jnp.where(lanes[:half] < 64, field[:half], swap_halves(field[half:]))


def attend_kernel(width, scale, side_ref, qkv_ref, out_ref, norm_ref, kept_ref, q_s, k_s, v_s, vt_s, top_s, stage_s, sems):
    bands, packed, _ = qkv_ref.shape
    band_tokens = packed * 2 // 3
    band_rows = band_tokens // width
    side_now = side_ref[0]

    def variant(side):
        tokens = side * side
        used = side // band_rows
        own = band_rows * side
        lanes = lane_ids(own)
        low = lanes < 64
        row_ids = lax.broadcasted_iota(jnp.int32, (128, 128), 0)
        col_ids = lax.broadcasted_iota(jnp.int32, (128, 128), 1)
        picks = jnp.where((row_ids < 64) == (col_ids < 64), 1.0, 0.0).astype(BF)

        def gather_band(band, norms):
            pairs = crop(qkv_ref[band, band_tokens:, :].astype(F32), width, side)
            keys = crop(qkv_ref[band, :band_tokens, :].astype(F32), width, side)
            queries = unpack_pairs(pairs) * (scale * LOG2E)
            head = queries.astype(BF).astype(F32)
            turned = swap_halves(keys)
            rows = pl.ds(pl.multiple_of(band * own, 16), own)
            q_s[rows, :] = jnp.where(low, head, swap_halves(queries - head)).astype(BF)
            k_s[rows, :] = jnp.where(low, keys, turned).astype(BF)
            v_s[rows, :] = jnp.where(low, turned, jnp.where(lanes == 64, 1.0, 0.0)).astype(BF)
            joint = jnp.where(low, queries, turned)
            sums = dot_nn((joint * joint).astype(BF), picks)
            return jnp.maximum(norms, jnp.max(sums, axis=0, keepdims=True))

        norms = lax.fori_loop(0, used, gather_band, jnp.zeros((1, 128), F32))
        step = block_of(tokens, (512, 256))
        for first in range(0, tokens, step):
            vt_s[:, first : first + step] = v_s[first : first + step, :].T
        first_lanes = lane_ids(1) < 64
        query_top = jnp.max(jnp.where(first_lanes, norms, 0.0))
        key_top = jnp.max(jnp.where(first_lanes, 0.0, norms))
        safe = query_top * key_top * 1.05 <= 100.0 * 100.0
        bq = block_of(tokens, (1024, 768, 256))
        bk = block_of(tokens, (1024, 768, 256))

        @pl.when(safe)
        def _():
            top_s[...] = jnp.zeros_like(top_s)

        @pl.when(jnp.logical_not(safe))
        def _():
            def tops(qi, _):
                cols = pl.ds(pl.multiple_of(qi * bq, 256), bq)
                queries = q_s[cols, :]

                def more(ki, top):
                    scores = dot_nt(k_s[pl.ds(pl.multiple_of(ki * bk, 256), bk), :], queries)
                    return jnp.maximum(top, jnp.max(scores, axis=0, keepdims=True))

                top = lax.fori_loop(0, tokens // bk, more, jnp.full((1, bq), -jnp.inf, F32))
                top_s[:, cols] = jnp.broadcast_to(top, (8, bq))
                return 0

            lax.fori_loop(0, tokens // bq, tops, 0)

        parts = bq // KEPT
        steps = tokens // bq
        slots = min(steps, stage_s.shape[0] // tokens, 3)

        def stores(qi, first=0, rows=tokens):
            slot = lax.rem(qi, slots)
            return [
                pltpu.make_async_copy(
                    stage_s.at[pl.ds(pl.multiple_of(slot * tokens + first, 128), rows), pl.ds(part * KEPT, KEPT)],
                    kept_ref.at[pl.ds(pl.multiple_of((qi * parts + part) * tokens + first, 256), rows)],
                    sems.at[slot, part],
                )
                for part in range(parts)
            ]

        def main(qi, _):
            cols = pl.ds(pl.multiple_of(qi * bq, 256), bq)
            queries = q_s[cols, :]
            top = top_s[0:1, cols]
            slot = lax.rem(qi, slots)

            @pl.when(qi >= slots)
            def _():
                for item in stores(qi - slots):
                    item.wait()

            total = jnp.zeros((80, bq), F32)
            for first in range(0, tokens, bk):
                scores = dot_nt(k_s[first : first + bk, :], queries)
                weights = jnp.exp2(scores - top).astype(BF)
                stage_s[pl.ds(pl.multiple_of(slot * tokens + first, 128), bk), :bq] = weights
                total = total + dot_nn(vt_s[0:80, first : first + bk], weights)
                for item in stores(qi, first, bk):
                    item.start()
            row_total = total[64:65]
            mixed = total[:64] / row_total
            extra = jnp.broadcast_to(1.0 / row_total, (64, bq))
            norm_ref[cols, :] = jnp.concatenate([mixed, extra], axis=0).T
            return 0

        lax.fori_loop(0, steps, main, 0)
        for qi in range(steps - slots, steps):
            for item in stores(qi):
                item.wait()

        def spread_band(band, _):
            rows = pl.ds(pl.multiple_of(band * own, 16), own)
            pairs = pack_pairs(norm_ref[rows, :], lanes)
            out_ref[band] = uncrop(pairs, width, side).astype(BF)
            return 0

        lax.fori_loop(0, used, spread_band, 0)
        if used < bands:
            out_ref[used:] = jnp.zeros((bands - used,) + out_ref.shape[1:], BF)

    for side in (width, width * 3 // 4, width // 2):
        pl.when(side_now == side)(partial(variant, side))


def attend(side, qkv, width, scale):
    bands, packed, _ = qkv.shape
    tokens = bands * packed * 2 // 3
    vm = pl.BlockSpec(memory_space=pltpu.VMEM)
    return pl.pallas_call(
        partial(attend_kernel, width, scale),
        out_shape=(
            jax.ShapeDtypeStruct((bands, packed // 3, 128), BF),
            jax.ShapeDtypeStruct((tokens, 128), F32),
            jax.ShapeDtypeStruct((tokens // KEPT * tokens, KEPT), BF),
        ),
        in_specs=[pl.BlockSpec(memory_space=pltpu.SMEM), vm],
        out_specs=(vm, vm, pl.BlockSpec(memory_space=pl.ANY)),
        scratch_shapes=[
            pltpu.VMEM((tokens, 128), BF),
            pltpu.VMEM((tokens, 128), BF),
            pltpu.VMEM((tokens, 128), BF),
            pltpu.VMEM((128, tokens), BF),
            pltpu.VMEM((8, tokens), F32),
            pltpu.VMEM((2 * tokens, 1024), BF),
            pltpu.SemaphoreType.DMA((3, 4)),
        ],
        compiler_params=pltpu.CompilerParams(vmem_limit_bytes=62 << 20),
        cost_estimate=pl.CostEstimate(
            flops=4 * 256 * tokens * tokens, bytes_accessed=8 << 20, transcendentals=tokens * tokens
        ),
        name="attend",
    )(side, qkv)


def attend_back_kernel(width, scale, side_ref, qkv_ref, grad_ref, norm_ref, kept_ref, out_ref,
                       k_s, g_s, gn_s, v_s, q_s, kt_s, dq_s, dkv_s, recip_s, stage_s, sems):
    bands, packed, _ = qkv_ref.shape
    band_tokens = packed * 2 // 3
    band_rows = band_tokens // width
    side_now = side_ref[0]

    def variant(side):
        tokens = side * side
        used = side // band_rows
        own = band_rows * side
        lanes = lane_ids(own)
        low = lanes < 64
        ones_high = jnp.where((lanes >= 64) & (lanes < 67), 1.0, 0.0)
        bq = block_of(tokens, (1024, 768, 256))
        bk = block_of(tokens, (512, 768, 256))
        parts = bq // KEPT
        steps = tokens // bq
        slots = min(steps, stage_s.shape[0] // tokens, 3)

        def loads(qi):
            slot = lax.rem(qi, slots)
            return [
                pltpu.make_async_copy(
                    kept_ref.at[pl.ds(pl.multiple_of((qi * parts + part) * tokens, 256), tokens)],
                    stage_s.at[pl.ds(pl.multiple_of(slot * tokens, 128), tokens), pl.ds(part * KEPT, KEPT)],
                    sems.at[slot, part],
                )
                for part in range(parts)
            ]

        ahead = steps if slots == steps else slots - 1
        for qi in range(ahead):
            for item in loads(qi):
                item.start()

        def gather_band(band, _):
            queries = unpack_pairs(crop(qkv_ref[band, band_tokens:, :].astype(F32), width, side))
            keys = crop(qkv_ref[band, :band_tokens, :].astype(F32), width, side)
            grads = unpack_pairs(crop(grad_ref[0, band].astype(F32), width, side))
            rows = pl.ds(pl.multiple_of(band * own, 16), own)
            mixed = norm_ref[rows, :]
            delta = jnp.sum(jnp.where(low, grads * mixed, 0.0), axis=1, keepdims=True)
            turned = swap_halves(keys)
            q_s[rows, :] = jnp.where(low, 0.0, swap_halves(queries)).astype(BF)
            gn_s[rows, :] = jnp.where(low, grads, 0.0).astype(BF)
            g_s[rows, :] = jnp.where(low, grads, extras(-delta, lanes, 64)).astype(BF)
            v_s[rows, :] = jnp.where(low, turned, ones_high).astype(BF)
            k_s[rows, :] = jnp.where(low, keys, 0.0).astype(BF)
            return 0

        lax.fori_loop(0, used, gather_band, 0)
        step = block_of(tokens, (512, 256))
        for first in range(0, tokens, step):
            kt_s[:, first : first + step] = k_s[first : first + step, :].T[:64]
            recip_s[:, first : first + step] = norm_ref[first : first + step, :].T[64:72]
        dkv_s[...] = jnp.zeros_like(dkv_s)

        def main(qi, _):
            cols = pl.ds(pl.multiple_of(qi * bq, 256), bq)
            slot = lax.rem(qi, slots)
            for item in loads(qi):
                item.wait()

            @pl.when(qi + ahead < steps)
            def _():
                for item in loads(qi + ahead):
                    item.start()

            grads = g_s[cols, :]
            plain = gn_s[cols, :]
            queries = q_s[cols, :]
            recip = recip_s[0:1, cols]
            total = jnp.zeros((64, bq), F32)
            for first in range(0, tokens, bk):
                lines = pl.ds(pl.multiple_of(slot * tokens + first, 128), bk)
                probs = stage_s[lines, :bq].astype(F32) * recip
                slopes = dot_nt(v_s[first : first + bk, :], grads)
                grad_scores = (probs * slopes).astype(BF)
                dkv_s[first : first + bk, :] += dot_nn(probs.astype(BF), plain) + dot_nn(grad_scores, queries)
                total = total + dot_nn(kt_s[:, first : first + bk], grad_scores)
            dq_s[:, cols] = total
            return 0

        lax.fori_loop(0, steps, main, 0)
        for first in range(0, tokens, step):
            turned = dq_s[:, first : first + step]
            v_s[first : first + step, :] = (
                jnp.concatenate([turned, turned], axis=0).T * scale
            ).astype(BF)

        def spread_band(band, _):
            rows = pl.ds(pl.multiple_of(band * own, 16), own)
            joint = swap_halves(dkv_s[rows, :])
            out_ref[band, :band_tokens] = uncrop(jnp.where(low, joint * scale, joint), width, side).astype(BF)
            pairs = pack_pairs(v_s[rows, :].astype(F32), lanes)
            out_ref[band, band_tokens:] = uncrop(pairs, width, side).astype(BF)
            return 0

        lax.fori_loop(0, used, spread_band, 0)
        if used < bands:
            out_ref[used:] = jnp.zeros((bands - used,) + out_ref.shape[1:], BF)

    for side in (width, width * 3 // 4, width // 2):
        pl.when(side_now == side)(partial(variant, side))


def attend_back(side, qkv, grads, spot, norms, kept, width, scale):
    bands, packed, _ = qkv.shape
    tokens = bands * packed * 2 // 3
    vm = pl.BlockSpec(memory_space=pltpu.VMEM)
    rows = pltpu.VMEM((tokens, 128), BF)
    return pl.pallas_call(
        partial(attend_back_kernel, width, scale),
        out_shape=jax.ShapeDtypeStruct((bands, packed, 128), BF),
        grid=(1,),
        in_specs=[
            pl.BlockSpec(memory_space=pltpu.SMEM),
            vm,
            pl.BlockSpec((1,) + grads.shape[1:], lambda at: (spot, 0, 0, 0)),
            vm,
            pl.BlockSpec(memory_space=pl.ANY),
        ],
        out_specs=vm,
        scratch_shapes=[rows] * 5
        + [
            pltpu.VMEM((64, tokens), BF),
            pltpu.VMEM((64, tokens), F32),
            pltpu.VMEM((tokens, 128), F32),
            pltpu.VMEM((8, tokens), F32),
            pltpu.VMEM((2 * tokens, 1024), BF),
            pltpu.SemaphoreType.DMA((3, 4)),
        ],
        compiler_params=pltpu.CompilerParams(vmem_limit_bytes=62 << 20),
        cost_estimate=pl.CostEstimate(
            flops=8 * 256 * tokens * tokens, bytes_accessed=40 << 20, transcendentals=0
        ),
        name="attend_back",
    )(side, qkv, grads, norms, kept)


def dot_tn(lhs, rhs):
    return lax.dot_general(lhs, rhs, (((0,), (0,)), ((), ())), preferred_element_type=F32)


def row_of(table, at):
    ids = lax.broadcasted_iota(jnp.int32, table.shape, 0)
    return jnp.sum(jnp.where(ids == at, table, 0.0), axis=0, keepdims=True)


def put_row(table_ref, at, row):
    ids = lax.broadcasted_iota(jnp.int32, table_ref.shape, 0)
    table_ref[...] = jnp.where(ids == at, row, table_ref[...])


def col_sum(field):
    return jnp.sum(field, axis=0, keepdims=True)


def vec(ref):
    return ref[...].astype(F32).reshape(1, -1)


def spread_lanes(tile, channels):
    return jnp.concatenate([tile] * (channels // 128), axis=1)


def token_ids(shape):
    return lax.broadcasted_iota(jnp.int32, (shape[0], 128), 0)


def pixel_inside(shape, first_row, side, width):
    token = token_ids(shape)
    row = first_row + lax.shift_right_logical(token, int(math.log2(width)))
    return spread_lanes((row >= 0) & (row < side) & ((token & (width - 1)) < side), shape[1])


def sigmoid(field):
    return 0.5 * jnp.tanh(0.5 * field) + 0.5


def moments(avg_ref, at):
    table = avg_ref[...]
    mean = row_of(table, 2 * at)
    return mean, lax.rsqrt(row_of(table, 2 * at + 1) - mean * mean + GN_EPS)


def put_taps(taps_s, first, field, width, flipped):
    channels = field.shape[1]
    column = token_ids(field.shape) & (width - 1)
    count = field.shape[0]
    left = jnp.where(spread_lanes(column == 0, channels), 0.0, pltpu.roll(field, 1, 0))
    right = jnp.where(spread_lanes(column == width - 1, channels), 0.0, pltpu.roll(field, count - 1, 0))
    order = (right, field, left) if flipped else (left, field, right)
    for at, part in enumerate(order):
        taps_s[first : first + count, at * channels : (at + 1) * channels] = part.astype(BF)


VMEM_WHOLE = pl.BlockSpec(memory_space=pltpu.VMEM)
SMEM_WHOLE = pl.BlockSpec(memory_space=pltpu.SMEM)


def image_block(tokens, channels):
    return pl.BlockSpec((1, tokens, channels), lambda at: (at, 0, 0))


def edge_block(width, channels):
    return pl.BlockSpec((2, 1, width, channels), lambda at: (0, at, 0, 0))


def table_block(channels, rows=8):
    return pl.BlockSpec((rows, channels), lambda at: (0, 0))


def vector_block(channels):
    return pl.BlockSpec((channels,), lambda at: (0,))


def fixed_block(shape):
    return pl.BlockSpec(shape, lambda at: (0,) * len(shape), pipeline_mode=pl.Buffered(1))


def greet_rows(me, bands):
    barrier = pltpu.get_barrier_semaphore()
    for away in range(1, bands):
        pl.semaphore_signal(
            barrier, inc=1, device_id={"rows": lax.rem(me + away, bands)},
            device_id_type=pl.DeviceIdType.MESH,
        )


def meet_rows(bands):
    pl.semaphore_wait(pltpu.get_barrier_semaphore(), bands - 1)


def row_copy(src, dst, send, recv, target):
    return pltpu.make_async_remote_copy(
        src_ref=src, dst_ref=dst, send_sem=send, recv_sem=recv, device_id={"rows": target},
        device_id_type=pl.DeviceIdType.MESH,
    )


def edge_copies(top, bottom, halo, at, send, recv, me, bands):
    return [
        row_copy(top, halo.at[1, at], send.at[0, at], recv.at[1, at], lax.rem(me + bands - 1, bands)),
        row_copy(bottom, halo.at[0, at], send.at[1, at], recv.at[0, at], lax.rem(me + 1, bands)),
    ]


def group_average(sums, weight_ref, sides, slots, send, recv, me, bands):
    slots[me] = sums
    copies = [
        row_copy(slots.at[me], slots.at[me], send.at[away], recv.at[me], lax.rem(me + away, bands))
        for away in range(1, bands)
    ]
    for item in copies:
        item.start()
    for away in range(1, bands):
        source = lax.rem(me + away, bands)
        row_copy(slots.at[source], slots.at[source], send.at[away], recv.at[source], source).wait_recv()
    total = slots[0]
    for at in range(1, bands):
        total = total + slots[at]
    for item in copies:
        item.wait_send()
    if weight_ref is not None:
        total = total * vec(weight_ref)
    image = lax.shift_right_logical(lax.broadcasted_iota(jnp.int32, total.shape, 0), 1)
    side = jnp.ones(total.shape, jnp.int32)
    for at in range(sides.shape[0]):
        side = jnp.where(image == at, sides[at], side)
    side = side.astype(F32)
    channels = total.shape[1]
    size = channels // GROUPS
    lane = lax.broadcasted_iota(jnp.int32, total.shape, 1)
    step = 1
    while step < size:
        total = total + jnp.where(
            (lane & step) == 0, pltpu.roll(total, channels - step, 1), pltpu.roll(total, step, 1)
        )
        step *= 2
    return total / (side * side * size)


def exchange_scratch(images, width, channels, bands):
    return [
        pltpu.VMEM((2, images, width, channels), BF),
        pltpu.VMEM((bands, 8, channels), F32),
        pltpu.SemaphoreType.DMA((2, images)),
        pltpu.SemaphoreType.DMA((2, images)),
        pltpu.SemaphoreType.DMA((bands,)),
        pltpu.SemaphoreType.DMA((bands,)),
    ]


def share_edges(grads, at, width, halo_ref, scratch, me, bands, met=False):
    edge_s, _, send, recv = scratch[:4]
    tokens = grads.shape[0]
    edge_s[0, at] = grads[:width].astype(BF)
    edge_s[1, at] = grads[tokens - width :].astype(BF)
    if not met:
        pl.when(at == 0)(partial(meet_rows, bands))
    for item in edge_copies(edge_s.at[0, at], edge_s.at[1, at], halo_ref, at, send, recv, me, bands):
        item.start()


def close_exchange(sums, weight_ref, sides, avg_ref, halo_ref, scratch, me, bands):
    edge_s, slots, send, recv, sum_send, sum_recv = scratch
    avg_ref[...] = group_average(sums, weight_ref, sides, slots, sum_send, sum_recv, me, bands)
    for at in range(edge_s.shape[1]):
        for item in edge_copies(
            edge_s.at[0, at], edge_s.at[1, at], halo_ref, at, send, recv, me, bands
        ):
            item.wait_send()
        for end in range(2):
            edge = halo_ref.at[end, at]
            row_copy(
                edge, edge, send.at[end, at], recv.at[end, at], lax.rem(me + 1, bands)
            ).wait_recv()


def begin_kernel(width, bands, place, sides, field_ref, whole_ref, avg_ref, halo_ref, sums_s, slots, send, recv, sum_send, sum_recv):
    at = pl.program_id(0)
    last = pl.num_programs(0) - 1
    me = lax.axis_index("rows")
    images, tokens, _ = whole_ref.shape

    def edges():
        return [
            edge_copies(
                whole_ref.at[image, pl.ds(0, width)], whole_ref.at[image, pl.ds(tokens - width, width)],
                halo_ref, image, send, recv, me, bands,
            )
            for image in range(images)
        ]

    @pl.when(at == 0)
    def _():
        greet_rows(me, bands)
        sums_s[...] = jnp.zeros_like(sums_s)
        meet_rows(bands)
        for pair in edges():
            for item in pair:
                item.start()

    field = field_ref[0].astype(F32)
    field = jnp.where(pixel_inside(field.shape, place[0], sides[at], width), field, 0.0)
    put_row(sums_s, 2 * at, col_sum(field))
    put_row(sums_s, 2 * at + 1, col_sum(field * field))

    @pl.when(at == last)
    def _():
        avg_ref[...] = group_average(
            sums_s[...], None, sides, slots, sum_send, sum_recv, me, bands
        )
        for image, pair in enumerate(edges()):
            for item in pair:
                item.wait_send()
            for end in range(2):
                edge = halo_ref.at[end, image]
                row_copy(
                    edge, edge, send.at[end, image], recv.at[end, image], lax.rem(me + 1, bands)
                ).wait_recv()


def begin(place, sides, field, width, bands):
    images, tokens, channels = field.shape
    anywhere = pl.BlockSpec(memory_space=pl.ANY)
    return pl.pallas_call(
        partial(begin_kernel, width, bands),
        grid=(images,),
        out_shape=(
            jax.ShapeDtypeStruct((8, channels), F32),
            jax.ShapeDtypeStruct((2, images, width, channels), BF),
        ),
        in_specs=[
            SMEM_WHOLE,
            SMEM_WHOLE,
            image_block(tokens, channels),
            anywhere,
        ],
        out_specs=(table_block(channels), anywhere),
        scratch_shapes=[pltpu.VMEM((8, channels), F32)]
        + exchange_scratch(images, width, channels, bands)[1:],
        compiler_params=pltpu.CompilerParams(collective_id=1, has_side_effects=True),
        name="begin",
    )(place, sides, field, field)


def conv_forward_kernel(width, bands, base_given, *refs):
    (place, sides, field_ref, halo_ref, avg_ref, gain_ref, bias_ref, weight_ref, shift_ref,
     base_ref, out_ref, next_avg, next_halo) = refs[:13]
    refs = refs[13:]
    if not base_given:
        ride_halo, ride_send, ride_recv = refs[0], refs[-2], refs[-1]
        refs = refs[1:-2]
    taps_s, stats_ref = refs[:2]
    scratch = refs[2:]
    me = lax.axis_index("rows")
    at = pl.program_id(0)
    last = pl.num_programs(0) - 1

    @pl.when(at == 0)
    def _():
        greet_rows(me, bands)
        stats_ref[...] = jnp.zeros_like(stats_ref)

    _, tokens, channels = field_ref.shape
    first_row = place[0]
    side = sides[at]
    mean, inv_std = moments(avg_ref, at)
    slope = inv_std * vec(gain_ref)
    offset = vec(bias_ref) - mean * slope

    def active(field, row):
        normed = field.astype(F32) * slope + offset
        inside = pixel_inside(normed.shape, row, side, width)
        return jnp.where(inside, normed * sigmoid(normed), 0.0)

    rows = tokens // width
    put_taps(taps_s, 0, active(halo_ref[0, 0], first_row - 1), width, False)
    put_taps(taps_s, width, active(field_ref[0], first_row), width, False)
    put_taps(taps_s, width + tokens, active(halo_ref[1, 0], first_row + rows), width, False)
    deep = 3 * channels
    total = dot_nn(taps_s[:tokens], weight_ref[:deep])
    for tap in (1, 2):
        total = total + dot_nn(
            taps_s[tap * width : tap * width + tokens], weight_ref[tap * deep : (tap + 1) * deep]
        )
    total = total + row_of(shift_ref[...], at)
    inside = pixel_inside(total.shape, first_row, side, width)
    if base_given:
        total = total + jnp.where(inside, base_ref[0].astype(F32), 0.0)
    out_ref[0] = total
    share_edges(total, at, width, next_halo, scratch, me, bands)
    if not base_given:
        ride = edge_copies(
            base_ref.at[at, pl.ds(0, width)], base_ref.at[at, pl.ds(tokens - width, width)], ride_halo,
            at, ride_send, ride_recv, me, bands,
        )
        for item in ride:
            item.start()
    masked = jnp.where(inside, total, 0.0)
    put_row(stats_ref, 2 * at, col_sum(masked))
    put_row(stats_ref, 2 * at + 1, col_sum(masked * masked))

    @pl.when(at == last)
    def _():
        close_exchange(stats_ref[...], None, sides, next_avg, next_halo, scratch, me, bands)
        if not base_given:
            for image in range(base_ref.shape[0]):
                for item in edge_copies(
                    base_ref.at[image, pl.ds(0, width)], base_ref.at[image, pl.ds(tokens - width, width)],
                    ride_halo, image, ride_send, ride_recv, me, bands,
                ):
                    item.wait_send()
                for end in range(2):
                    edge = ride_halo.at[end, image]
                    row_copy(
                        edge, edge, ride_send.at[end, image], ride_recv.at[end, image], lax.rem(me + 1, bands)
                    ).wait_recv()


def conv_forward(place, sides, field, halo, avg, gain, bias, weight, shift, base, added, width,
                 bands):
    images, tokens, channels = field.shape
    anywhere = pl.BlockSpec(memory_space=pl.ANY)
    halos = jax.ShapeDtypeStruct((2, images, width, channels), BF)
    return pl.pallas_call(
        partial(conv_forward_kernel, width, bands, added),
        grid=(images,),
        out_shape=(
            jax.ShapeDtypeStruct(field.shape, F32),
            jax.ShapeDtypeStruct((8, channels), F32),
            halos,
        )
        + (() if added else (halos,)),
        in_specs=[
            SMEM_WHOLE,
            SMEM_WHOLE,
            image_block(tokens, channels),
            edge_block(width, channels),
            table_block(channels),
            vector_block(channels),
            vector_block(channels),
            fixed_block(weight.shape),
            table_block(channels),
            image_block(tokens, channels) if added else anywhere,
        ],
        out_specs=(image_block(tokens, channels), table_block(channels), anywhere)
        + (() if added else (anywhere,)),
        scratch_shapes=[
            pltpu.VMEM((tokens + 2 * width, 3 * channels), BF),
            pltpu.VMEM((8, channels), F32),
        ]
        + exchange_scratch(images, width, channels, bands)
        + ([] if added else [pltpu.SemaphoreType.DMA((2, images))] * 2),
        compiler_params=pltpu.CompilerParams(
            vmem_limit_bytes=62 << 20, collective_id=2 if added else 3, has_side_effects=True
        ),
        name="conv_forward",
    )(place, sides, field, halo, avg, gain, bias, weight, shift, base)


class BandFold:
    def __init__(self, parts, scratch, me):
        self.parts, self.me = parts, me
        count = len(parts)
        self.own, self.pair, self.first, self.second_s = (
            scratch[at * count : (at + 1) * count] for at in range(4)
        )
        self.load, self.pair_send, self.pair_recv, self.hop_send, self.hop_recv = scratch[4 * count :]
        self.core, self.chip = lax.rem(me, 2), me // 2
        self.chunks = fold_chunks([part.shape for part in parts])

    def loads(self, which):
        size = self.parts[which].shape[0] // 8
        return [
            pltpu.make_async_copy(
                self.parts[which].at[pl.ds(pl.multiple_of((2 * spot + self.core) * size, 16), size)],
                self.own[which].at[spot],
                self.load.at[which, spot],
            )
            for spot in range(4)
        ]

    def pairs(self, which):
        size = self.parts[which].shape[0] // 8
        return [
            row_copy(
                self.parts[which].at[pl.ds(pl.multiple_of((2 * spot + 1 - self.core) * size, 16), size)],
                self.pair[which].at[spot],
                self.pair_send.at[which, spot],
                self.pair_recv.at[which, spot],
                self.me + 1 - 2 * self.core,
            )
            for spot in range(4)
        ]

    def hops(self, at):
        which, first, wide, one, two = self.chunks[at]
        cols = pl.ds(first, wide)
        near, far = jnp.bitwise_xor(self.chip, one), jnp.bitwise_xor(self.chip, two)

        def hop(spot, dst, step, chip):
            return row_copy(
                self.own[which].at[spot, :, cols], dst, self.hop_send.at[at, step], self.hop_recv.at[at, step],
                2 * chip + self.core,
            )

        return [
            hop(near, self.first[which].at[0, :, cols], 0, near),
            hop(jnp.bitwise_xor(near, two), self.first[which].at[1, :, cols], 1, near),
            hop(far, self.second_s[which].at[:, cols], 2, far),
        ]

    def start(self):
        for which in range(len(self.parts)):
            for item in self.loads(which) + self.pairs(which):
                item.start()

    def spread(self):
        for which in range(len(self.parts)):
            for item in self.loads(which):
                item.wait()
            for item in self.pairs(which):
                item.wait_recv()
            for spot in range(4):
                self.own[which][spot] = (
                    self.own[which][spot].astype(F32) + self.pair[which][spot].astype(F32)
                ).astype(BF)
        for at in range(len(self.chunks)):
            for item in self.hops(at)[:2]:
                item.start()

    def second(self):
        for at, (which, first, wide, _, two) in enumerate(self.chunks):
            cols = pl.ds(first, wide)
            for step, item in enumerate(self.hops(at)[:2]):
                item.wait()
                spot = jnp.bitwise_xor(self.chip, two) if step else self.chip
                self.own[which][spot, :, cols] = (
                    self.own[which][spot, :, cols].astype(F32) + self.first[which][step, :, cols].astype(F32)
                ).astype(BF)
            self.hops(at)[2].start()

    def finish(self, outs):
        for at, (which, first, wide, _, _) in enumerate(self.chunks):
            cols = pl.ds(first, wide)
            self.hops(at)[2].wait()
            outs[which][:, cols] = (
                self.own[which][self.chip, :, cols].astype(F32) + self.second_s[which][:, cols].astype(F32)
            ).astype(BF)
        for which in range(len(self.parts)):
            for item in self.pairs(which):
                item.wait_send()


def fold_chunks(shapes):
    total = sum(rows * cols for rows, cols in shapes)
    rows, cols = shapes[0]
    wide = (total // 2 // rows + 64) // 128 * 128
    chunks = [(0, 0, wide, 1, 2), (0, wide, cols - wide, 2, 1)]
    return chunks + [(at, 0, shape[1], 2, 1) for at, shape in enumerate(shapes) if at]


def fold_scratch(shapes):
    def bufs(lead):
        return [pltpu.VMEM(lead + (rows // 8, cols), BF) for rows, cols in shapes]

    chunks = len(fold_chunks(shapes))
    return (
        bufs((4,)) + bufs((4,)) + bufs((2,)) + bufs(())
        + [pltpu.SemaphoreType.DMA((len(shapes), 4))] * 3
        + [pltpu.SemaphoreType.DMA((chunks, 3))] * 2
    )


class GroupTree:
    def __init__(self, fields, outs, scratch, group):
        self.fields, self.outs, self.group = fields, outs, group
        count = len(fields)
        self.near_s, self.far_s = scratch[:count], scratch[count : 2 * count]
        self.send, self.recv = scratch[2 * count :]
        self.odd = lax.rem(group, 2)

    def half(self, which, odd):
        size = self.fields[which].shape[0] // 2
        return pl.ds(pl.multiple_of(odd * size, 16), size)

    def copies(self, which, step):
        mine, theirs = self.half(which, self.odd), self.half(which, 1 - self.odd)
        out = self.outs[which].at[mine]
        src, dst, bit = (
            (self.fields[which].at[theirs], self.near_s[which], 1),
            (self.fields[which].at[mine], self.far_s[which], 2),
            (out, out, 1),
        )[step]
        return pltpu.make_async_remote_copy(
            src_ref=src, dst_ref=dst, send_sem=self.send.at[which, step], recv_sem=self.recv.at[which, step],
            device_id={"heads": jnp.bitwise_xor(self.group, bit)}, device_id_type=pl.DeviceIdType.MESH,
        )

    def near(self):
        for which in range(len(self.fields)):
            self.copies(which, 0).start()

    def far(self):
        for which in range(len(self.fields)):
            mine = self.half(which, self.odd)
            self.copies(which, 0).wait()
            self.fields[which][mine] = (
                self.fields[which][mine].astype(F32) + self.near_s[which][...].astype(F32)
            ).astype(BF)
            self.copies(which, 1).start()

    def back(self):
        for which in range(len(self.fields)):
            mine = self.half(which, self.odd)
            self.copies(which, 1).wait()
            self.outs[which][mine] = (
                self.fields[which][mine].astype(F32) + self.far_s[which][...].astype(F32)
            ).astype(BF)
            self.copies(which, 2).start()

    def end(self):
        for which in range(len(self.fields)):
            self.copies(which, 2).wait_send()
            theirs = self.outs[which].at[self.half(which, 1 - self.odd)]
            pltpu.make_async_remote_copy(
                src_ref=theirs, dst_ref=theirs, send_sem=self.send.at[which, 2],
                recv_sem=self.recv.at[which, 2], device_id={"heads": jnp.bitwise_xor(self.group, 1)},
                device_id_type=pl.DeviceIdType.MESH,
            ).wait_recv()


def tree_scratch(shapes):
    return [pltpu.VMEM((rows // 2, cols), BF) for rows, cols in shapes] * 2 + [
        pltpu.SemaphoreType.DMA((len(shapes), 3))
    ] * 2


def conv_backward_kernel(width, bands, added, late, summed, *refs):
    refs = list(refs)
    late_refs, refs = refs[:late], refs[late:]
    summed_refs, refs = refs[:summed], refs[summed:]
    me = lax.axis_index("rows")
    (place, sides, grad_ref, grad_halo, field_ref, field_halo, avg_ref, back_avg, gain_ref) = refs[:9]
    refs = refs[9:]
    if added:
        add_ref, add_halo = refs[:2]
        refs = refs[2:]
    (weight_ref, prior_ref, prior_avg, prior_gain, prior_bias) = refs[:5]
    refs = refs[5:]
    late_outs, refs = refs[:late], refs[late:]
    summed_outs, refs = refs[:summed], refs[summed:]
    if added:
        kept_ref = refs[0]
        refs = refs[1:]
    out_ref, next_avg, stats_ref, sums_ref, weight_grad = refs[:5]
    next_halo = None
    if added:
        next_halo = refs[5]
        refs = refs[1:]
    taps_s, act_s, total_s = refs[5:8]
    scratch = refs[8:]
    if late:
        base = 6 if added else 3
        after = base + 4 * late + 5
        fold = BandFold(late_refs, scratch[base:after], me)
        if summed:
            fields, made = scratch[after : after + summed], scratch[after + summed : after + 2 * summed]
            group = lax.axis_index("heads")
            tree = GroupTree(fields, made, scratch[after + 2 * summed :], group)
        scratch = scratch[:base]
    at = pl.program_id(0)
    last = pl.num_programs(0) - 1
    _, tokens, channels = grad_ref.shape
    first_row = place[0]
    side = sides[at]
    mean, inv_std = moments(avg_ref, at)
    back = back_avg[...]
    back_mean, back_cross = row_of(back, 2 * at), row_of(back, 2 * at + 1)
    gain = vec(gain_ref)
    grad_slope = inv_std * gain
    field_slope = inv_std * inv_std * back_cross
    offset = inv_std * back_mean - mean * field_slope

    def through(grads, field, extra, row):
        moved = grads.astype(F32) * grad_slope - field.astype(F32) * field_slope - offset
        if extra is not None:
            moved = moved + extra.astype(F32)
        return jnp.where(pixel_inside(moved.shape, row, side, width), moved, 0.0)

    rows = tokens // width
    own = through(grad_ref[0], field_ref[0], add_ref[0] if added else None, first_row)
    put_taps(taps_s, width, own, width, True)
    for end, row, first in ((0, first_row - 1, 0), (1, first_row + rows, width + tokens)):
        put_taps(
            taps_s,
            first,
            through(grad_halo[end, 0], field_halo[end, 0], add_halo[end, 0] if added else None, row),
            width,
            True,
        )
    if added:
        kept_ref[0] = own

    @pl.when(at == 0)
    def _():
        greet_rows(me, bands)
        stats_ref[...] = jnp.zeros_like(stats_ref)
        sums_ref[...] = jnp.zeros_like(sums_ref)
        if summed:
            for bit in (1, 2):
                pl.semaphore_signal(
                    pltpu.get_barrier_semaphore(), inc=1, device_id={"heads": jnp.bitwise_xor(group, bit)},
                    device_id_type=pl.DeviceIdType.MESH,
                )
            for field, ref in zip(fields, summed_refs):
                field[...] = ref[...]
        if late:
            meet_rows(bands + 2 if summed else bands)
            fold.start()
        if summed:
            tree.near()
        total_s[...] = jnp.zeros_like(total_s)

    put_row(sums_ref, at, col_sum(own))
    prior_mean, prior_std = moments(prior_avg, at)
    centred = (prior_ref[0].astype(F32) - prior_mean) * prior_std
    normed = centred * vec(prior_gain) + vec(prior_bias)
    gate = sigmoid(normed)
    inside = pixel_inside(normed.shape, first_row, side, width)
    act_s[...] = jnp.where(inside, normed * gate, 0.0).T.astype(BF)
    act_t = act_s[...]
    moved = None
    for down in range(3):
        lines = pl.ds((2 - down) * width, tokens)
        for across in range(3):
            tap = 3 * down + across
            low = taps_s[lines, across * channels : (across + 1) * channels]
            part = slice(tap * channels, (tap + 1) * channels)
            term = dot_nt(low, weight_ref[part])
            moved = term if moved is None else moved + term
            total_s[part] += dot_nn(act_t, low)
        if late and down == 1:
            pl.when(at == 0)(fold.spread)
    if late:
        pl.when(at == 2)(fold.second)
    if summed:
        pl.when(at == 1)(tree.far)
        pl.when(at == 2)(tree.back)
    grads = jnp.where(inside, moved * (gate + normed * gate * (1.0 - gate)), 0.0)
    out_ref[0] = grads
    if added:
        share_edges(grads, at, width, next_halo, scratch, me, bands, late > 0)
    put_row(stats_ref, 2 * at, col_sum(grads))
    put_row(stats_ref, 2 * at + 1, col_sum(grads * centred))

    @pl.when(at == last)
    def _():
        if late:
            fold.finish(late_outs)
        if summed:
            tree.end()
            for out, field in zip(summed_outs, made):
                out[...] = field[...]
        if added:
            close_exchange(stats_ref[...], prior_gain, sides, next_avg, next_halo, scratch, me, bands)
        else:
            if not late:
                meet_rows(bands)
            next_avg[...] = group_average(stats_ref[...], prior_gain, sides, *scratch, me, bands)
        weight_grad[...] = total_s[...].astype(BF)


def conv_backward(place, sides, grads, grad_halo, field, field_halo, avg, back_avg, gain, extra,
                  extra_halo, weight, prior, prior_avg, prior_gain, prior_bias, late, summed, width, bands):
    images, tokens, channels = grads.shape
    added = extra is not None
    tok = image_block(tokens, channels)
    edge = edge_block(width, channels)
    table = table_block(channels)
    vector = vector_block(channels)
    anywhere = pl.BlockSpec(memory_space=pl.ANY)
    ins = [*late, *summed, place, sides, grads, grad_halo, field, field_halo, avg, back_avg, gain]
    specs = [anywhere] * len(late) + [fixed_block(part.shape) for part in summed] + [SMEM_WHOLE, SMEM_WHOLE, tok, edge, tok, edge, table, table, vector]
    if added:
        ins += [extra, extra_halo]
        specs += [tok, edge]
    ins += [weight, prior, prior_avg, prior_gain, prior_bias]
    specs += [fixed_block(weight.shape), tok, table, vector, vector]
    outs = [
        jax.ShapeDtypeStruct(grads.shape, F32),
        jax.ShapeDtypeStruct((8, channels), F32),
        jax.ShapeDtypeStruct((8, channels), F32),
        jax.ShapeDtypeStruct((8, channels), F32),
        jax.ShapeDtypeStruct(weight.shape, BF),
    ]
    out_specs = [tok, table, table, table, fixed_block(weight.shape)]
    if added:
        outs.append(jax.ShapeDtypeStruct((2, images, width, channels), BF))
        out_specs.append(pl.BlockSpec(memory_space=pl.ANY))
        outs.insert(0, jax.ShapeDtypeStruct(grads.shape, F32))
        out_specs.insert(0, tok)
    shapes = [(part.shape[0] // 8, part.shape[1]) for part in late] + [part.shape for part in summed]
    outs = [jax.ShapeDtypeStruct(shape, BF) for shape in shapes] + outs
    out_specs = [fixed_block(shape) for shape in shapes] + out_specs
    return pl.pallas_call(
        partial(conv_backward_kernel, width, bands, added, len(late), len(summed)),
        grid=(images,),
        out_shape=outs,
        in_specs=specs,
        out_specs=out_specs,
        scratch_shapes=[
            pltpu.VMEM((tokens + 2 * width, 3 * channels), BF),
            pltpu.VMEM((channels, tokens), BF),
            pltpu.VMEM(weight.shape, F32),
        ]
        + (
            exchange_scratch(images, width, channels, bands)
            if added
            else [
                pltpu.VMEM((bands, 8, channels), F32),
                pltpu.SemaphoreType.DMA((bands,)),
                pltpu.SemaphoreType.DMA((bands,)),
            ]
        )
        + (fold_scratch([part.shape for part in late]) if late else [])
        + [pltpu.VMEM(part.shape, BF) for part in (*summed, *summed)]
        + (tree_scratch([part.shape for part in summed]) if summed else []),
        compiler_params=pltpu.CompilerParams(
            vmem_limit_bytes=62 << 20, collective_id=4 if added else 6, has_side_effects=True
        ),
        name="conv_backward",
    )(*ins)


def layer_stats(field):
    centre = jnp.mean(field, axis=-1, keepdims=True)
    centred = field - centre
    inv_std = lax.rsqrt(jnp.mean(centred * centred, axis=-1, keepdims=True) + LN_EPS)
    return centred * inv_std, inv_std


def layer_back(grads, gain, centred, inv_std):
    scaled = grads * gain
    return inv_std * (
        scaled
        - jnp.mean(scaled, axis=-1, keepdims=True)
        - centred * jnp.mean(scaled * centred, axis=-1, keepdims=True)
    )


def turn_qkv(weight_ref, turned_s):
    rows, channels = weight_ref.shape[0], weight_ref.shape[1] // 3
    low = lane_ids(rows) < 64
    for head in range(HEADS):
        first = (head // 2) * 128
        keys = weight_ref[:, channels + first : channels + first + 128].astype(F32)
        values = weight_ref[:, 2 * channels + first : 2 * channels + first + 128].astype(F32)
        if head % 2 == 0:
            joint = jnp.where(low, keys, swap_halves(values))
        else:
            joint = jnp.where(low, swap_halves(keys), values)
        turned_s[:, head * 128 : head * 128 + 128] = joint.astype(BF)
    turned_s[:, 2 * channels :] = weight_ref[:, :channels]


def entry_kernel(bands, direct, field_ref, avg_ref, gain_ref, bias_ref, proj_ref, proj_bias, ln_gain,
                 ln_bias, qkv_ref, stream_ref, *refs):
    images = pl.num_programs(0)
    at = pl.program_id(0)
    if direct:
        count = len(refs) - 4
        sent_refs, (turned_s, first_s, send, recv) = refs[:count], refs[count:]
        me = lax.axis_index("rows")
    else:
        sent_refs, turned_s = refs[:-1], refs[-1]
    _, tokens, channels = field_ref.shape
    half = tokens // 2

    @pl.when(at == 0)
    def _():
        if direct:
            greet_rows(me, bands)
        turn_qkv(qkv_ref, turned_s)

    mean, inv_std = moments(avg_ref, at)
    slope = inv_std * vec(gain_ref)
    flat = (field_ref[0] * slope + (vec(bias_ref) - mean * slope)).astype(BF)
    stream = dot_nn(flat, proj_ref[...]) + vec(proj_bias)
    stream_ref[0] = stream
    centred, _ = layer_stats(stream)
    joint = dot_nn((centred * vec(ln_gain) + vec(ln_bias)).astype(BF), turned_s[...])
    low = lane_ids(half) < 64

    def put(out):
        for head in range(HEADS):
            out[head, :tokens] = joint[:, head * 128 : head * 128 + 128].astype(BF)
            first = 2 * channels + (head // 2) * 128
            upper, lower = joint[:half, first : first + 128], joint[half:, first : first + 128]
            if head % 2 == 0:
                pairs = jnp.where(low, upper, swap_halves(lower))
            else:
                pairs = jnp.where(low, swap_halves(upper), lower)
            out[head, tokens:] = pairs.astype(BF)

    for image, out in enumerate(sent_refs):
        pl.when(at == image)(partial(put, first_s if direct and image == 0 else out))
    if not direct:
        return
    copies = [
        row_copy(
            first_s.at[lax.rem(me + away, bands)], sent_refs[0].at[me], send.at[away], recv.at[me],
            lax.rem(me + away, bands),
        )
        for away in range(1, bands)
    ]
    own = pltpu.make_async_copy(first_s.at[me], sent_refs[0].at[me], recv.at[me])

    @pl.when(at == 0)
    def _():
        meet_rows(bands)
        for item in copies:
            item.start()
        own.start()

    @pl.when(at == images - 1)
    def _():
        own.wait()
        for away, item in enumerate(copies):
            item.wait_send()
            source = lax.rem(me + away + 1, bands)
            row_copy(
                sent_refs[0].at[source], sent_refs[0].at[source], send.at[away + 1], recv.at[source], source
            ).wait_recv()


def entry(field, avg, gain, bias, proj, proj_bias, ln_gain, ln_bias, qkv, bands):
    images, tokens, channels = field.shape
    vector = vector_block(channels)
    direct = bands == HEADS
    packed = (HEADS, tokens * 3 // 2, 128)
    anywhere = pl.BlockSpec(memory_space=pl.ANY)
    params = {"collective_id": 9, "has_side_effects": True} if direct else {}
    return pl.pallas_call(
        partial(entry_kernel, bands, direct),
        grid=(images,),
        out_shape=(jax.ShapeDtypeStruct(field.shape, F32),)
        + (jax.ShapeDtypeStruct(packed, BF),) * images,
        in_specs=[
            image_block(tokens, channels),
            table_block(channels),
            vector,
            vector,
            fixed_block(proj.shape),
            vector,
            vector,
            vector,
            fixed_block(qkv.shape),
        ],
        out_specs=(image_block(tokens, channels),)
        + ((anywhere,) if direct else (fixed_block(packed),))
        + (fixed_block(packed),) * (images - 1),
        scratch_shapes=[pltpu.VMEM(qkv.shape, BF)]
        + (
            [
                pltpu.VMEM(packed, BF),
                pltpu.SemaphoreType.DMA((bands,)),
                pltpu.SemaphoreType.DMA((bands,)),
            ]
            if direct
            else []
        ),
        compiler_params=pltpu.CompilerParams(vmem_limit_bytes=62 << 20, **params),
        name="entry",
    )(field, avg, gain, bias, proj, proj_bias, ln_gain, ln_bias, qkv)


def join_heads(pairs_ref, at):
    half = pairs_ref.shape[-2]
    low = lane_ids(half) < 64
    upper, lower = [], []
    for head in range(0, HEADS, 2):
        one, two = pairs_ref[at, head].astype(F32), pairs_ref[at, head + 1].astype(F32)
        upper.append(jnp.where(low, one, swap_halves(two)))
        lower.append(jnp.where(low, swap_halves(one), two))
    return jnp.concatenate(
        [jnp.concatenate(upper, axis=1), jnp.concatenate(lower, axis=1)], axis=0
    ).astype(BF)


def split_heads(field, out_ref, at):
    half = field.shape[0] // 2
    low = lane_ids(half) < 64
    for head in range(HEADS):
        first = (head // 2) * 128
        upper, lower = field[:half, first : first + 128], field[half:, first : first + 128]
        if head % 2 == 0:
            pairs = jnp.where(low, upper, swap_halves(lower))
        else:
            pairs = jnp.where(low, swap_halves(upper), lower)
        out_ref[at, head] = pairs.astype(BF)


def feed_pieces(channels, wide, hidden, bands):
    size = channels // bands
    geglu = [(at * size, size) for at in range(wide // channels)]
    first = wide // bands
    return (
        geglu,
        [(first, hidden // bands)],
        [(first + hidden // bands, size)],
        [(first + hidden // bands + size, size)],
    )


def feed_kernel(width, bands, per_band, halving, place, sides, *refs):
    given, refs = refs[:per_band], refs[per_band:]
    count = 4 if halving else 1
    grads_ref, refs = refs[17 : 17 + count], refs[:17] + refs[17 + count :]
    (stream_ref, residual_ref, cot_ref, cross_ref, attn_ref, attn_bias, ln_gain, ln_bias,
     geglu_ref, geglu_bias, feed_ref, feed_bias, proj_ref, proj_bias,
     out_ref, three_ref, back_ref, sums_ref, cross_sum, pair_sums, geglu_s, feed_s, proj_s, attn_s,
     turned_s, mixed_s, sent_s, out_send, out_recv, back_send, back_recv, *more) = refs
    if halving:
        given_s, taken_s, pair_sems = more
    at = pl.program_id(0)
    images = pl.num_programs(0)
    last = images - 1
    me = lax.axis_index("rows")

    def move(src, dst, send, recv, target):
        @pl.when(target != me)
        def _():
            pltpu.make_async_remote_copy(
                src_ref=src, dst_ref=dst, send_sem=send, recv_sem=recv, device_id={"rows": target},
                device_id_type=pl.DeviceIdType.MESH,
            ).start()

        @pl.when(target == me)
        def _():
            pltpu.make_async_copy(src, dst, recv).start()

    def arrived(dst, send, recv, source):
        @pl.when(source != me)
        def _():
            pltpu.make_async_remote_copy(
                src_ref=dst, dst_ref=dst, send_sem=send, recv_sem=recv, device_id={"rows": source},
                device_id_type=pl.DeviceIdType.MESH,
            ).wait_recv()

        @pl.when(source == me)
        def _():
            pltpu.make_async_copy(dst, dst, recv).wait()

    def left(src, send, recv, target):
        @pl.when(target != me)
        def _():
            pltpu.make_async_remote_copy(
                src_ref=src, dst_ref=src, send_sem=send, recv_sem=recv, device_id={"rows": target},
                device_id_type=pl.DeviceIdType.MESH,
            ).wait_send()

    def send_spot(spot):
        item = me * per_band + spot
        head, image = item // images, lax.rem(item, images)
        for away in range(bands):
            band = lax.rem(me + away, bands)
            move(
                given[spot].at[band], mixed_s.at[image, head], out_send.at[spot, away],
                out_recv.at[image, head], band,
            )

    @pl.when(at == 0)
    def _():
        greet_rows(me, bands)
        meet_rows(bands)
        send_spot(0)

    for head in range(HEADS):
        arrived(
            mixed_s.at[at, head], out_send.at[0, 0], out_recv.at[at, head], (head * images + at) // per_band
        )
    for spot in range(1, per_band):
        pl.when(at == spot - 1)(partial(send_spot, spot))
    _, tokens, channels = stream_ref.shape
    hidden = feed_ref.shape[0]
    side = sides[at]
    inside = pixel_inside((tokens, channels), place[0], side, width)

    @pl.when(at == 0)
    def _():
        for ref in (sums_ref, cross_sum, pair_sums, geglu_s, feed_s, proj_s, attn_s):
            ref[...] = jnp.zeros_like(ref)

    mixed = join_heads(mixed_s, at)
    three = stream_ref[0] + dot_nn(mixed, attn_ref[...]) + (vec(attn_bias) + row_of(cross_ref[...], at))
    centred, inv_std = layer_stats(three)
    feed_in = (centred * vec(ln_gain) + vec(ln_bias)).astype(BF)
    grad_out = jnp.where(inside, cot_ref[0].astype(F32), 0.0)
    branch = grad_out.astype(BF)
    grad_four = dot_nt(branch, proj_ref[...])
    low_feed = grad_four.astype(BF)
    low_feed_t = grad_four.T.astype(BF)
    feed_in_t = (centred * vec(ln_gain) + vec(ln_bias)).T.astype(BF)
    four = three + vec(feed_bias)
    grad_in = jnp.zeros((tokens, channels), F32)
    step = 512

    pair_bias = vec(geglu_bias)

    def products(first):
        own = slice(first, first + step)
        gates = slice(hidden + first, hidden + first + step)
        value = dot_nn(feed_in, geglu_ref[:, own]) + pair_bias[:, own]
        gate = dot_nn(feed_in, geglu_ref[:, gates]) + pair_bias[:, gates]
        return value, gate, dot_nt(low_feed, feed_ref[own])

    ahead = products(0)
    for first in range(0, hidden, step):
        own = slice(first, first + step)
        gates = slice(hidden + first, hidden + first + step)
        value, gate, back = ahead
        if first + step < hidden:
            ahead = products(first + step)
        below = 0.5 + 0.5 * lax.erf(gate * math.sqrt(0.5))
        bell = jnp.exp(gate * gate * -0.5) * (1.0 / math.sqrt(2.0 * math.pi))
        act = gate * below
        gated = (value * act).astype(BF)
        four = four + dot_nn(gated, feed_ref[own])
        feed_s[:, own] += dot_nn(low_feed_t, gated)
        grad_value = back * act
        grad_gate = back * value * (below + gate * bell)
        pair_sums[:, own] += col_sum(grad_value)
        pair_sums[:, gates] += col_sum(grad_gate)
        low_value, low_gate = grad_value.astype(BF), grad_gate.astype(BF)
        geglu_s[:, own] += dot_nn(feed_in_t, low_value)
        geglu_s[:, gates] += dot_nn(feed_in_t, low_gate)
        grad_in = grad_in + dot_nt(low_value, geglu_ref[:, own]) + dot_nt(low_gate, geglu_ref[:, gates])
    last_in = four.astype(BF)
    proj_s[...] += dot_tn(last_in, branch)
    output = residual_ref[0] + dot_nn(last_in, proj_ref[...]) + vec(proj_bias)
    out_ref[0] = jnp.where(inside, output, 0.0).astype(BF)
    grad_three = grad_four + layer_back(grad_in, vec(ln_gain), centred, inv_std)
    three_ref[0] = grad_three
    low_attn = grad_three.astype(BF)
    attn_s[...] += dot_tn(mixed, low_attn)
    split_heads(dot_nt(low_attn, attn_ref[...]), sent_s, at)
    for head in range(HEADS):
        item = head * images + at
        move(
            sent_s.at[at, head], back_ref.at[lax.rem(item, per_band), me], back_send.at[at, head],
            back_recv.at[lax.rem(item, per_band), me], item // per_band,
        )
    put_row(cross_sum, at, col_sum(grad_three))
    ids = lax.broadcasted_iota(jnp.int32, sums_ref.shape, 0)
    for row, total in enumerate(
        (col_sum(grad_out), col_sum(grad_four), col_sum(grad_in * centred), col_sum(grad_in))
    ):
        sums_ref[...] += jnp.where(ids == row, total, 0.0)

    @pl.when(at == last)
    def _():
        def settle():
            for spot in range(per_band):
                for away in range(bands):
                    band = lax.rem(me + away, bands)
                    left(given[spot].at[band], out_send.at[spot, away], out_recv.at[0, 0], band)
                    arrived(back_ref.at[spot, band], back_send.at[0, 0], back_recv.at[spot, band], band)
            for image in range(sent_s.shape[0]):
                for head in range(HEADS):
                    left(
                        sent_s.at[image, head], back_send.at[image, head], back_recv.at[0, 0],
                        (head * sent_s.shape[0] + image) // per_band,
                    )

        pieces = feed_pieces(channels, 2 * hidden, hidden, bands)

        def put(place_of, band):
            for total, parts in zip((geglu_s, feed_s, proj_s, attn_s), pieces):
                for at_col, (first, size) in enumerate(parts):
                    if total is feed_s:
                        part = turned_s[pl.ds(pl.multiple_of(band * size, 16), size)]
                    else:
                        part = total[
                            pl.ds(pl.multiple_of(band * size, 16), size),
                            at_col * channels : (at_col + 1) * channels,
                        ]
                    ref, own, skip = place_of(first)
                    ref[own + (pl.ds(first - skip, size),)] = part.astype(BF)

        for first in range(0, hidden, step):
            turned_s[first : first + step, :] = feed_s[:, first : first + step].T.astype(BF)

        if not halving:
            for band in range(bands):
                put(lambda first, band=band: (grads_ref[0], (band,), 0), band)
            settle()
            return
        rows = given_s.shape[-2] // 2
        for apart in range(bands // 2):
            own = (apart & 1, apart >> 1)
            put(lambda first, own=own: (given_s, own, 0), jnp.bitwise_xor(me, 2 * apart + 1))
        item = row_copy(given_s, taken_s, pair_sems.at[0], pair_sems.at[1], jnp.bitwise_xor(me, 1))
        item.start()
        for apart in range(bands // 2):
            over_x, over_y = apart & 1, apart >> 1

            def half(first, over_x=over_x, over_y=over_y):
                return (
                    (grads_ref[over_x], (over_y,), 0)
                    if first < rows
                    else (grads_ref[2 + over_y], (over_x,), rows)
                )

            put(half, jnp.bitwise_xor(me, 2 * apart))
        item.wait()
        for apart in range(bands // 2):
            over_x, over_y = apart & 1, apart >> 1
            for ref, spot, lines in (
                (grads_ref[over_x], over_y, slice(0, rows)),
                (grads_ref[2 + over_y], over_x, slice(rows, 2 * rows)),
            ):
                ref[spot] = (ref[spot].astype(F32) + taken_s[over_x, over_y, lines].astype(F32)).astype(BF)
        settle()


def feed(place, sides, mixed, stream, residual, cot, cross, attn, attn_bias, ln_gain, ln_bias, geglu,
         geglu_bias, feed_out, feed_bias, proj, proj_bias, width, bands, halving):
    images, tokens, channels = stream.shape
    tok = image_block(tokens, channels)
    vector = vector_block(channels)
    table = table_block(channels)
    half = tokens // 2
    per_band = len(mixed)
    anywhere = pl.BlockSpec(memory_space=pl.ANY)
    wide = geglu.shape[1]
    weights = (geglu, feed_out, proj, attn)
    rows = sum(w.size for w in weights) // channels // bands
    lead = (2, 2) if halving else (bands,)
    grads = lead + (rows, channels)
    given = [(2, rows // 2, channels)] * 4 if halving else [grads]
    return pl.pallas_call(
        partial(feed_kernel, width, bands, per_band, halving),
        grid=(images,),
        out_shape=(
            jax.ShapeDtypeStruct(stream.shape, BF),
            jax.ShapeDtypeStruct(stream.shape, F32),
            jax.ShapeDtypeStruct((per_band, bands, half, 128), BF),
        )
        + tuple(jax.ShapeDtypeStruct(shape, BF) for shape in given)
        + (
            jax.ShapeDtypeStruct((8, channels), F32),
            jax.ShapeDtypeStruct((8, channels), F32),
            jax.ShapeDtypeStruct((1, wide), F32),
        ),
        in_specs=[
            SMEM_WHOLE,
            SMEM_WHOLE,
        ]
        + [anywhere] * per_band
        + [
            tok,
            tok,
            tok,
            table,
            fixed_block(attn.shape),
            vector,
            vector,
            vector,
            fixed_block(geglu.shape),
            vector_block(wide),
            fixed_block(feed_out.shape),
            vector,
            fixed_block(proj.shape),
            vector,
        ],
        out_specs=(tok, tok, anywhere)
        + tuple(fixed_block(shape) for shape in given)
        + (table, table, table_block(wide, 1)),
        scratch_shapes=[
            pltpu.VMEM(geglu.shape, F32),
            pltpu.VMEM(feed_out.shape[::-1], F32),
            pltpu.VMEM(proj.shape, F32),
            pltpu.VMEM(attn.shape, F32),
            pltpu.VMEM(feed_out.shape, BF),
        ]
        + [pltpu.VMEM((images, HEADS, half, 128), BF)] * 2
        + [
            pltpu.SemaphoreType.DMA((per_band, bands)),
            pltpu.SemaphoreType.DMA((images, HEADS)),
            pltpu.SemaphoreType.DMA((images, HEADS)),
            pltpu.SemaphoreType.DMA((per_band, bands)),
        ]
        + ([pltpu.VMEM(grads, BF)] * 2 + [pltpu.SemaphoreType.DMA((2,))] if halving else []),
        compiler_params=pltpu.CompilerParams(
            vmem_limit_bytes=62 << 20, collective_id=5, has_side_effects=True
        ),
        name="feed",
    )(place, sides, *mixed, stream, residual, cot, cross, attn, attn_bias, ln_gain, ln_bias, geglu,
      geglu_bias, feed_out, feed_bias, proj, proj_bias)


def leave_kernel(width, bands, images, place, sides, *refs):
    direct = bands == HEADS
    if direct:
        *arrays, raw_ref = refs[:images]
        refs = refs[images:]
    else:
        packed_ref, refs = refs[0], refs[1:]
    (stream_ref, three_ref, field_ref, avg_ref, gain_ref, bias_ref, proj_ref, ln_gain, ln_bias,
     qkv_ref, out_ref, next_avg, next_halo, stats_ref, sums_ref, grad_qkv, grad_proj, qkv_s,
     proj_s, turned_s) = refs[:20]
    scratch = refs[20:26]
    me = lax.axis_index("rows")
    at = pl.program_id(0)
    last = pl.num_programs(0) - 1
    _, tokens, channels = stream_ref.shape
    inside = pixel_inside((tokens, channels), place[0], sides[at], width)

    @pl.when(at == 0)
    def _():
        greet_rows(me, bands)
        for ref in (stats_ref, sums_ref, qkv_s, proj_s):
            ref[...] = jnp.zeros_like(ref)
        turn_qkv(qkv_ref, turned_s)

    if direct:
        item_s, last_s, item_sems, last_send, last_recv = refs[26:]
        fetch = [
            pltpu.make_async_copy(array, item_s.at[image % 2], item_sems.at[image % 2])
            for image, array in enumerate(arrays)
        ]
        send_last = [
            row_copy(
                raw_ref.at[lax.rem(me + away, bands)], last_s.at[me], last_send.at[away], last_recv.at[me],
                lax.rem(me + away, bands),
            )
            for away in range(1, bands)
        ]
        keep_last = pltpu.make_async_copy(raw_ref.at[me], last_s.at[me], last_recv.at[me])

        @pl.when(at == 0)
        def _():
            fetch[0].start()
            meet_rows(bands)
            for item in send_last:
                item.start()
            keep_last.start()

        for image in range(len(fetch)):

            @pl.when(at == image)
            def _(image=image):
                if image + 1 < len(fetch):
                    fetch[image + 1].start()
                fetch[image].wait()

        @pl.when(at == last)
        def _():
            keep_last.wait()
            for away in range(1, bands):
                source = lax.rem(me + away, bands)
                row_copy(
                    last_s.at[source], last_s.at[source], last_send.at[away], last_recv.at[source], source
                ).wait_recv()
            item_s[(images - 1) % 2] = last_s[...]
            for item in send_last:
                item.wait_send()

        packed_ref, spot = item_s, lax.rem(at, 2)
    else:
        spot = 0
    queries = join_heads(packed_ref.at[:, :, tokens:, :], spot)
    joint = jnp.concatenate([packed_ref[spot, head, :tokens] for head in range(HEADS)] + [queries], axis=1)
    centred, inv_std = layer_stats(stream_ref[0])
    attn_in = (centred * vec(ln_gain) + vec(ln_bias)).astype(BF)
    qkv_s[...] += dot_tn(attn_in, joint)
    grads = dot_nt(joint, turned_s[...])
    grad_stream = three_ref[0] + layer_back(grads, vec(ln_gain), centred, inv_std)
    low_in = grad_stream.astype(BF)
    mean, deviation = moments(avg_ref, at)
    normed = (field_ref[0] - mean) * deviation
    flat = (normed * vec(gain_ref) + vec(bias_ref)).astype(BF)
    proj_s[...] += dot_tn(flat, low_in)
    moved = jnp.where(inside, dot_nt(low_in, proj_ref[...]), 0.0)
    out_ref[0] = moved
    share_edges(moved, at, width, next_halo, scratch, me, bands, direct)
    put_row(stats_ref, 2 * at, col_sum(moved))
    put_row(stats_ref, 2 * at + 1, col_sum(moved * normed))
    ids = lax.broadcasted_iota(jnp.int32, sums_ref.shape, 0)
    for row, total in enumerate((col_sum(grads * centred), col_sum(grads), col_sum(grad_stream))):
        sums_ref[...] += jnp.where(ids == row, total, 0.0)

    @pl.when(at == last)
    def _():
        close_exchange(stats_ref[...], gain_ref, sides, next_avg, next_halo, scratch, me, bands)
        grad_qkv[...] = qkv_s[...].astype(BF)
        grad_proj[...] = proj_s[...].astype(BF)


def leave(place, sides, packed, stream, three, field, avg, gain, bias, proj, ln_gain, ln_bias, qkv, width,
          bands):
    images, tokens, channels = stream.shape
    direct = bands == HEADS
    tok = image_block(tokens, channels)
    vector = vector_block(channels)
    table = table_block(channels)
    return pl.pallas_call(
        partial(leave_kernel, width, bands, images),
        grid=(images,),
        out_shape=(
            jax.ShapeDtypeStruct(stream.shape, F32),
            jax.ShapeDtypeStruct((8, channels), F32),
            jax.ShapeDtypeStruct((2, images, width, channels), BF),
            jax.ShapeDtypeStruct((8, channels), F32),
            jax.ShapeDtypeStruct((8, channels), F32),
            jax.ShapeDtypeStruct(qkv.shape, BF),
            jax.ShapeDtypeStruct(proj.shape, BF),
        ),
        in_specs=[
            SMEM_WHOLE,
            SMEM_WHOLE,
        ]
        + (
            [pl.BlockSpec(memory_space=pl.ANY)] * images
            if direct
            else [pl.BlockSpec((1,) + packed[0].shape[1:], lambda at: (at, 0, 0, 0))]
        )
        + [
            tok,
            tok,
            tok,
            table,
            vector,
            vector,
            fixed_block(proj.shape),
            vector,
            vector,
            fixed_block(qkv.shape),
        ],
        out_specs=(
            tok,
            table,
            pl.BlockSpec(memory_space=pl.ANY),
            table,
            table,
            fixed_block(qkv.shape),
            fixed_block(proj.shape),
        ),
        scratch_shapes=[
            pltpu.VMEM(qkv.shape, F32), pltpu.VMEM(proj.shape, F32), pltpu.VMEM(qkv.shape, BF)
        ]
        + exchange_scratch(images, width, channels, bands)
        + (
            [
                pltpu.VMEM((2,) + packed[0].shape, BF),
                pltpu.VMEM(packed[0].shape, BF),
                pltpu.SemaphoreType.DMA((2,)),
                pltpu.SemaphoreType.DMA((bands,)),
                pltpu.SemaphoreType.DMA((bands,)),
            ]
            if direct
            else []
        ),
        compiler_params=pltpu.CompilerParams(
            vmem_limit_bytes=62 << 20, collective_id=7, has_side_effects=True
        ),
        name="leave",
    )(place, sides, *packed, stream, three, field, avg, gain, bias, proj, ln_gain, ln_bias, qkv)

def rounded(field):
    return field.astype(BF)


def join_sums(table_ref, cross, hidden, first, second, third, residual, leaves, feeds, pairs):
    images = cross.shape[0] // 2
    channels = cross.shape[1]
    ids = lax.broadcasted_iota(jnp.int32, cross.shape, 0)

    def total(ref, step, offset, count):
        return col_sum(jnp.where((ids < count) & (lax.rem(ids, step) == offset), ref[...], 0.0))

    rows = [row_of(cross[...], at) for at in range(images)] + [row_of(hidden[...], at) for at in range(images)]
    for ref in (first, second, third):
        rows += [total(ref, 2, 1, 2 * images), total(ref, 2, 0, 2 * images)]
    rows.append(total(residual, 1, 0, images))
    rows += [row_of(leaves[...], at) for at in range(3)] + [row_of(feeds[...], at) for at in range(4)]
    rows += [pairs[:, first : first + channels] for first in range(0, pairs.shape[1], channels)]
    table_ref[...] = jnp.zeros_like(table_ref)
    for at, row in enumerate(rows):
        put_row(table_ref.at[pl.ds(at // 8 * 8, 8)], at % 8, row)


def reduce_kernel(count, bands, groups, *refs):
    last_ref, bands_refs = refs[0], refs[1 : 1 + count]
    half_ref, tables = refs[1 + count], refs[2 + count : 11 + count]
    refs = refs[11 + count :]
    last_out, bands_outs, (gathered, other_ref) = refs[0], refs[1 : 1 + count], refs[1 + count : 3 + count]
    refs = refs[3 + count :]
    table_ref, slots, table_send, table_recv, far_send, far_recv, half_sems = refs[:7]
    sum_s, fields = refs[7], refs[8 : 8 + count]
    refs = refs[8 + count :]
    me, group = lax.axis_index("rows"), lax.axis_index("heads")
    fold = BandFold([last_ref], refs[:9], me)
    tree = GroupTree(fields, bands_outs, refs[9 : 11 + 2 * count], group)
    last_tree = GroupTree([sum_s], [last_out], refs[11 + 2 * count :], group)
    row_peers = [lax.rem(me + away, bands) for away in range(1, bands)]
    far_peers = [lax.rem(group + away, groups) for away in range(1, groups)]
    barrier = pltpu.get_barrier_semaphore()
    for axis, peers in (("rows", row_peers), ("heads", far_peers)):
        for peer in peers:
            pl.semaphore_signal(
                barrier, inc=1, device_id={axis: peer}, device_id_type=pl.DeviceIdType.MESH
            )
    for field, ref in zip(fields, bands_refs):
        field[...] = ref[...]
    join_sums(table_ref, *tables)
    pl.semaphore_wait(barrier, bands + groups - 2)

    def copy(src, dst, send, recv, axis, peer):
        return pltpu.make_async_remote_copy(
            src_ref=src,
            dst_ref=dst,
            send_sem=send,
            recv_sem=recv,
            device_id={axis: peer},
            device_id_type=pl.DeviceIdType.MESH,
        )

    near = [
        copy(table_ref, slots.at[away], table_send.at[away], table_recv.at[away], "rows", peer)
        for away, peer in enumerate(row_peers)
    ]
    for item in near:
        item.start()
    fold.start()
    tree.near()
    half = copy(half_ref, other_ref, half_sems.at[0], half_sems.at[1], "heads", jnp.bitwise_xor(group, 1))
    half.start()
    fold.spread()
    for item in near:
        item.wait_recv()
    total = table_ref[...]
    for away in range(bands - 1):
        total = total + slots[away]
    gathered[group] = total
    far = [
        copy(gathered.at[group], gathered.at[group], far_send.at[away], far_recv.at[away], "heads", peer)
        for away, peer in enumerate(far_peers)
    ]
    for item in far:
        item.start()
    tree.far()
    fold.second()
    fold.finish([sum_s])
    last_tree.near()
    tree.back()
    last_tree.far()
    last_tree.back()
    for away in range(groups - 1):
        source = lax.rem(group - (away + 1) + groups, groups)
        copy(
            gathered.at[source], gathered.at[source], far_send.at[away], far_recv.at[away], "heads", source
        ).wait_recv()
    tree.end()
    last_tree.end()
    half.wait_recv()
    for item in [half] + near + far:
        item.wait_send()


def reduce_parts(last, parts, half, bands, groups, sums):
    shapes = [part.shape for part in parts]
    own = (last.shape[0] // bands, last.shape[1])
    rows = 2 * (sums[0].shape[0] // 2) + 14 + sums[-1].shape[1] // last.shape[1]
    table = (-(-rows // 8) * 8, last.shape[1])
    return pl.pallas_call(
        partial(reduce_kernel, len(parts), bands, groups),
        out_shape=(jax.ShapeDtypeStruct(own, BF),)
        + tuple(jax.ShapeDtypeStruct(shape, BF) for shape in shapes)
        + (
            jax.ShapeDtypeStruct((groups,) + table, F32),
            jax.ShapeDtypeStruct(half.shape, BF),
        ),
        in_specs=[pl.BlockSpec(memory_space=pl.ANY)] + [VMEM_WHOLE] * (len(parts) + 1 + len(sums)),
        out_specs=(VMEM_WHOLE,) * (len(parts) + 3),
        scratch_shapes=[pltpu.VMEM(table, F32), pltpu.VMEM((bands - 1,) + table, F32)]
        + [pltpu.SemaphoreType.DMA((bands - 1,))] * 2
        + [pltpu.SemaphoreType.DMA((groups - 1,))] * 2
        + [pltpu.SemaphoreType.DMA((2,)), pltpu.VMEM(own, BF)]
        + [pltpu.VMEM(shape, BF) for shape in shapes]
        + fold_scratch([last.shape])
        + tree_scratch(shapes)
        + tree_scratch([own]),
        compiler_params=pltpu.CompilerParams(
            vmem_limit_bytes=62 << 20, collective_id=8, has_side_effects=True
        ),
        name="reduce_parts",
    )(last, *parts, half, *sums)


def halve_rows(kept, given, step):
    pairs = [(band, band ^ (1 << step)) for band in range(8)]
    return rounded(kept.astype(F32) + lax.ppermute(given, "rows", pairs).astype(F32))


def sum_groups(part, step, groups):
    odd = lax.rem(lax.axis_index("heads"), 2)
    near = [(at, at ^ 1) for at in range(groups)]
    far = [(at, at ^ 2) for at in range(groups)]
    if step == 0:
        one, two = part
        kept, sent = jnp.where(odd == 0, one, two), jnp.where(odd == 0, two, one)
        return rounded(kept.astype(F32) + lax.ppermute(sent, "heads", near).astype(F32))
    if step == 1:
        return rounded(part.astype(F32) + lax.ppermute(part, "heads", far).astype(F32))
    other = lax.ppermute(part, "heads", near)
    return jnp.where(odd == 0, jnp.concatenate([part, other]), jnp.concatenate([other, part]))


def finals_kernel(pieces, *refs):
    (odd, conv_two, conv_one, qkv, proj_in, kept, other, table, value, context, hot, embed, cross_out,
     cross_value, out_conv_two, out_conv_one, out_qkv, out_proj_in, out_geglu, out_feed, out_proj_out,
     out_attn_out, out_class, out_cross_value, out_cross_out, out_time) = refs
    out_conv_two[...] = conv_two[...].astype(F32)
    out_conv_one[...] = conv_one[...].astype(F32)
    out_proj_in[...] = proj_in[...].astype(F32)
    rows, channels = out_proj_in.shape
    low = lane_ids(rows) < 64
    out_qkv[:, :channels] = qkv[:, 2 * channels :].astype(F32)
    for first in range(0, channels, 128):
        one = qkv[:, 2 * first : 2 * first + 128].astype(F32)
        two = qkv[:, 2 * first + 128 : 2 * first + 256].astype(F32)
        out_qkv[:, channels + first : channels + first + 128] = jnp.where(low, one, swap_halves(two))
        out_qkv[:, 2 * channels + first : 2 * channels + first + 128] = jnp.where(
            low, swap_halves(one), two
        )
    flag = jnp.full((1, channels), odd[0], jnp.int32) == 0
    one, two = kept[...].astype(F32), other[...].astype(F32)
    early = jnp.concatenate([jnp.where(flag, one, two), jnp.where(flag, two, one)], axis=0)
    for at, (first, size) in enumerate(pieces[0]):
        out_geglu[:, at * channels : (at + 1) * channels] = early[first : first + size]
    for out, ((first, size),) in zip((out_feed, out_proj_out, out_attn_out), pieces[1:]):
        out[...] = early[first : first + size]
    per_group = value.shape[0] // table.shape[0]

    def joined(first):
        return jnp.concatenate(
            [table[group, first : first + per_group] for group in range(table.shape[0])], axis=0
        )

    def exact(lhs, rhs, dims):
        return lax.dot_general(lhs, rhs, (dims, ((), ())), precision=HIGH, preferred_element_type=F32)

    crossed, shifted = joined(0), joined(per_group)
    out_cross_out[...] = exact(value[...], crossed, ((0,), (0,)))
    grad_value = exact(crossed, cross_out[...].astype(F32), ((1,), (1,)))
    out_cross_value[...] = exact(context[...], grad_value, ((0,), (0,)))
    grad_context = exact(grad_value, cross_value[...].astype(F32), ((1,), (1,)))
    out_class[...] = exact(hot[...], grad_context, ((0,), (0,)))
    out_time[...] = exact(embed[...], shifted, ((0,), (0,)))


def finals(odd, parts, kept, other, table, value, context, hot, embed, cross_out, cross_value, pieces):
    conv_two, conv_one, qkv, proj_in = parts
    rows, channels = proj_in.shape
    shapes = [part.shape for part in parts] + [
        (rows, len(pieces[0]) * channels),
        (pieces[1][0][1], channels),
        (rows, channels),
        (rows, channels),
        (hot.shape[1], rows),
        (rows, channels),
        (rows, channels),
        (embed.shape[1], channels),
    ]
    return pl.pallas_call(
        partial(finals_kernel, pieces),
        out_shape=tuple(jax.ShapeDtypeStruct(shape, F32) for shape in shapes),
        in_specs=[SMEM_WHOLE] + [VMEM_WHOLE] * 13,
        out_specs=(VMEM_WHOLE,) * len(shapes),
        compiler_params=pltpu.CompilerParams(vmem_limit_bytes=62 << 20),
        name="finals",
    )(odd, *parts, kept, other, table, value, context, hot, embed, cross_out, cross_value)


def finish_kernel(width, place, sides, kept_ref, grad_ref, field_ref, avg_ref, back_avg, gain_ref, made_ref,
                  out_ref, pass_ref):
    pass_ref[...] = made_ref[...]
    at = pl.program_id(0)
    mean, inv_std = moments(avg_ref, at)
    back = back_avg[...]
    field_slope = inv_std * inv_std * row_of(back, 2 * at + 1)
    offset = inv_std * row_of(back, 2 * at) - mean * field_slope
    moved = grad_ref[0] * (inv_std * vec(gain_ref)) - field_ref[0].astype(F32) * field_slope - offset
    inside = pixel_inside(moved.shape, place[0], sides[at], width)
    out_ref[0] = jnp.where(inside, kept_ref[0] + moved, 0.0)


def finish(place, sides, kept, grads, field, avg, back_avg, gain, made, width):
    images, tokens, channels = kept.shape
    tok = image_block(tokens, channels)
    table = table_block(channels)
    return pl.pallas_call(
        partial(finish_kernel, width),
        grid=(images,),
        out_shape=(jax.ShapeDtypeStruct(kept.shape, F32), jax.ShapeDtypeStruct(made.shape, BF)),
        in_specs=[SMEM_WHOLE, SMEM_WHOLE, tok, tok, tok, table, table, vector_block(channels), tok],
        out_specs=(tok, tok),
        compiler_params=pltpu.CompilerParams(vmem_limit_bytes=62 << 20),
        name="finish",
    )(place, sides, kept, grads, field, avg, back_avg, gain, made)


def time_features(time_steps, dims):
    half_dim = dims // 2
    frequency = jnp.exp(-math.log(10000.0) * jnp.arange(half_dim, dtype=jnp.float32) / half_dim)
    angles = time_steps.astype(jnp.float32)[:, None] * frequency[None, :]
    return jnp.concatenate([jnp.cos(angles), jnp.sin(angles)], axis=-1)


def pad_rows(table):
    return jnp.pad(table, ((0, 8 - table.shape[0]), (0, 0)))


def to_items(sent, bands):
    images, heads = len(sent), sent[0].shape[0]
    per_band = heads * images // bands
    if bands == heads:
        first, *parts = sent
    else:
        items = jnp.stack(sent, axis=1).reshape((bands, per_band) + sent[0].shape[1:])
        parts = [items[:, at] for at in range(per_band)]
    parts = [lax.all_to_all(part, "rows", split_axis=0, concat_axis=0, tiled=True) for part in parts]
    return [first] + parts if bands == heads else parts


def from_items(results, images, bands):
    if bands == HEADS:
        return [
            lax.all_to_all(result, "rows", split_axis=0, concat_axis=0, tiled=True)
            for result in results[:-1]
        ] + results[-1:]
    back = [
        lax.all_to_all(result, "rows", split_axis=0, concat_axis=0, tiled=True)
        for result in results
    ]
    joint = jnp.stack(back, axis=1)
    return [jnp.swapaxes(joint.reshape((HEADS, images) + joint.shape[2:]), 0, 1)]


def per_device(
    images,
    image_sides,
    labels,
    timesteps,
    cotangent,
    first_gain,
    first_bias,
    conv_one,
    time_proj,
    time_bias,
    second_gain,
    second_bias,
    conv_two,
    conv_bias,
    third_gain,
    third_bias,
    proj_in,
    proj_in_bias,
    attn_gain,
    attn_bias,
    qkv_proj,
    attn_out,
    attn_out_bias,
    class_table,
    cross_value,
    cross_out,
    feed_gain,
    feed_bias,
    geglu_proj,
    geglu_bias,
    feed_out,
    feed_out_bias,
    proj_out,
    proj_out_bias,
):
    image_count, band_rows, width, channels = images.shape
    tokens = band_rows * width
    head_dim = channels // HEADS
    score_scale = head_dim ** (-0.5)
    bands = lax.axis_size("rows")
    groups = lax.axis_size("heads")
    halving = bands == 8 and groups == 4 and channels == 512
    me = lax.axis_index("rows")
    first_image = lax.axis_index("heads") * image_count
    sides = lax.dynamic_slice_in_dim(image_sides, first_image, image_count)
    place = jnp.stack([me * band_rows, me]).astype(jnp.int32)

    field = images.reshape(image_count, tokens, channels)
    cot = cotangent.reshape(image_count, tokens, channels)

    hot = rounded(
        (labels[:, None] == jnp.arange(class_table.shape[0], dtype=jnp.int32)[None, :]).astype(F32)
    )
    context = jnp.dot(hot, class_table, preferred_element_type=F32)
    value = rounded(jnp.dot(rounded(context), cross_value, preferred_element_type=F32))
    cross = jnp.dot(value, cross_out, preferred_element_type=F32)
    cross = pad_rows(lax.dynamic_slice_in_dim(cross, first_image, image_count))
    embed = rounded(jax.nn.silu(time_features(timesteps, time_proj.shape[0])))
    shift = jnp.dot(embed, time_proj, preferred_element_type=F32) + time_bias.astype(F32)
    shift = pad_rows(lax.dynamic_slice_in_dim(shift, first_image, image_count))

    avg_one, halo_images = begin(place, sides, field, width, bands)
    hidden, avg_two, halo_hidden, halo_cot = conv_forward(
        place, sides, field, halo_images, avg_one, first_gain, first_bias, conv_one,
        shift, cot, False, width, bands,
    )
    residual, avg_three, halo_residual = conv_forward(
        place, sides, hidden, halo_hidden, avg_two, second_gain, second_bias, conv_two,
        jnp.broadcast_to(conv_bias.astype(F32), (8, channels)), field, True, width, bands,
    )
    stream, *sent = entry(
        residual, avg_three, third_gain, third_bias, proj_in, proj_in_bias,
        attn_gain, attn_bias, qkv_proj, bands,
    )
    chunks = to_items(sent, bands)
    first_item = me * len(chunks)
    item_sides = [
        lax.dynamic_slice_in_dim(sides, lax.rem(first_item + at, image_count), 1)
        for at in range(len(chunks))
    ]
    attended = [attend(side, chunk, width, score_scale) for side, chunk in zip(item_sides, chunks)]
    mixed = [pairs for pairs, _, _ in attended]
    (
        output, three, grad_chunks, *feed_grads, feed_sums, cross_sum, pair_sums,
    ) = feed(
        place, sides, mixed, stream, residual, cot, cross, attn_out, attn_out_bias,
        feed_gain, feed_bias, geglu_proj, geglu_bias, feed_out,
        feed_out_bias, proj_out, proj_out_bias, width, bands, halving,
    )
    halved = (feed_grads[0:2], feed_grads[2:4]) if halving else None
    results = []
    for spot, (side, chunk, (_, norms, kept)) in enumerate(zip(item_sides, chunks, attended)):
        if halving and spot in (1, 2):
            halved = [
                halve_rows(kept, given, spot if at == 0 else 3 - spot) for at, (kept, given) in enumerate(halved)
            ]
            *halved, norms = lax.optimization_barrier((*halved, norms))
            halved = [(part[0], part[1]) for part in halved] if spot == 1 else halved
        results.append(attend_back(side, chunk, grad_chunks, spot, norms, kept, width, score_scale))
    grad_qkv = from_items(results, image_count, bands)
    if halving:
        early = halved
    else:
        early = feed_grads[0].reshape((bands,) + feed_grads[0].shape[-2:])
        early = lax.psum_scatter(early, "rows", scatter_dimension=0, tiled=True)[0]
        early = lax.psum(early, "heads")
    moved, back_three, halo_moved, third_sums, leave_sums, grad_qkv_proj, grad_proj_in = leave(
        place, sides, grad_qkv, stream, three, residual, avg_three, third_gain,
        third_bias, proj_in, attn_gain, attn_bias, qkv_proj, width, bands,
    )
    if halving:
        *early, back_three = lax.optimization_barrier((*early, back_three))
        early = sum_groups(early, 0, groups)
    *folded, grad_residual, moved, back_two, second_sums, residual_sums, grad_conv_two, halo_moved = conv_backward(
        place, sides, moved, halo_moved, residual, halo_residual, avg_three, back_three,
        third_gain, cot, halo_cot, conv_two, hidden, avg_two, second_gain,
        second_bias, (grad_qkv_proj, grad_proj_in) if halving else (), (), width, bands,
    )
    if halving:
        early, back_two = lax.optimization_barrier((early, back_two))
        early = sum_groups(early, 1, groups)
    *folded, moved, back_one, first_sums, hidden_sums, grad_conv_one = conv_backward(
        place, sides, moved, halo_moved, hidden, halo_hidden, avg_two, back_two, second_gain,
        None, None, conv_one, field, avg_one, first_gain, first_bias,
        (grad_conv_two,) if halving else (), folded, width, bands,
    )
    if halving:
        early, back_one = lax.optimization_barrier((early, back_one))
    grad_images, output = finish(
        place, sides, grad_residual, moved, field, avg_one, back_one, first_gain, output, width
    )
    grad_images = grad_images.reshape(images.shape)

    def own(whole, axis=0):
        size = whole.shape[axis] // bands
        return lax.dynamic_slice_in_dim(whole, me * size, size, axis)

    def reduced(part):
        part = lax.psum_scatter(part, "rows", scatter_dimension=0, tiled=True)
        return lax.psum(part, "heads").astype(F32)

    used = 2 * image_count
    pieces = feed_pieces(channels, geglu_proj.shape[1], feed_out.shape[0], bands)
    own_value, own_context = own(value.astype(F32), 1), own(context, 1)
    own_embed, own_cross = own(embed.astype(F32), 1), own(cross_value)
    hot = hot.astype(F32)
    if halving:
        grad_images, first_sums = lax.optimization_barrier((grad_images, first_sums))
        rows_two, rows_qkv, rows_in = folded
        rows_one, rows_two, table, other = reduce_parts(
            grad_conv_one, (rows_two,), early, bands, groups,
            (cross_sum, hidden_sums, first_sums, second_sums, third_sums, residual_sums, leave_sums, feed_sums,
             pair_sums),
        )
        late = (rows_two, rows_one, rows_qkv, rows_in)
        odd = lax.rem(lax.axis_index("heads"), 2).astype(jnp.int32).reshape(1)
        (
            rows_conv_two, rows_conv_one, rows_qkv, rows_proj_in, rows_geglu, rows_feed, rows_proj_out,
            rows_attn_out, grad_class_table, grad_cross_value, grad_cross_out, grad_time_proj,
        ) = finals(
            odd, late, early, other, table, own_value, own_context, hot, own_embed, cross_out, own_cross,
            pieces,
        )
    else:
        table = jnp.concatenate(
            [
                cross_sum[:image_count],
                hidden_sums[:image_count],
                jnp.stack(
                    [
                        jnp.sum(first_sums[1:used:2], axis=0),
                        jnp.sum(first_sums[0:used:2], axis=0),
                        jnp.sum(second_sums[1:used:2], axis=0),
                        jnp.sum(second_sums[0:used:2], axis=0),
                        jnp.sum(third_sums[1:used:2], axis=0),
                        jnp.sum(third_sums[0:used:2], axis=0),
                        jnp.sum(residual_sums[:image_count], axis=0),
                    ]
                ),
                leave_sums[:3],
                feed_sums[:4],
                pair_sums.reshape(-1, channels),
            ]
        )
        table = jnp.pad(table, ((0, -table.shape[0] % 8), (0, 0)))
        table = lax.all_gather(lax.psum(table, "rows"), "heads")
        rows_conv_two, rows_qkv, rows_proj_in, rows_conv_one = (
            reduced(part) for part in (grad_conv_two, grad_qkv_proj, grad_proj_in, grad_conv_one)
        )
        keys_values = rows_qkv[:, : 2 * channels].reshape(-1, HEADS, 2, head_dim)
        rows_qkv = jnp.concatenate(
            [
                rows_qkv[:, 2 * channels :],
                keys_values[:, :, 0].reshape(-1, channels),
                keys_values[:, :, 1].reshape(-1, channels),
            ],
            axis=1,
        )
        early = early.astype(F32)
        rows_geglu = jnp.concatenate([early[first : first + size] for first, size in pieces[0]], axis=1)
        rows_feed, rows_proj_out, rows_attn_out = (
            early[first : first + size] for ((first, size),) in pieces[1:]
        )
    all_cross = table[:, :image_count].reshape(-1, channels)
    all_shift = table[:, image_count : 2 * image_count].reshape(-1, channels)
    if not halving:
        grad_cross_out = jnp.dot(own_value.T, all_cross, precision=HIGH)
        grad_value = jnp.dot(all_cross, cross_out.astype(F32).T, precision=HIGH)
        grad_cross_value = jnp.dot(own_context.T, grad_value, precision=HIGH)
        grad_context = jnp.dot(grad_value, own_cross.astype(F32).T, precision=HIGH)
        grad_class_table = jnp.dot(hot.T, grad_context, precision=HIGH)
        grad_time_proj = jnp.dot(own_embed.T, all_shift, precision=HIGH)
    joint = jnp.concatenate(
        [jnp.sum(table[:, 2 * image_count :], axis=0), jnp.sum(all_cross, axis=0)[None],
         jnp.sum(all_shift, axis=0)[None]]
    )
    mine = own(joint, 1)
    singles = [mine[at] for at in range(14)]
    grad_geglu_bias = own(joint[14 : 14 + geglu_bias.shape[0] // channels].reshape(-1))
    return (
        output.reshape(images.shape),
        grad_images,
        singles[0],
        singles[1],
        rows_conv_one,
        grad_time_proj,
        mine[-1],
        singles[2],
        singles[3],
        rows_conv_two,
        singles[6],
        singles[4],
        singles[5],
        rows_proj_in,
        singles[9],
        singles[7],
        singles[8],
        rows_qkv,
        rows_attn_out,
        mine[-2],
        grad_class_table,
        grad_cross_value,
        grad_cross_out,
        singles[12],
        singles[13],
        rows_geglu,
        grad_geglu_bias,
        rows_feed,
        singles[11],
        rows_proj_out,
        singles[10],
    )


def solution(mesh):
    return jax.shard_map(
        per_device,
        mesh=mesh,
        in_specs=(
            P("heads", "rows", None, None),
            P(),
            P(),
            P(),
            P("heads", "rows", None, None),
            P(),
            P(),
            P(),
            P(),
            P(),
            P(),
            P(),
            P(),
            P(),
            P(),
            P(),
            P(),
            P(),
            P(),
            P(),
            P(),
            P(),
            P(),
            P(),
            P(),
            P(),
            P(),
            P(),
            P(),
            P(),
            P(),
            P(),
            P(),
            P(),
        ),
        out_specs=(
            P("heads", "rows", None, None),
            P("heads", "rows", None, None),
            P("rows"),
            P("rows"),
            P("rows", None),
            P("rows", None),
            P("rows"),
            P("rows"),
            P("rows"),
            P("rows", None),
            P("rows"),
            P("rows"),
            P("rows"),
            P("rows", None),
            P("rows"),
            P("rows"),
            P("rows"),
            P("rows", None),
            P("rows", None),
            P("rows"),
            P(None, "rows"),
            P("rows", None),
            P("rows", None),
            P("rows"),
            P("rows"),
            P("rows", None),
            P("rows"),
            P("rows", None),
            P("rows"),
            P("rows", None),
            P("rows"),
        ),
        check_vma=False,
    )
```

```python
from functools import partial
import math

import jax
import jax.numpy as jnp
from jax import lax
from jax.experimental import pallas as pl
from jax.experimental.pallas import tpu as pltpu
from jax.sharding import PartitionSpec as P

HEADS = 8
GROUPS = 32
GN_EPS = 1e-06
LN_EPS = 1e-05
HIGH = lax.Precision.HIGHEST
LOG2E = math.log2(math.e)
BF = jnp.bfloat16
F32 = jnp.float32
KEPT = 256
APART = 80

def dot_nt(lhs, rhs):
    return lax.dot_general(lhs, rhs, (((1,), (1,)), ((), ())), preferred_element_type=F32)


def dot_nn(lhs, rhs):
    return lax.dot_general(lhs, rhs, (((1,), (0,)), ((), ())), preferred_element_type=F32)


def lane_ids(rows):
    return lax.broadcasted_iota(jnp.int32, (rows, 128), 1)


def swap_halves(field):
    return pltpu.roll(field, 64, 1)


def pieces_of(column):
    top = column.astype(BF).astype(F32)
    rest = column - top
    mid = rest.astype(BF).astype(F32)
    return (top, mid, rest - mid)


def extras(column, lanes, first):
    top, mid, low = pieces_of(column)
    return jnp.where(
        lanes == first, top, jnp.where(lanes == first + 1, mid, jnp.where(lanes == first + 2, low, 0.0))
    )


def block_of(count, pref):
    for size in pref:
        if count % size == 0:
            return size
    return count


def crop(field, width, side):
    rows = field.shape[0] // width
    if side == width:
        return field
    return field.reshape(rows, width, 128)[:, :side].reshape(rows * side, 128)


def uncrop(field, width, side):
    if side == width:
        return field
    rows = field.shape[0] // side
    spread = field.reshape(rows, side, 128)
    return jnp.concatenate(
        [spread, jnp.zeros((rows, width - side, 128), field.dtype)], axis=1
    ).reshape(rows * width, 128)


def unpack_pairs(pairs):
    return jnp.concatenate([pairs, swap_halves(pairs)], axis=0)


def pack_pairs(field, lanes):
    half = field.shape[0] // 2
    return jnp.where(lanes[:half] < 64, field[:half], swap_halves(field[half:]))


def attend_kernel(width, scale, side_ref, qkv_ref, out_ref, norm_ref, kept_ref, q_s, k_s, v_s, vt_s, top_s, stage_s, sems):
    bands, packed, _ = qkv_ref.shape
    band_tokens = packed * 2 // 3
    band_rows = band_tokens // width
    side_now = side_ref[0]

    def variant(side):
        tokens = side * side
        used = side // band_rows
        own = band_rows * side
        lanes = lane_ids(own)
        low = lanes < 64
        row_ids = lax.broadcasted_iota(jnp.int32, (128, 128), 0)
        col_ids = lax.broadcasted_iota(jnp.int32, (128, 128), 1)
        picks = jnp.where((row_ids < 64) == (col_ids < 64), 1.0, 0.0).astype(BF)

        def gather_band(band, norms):
            pairs = crop(qkv_ref[band, band_tokens:, :].astype(F32), width, side)
            keys = crop(qkv_ref[band, :band_tokens, :].astype(F32), width, side)
            queries = unpack_pairs(pairs) * (scale * LOG2E)
            head = queries.astype(BF).astype(F32)
            turned = swap_halves(keys)
            rows = pl.ds(pl.multiple_of(band * own, 16), own)
            q_s[rows, :] = jnp.where(low, head, swap_halves(queries - head)).astype(BF)
            k_s[rows, :] = jnp.where(low, keys, turned).astype(BF)
            v_s[rows, :] = jnp.where(low, turned, jnp.where(lanes == 64, 1.0, 0.0)).astype(BF)
            joint = jnp.where(low, queries, turned)
            sums = dot_nn((joint * joint).astype(BF), picks)
            return jnp.maximum(norms, jnp.max(sums, axis=0, keepdims=True))

        norms = lax.fori_loop(0, used, gather_band, jnp.zeros((1, 128), F32))
        step = block_of(tokens, (512, 256))
        for first in range(0, tokens, step):
            vt_s[:, first : first + step] = v_s[first : first + step, :].T
        first_lanes = lane_ids(1) < 64
        query_top = jnp.max(jnp.where(first_lanes, norms, 0.0))
        key_top = jnp.max(jnp.where(first_lanes, 0.0, norms))
        safe = query_top * key_top * 1.05 <= 100.0 * 100.0
        bq = block_of(tokens, (1024, 768, 256))
        bk = block_of(tokens, (1024, 768, 256))

        @pl.when(safe)
        def _():
            top_s[...] = jnp.zeros_like(top_s)

        @pl.when(jnp.logical_not(safe))
        def _():
            def tops(qi, _):
                cols = pl.ds(pl.multiple_of(qi * bq, 256), bq)
                queries = q_s[cols, :]

                def more(ki, top):
                    scores = dot_nt(k_s[pl.ds(pl.multiple_of(ki * bk, 256), bk), :], queries)
                    return jnp.maximum(top, jnp.max(scores, axis=0, keepdims=True))

                top = lax.fori_loop(0, tokens // bk, more, jnp.full((1, bq), -jnp.inf, F32))
                top_s[:, cols] = jnp.broadcast_to(top, (8, bq))
                return 0

            lax.fori_loop(0, tokens // bq, tops, 0)

        parts = bq // KEPT
        steps = tokens // bq
        slots = min(steps, stage_s.shape[0] // tokens, 3)

        def stores(qi, first=0, rows=tokens):
            slot = lax.rem(qi, slots)
            return [
                pltpu.make_async_copy(
                    stage_s.at[pl.ds(pl.multiple_of(slot * tokens + first, 128), rows), pl.ds(part * KEPT, KEPT)],
                    kept_ref.at[pl.ds(pl.multiple_of((qi * parts + part) * (tokens + APART) + first, 16), rows)],
                    sems.at[slot, part],
                )
                for part in range(parts)
            ]

        def main(qi, _):
            cols = pl.ds(pl.multiple_of(qi * bq, 256), bq)
            queries = q_s[cols, :]
            top = top_s[0:1, cols]
            slot = lax.rem(qi, slots)

            @pl.when(qi >= slots)
            def _():
                for item in stores(qi - slots):
                    item.wait()

            total = jnp.zeros((80, bq), F32)
            for first in range(0, tokens, bk):
                scores = dot_nt(k_s[first : first + bk, :], queries)
                weights = jnp.exp2(scores - top).astype(BF)
                stage_s[pl.ds(pl.multiple_of(slot * tokens + first, 128), bk), :bq] = weights
                total = total + dot_nn(vt_s[0:80, first : first + bk], weights)
                for item in stores(qi, first, bk):
                    item.start()
            row_total = total[64:65]
            mixed = total[:64] / row_total
            extra = jnp.broadcast_to(1.0 / row_total, (64, bq))
            norm_ref[cols, :] = jnp.concatenate([mixed, extra], axis=0).T
            return 0

        lax.fori_loop(0, steps, main, 0)
        for qi in range(steps - slots, steps):
            for item in stores(qi):
                item.wait()

        def spread_band(band, _):
            rows = pl.ds(pl.multiple_of(band * own, 16), own)
            pairs = pack_pairs(norm_ref[rows, :], lanes)
            out_ref[band] = uncrop(pairs, width, side).astype(BF)
            return 0

        lax.fori_loop(0, used, spread_band, 0)
        if used < bands:
            out_ref[used:] = jnp.zeros((bands - used,) + out_ref.shape[1:], BF)

    for side in (width, width * 3 // 4, width // 2):
        pl.when(side_now == side)(partial(variant, side))


def attend(side, qkv, width, scale):
    bands, packed, _ = qkv.shape
    tokens = bands * packed * 2 // 3
    vm = pl.BlockSpec(memory_space=pltpu.VMEM)
    return pl.pallas_call(
        partial(attend_kernel, width, scale),
        out_shape=(
            jax.ShapeDtypeStruct((bands, packed // 3, 128), BF),
            jax.ShapeDtypeStruct((tokens, 128), F32),
            jax.ShapeDtypeStruct((tokens // KEPT * (tokens + APART), KEPT), BF),
        ),
        in_specs=[pl.BlockSpec(memory_space=pltpu.SMEM), vm],
        out_specs=(vm, vm, pl.BlockSpec(memory_space=pl.ANY)),
        scratch_shapes=[
            pltpu.VMEM((tokens, 128), BF),
            pltpu.VMEM((tokens, 128), BF),
            pltpu.VMEM((tokens, 128), BF),
            pltpu.VMEM((128, tokens), BF),
            pltpu.VMEM((8, tokens), F32),
            pltpu.VMEM((2 * tokens, 1024), BF),
            pltpu.SemaphoreType.DMA((3, 4)),
        ],
        compiler_params=pltpu.CompilerParams(vmem_limit_bytes=62 << 20),
        cost_estimate=pl.CostEstimate(
            flops=4 * 256 * tokens * tokens, bytes_accessed=8 << 20, transcendentals=tokens * tokens
        ),
        name="attend",
    )(side, qkv)


def attend_back_kernel(width, scale, side_ref, qkv_ref, grad_ref, norm_ref, kept_ref, out_ref,
                       k_s, g_s, gn_s, v_s, q_s, kt_s, dq_s, dkv_s, recip_s, stage_s, sems):
    bands, packed, _ = qkv_ref.shape
    band_tokens = packed * 2 // 3
    band_rows = band_tokens // width
    side_now = side_ref[0]

    def variant(side):
        tokens = side * side
        used = side // band_rows
        own = band_rows * side
        lanes = lane_ids(own)
        low = lanes < 64
        ones_high = jnp.where((lanes >= 64) & (lanes < 67), 1.0, 0.0)
        bq = block_of(tokens, (1024, 768, 256))
        bk = block_of(tokens, (512, 768, 256))
        parts = bq // KEPT
        steps = tokens // bq
        slots = min(steps, stage_s.shape[0] // tokens, 3)

        def loads(qi):
            slot = lax.rem(qi, slots)
            return [
                pltpu.make_async_copy(
                    kept_ref.at[pl.ds(pl.multiple_of((qi * parts + part) * (tokens + APART), 16), tokens)],
                    stage_s.at[pl.ds(pl.multiple_of(slot * tokens, 128), tokens), pl.ds(part * KEPT, KEPT)],
                    sems.at[slot, part],
                )
                for part in range(parts)
            ]

        ahead = steps if slots == steps else slots - 1
        for qi in range(ahead):
            for item in loads(qi):
                item.start()

        def gather_band(band, _):
            queries = unpack_pairs(crop(qkv_ref[band, band_tokens:, :].astype(F32), width, side))
            keys = crop(qkv_ref[band, :band_tokens, :].astype(F32), width, side)
            grads = unpack_pairs(crop(grad_ref[0, band].astype(F32), width, side))
            rows = pl.ds(pl.multiple_of(band * own, 16), own)
            mixed = norm_ref[rows, :]
            delta = jnp.sum(jnp.where(low, grads * mixed, 0.0), axis=1, keepdims=True)
            turned = swap_halves(keys)
            q_s[rows, :] = jnp.where(low, 0.0, swap_halves(queries)).astype(BF)
            gn_s[rows, :] = jnp.where(low, grads, 0.0).astype(BF)
            g_s[rows, :] = jnp.where(low, grads, extras(-delta, lanes, 64)).astype(BF)
            v_s[rows, :] = jnp.where(low, turned, ones_high).astype(BF)
            k_s[rows, :] = jnp.where(low, keys, 0.0).astype(BF)
            return 0

        lax.fori_loop(0, used, gather_band, 0)
        step = block_of(tokens, (512, 256))
        for first in range(0, tokens, step):
            kt_s[:, first : first + step] = k_s[first : first + step, :].T[:64]
            recip_s[:, first : first + step] = norm_ref[first : first + step, :].T[64:72]
        dkv_s[...] = jnp.zeros_like(dkv_s)

        def main(qi, _):
            cols = pl.ds(pl.multiple_of(qi * bq, 256), bq)
            slot = lax.rem(qi, slots)
            for item in loads(qi):
                item.wait()

            @pl.when(qi + ahead < steps)
            def _():
                for item in loads(qi + ahead):
                    item.start()

            grads = g_s[cols, :]
            plain = gn_s[cols, :]
            queries = q_s[cols, :]
            recip = recip_s[0:1, cols]
            total = jnp.zeros((64, bq), F32)
            for first in range(0, tokens, bk):
                lines = pl.ds(pl.multiple_of(slot * tokens + first, 128), bk)
                probs = stage_s[lines, :bq].astype(F32) * recip
                slopes = dot_nt(v_s[first : first + bk, :], grads)
                grad_scores = (probs * slopes).astype(BF)
                dkv_s[first : first + bk, :] += dot_nn(probs.astype(BF), plain) + dot_nn(grad_scores, queries)
                total = total + dot_nn(kt_s[:, first : first + bk], grad_scores)
            dq_s[:, cols] = total
            return 0

        lax.fori_loop(0, steps, main, 0)
        for first in range(0, tokens, step):
            turned = dq_s[:, first : first + step]
            v_s[first : first + step, :] = (
                jnp.concatenate([turned, turned], axis=0).T * scale
            ).astype(BF)

        def spread_band(band, _):
            rows = pl.ds(pl.multiple_of(band * own, 16), own)
            joint = swap_halves(dkv_s[rows, :])
            out_ref[band, :band_tokens] = uncrop(jnp.where(low, joint * scale, joint), width, side).astype(BF)
            pairs = pack_pairs(v_s[rows, :].astype(F32), lanes)
            out_ref[band, band_tokens:] = uncrop(pairs, width, side).astype(BF)
            return 0

        lax.fori_loop(0, used, spread_band, 0)
        if used < bands:
            out_ref[used:] = jnp.zeros((bands - used,) + out_ref.shape[1:], BF)

    for side in (width, width * 3 // 4, width // 2):
        pl.when(side_now == side)(partial(variant, side))


def attend_back(side, qkv, grads, spot, norms, kept, width, scale):
    bands, packed, _ = qkv.shape
    tokens = bands * packed * 2 // 3
    vm = pl.BlockSpec(memory_space=pltpu.VMEM)
    rows = pltpu.VMEM((tokens, 128), BF)
    return pl.pallas_call(
        partial(attend_back_kernel, width, scale),
        out_shape=jax.ShapeDtypeStruct((bands, packed, 128), BF),
        grid=(1,),
        in_specs=[
            pl.BlockSpec(memory_space=pltpu.SMEM),
            vm,
            pl.BlockSpec((1,) + grads.shape[1:], lambda at: (spot, 0, 0, 0)),
            vm,
            pl.BlockSpec(memory_space=pl.ANY),
        ],
        out_specs=vm,
        scratch_shapes=[rows] * 5
        + [
            pltpu.VMEM((64, tokens), BF),
            pltpu.VMEM((64, tokens), F32),
            pltpu.VMEM((tokens, 128), F32),
            pltpu.VMEM((8, tokens), F32),
            pltpu.VMEM((2 * tokens, 1024), BF),
            pltpu.SemaphoreType.DMA((3, 4)),
        ],
        compiler_params=pltpu.CompilerParams(vmem_limit_bytes=62 << 20),
        cost_estimate=pl.CostEstimate(
            flops=8 * 256 * tokens * tokens, bytes_accessed=40 << 20, transcendentals=0
        ),
        name="attend_back",
    )(side, qkv, grads, norms, kept)


def dot_tn(lhs, rhs):
    return lax.dot_general(lhs, rhs, (((0,), (0,)), ((), ())), preferred_element_type=F32)


def row_of(table, at):
    ids = lax.broadcasted_iota(jnp.int32, table.shape, 0)
    return jnp.sum(jnp.where(ids == at, table, 0.0), axis=0, keepdims=True)


def put_row(table_ref, at, row):
    ids = lax.broadcasted_iota(jnp.int32, table_ref.shape, 0)
    table_ref[...] = jnp.where(ids == at, row, table_ref[...])


def col_sum(field):
    return jnp.sum(field, axis=0, keepdims=True)


def vec(ref):
    return ref[...].astype(F32).reshape(1, -1)


def spread_lanes(tile, channels):
    return jnp.concatenate([tile] * (channels // 128), axis=1)


def token_ids(shape):
    return lax.broadcasted_iota(jnp.int32, (shape[0], 128), 0)


def pixel_inside(shape, first_row, side, width):
    token = token_ids(shape)
    row = first_row + lax.shift_right_logical(token, int(math.log2(width)))
    return spread_lanes((row >= 0) & (row < side) & ((token & (width - 1)) < side), shape[1])


def sigmoid(field):
    return 0.5 * jnp.tanh(0.5 * field) + 0.5


def moments(avg_ref, at):
    table = avg_ref[...]
    mean = row_of(table, 2 * at)
    return mean, lax.rsqrt(row_of(table, 2 * at + 1) - mean * mean + GN_EPS)


def put_taps(taps_s, first, field, width, flipped):
    channels = field.shape[1]
    column = token_ids(field.shape) & (width - 1)
    count = field.shape[0]
    left = jnp.where(spread_lanes(column == 0, channels), 0.0, pltpu.roll(field, 1, 0))
    right = jnp.where(spread_lanes(column == width - 1, channels), 0.0, pltpu.roll(field, count - 1, 0))
    order = (right, field, left) if flipped else (left, field, right)
    for at, part in enumerate(order):
        taps_s[first : first + count, at * channels : (at + 1) * channels] = part.astype(BF)


VMEM_WHOLE = pl.BlockSpec(memory_space=pltpu.VMEM)
SMEM_WHOLE = pl.BlockSpec(memory_space=pltpu.SMEM)


def image_block(tokens, channels):
    return pl.BlockSpec((1, tokens, channels), lambda at: (at, 0, 0))


def edge_block(width, channels):
    return pl.BlockSpec((2, 1, width, channels), lambda at: (0, at, 0, 0))


def table_block(channels, rows=8):
    return pl.BlockSpec((rows, channels), lambda at: (0, 0))


def vector_block(channels):
    return pl.BlockSpec((channels,), lambda at: (0,))


def fixed_block(shape):
    return pl.BlockSpec(shape, lambda at: (0,) * len(shape), pipeline_mode=pl.Buffered(1))


def greet_rows(me, bands):
    barrier = pltpu.get_barrier_semaphore()
    for away in range(1, bands):
        pl.semaphore_signal(
            barrier, inc=1, device_id={"rows": lax.rem(me + away, bands)},
            device_id_type=pl.DeviceIdType.MESH,
        )


def meet_rows(bands):
    pl.semaphore_wait(pltpu.get_barrier_semaphore(), bands - 1)


def row_copy(src, dst, send, recv, target):
    return pltpu.make_async_remote_copy(
        src_ref=src, dst_ref=dst, send_sem=send, recv_sem=recv, device_id={"rows": target},
        device_id_type=pl.DeviceIdType.MESH,
    )


def edge_copies(top, bottom, halo, at, send, recv, me, bands):
    return [
        row_copy(top, halo.at[1, at], send.at[0, at], recv.at[1, at], lax.rem(me + bands - 1, bands)),
        row_copy(bottom, halo.at[0, at], send.at[1, at], recv.at[0, at], lax.rem(me + 1, bands)),
    ]


def group_average(sums, weight_ref, sides, slots, send, recv, me, bands):
    slots[me] = sums
    copies = [
        row_copy(slots.at[me], slots.at[me], send.at[away], recv.at[me], lax.rem(me + away, bands))
        for away in range(1, bands)
    ]
    for item in copies:
        item.start()
    for away in range(1, bands):
        source = lax.rem(me + away, bands)
        row_copy(slots.at[source], slots.at[source], send.at[away], recv.at[source], source).wait_recv()
    total = slots[0]
    for at in range(1, bands):
        total = total + slots[at]
    for item in copies:
        item.wait_send()
    if weight_ref is not None:
        total = total * vec(weight_ref)
    image = lax.shift_right_logical(lax.broadcasted_iota(jnp.int32, total.shape, 0), 1)
    side = jnp.ones(total.shape, jnp.int32)
    for at in range(sides.shape[0]):
        side = jnp.where(image == at, sides[at], side)
    side = side.astype(F32)
    channels = total.shape[1]
    size = channels // GROUPS
    lane = lax.broadcasted_iota(jnp.int32, total.shape, 1)
    step = 1
    while step < size:
        total = total + jnp.where(
            (lane & step) == 0, pltpu.roll(total, channels - step, 1), pltpu.roll(total, step, 1)
        )
        step *= 2
    return total / (side * side * size)


def exchange_scratch(images, width, channels, bands):
    return [
        pltpu.VMEM((2, images, width, channels), BF),
        pltpu.VMEM((bands, 8, channels), F32),
        pltpu.SemaphoreType.DMA((2, images)),
        pltpu.SemaphoreType.DMA((2, images)),
        pltpu.SemaphoreType.DMA((bands,)),
        pltpu.SemaphoreType.DMA((bands,)),
    ]


def share_edges(grads, at, width, halo_ref, scratch, me, bands, met=False):
    edge_s, _, send, recv = scratch[:4]
    tokens = grads.shape[0]
    edge_s[0, at] = grads[:width].astype(BF)
    edge_s[1, at] = grads[tokens - width :].astype(BF)
    if not met:
        pl.when(at == 0)(partial(meet_rows, bands))
    for item in edge_copies(edge_s.at[0, at], edge_s.at[1, at], halo_ref, at, send, recv, me, bands):
        item.start()


def close_exchange(sums, weight_ref, sides, avg_ref, halo_ref, scratch, me, bands):
    edge_s, slots, send, recv, sum_send, sum_recv = scratch
    avg_ref[...] = group_average(sums, weight_ref, sides, slots, sum_send, sum_recv, me, bands)
    for at in range(edge_s.shape[1]):
        for item in edge_copies(
            edge_s.at[0, at], edge_s.at[1, at], halo_ref, at, send, recv, me, bands
        ):
            item.wait_send()
        for end in range(2):
            edge = halo_ref.at[end, at]
            row_copy(
                edge, edge, send.at[end, at], recv.at[end, at], lax.rem(me + 1, bands)
            ).wait_recv()


def begin_kernel(width, bands, place, sides, field_ref, whole_ref, avg_ref, halo_ref, sums_s, slots, send, recv, sum_send, sum_recv):
    at = pl.program_id(0)
    last = pl.num_programs(0) - 1
    me = lax.axis_index("rows")
    images, tokens, _ = whole_ref.shape

    def edges():
        return [
            edge_copies(
                whole_ref.at[image, pl.ds(0, width)], whole_ref.at[image, pl.ds(tokens - width, width)],
                halo_ref, image, send, recv, me, bands,
            )
            for image in range(images)
        ]

    @pl.when(at == 0)
    def _():
        greet_rows(me, bands)
        sums_s[...] = jnp.zeros_like(sums_s)

    @pl.when(at == 1)
    def _():
        meet_rows(bands)
        for pair in edges():
            for item in pair:
                item.start()

    field = field_ref[0].astype(F32)
    field = jnp.where(pixel_inside(field.shape, place[0], sides[at], width), field, 0.0)
    put_row(sums_s, 2 * at, col_sum(field))
    put_row(sums_s, 2 * at + 1, col_sum(field * field))

    @pl.when(at == last)
    def _():
        avg_ref[...] = group_average(
            sums_s[...], None, sides, slots, sum_send, sum_recv, me, bands
        )
        for image, pair in enumerate(edges()):
            for item in pair:
                item.wait_send()
            for end in range(2):
                edge = halo_ref.at[end, image]
                row_copy(
                    edge, edge, send.at[end, image], recv.at[end, image], lax.rem(me + 1, bands)
                ).wait_recv()


def begin(place, sides, field, width, bands):
    images, tokens, channels = field.shape
    anywhere = pl.BlockSpec(memory_space=pl.ANY)
    return pl.pallas_call(
        partial(begin_kernel, width, bands),
        grid=(images,),
        out_shape=(
            jax.ShapeDtypeStruct((8, channels), F32),
            jax.ShapeDtypeStruct((2, images, width, channels), BF),
        ),
        in_specs=[
            SMEM_WHOLE,
            SMEM_WHOLE,
            image_block(tokens, channels),
            anywhere,
        ],
        out_specs=(table_block(channels), anywhere),
        scratch_shapes=[pltpu.VMEM((8, channels), F32)]
        + exchange_scratch(images, width, channels, bands)[1:],
        compiler_params=pltpu.CompilerParams(collective_id=1, has_side_effects=True),
        name="begin",
    )(place, sides, field, field)


def conv_forward_kernel(width, bands, base_given, *refs):
    place, sides, field_ref, halo_ref, avg_ref, gain_ref, bias_ref, weight_ref, shift_ref = refs[:9]
    refs = refs[9:]
    if base_given:
        base_ref, refs = refs[0], refs[1:]
    out_ref, next_avg, next_halo = refs[:3]
    refs = refs[3:]
    taps_s, stats_ref = refs[:2]
    scratch = refs[2:]
    me = lax.axis_index("rows")
    at = pl.program_id(0)
    last = pl.num_programs(0) - 1

    @pl.when(at == 0)
    def _():
        greet_rows(me, bands)
        stats_ref[...] = jnp.zeros_like(stats_ref)

    _, tokens, channels = field_ref.shape
    first_row = place[0]
    side = sides[at]
    mean, inv_std = moments(avg_ref, at)
    slope = inv_std * vec(gain_ref)
    offset = vec(bias_ref) - mean * slope

    def active(field, row):
        normed = field.astype(F32) * slope + offset
        inside = pixel_inside(normed.shape, row, side, width)
        return jnp.where(inside, normed * sigmoid(normed), 0.0)

    rows = tokens // width
    put_taps(taps_s, 0, active(halo_ref[0, 0], first_row - 1), width, False)
    put_taps(taps_s, width, active(field_ref[0], first_row), width, False)
    put_taps(taps_s, width + tokens, active(halo_ref[1, 0], first_row + rows), width, False)
    deep = 3 * channels
    total = dot_nn(taps_s[:tokens], weight_ref[:deep])
    for tap in (1, 2):
        total = total + dot_nn(
            taps_s[tap * width : tap * width + tokens], weight_ref[tap * deep : (tap + 1) * deep]
        )
    total = total + row_of(shift_ref[...], at)
    inside = pixel_inside(total.shape, first_row, side, width)
    if base_given:
        total = total + jnp.where(inside, base_ref[0].astype(F32), 0.0)
    out_ref[0] = total
    share_edges(total, at, width, next_halo, scratch, me, bands)
    masked = jnp.where(inside, total, 0.0)
    put_row(stats_ref, 2 * at, col_sum(masked))
    put_row(stats_ref, 2 * at + 1, col_sum(masked * masked))

    @pl.when(at == last)
    def _():
        close_exchange(stats_ref[...], None, sides, next_avg, next_halo, scratch, me, bands)


def conv_forward(place, sides, field, halo, avg, gain, bias, weight, shift, base, width, bands):
    images, tokens, channels = field.shape
    added = base is not None
    tok = image_block(tokens, channels)
    return pl.pallas_call(
        partial(conv_forward_kernel, width, bands, added),
        grid=(images,),
        out_shape=(
            jax.ShapeDtypeStruct(field.shape, F32),
            jax.ShapeDtypeStruct((8, channels), F32),
            jax.ShapeDtypeStruct((2, images, width, channels), BF),
        ),
        in_specs=[
            SMEM_WHOLE,
            SMEM_WHOLE,
            tok,
            edge_block(width, channels),
            table_block(channels),
            vector_block(channels),
            vector_block(channels),
            fixed_block(weight.shape),
            table_block(channels),
        ]
        + ([tok] if added else []),
        out_specs=(tok, table_block(channels), pl.BlockSpec(memory_space=pl.ANY)),
        scratch_shapes=[
            pltpu.VMEM((tokens + 2 * width, 3 * channels), BF),
            pltpu.VMEM((8, channels), F32),
        ]
        + exchange_scratch(images, width, channels, bands),
        compiler_params=pltpu.CompilerParams(
            vmem_limit_bytes=62 << 20, collective_id=2 if added else 3, has_side_effects=True
        ),
        name="conv_forward",
    )(place, sides, field, halo, avg, gain, bias, weight, shift, *([base] if added else []))


class BandFold:
    def __init__(self, parts, scratch, me):
        self.parts, self.me = parts, me
        count = len(parts)
        self.own, self.pair, self.first, self.second_s = (
            scratch[at * count : (at + 1) * count] for at in range(4)
        )
        self.load, self.pair_send, self.pair_recv, self.hop_send, self.hop_recv = scratch[4 * count :]
        self.core, self.chip = lax.rem(me, 2), me // 2
        self.chunks = fold_chunks([part.shape for part in parts])

    def loads(self, which):
        size = self.parts[which].shape[0] // 8
        return [
            pltpu.make_async_copy(
                self.parts[which].at[pl.ds(pl.multiple_of((2 * spot + self.core) * size, 16), size)],
                self.own[which].at[spot],
                self.load.at[which, spot],
            )
            for spot in range(4)
        ]

    def pairs(self, which):
        size = self.parts[which].shape[0] // 8
        return [
            row_copy(
                self.parts[which].at[pl.ds(pl.multiple_of((2 * spot + 1 - self.core) * size, 16), size)],
                self.pair[which].at[spot],
                self.pair_send.at[which, spot],
                self.pair_recv.at[which, spot],
                self.me + 1 - 2 * self.core,
            )
            for spot in range(4)
        ]

    def hops(self, at):
        which, first, wide, one, two = self.chunks[at]
        cols = pl.ds(first, wide)
        near, far = jnp.bitwise_xor(self.chip, one), jnp.bitwise_xor(self.chip, two)

        def hop(spot, dst, step, chip):
            return row_copy(
                self.own[which].at[spot, :, cols], dst, self.hop_send.at[at, step], self.hop_recv.at[at, step],
                2 * chip + self.core,
            )

        return [
            hop(near, self.first[which].at[0, :, cols], 0, near),
            hop(jnp.bitwise_xor(near, two), self.first[which].at[1, :, cols], 1, near),
            hop(far, self.second_s[which].at[:, cols], 2, far),
        ]

    def start(self):
        for which in range(len(self.parts)):
            for item in self.loads(which) + self.pairs(which):
                item.start()

    def spread(self):
        for which in range(len(self.parts)):
            for item in self.loads(which):
                item.wait()
            for item in self.pairs(which):
                item.wait_recv()
            for spot in range(4):
                self.own[which][spot] = self.own[which][spot] + self.pair[which][spot]
        for at in range(len(self.chunks)):
            for item in self.hops(at)[:2]:
                item.start()

    def second(self):
        for at, (which, first, wide, _, two) in enumerate(self.chunks):
            cols = pl.ds(first, wide)
            for step, item in enumerate(self.hops(at)[:2]):
                item.wait()
                spot = jnp.bitwise_xor(self.chip, two) if step else self.chip
                self.own[which][spot, :, cols] = (
                    self.own[which][spot, :, cols] + self.first[which][step, :, cols]
                )
            self.hops(at)[2].start()

    def finish(self, outs):
        for at, (which, first, wide, _, _) in enumerate(self.chunks):
            cols = pl.ds(first, wide)
            self.hops(at)[2].wait()
            outs[which][:, cols] = self.own[which][self.chip, :, cols] + self.second_s[which][:, cols]
        for which in range(len(self.parts)):
            for item in self.pairs(which):
                item.wait_send()


def fold_chunks(shapes):
    total = sum(rows * cols for rows, cols in shapes)
    rows, cols = shapes[0]
    wide = (total // 2 // rows + 64) // 128 * 128
    chunks = [(0, 0, wide, 1, 2), (0, wide, cols - wide, 2, 1)]
    return chunks + [(at, 0, shape[1], 2, 1) for at, shape in enumerate(shapes) if at]


def fold_scratch(shapes):
    def bufs(lead):
        return [pltpu.VMEM(lead + (rows // 8, cols), BF) for rows, cols in shapes]

    chunks = len(fold_chunks(shapes))
    return (
        bufs((4,)) + bufs((4,)) + bufs((2,)) + bufs(())
        + [pltpu.SemaphoreType.DMA((len(shapes), 4))] * 3
        + [pltpu.SemaphoreType.DMA((chunks, 3))] * 2
    )


class GroupTree:
    def __init__(self, fields, outs, scratch, group):
        self.fields, self.outs, self.group = fields, outs, group
        count = len(fields)
        self.near_s, self.far_s = scratch[:count], scratch[count : 2 * count]
        self.send, self.recv = scratch[2 * count :]
        self.odd = lax.rem(group, 2)

    def half(self, which, odd):
        size = self.fields[which].shape[0] // 2
        return pl.ds(pl.multiple_of(odd * size, 16), size)

    def copies(self, which, step):
        mine, theirs = self.half(which, self.odd), self.half(which, 1 - self.odd)
        out = self.outs[which].at[mine]
        src, dst, bit = (
            (self.fields[which].at[theirs], self.near_s[which], 1),
            (self.fields[which].at[mine], self.far_s[which], 2),
            (out, out, 1),
        )[step]
        return pltpu.make_async_remote_copy(
            src_ref=src, dst_ref=dst, send_sem=self.send.at[which, step], recv_sem=self.recv.at[which, step],
            device_id={"heads": jnp.bitwise_xor(self.group, bit)}, device_id_type=pl.DeviceIdType.MESH,
        )

    def near(self):
        for which in range(len(self.fields)):
            self.copies(which, 0).start()

    def far(self):
        for which in range(len(self.fields)):
            mine = self.half(which, self.odd)
            self.copies(which, 0).wait()
            self.fields[which][mine] = (
                self.fields[which][mine].astype(F32) + self.near_s[which][...].astype(F32)
            ).astype(BF)
            self.copies(which, 1).start()

    def back(self):
        for which in range(len(self.fields)):
            mine = self.half(which, self.odd)
            self.copies(which, 1).wait()
            self.outs[which][mine] = (
                self.fields[which][mine].astype(F32) + self.far_s[which][...].astype(F32)
            ).astype(BF)
            self.copies(which, 2).start()

    def end(self):
        for which in range(len(self.fields)):
            self.copies(which, 2).wait_send()
            theirs = self.outs[which].at[self.half(which, 1 - self.odd)]
            pltpu.make_async_remote_copy(
                src_ref=theirs, dst_ref=theirs, send_sem=self.send.at[which, 2],
                recv_sem=self.recv.at[which, 2], device_id={"heads": jnp.bitwise_xor(self.group, 1)},
                device_id_type=pl.DeviceIdType.MESH,
            ).wait_recv()


def tree_scratch(shapes):
    return [pltpu.VMEM((rows // 2, cols), BF) for rows, cols in shapes] * 2 + [
        pltpu.SemaphoreType.DMA((len(shapes), 3))
    ] * 2


def conv_backward_kernel(width, bands, added, late, summed, *refs):
    refs = list(refs)
    late_refs, refs = refs[:late], refs[late:]
    summed_refs, refs = refs[:summed], refs[summed:]
    me = lax.axis_index("rows")
    (place, sides, grad_ref, grad_halo, field_ref, field_halo, avg_ref, back_avg, gain_ref) = refs[:9]
    refs = refs[9:]
    if added:
        add_ref, add_halo = refs[:2]
        refs = refs[2:]
    (weight_ref, prior_ref, prior_avg, prior_gain, prior_bias) = refs[:5]
    refs = refs[5:]
    late_outs, refs = refs[:late], refs[late:]
    summed_outs, refs = refs[:summed], refs[summed:]
    if added:
        kept_ref = refs[0]
        refs = refs[1:]
    out_ref, next_avg, stats_ref, sums_ref, weight_grad = refs[:5]
    next_halo = None
    if added:
        next_halo = refs[5]
        refs = refs[1:]
    taps_s, act_s, total_s = refs[5:8]
    scratch = refs[8:]
    if late:
        base = 6 if added else 3
        after = base + 4 * late + 5
        fold = BandFold(late_refs, scratch[base:after], me)
        if summed:
            fields, made = scratch[after : after + summed], scratch[after + summed : after + 2 * summed]
            group = lax.axis_index("heads")
            tree = GroupTree(fields, made, scratch[after + 2 * summed :], group)
        scratch = scratch[:base]
    at = pl.program_id(0)
    last = pl.num_programs(0) - 1
    _, tokens, channels = grad_ref.shape
    first_row = place[0]
    side = sides[at]
    mean, inv_std = moments(avg_ref, at)
    back = back_avg[...]
    back_mean, back_cross = row_of(back, 2 * at), row_of(back, 2 * at + 1)
    gain = vec(gain_ref)
    grad_slope = inv_std * gain
    field_slope = inv_std * inv_std * back_cross
    offset = inv_std * back_mean - mean * field_slope

    def through(grads, field, extra, row):
        moved = grads.astype(F32) * grad_slope - field.astype(F32) * field_slope - offset
        if extra is not None:
            moved = moved + extra.astype(F32)
        return jnp.where(pixel_inside(moved.shape, row, side, width), moved, 0.0)

    rows = tokens // width
    own = through(grad_ref[0], field_ref[0], add_ref[0] if added else None, first_row)
    put_taps(taps_s, width, own, width, True)
    for end, row, first in ((0, first_row - 1, 0), (1, first_row + rows, width + tokens)):
        put_taps(
            taps_s,
            first,
            through(grad_halo[end, 0], field_halo[end, 0], add_halo[end, 0] if added else None, row),
            width,
            True,
        )
    if added:
        kept_ref[0] = own

    @pl.when(at == 0)
    def _():
        greet_rows(me, bands)
        stats_ref[...] = jnp.zeros_like(stats_ref)
        sums_ref[...] = jnp.zeros_like(sums_ref)
        if summed:
            for bit in (1, 2):
                pl.semaphore_signal(
                    pltpu.get_barrier_semaphore(), inc=1, device_id={"heads": jnp.bitwise_xor(group, bit)},
                    device_id_type=pl.DeviceIdType.MESH,
                )
            for field, ref in zip(fields, summed_refs):
                field[...] = ref[...]
        if late:
            meet_rows(bands + 2 if summed else bands)
            fold.start()
        if summed:
            tree.near()
        total_s[...] = jnp.zeros_like(total_s)

    put_row(sums_ref, at, col_sum(own))
    prior_mean, prior_std = moments(prior_avg, at)
    centred = (prior_ref[0].astype(F32) - prior_mean) * prior_std
    normed = centred * vec(prior_gain) + vec(prior_bias)
    gate = sigmoid(normed)
    inside = pixel_inside(normed.shape, first_row, side, width)
    act_s[...] = jnp.where(inside, normed * gate, 0.0).astype(BF).T
    act_t = act_s[...]
    moved = None
    for down in range(3):
        lines = pl.ds((2 - down) * width, tokens)
        for across in range(3):
            tap = 3 * down + across
            low = taps_s[lines, across * channels : (across + 1) * channels]
            part = slice(tap * channels, (tap + 1) * channels)
            term = dot_nt(low, weight_ref[part])
            moved = term if moved is None else moved + term
            total_s[part] += dot_nn(act_t, low)
    if late:
        pl.when(at == 0)(fold.spread)
        pl.when(at == 2)(fold.second)
    if summed:
        pl.when(at == 1)(tree.far)
        pl.when(at == 2)(tree.back)
    grads = jnp.where(inside, moved * (gate + normed * gate * (1.0 - gate)), 0.0)
    out_ref[0] = grads
    if added:
        share_edges(grads, at, width, next_halo, scratch, me, bands, late > 0)
    put_row(stats_ref, 2 * at, col_sum(grads))
    put_row(stats_ref, 2 * at + 1, col_sum(grads * centred))

    @pl.when(at == last)
    def _():
        if late:
            fold.finish(late_outs)
        if summed:
            tree.end()
            for out, field in zip(summed_outs, made):
                out[...] = field[...]
        if added:
            close_exchange(stats_ref[...], prior_gain, sides, next_avg, next_halo, scratch, me, bands)
        else:
            if not late:
                meet_rows(bands)
            next_avg[...] = group_average(stats_ref[...], prior_gain, sides, *scratch, me, bands)
        weight_grad[...] = total_s[...].astype(BF)


def conv_backward(place, sides, grads, grad_halo, field, field_halo, avg, back_avg, gain, extra,
                  extra_halo, weight, prior, prior_avg, prior_gain, prior_bias, late, summed, width, bands):
    images, tokens, channels = grads.shape
    added = extra is not None
    tok = image_block(tokens, channels)
    edge = edge_block(width, channels)
    table = table_block(channels)
    vector = vector_block(channels)
    anywhere = pl.BlockSpec(memory_space=pl.ANY)
    ins = [*late, *summed, place, sides, grads, grad_halo, field, field_halo, avg, back_avg, gain]
    specs = [anywhere] * len(late) + [fixed_block(part.shape) for part in summed] + [SMEM_WHOLE, SMEM_WHOLE, tok, edge, tok, edge, table, table, vector]
    if added:
        ins += [extra, extra_halo]
        specs += [tok, edge]
    ins += [weight, prior, prior_avg, prior_gain, prior_bias]
    specs += [fixed_block(weight.shape), tok, table, vector, vector]
    outs = [
        jax.ShapeDtypeStruct(grads.shape, F32),
        jax.ShapeDtypeStruct((8, channels), F32),
        jax.ShapeDtypeStruct((8, channels), F32),
        jax.ShapeDtypeStruct((8, channels), F32),
        jax.ShapeDtypeStruct(weight.shape, BF),
    ]
    out_specs = [tok, table, table, table, fixed_block(weight.shape)]
    if added:
        outs.append(jax.ShapeDtypeStruct((2, images, width, channels), BF))
        out_specs.append(pl.BlockSpec(memory_space=pl.ANY))
        outs.insert(0, jax.ShapeDtypeStruct(grads.shape, F32))
        out_specs.insert(0, tok)
    shapes = [(part.shape[0] // 8, part.shape[1]) for part in late] + [part.shape for part in summed]
    outs = [jax.ShapeDtypeStruct(shape, BF) for shape in shapes] + outs
    out_specs = [fixed_block(shape) for shape in shapes] + out_specs
    return pl.pallas_call(
        partial(conv_backward_kernel, width, bands, added, len(late), len(summed)),
        grid=(images,),
        out_shape=outs,
        in_specs=specs,
        out_specs=out_specs,
        scratch_shapes=[
            pltpu.VMEM((tokens + 2 * width, 3 * channels), BF),
            pltpu.VMEM((channels, tokens), BF),
            pltpu.VMEM(weight.shape, F32),
        ]
        + (
            exchange_scratch(images, width, channels, bands)
            if added
            else [
                pltpu.VMEM((bands, 8, channels), F32),
                pltpu.SemaphoreType.DMA((bands,)),
                pltpu.SemaphoreType.DMA((bands,)),
            ]
        )
        + (fold_scratch([part.shape for part in late]) if late else [])
        + [pltpu.VMEM(part.shape, BF) for part in (*summed, *summed)]
        + (tree_scratch([part.shape for part in summed]) if summed else []),
        compiler_params=pltpu.CompilerParams(
            vmem_limit_bytes=62 << 20, collective_id=4 if added else 6, has_side_effects=True
        ),
        name="conv_backward",
    )(*ins)


def layer_stats(field):
    centre = jnp.mean(field, axis=-1, keepdims=True)
    centred = field - centre
    inv_std = lax.rsqrt(jnp.mean(centred * centred, axis=-1, keepdims=True) + LN_EPS)
    return centred * inv_std, inv_std


def layer_back(grads, gain, centred, inv_std):
    scaled = grads * gain
    return inv_std * (
        scaled
        - jnp.mean(scaled, axis=-1, keepdims=True)
        - centred * jnp.mean(scaled * centred, axis=-1, keepdims=True)
    )


def turn_qkv(weight_ref, turned_s):
    rows, channels = weight_ref.shape[0], weight_ref.shape[1] // 3
    low = lane_ids(rows) < 64
    for head in range(HEADS):
        first = (head // 2) * 128
        keys = weight_ref[:, channels + first : channels + first + 128].astype(F32)
        values = weight_ref[:, 2 * channels + first : 2 * channels + first + 128].astype(F32)
        if head % 2 == 0:
            joint = jnp.where(low, keys, swap_halves(values))
        else:
            joint = jnp.where(low, swap_halves(keys), values)
        turned_s[:, head * 128 : head * 128 + 128] = joint.astype(BF)
    turned_s[:, 2 * channels :] = weight_ref[:, :channels]


def entry_kernel(bands, direct, field_ref, avg_ref, gain_ref, bias_ref, proj_ref, proj_bias, ln_gain,
                 ln_bias, qkv_ref, stream_ref, *refs):
    images = pl.num_programs(0)
    at = pl.program_id(0)
    if direct:
        count = len(refs) - 4
        sent_refs, (turned_s, first_s, send, recv) = refs[:count], refs[count:]
        me = lax.axis_index("rows")
    else:
        sent_refs, turned_s = refs[:-1], refs[-1]
    _, tokens, channels = field_ref.shape
    half = tokens // 2

    @pl.when(at == 0)
    def _():
        if direct:
            greet_rows(me, bands)
        turn_qkv(qkv_ref, turned_s)

    mean, inv_std = moments(avg_ref, at)
    slope = inv_std * vec(gain_ref)
    flat = (field_ref[0] * slope + (vec(bias_ref) - mean * slope)).astype(BF)
    stream = dot_nn(flat, proj_ref[...]) + vec(proj_bias)
    stream_ref[0] = stream
    centred, _ = layer_stats(stream)
    joint = dot_nn((centred * vec(ln_gain) + vec(ln_bias)).astype(BF), turned_s[...])
    low = lane_ids(half) < 64

    def put(out):
        for head in range(HEADS):
            out[head, :tokens] = joint[:, head * 128 : head * 128 + 128].astype(BF)
            first = 2 * channels + (head // 2) * 128
            upper, lower = joint[:half, first : first + 128], joint[half:, first : first + 128]
            if head % 2 == 0:
                pairs = jnp.where(low, upper, swap_halves(lower))
            else:
                pairs = jnp.where(low, swap_halves(upper), lower)
            out[head, tokens:] = pairs.astype(BF)

    for image, out in enumerate(sent_refs):
        pl.when(at == image)(partial(put, first_s if direct and image == 0 else out))
    if not direct:
        return
    copies = [
        row_copy(
            first_s.at[lax.rem(me + away, bands)], sent_refs[0].at[me], send.at[away], recv.at[me],
            lax.rem(me + away, bands),
        )
        for away in range(1, bands)
    ]
    own = pltpu.make_async_copy(first_s.at[me], sent_refs[0].at[me], recv.at[me])

    @pl.when(at == 0)
    def _():
        meet_rows(bands)
        for item in copies:
            item.start()
        own.start()

    @pl.when(at == images - 1)
    def _():
        own.wait()
        for away, item in enumerate(copies):
            item.wait_send()
            source = lax.rem(me + away + 1, bands)
            row_copy(
                sent_refs[0].at[source], sent_refs[0].at[source], send.at[away + 1], recv.at[source], source
            ).wait_recv()


def entry(field, avg, gain, bias, proj, proj_bias, ln_gain, ln_bias, qkv, bands):
    images, tokens, channels = field.shape
    vector = vector_block(channels)
    direct = bands == HEADS
    packed = (HEADS, tokens * 3 // 2, 128)
    anywhere = pl.BlockSpec(memory_space=pl.ANY)
    params = {"collective_id": 9, "has_side_effects": True} if direct else {}
    return pl.pallas_call(
        partial(entry_kernel, bands, direct),
        grid=(images,),
        out_shape=(jax.ShapeDtypeStruct(field.shape, F32),)
        + (jax.ShapeDtypeStruct(packed, BF),) * images,
        in_specs=[
            image_block(tokens, channels),
            table_block(channels),
            vector,
            vector,
            fixed_block(proj.shape),
            vector,
            vector,
            vector,
            fixed_block(qkv.shape),
        ],
        out_specs=(image_block(tokens, channels),)
        + ((anywhere,) if direct else (fixed_block(packed),))
        + (fixed_block(packed),) * (images - 1),
        scratch_shapes=[pltpu.VMEM(qkv.shape, BF)]
        + (
            [
                pltpu.VMEM(packed, BF),
                pltpu.SemaphoreType.DMA((bands,)),
                pltpu.SemaphoreType.DMA((bands,)),
            ]
            if direct
            else []
        ),
        compiler_params=pltpu.CompilerParams(vmem_limit_bytes=62 << 20, **params),
        name="entry",
    )(field, avg, gain, bias, proj, proj_bias, ln_gain, ln_bias, qkv)


def join_heads(pairs_ref, at):
    half = pairs_ref.shape[-2]
    low = lane_ids(half) < 64
    upper, lower = [], []
    for head in range(0, HEADS, 2):
        one, two = pairs_ref[at, head].astype(F32), pairs_ref[at, head + 1].astype(F32)
        upper.append(jnp.where(low, one, swap_halves(two)))
        lower.append(jnp.where(low, swap_halves(one), two))
    return jnp.concatenate(
        [jnp.concatenate(upper, axis=1), jnp.concatenate(lower, axis=1)], axis=0
    ).astype(BF)


def split_heads(field, out_ref, at):
    half = field.shape[0] // 2
    low = lane_ids(half) < 64
    for head in range(HEADS):
        first = (head // 2) * 128
        upper, lower = field[:half, first : first + 128], field[half:, first : first + 128]
        if head % 2 == 0:
            pairs = jnp.where(low, upper, swap_halves(lower))
        else:
            pairs = jnp.where(low, swap_halves(upper), lower)
        out_ref[at, head] = pairs.astype(BF)


def feed_pieces(channels, wide, hidden, bands):
    size = channels // bands
    geglu = [(at * size, size) for at in range(wide // channels)]
    first = wide // bands
    return (
        geglu,
        [(first, hidden // bands)],
        [(first + hidden // bands, size)],
        [(first + hidden // bands + size, size)],
    )


def feed_kernel(width, bands, per_band, halving, place, sides, *refs):
    given, refs = refs[:per_band], refs[per_band:]
    cot_hbm, refs = refs[0], refs[1:]
    count = 4 if halving else 1
    grads_ref, refs = refs[18 : 18 + count], refs[:18] + refs[18 + count :]
    (stream_ref, residual_ref, cot_ref, cross_ref, attn_ref, attn_bias, ln_gain, ln_bias,
     geglu_hbm, geglu_bias, feed_hbm, feed_bias, proj_ref, proj_bias,
     out_ref, three_ref, back_ref, ride_halo, sums_ref, cross_sum, pair_sums, geglu_s, feed_s, proj_s, attn_s,
     geglu_ref, feed_ref, weight_sems, ride_send, ride_recv, turned_s, mixed_s, sent_s, out_send, out_recv, back_send, back_recv, *more) = refs
    if halving:
        given_s, taken_s, pair_sems = more
    at = pl.program_id(0)
    images = pl.num_programs(0)
    last = images - 1
    me = lax.axis_index("rows")

    def move(src, dst, send, recv, target):
        @pl.when(target != me)
        def _():
            pltpu.make_async_remote_copy(
                src_ref=src, dst_ref=dst, send_sem=send, recv_sem=recv, device_id={"rows": target},
                device_id_type=pl.DeviceIdType.MESH,
            ).start()

        @pl.when(target == me)
        def _():
            pltpu.make_async_copy(src, dst, recv).start()

    def arrived(dst, send, recv, source):
        @pl.when(source != me)
        def _():
            pltpu.make_async_remote_copy(
                src_ref=dst, dst_ref=dst, send_sem=send, recv_sem=recv, device_id={"rows": source},
                device_id_type=pl.DeviceIdType.MESH,
            ).wait_recv()

        @pl.when(source == me)
        def _():
            pltpu.make_async_copy(dst, dst, recv).wait()

    def left(src, send, recv, target):
        @pl.when(target != me)
        def _():
            pltpu.make_async_remote_copy(
                src_ref=src, dst_ref=src, send_sem=send, recv_sem=recv, device_id={"rows": target},
                device_id_type=pl.DeviceIdType.MESH,
            ).wait_send()

    def send_spot(spot):
        item = me * per_band + spot
        head, image = item // images, lax.rem(item, images)
        for away in range(bands):
            band = lax.rem(me + away, bands)
            move(
                given[spot].at[band], mixed_s.at[image, head], out_send.at[spot, away],
                out_recv.at[image, head], band,
            )

    loads = [
        pltpu.make_async_copy(src, dst, weight_sems.at[spot])
        for spot, (src, dst) in enumerate(((geglu_hbm, geglu_ref), (feed_hbm, feed_ref)))
    ]

    @pl.when(at == 0)
    def _():
        greet_rows(me, bands)
        meet_rows(bands)
        send_spot(0)
        for item in loads:
            item.start()

    for head in range(HEADS):
        arrived(
            mixed_s.at[at, head], out_send.at[0, 0], out_recv.at[at, head], (head * images + at) // per_band
        )
    @pl.when(at == 0)
    def _():
        for item in loads:
            item.wait()

    def ride(image):
        below = cot_hbm.shape[1] - width
        return edge_copies(
            cot_hbm.at[image, pl.ds(0, width)], cot_hbm.at[image, pl.ds(below, width)], ride_halo, image,
            ride_send, ride_recv, me, bands,
        )

    @pl.when(at == images - 1)
    def _():
        for image in range(sent_s.shape[0]):
            for item in ride(image):
                item.start()

    for spot in range(1, per_band):
        pl.when(at == spot - 1)(partial(send_spot, spot))
    _, tokens, channels = stream_ref.shape
    hidden = feed_ref.shape[0]
    side = sides[at]
    inside = pixel_inside((tokens, channels), place[0], side, width)

    @pl.when(at == 0)
    def _():
        for ref in (sums_ref, cross_sum, pair_sums, geglu_s, feed_s, proj_s, attn_s):
            ref[...] = jnp.zeros_like(ref)

    mixed = join_heads(mixed_s, at)
    three = stream_ref[0] + dot_nn(mixed, attn_ref[...]) + (vec(attn_bias) + row_of(cross_ref[...], at))
    centred, inv_std = layer_stats(three)
    feed_in = (centred * vec(ln_gain) + vec(ln_bias)).astype(BF)
    grad_out = jnp.where(inside, cot_ref[0].astype(F32), 0.0)
    branch = grad_out.astype(BF)
    grad_four = dot_nt(branch, proj_ref[...])
    low_feed = grad_four.astype(BF)
    low_feed_t = low_feed.T
    feed_in_t = feed_in.T
    four = three + vec(feed_bias)
    grad_in = jnp.zeros((tokens, channels), F32)
    step = 512

    pair_bias = vec(geglu_bias)

    def products(first):
        own = slice(first, first + step)
        gates = slice(hidden + first, hidden + first + step)
        value = dot_nn(feed_in, geglu_ref[:, own]) + pair_bias[:, own]
        gate = dot_nn(feed_in, geglu_ref[:, gates]) + pair_bias[:, gates]
        return value, gate, dot_nt(low_feed, feed_ref[own])

    ahead = products(0)
    for first in range(0, hidden, step):
        own = slice(first, first + step)
        gates = slice(hidden + first, hidden + first + step)
        value, gate, back = ahead
        if first + step < hidden:
            ahead = products(first + step)
        below = 0.5 + 0.5 * lax.erf(gate * math.sqrt(0.5))
        bell = jnp.exp(gate * gate * -0.5) * (1.0 / math.sqrt(2.0 * math.pi))
        act = gate * below
        gated = (value * act).astype(BF)
        four = four + dot_nn(gated, feed_ref[own])
        feed_s[:, own] += dot_nn(low_feed_t, gated)
        grad_value = back * act
        grad_gate = back * value * (below + gate * bell)
        pair_sums[:, own] += col_sum(grad_value)
        pair_sums[:, gates] += col_sum(grad_gate)
        low_value, low_gate = grad_value.astype(BF), grad_gate.astype(BF)
        geglu_s[:, own] += dot_nn(feed_in_t, low_value)
        geglu_s[:, gates] += dot_nn(feed_in_t, low_gate)
        grad_in = grad_in + dot_nt(low_value, geglu_ref[:, own]) + dot_nt(low_gate, geglu_ref[:, gates])
    last_in = four.astype(BF)
    proj_s[...] += dot_tn(last_in, branch)
    output = residual_ref[0] + dot_nn(last_in, proj_ref[...]) + vec(proj_bias)
    out_ref[0] = jnp.where(inside, output, 0.0).astype(BF)
    grad_three = grad_four + layer_back(grad_in, vec(ln_gain), centred, inv_std)
    three_ref[0] = grad_three
    low_attn = grad_three.astype(BF)
    attn_s[...] += dot_tn(mixed, low_attn)
    split_heads(dot_nt(low_attn, attn_ref[...]), sent_s, at)
    for head in range(HEADS):
        item = head * images + at
        move(
            sent_s.at[at, head], back_ref.at[lax.rem(item, per_band), me], back_send.at[at, head],
            back_recv.at[lax.rem(item, per_band), me], item // per_band,
        )
    put_row(cross_sum, at, col_sum(grad_three))
    ids = lax.broadcasted_iota(jnp.int32, sums_ref.shape, 0)
    for row, total in enumerate(
        (col_sum(grad_out), col_sum(grad_four), col_sum(grad_in * centred), col_sum(grad_in))
    ):
        sums_ref[...] += jnp.where(ids == row, total, 0.0)

    @pl.when(at == last)
    def _():
        def settle():
            for image in range(sent_s.shape[0]):
                for item in ride(image):
                    item.wait_send()
                for end in range(2):
                    edge = ride_halo.at[end, image]
                    row_copy(
                        edge, edge, ride_send.at[end, image], ride_recv.at[end, image],
                        lax.rem(me + 1, bands),
                    ).wait_recv()
            for spot in range(per_band):
                for away in range(bands):
                    band = lax.rem(me + away, bands)
                    left(given[spot].at[band], out_send.at[spot, away], out_recv.at[0, 0], band)
                    arrived(back_ref.at[spot, band], back_send.at[0, 0], back_recv.at[spot, band], band)
            for image in range(sent_s.shape[0]):
                for head in range(HEADS):
                    left(
                        sent_s.at[image, head], back_send.at[image, head], back_recv.at[0, 0],
                        (head * sent_s.shape[0] + image) // per_band,
                    )

        pieces = feed_pieces(channels, 2 * hidden, hidden, bands)

        def put(place_of, band):
            for total, parts in zip((geglu_s, feed_s, proj_s, attn_s), pieces):
                for at_col, (first, size) in enumerate(parts):
                    if total is feed_s:
                        part = turned_s[pl.ds(pl.multiple_of(band * size, 16), size)]
                    else:
                        part = total[
                            pl.ds(pl.multiple_of(band * size, 16), size),
                            at_col * channels : (at_col + 1) * channels,
                        ]
                    ref, own, skip = place_of(first)
                    ref[own + (pl.ds(first - skip, size),)] = part.astype(BF)

        for first in range(0, hidden, step):
            turned_s[first : first + step, :] = feed_s[:, first : first + step].T.astype(BF)

        if not halving:
            for band in range(bands):
                put(lambda first, band=band: (grads_ref[0], (band,), 0), band)
            settle()
            return
        rows = given_s.shape[-2] // 2
        for apart in range(bands // 2):
            own = (apart & 1, apart >> 1)
            put(lambda first, own=own: (given_s, own, 0), jnp.bitwise_xor(me, 2 * apart + 1))
        item = row_copy(given_s, taken_s, pair_sems.at[0], pair_sems.at[1], jnp.bitwise_xor(me, 1))
        item.start()
        for apart in range(bands // 2):
            over_x, over_y = apart & 1, apart >> 1

            def half(first, over_x=over_x, over_y=over_y):
                return (
                    (grads_ref[over_x], (over_y,), 0)
                    if first < rows
                    else (grads_ref[2 + over_y], (over_x,), rows)
                )

            put(half, jnp.bitwise_xor(me, 2 * apart))
        item.wait()
        for apart in range(bands // 2):
            over_x, over_y = apart & 1, apart >> 1
            for ref, spot, lines in (
                (grads_ref[over_x], over_y, slice(0, rows)),
                (grads_ref[2 + over_y], over_x, slice(rows, 2 * rows)),
            ):
                ref[spot] = (ref[spot].astype(F32) + taken_s[over_x, over_y, lines].astype(F32)).astype(BF)
        settle()


def feed(place, sides, mixed, stream, residual, cot, cross, attn, attn_bias, ln_gain, ln_bias, geglu,
         geglu_bias, feed_out, feed_bias, proj, proj_bias, width, bands, halving):
    images, tokens, channels = stream.shape
    tok = image_block(tokens, channels)
    vector = vector_block(channels)
    table = table_block(channels)
    half = tokens // 2
    per_band = len(mixed)
    anywhere = pl.BlockSpec(memory_space=pl.ANY)
    wide = geglu.shape[1]
    weights = (geglu, feed_out, proj, attn)
    rows = sum(w.size for w in weights) // channels // bands
    lead = (2, 2) if halving else (bands,)
    grads = lead + (rows, channels)
    given = [(2, rows // 2, channels)] * 4 if halving else [grads]
    return pl.pallas_call(
        partial(feed_kernel, width, bands, per_band, halving),
        grid=(images,),
        out_shape=(
            jax.ShapeDtypeStruct(stream.shape, BF),
            jax.ShapeDtypeStruct(stream.shape, F32),
            jax.ShapeDtypeStruct((per_band, bands, half, 128), BF),
            jax.ShapeDtypeStruct((2, images, width, channels), BF),
        )
        + tuple(jax.ShapeDtypeStruct(shape, BF) for shape in given)
        + (
            jax.ShapeDtypeStruct((8, channels), F32),
            jax.ShapeDtypeStruct((8, channels), F32),
            jax.ShapeDtypeStruct((1, wide), F32),
        ),
        in_specs=[
            SMEM_WHOLE,
            SMEM_WHOLE,
        ]
        + [anywhere] * (per_band + 1)
        + [
            tok,
            tok,
            tok,
            table,
            fixed_block(attn.shape),
            vector,
            vector,
            vector,
            anywhere,
            vector_block(wide),
            anywhere,
            vector,
            fixed_block(proj.shape),
            vector,
        ],
        out_specs=(tok, tok, anywhere, anywhere)
        + tuple(fixed_block(shape) for shape in given)
        + (table, table, table_block(wide, 1)),
        scratch_shapes=[
            pltpu.VMEM(geglu.shape, F32),
            pltpu.VMEM(feed_out.shape[::-1], F32),
            pltpu.VMEM(proj.shape, F32),
            pltpu.VMEM(attn.shape, F32),
            pltpu.VMEM(geglu.shape, BF),
            pltpu.VMEM(feed_out.shape, BF),
            pltpu.SemaphoreType.DMA((2,)),
            pltpu.SemaphoreType.DMA((2, images)),
            pltpu.SemaphoreType.DMA((2, images)),
            pltpu.VMEM(feed_out.shape, BF),
        ]
        + [pltpu.VMEM((images, HEADS, half, 128), BF)] * 2
        + [
            pltpu.SemaphoreType.DMA((per_band, bands)),
            pltpu.SemaphoreType.DMA((images, HEADS)),
            pltpu.SemaphoreType.DMA((images, HEADS)),
            pltpu.SemaphoreType.DMA((per_band, bands)),
        ]
        + ([pltpu.VMEM(grads, BF)] * 2 + [pltpu.SemaphoreType.DMA((2,))] if halving else []),
        compiler_params=pltpu.CompilerParams(
            vmem_limit_bytes=62 << 20, collective_id=5, has_side_effects=True
        ),
        name="feed",
    )(place, sides, *mixed, cot, stream, residual, cot, cross, attn, attn_bias, ln_gain, ln_bias, geglu,
      geglu_bias, feed_out, feed_bias, proj, proj_bias)


def leave_kernel(width, bands, images, place, sides, *refs):
    direct = bands == HEADS
    if direct:
        *arrays, raw_ref = refs[:images]
        refs = refs[images:]
    else:
        packed_ref, refs = refs[0], refs[1:]
    (stream_ref, three_ref, field_ref, avg_ref, gain_ref, bias_ref, proj_ref, ln_gain, ln_bias,
     qkv_ref, out_ref, next_avg, next_halo, stats_ref, sums_ref, grad_qkv, grad_proj, qkv_s,
     proj_s, turned_s) = refs[:20]
    scratch = refs[20:26]
    me = lax.axis_index("rows")
    at = pl.program_id(0)
    last = pl.num_programs(0) - 1
    _, tokens, channels = stream_ref.shape
    inside = pixel_inside((tokens, channels), place[0], sides[at], width)

    @pl.when(at == 0)
    def _():
        greet_rows(me, bands)
        for ref in (stats_ref, sums_ref, qkv_s, proj_s):
            ref[...] = jnp.zeros_like(ref)
        turn_qkv(qkv_ref, turned_s)

    if direct:
        item_s, last_s, item_sems, last_send, last_recv = refs[26:]
        fetch = [
            pltpu.make_async_copy(array, item_s.at[image % 2], item_sems.at[image % 2])
            for image, array in enumerate(arrays)
        ]
        send_last = [
            row_copy(
                raw_ref.at[lax.rem(me + away, bands)], last_s.at[me], last_send.at[away], last_recv.at[me],
                lax.rem(me + away, bands),
            )
            for away in range(1, bands)
        ]
        keep_last = pltpu.make_async_copy(raw_ref.at[me], last_s.at[me], last_recv.at[me])

        @pl.when(at == 0)
        def _():
            fetch[0].start()
            meet_rows(bands)
            for item in send_last:
                item.start()
            keep_last.start()

        for image in range(len(fetch)):

            @pl.when(at == image)
            def _(image=image):
                if image + 1 < len(fetch):
                    fetch[image + 1].start()
                fetch[image].wait()

        @pl.when(at == last)
        def _():
            keep_last.wait()
            for away in range(1, bands):
                source = lax.rem(me + away, bands)
                row_copy(
                    last_s.at[source], last_s.at[source], last_send.at[away], last_recv.at[source], source
                ).wait_recv()
            item_s[(images - 1) % 2] = last_s[...]
            for item in send_last:
                item.wait_send()

        packed_ref, spot = item_s, lax.rem(at, 2)
    else:
        spot = 0
    queries = join_heads(packed_ref.at[:, :, tokens:, :], spot)
    joint = jnp.concatenate([packed_ref[spot, head, :tokens] for head in range(HEADS)] + [queries], axis=1)
    centred, inv_std = layer_stats(stream_ref[0])
    attn_in = (centred * vec(ln_gain) + vec(ln_bias)).astype(BF)
    qkv_s[...] += dot_tn(attn_in, joint)
    grads = dot_nt(joint, turned_s[...])
    grad_stream = three_ref[0] + layer_back(grads, vec(ln_gain), centred, inv_std)
    low_in = grad_stream.astype(BF)
    mean, deviation = moments(avg_ref, at)
    normed = (field_ref[0] - mean) * deviation
    flat = (normed * vec(gain_ref) + vec(bias_ref)).astype(BF)
    proj_s[...] += dot_tn(flat, low_in)
    moved = jnp.where(inside, dot_nt(low_in, proj_ref[...]), 0.0)
    out_ref[0] = moved
    share_edges(moved, at, width, next_halo, scratch, me, bands, direct)
    put_row(stats_ref, 2 * at, col_sum(moved))
    put_row(stats_ref, 2 * at + 1, col_sum(moved * normed))
    ids = lax.broadcasted_iota(jnp.int32, sums_ref.shape, 0)
    for row, total in enumerate((col_sum(grads * centred), col_sum(grads), col_sum(grad_stream))):
        sums_ref[...] += jnp.where(ids == row, total, 0.0)

    @pl.when(at == last)
    def _():
        close_exchange(stats_ref[...], gain_ref, sides, next_avg, next_halo, scratch, me, bands)
        grad_qkv[...] = qkv_s[...].astype(BF)
        grad_proj[...] = proj_s[...].astype(BF)


def leave(place, sides, packed, stream, three, field, avg, gain, bias, proj, ln_gain, ln_bias, qkv, width,
          bands):
    images, tokens, channels = stream.shape
    direct = bands == HEADS
    tok = image_block(tokens, channels)
    vector = vector_block(channels)
    table = table_block(channels)
    return pl.pallas_call(
        partial(leave_kernel, width, bands, images),
        grid=(images,),
        out_shape=(
            jax.ShapeDtypeStruct(stream.shape, F32),
            jax.ShapeDtypeStruct((8, channels), F32),
            jax.ShapeDtypeStruct((2, images, width, channels), BF),
            jax.ShapeDtypeStruct((8, channels), F32),
            jax.ShapeDtypeStruct((8, channels), F32),
            jax.ShapeDtypeStruct(qkv.shape, BF),
            jax.ShapeDtypeStruct(proj.shape, BF),
        ),
        in_specs=[
            SMEM_WHOLE,
            SMEM_WHOLE,
        ]
        + (
            [pl.BlockSpec(memory_space=pl.ANY)] * images
            if direct
            else [pl.BlockSpec((1,) + packed[0].shape[1:], lambda at: (at, 0, 0, 0))]
        )
        + [
            tok,
            tok,
            tok,
            table,
            vector,
            vector,
            fixed_block(proj.shape),
            vector,
            vector,
            fixed_block(qkv.shape),
        ],
        out_specs=(
            tok,
            table,
            pl.BlockSpec(memory_space=pl.ANY),
            table,
            table,
            fixed_block(qkv.shape),
            fixed_block(proj.shape),
        ),
        scratch_shapes=[
            pltpu.VMEM(qkv.shape, F32), pltpu.VMEM(proj.shape, F32), pltpu.VMEM(qkv.shape, BF)
        ]
        + exchange_scratch(images, width, channels, bands)
        + (
            [
                pltpu.VMEM((2,) + packed[0].shape, BF),
                pltpu.VMEM(packed[0].shape, BF),
                pltpu.SemaphoreType.DMA((2,)),
                pltpu.SemaphoreType.DMA((bands,)),
                pltpu.SemaphoreType.DMA((bands,)),
            ]
            if direct
            else []
        ),
        compiler_params=pltpu.CompilerParams(
            vmem_limit_bytes=62 << 20, collective_id=7, has_side_effects=True
        ),
        name="leave",
    )(place, sides, *packed, stream, three, field, avg, gain, bias, proj, ln_gain, ln_bias, qkv)

def rounded(field):
    return field.astype(BF)


def join_sums(table_ref, cross, hidden, first, second, third, residual, leaves, feeds, pairs):
    images = cross.shape[0] // 2
    channels = cross.shape[1]
    ids = lax.broadcasted_iota(jnp.int32, cross.shape, 0)

    def total(ref, step, offset, count):
        return col_sum(jnp.where((ids < count) & (lax.rem(ids, step) == offset), ref[...], 0.0))

    rows = [row_of(cross[...], at) for at in range(images)] + [row_of(hidden[...], at) for at in range(images)]
    for ref in (first, second, third):
        rows += [total(ref, 2, 1, 2 * images), total(ref, 2, 0, 2 * images)]
    rows.append(total(residual, 1, 0, images))
    rows += [row_of(leaves[...], at) for at in range(3)] + [row_of(feeds[...], at) for at in range(4)]
    rows += [pairs[:, first : first + channels] for first in range(0, pairs.shape[1], channels)]
    table_ref[...] = jnp.zeros_like(table_ref)
    for at, row in enumerate(rows):
        put_row(table_ref.at[pl.ds(at // 8 * 8, 8)], at % 8, row)


def reduce_kernel(count, bands, groups, *refs):
    last_ref, bands_refs = refs[0], refs[1 : 1 + count]
    half_ref, tables = refs[1 + count], refs[2 + count : 11 + count]
    refs = refs[11 + count :]
    last_out, bands_outs, (gathered, other_ref) = refs[0], refs[1 : 1 + count], refs[1 + count : 3 + count]
    refs = refs[3 + count :]
    table_ref, slots, table_send, table_recv, far_send, far_recv, half_sems = refs[:7]
    sum_s, fields = refs[7], refs[8 : 8 + count]
    refs = refs[8 + count :]
    me, group = lax.axis_index("rows"), lax.axis_index("heads")
    fold = BandFold([last_ref], refs[:9], me)
    tree = GroupTree(fields, bands_outs, refs[9 : 11 + 2 * count], group)
    last_tree = GroupTree([sum_s], [last_out], refs[11 + 2 * count :], group)
    row_peers = [lax.rem(me + away, bands) for away in range(1, bands)]
    far_peers = [lax.rem(group + away, groups) for away in range(1, groups)]
    barrier = pltpu.get_barrier_semaphore()
    for axis, peers in (("rows", row_peers), ("heads", far_peers)):
        for peer in peers:
            pl.semaphore_signal(
                barrier, inc=1, device_id={axis: peer}, device_id_type=pl.DeviceIdType.MESH
            )
    for field, ref in zip(fields, bands_refs):
        field[...] = ref[...]
    join_sums(table_ref, *tables)
    pl.semaphore_wait(barrier, bands + groups - 2)

    def copy(src, dst, send, recv, axis, peer):
        return pltpu.make_async_remote_copy(
            src_ref=src,
            dst_ref=dst,
            send_sem=send,
            recv_sem=recv,
            device_id={axis: peer},
            device_id_type=pl.DeviceIdType.MESH,
        )

    near = [
        copy(table_ref, slots.at[away], table_send.at[away], table_recv.at[away], "rows", peer)
        for away, peer in enumerate(row_peers)
    ]
    for item in near:
        item.start()
    fold.start()
    tree.near()
    half = copy(half_ref, other_ref, half_sems.at[0], half_sems.at[1], "heads", jnp.bitwise_xor(group, 1))
    half.start()
    fold.spread()
    for item in near:
        item.wait_recv()
    total = table_ref[...]
    for away in range(bands - 1):
        total = total + slots[away]
    gathered[group] = total
    far = [
        copy(gathered.at[group], gathered.at[group], far_send.at[away], far_recv.at[away], "heads", peer)
        for away, peer in enumerate(far_peers)
    ]
    for item in far:
        item.start()
    tree.far()
    fold.second()
    fold.finish([sum_s])
    last_tree.near()
    tree.back()
    last_tree.far()
    last_tree.back()
    for away in range(groups - 1):
        source = lax.rem(group - (away + 1) + groups, groups)
        copy(
            gathered.at[source], gathered.at[source], far_send.at[away], far_recv.at[away], "heads", source
        ).wait_recv()
    tree.end()
    last_tree.end()
    half.wait_recv()
    for item in [half] + near + far:
        item.wait_send()


def reduce_parts(last, parts, half, bands, groups, sums):
    shapes = [part.shape for part in parts]
    own = (last.shape[0] // bands, last.shape[1])
    rows = 2 * (sums[0].shape[0] // 2) + 14 + sums[-1].shape[1] // last.shape[1]
    table = (-(-rows // 8) * 8, last.shape[1])
    return pl.pallas_call(
        partial(reduce_kernel, len(parts), bands, groups),
        out_shape=(jax.ShapeDtypeStruct(own, BF),)
        + tuple(jax.ShapeDtypeStruct(shape, BF) for shape in shapes)
        + (
            jax.ShapeDtypeStruct((groups,) + table, F32),
            jax.ShapeDtypeStruct(half.shape, BF),
        ),
        in_specs=[pl.BlockSpec(memory_space=pl.ANY)] + [VMEM_WHOLE] * (len(parts) + 1 + len(sums)),
        out_specs=(VMEM_WHOLE,) * (len(parts) + 3),
        scratch_shapes=[pltpu.VMEM(table, F32), pltpu.VMEM((bands - 1,) + table, F32)]
        + [pltpu.SemaphoreType.DMA((bands - 1,))] * 2
        + [pltpu.SemaphoreType.DMA((groups - 1,))] * 2
        + [pltpu.SemaphoreType.DMA((2,)), pltpu.VMEM(own, BF)]
        + [pltpu.VMEM(shape, BF) for shape in shapes]
        + fold_scratch([last.shape])
        + tree_scratch(shapes)
        + tree_scratch([own]),
        compiler_params=pltpu.CompilerParams(
            vmem_limit_bytes=62 << 20, collective_id=8, has_side_effects=True
        ),
        name="reduce_parts",
    )(last, *parts, half, *sums)


def halve_rows(kept, given, step):
    pairs = [(band, band ^ (1 << step)) for band in range(8)]
    return rounded(kept.astype(F32) + lax.ppermute(given, "rows", pairs).astype(F32))


def sum_groups(part, step, groups):
    odd = lax.rem(lax.axis_index("heads"), 2)
    near = [(at, at ^ 1) for at in range(groups)]
    far = [(at, at ^ 2) for at in range(groups)]
    if step == 0:
        one, two = part
        kept, sent = jnp.where(odd == 0, one, two), jnp.where(odd == 0, two, one)
        return rounded(kept.astype(F32) + lax.ppermute(sent, "heads", near).astype(F32))
    if step == 1:
        return rounded(part.astype(F32) + lax.ppermute(part, "heads", far).astype(F32))
    other = lax.ppermute(part, "heads", near)
    return jnp.where(odd == 0, jnp.concatenate([part, other]), jnp.concatenate([other, part]))


def finals_kernel(pieces, *refs):
    (odd, conv_two, conv_one, qkv, proj_in, kept, other, table, value, context, hot, embed, cross_out,
     cross_value, out_conv_two, out_conv_one, out_qkv, out_proj_in, out_geglu, out_feed, out_proj_out,
     out_attn_out, out_class, out_cross_value, out_cross_out, out_time, rows_s) = refs
    out_conv_two[...] = conv_two[...].astype(F32)
    out_conv_one[...] = conv_one[...].astype(F32)
    out_proj_in[...] = proj_in[...].astype(F32)
    rows, channels = out_proj_in.shape
    low = lane_ids(rows) < 64
    out_qkv[:, :channels] = qkv[:, 2 * channels :].astype(F32)
    for first in range(0, channels, 128):
        one = qkv[:, 2 * first : 2 * first + 128].astype(F32)
        two = qkv[:, 2 * first + 128 : 2 * first + 256].astype(F32)
        out_qkv[:, channels + first : channels + first + 128] = jnp.where(low, one, swap_halves(two))
        out_qkv[:, 2 * channels + first : 2 * channels + first + 128] = jnp.where(
            low, swap_halves(one), two
        )
    flag = jnp.full((1, channels), odd[0], jnp.int32) == 0
    one, two = kept[...].astype(F32), other[...].astype(F32)
    early = jnp.concatenate([jnp.where(flag, one, two), jnp.where(flag, two, one)], axis=0)
    for at, (first, size) in enumerate(pieces[0]):
        out_geglu[:, at * channels : (at + 1) * channels] = early[first : first + size]
    for out, ((first, size),) in zip((out_feed, out_proj_out, out_attn_out), pieces[1:]):
        out[...] = early[first : first + size]
    per_group = value.shape[0] // table.shape[0]

    def joined(first):
        return jnp.concatenate(
            [table[group, first : first + per_group] for group in range(table.shape[0])], axis=0
        )

    def exact(lhs, rhs, dims):
        return lax.dot_general(lhs, rhs, (dims, ((), ())), precision=HIGH, preferred_element_type=F32)

    crossed, shifted = joined(0), joined(per_group)
    own = pl.ds(pl.multiple_of(odd[1] * rows, 16), rows)
    tile = pl.ds(pl.multiple_of(odd[1] * rows // 128 * 128, 128), 128)
    inner = pl.ds(pl.multiple_of(lax.rem(odd[1] * rows, 128), 16), rows)
    rows_s[...] = exact(value[:, tile].astype(F32), crossed, ((0,), (0,)))
    out_cross_out[...] = rows_s[inner]
    grad_value = exact(crossed, cross_out[...].astype(F32), ((1,), (1,)))
    rows_s[...] = exact(context[:, tile], grad_value, ((0,), (0,)))
    out_cross_value[...] = rows_s[inner]
    grad_context = exact(grad_value, cross_value[own].astype(F32), ((1,), (1,)))
    out_class[...] = exact(hot[...].astype(F32), grad_context, ((0,), (0,)))
    times = out_time.shape[0]
    columns = pl.ds(pl.multiple_of(odd[1] * times, 128), times)
    out_time[...] = exact(embed[:, columns].astype(F32), shifted, ((0,), (0,)))


def finals(odd, parts, kept, other, table, value, context, hot, embed, cross_out, cross_value, pieces):
    conv_two, conv_one, qkv, proj_in = parts
    rows, channels = proj_in.shape
    shapes = [part.shape for part in parts] + [
        (rows, len(pieces[0]) * channels),
        (pieces[1][0][1], channels),
        (rows, channels),
        (rows, channels),
        (hot.shape[1], rows),
        (rows, channels),
        (rows, channels),
        (embed.shape[1] * rows // channels, channels),
    ]
    return pl.pallas_call(
        partial(finals_kernel, pieces),
        out_shape=tuple(jax.ShapeDtypeStruct(shape, F32) for shape in shapes),
        in_specs=[SMEM_WHOLE] + [VMEM_WHOLE] * 13,
        out_specs=(VMEM_WHOLE,) * len(shapes),
        scratch_shapes=[pltpu.VMEM((128, channels), F32)],
        compiler_params=pltpu.CompilerParams(vmem_limit_bytes=62 << 20),
        name="finals",
    )(odd, *parts, kept, other, table, value, context, hot, embed, cross_out, cross_value)


def finish_kernel(width, place, sides, kept_ref, grad_ref, field_ref, avg_ref, back_avg, gain_ref, made_ref,
                  out_ref, pass_ref):
    pass_ref[...] = made_ref[...]
    at = pl.program_id(0)
    mean, inv_std = moments(avg_ref, at)
    back = back_avg[...]
    field_slope = inv_std * inv_std * row_of(back, 2 * at + 1)
    offset = inv_std * row_of(back, 2 * at) - mean * field_slope
    moved = grad_ref[0] * (inv_std * vec(gain_ref)) - field_ref[0].astype(F32) * field_slope - offset
    inside = pixel_inside(moved.shape, place[0], sides[at], width)
    out_ref[0] = jnp.where(inside, kept_ref[0] + moved, 0.0)


def finish(place, sides, kept, grads, field, avg, back_avg, gain, made, width):
    images, tokens, channels = kept.shape
    tok = image_block(tokens, channels)
    table = table_block(channels)
    return pl.pallas_call(
        partial(finish_kernel, width),
        grid=(images,),
        out_shape=(jax.ShapeDtypeStruct(kept.shape, F32), jax.ShapeDtypeStruct(made.shape, BF)),
        in_specs=[SMEM_WHOLE, SMEM_WHOLE, tok, tok, tok, table, table, vector_block(channels), tok],
        out_specs=(tok, tok),
        compiler_params=pltpu.CompilerParams(vmem_limit_bytes=62 << 20),
        name="finish",
    )(place, sides, kept, grads, field, avg, back_avg, gain, made)


def time_features(time_steps, dims):
    half_dim = dims // 2
    frequency = jnp.exp(-math.log(10000.0) * jnp.arange(half_dim, dtype=jnp.float32) / half_dim)
    angles = time_steps.astype(jnp.float32)[:, None] * frequency[None, :]
    return jnp.concatenate([jnp.cos(angles), jnp.sin(angles)], axis=-1)


def pad_rows(table):
    return jnp.pad(table, ((0, 8 - table.shape[0]), (0, 0)))


def to_items(sent, bands):
    images, heads = len(sent), sent[0].shape[0]
    per_band = heads * images // bands
    if bands == heads:
        first, *parts = sent
    else:
        items = jnp.stack(sent, axis=1).reshape((bands, per_band) + sent[0].shape[1:])
        parts = [items[:, at] for at in range(per_band)]
    parts = [lax.all_to_all(part, "rows", split_axis=0, concat_axis=0, tiled=True) for part in parts]
    return [first] + parts if bands == heads else parts


def from_items(results, images, bands):
    if bands == HEADS:
        return [
            lax.all_to_all(result, "rows", split_axis=0, concat_axis=0, tiled=True)
            for result in results[:-1]
        ] + results[-1:]
    back = [
        lax.all_to_all(result, "rows", split_axis=0, concat_axis=0, tiled=True)
        for result in results
    ]
    joint = jnp.stack(back, axis=1)
    return [jnp.swapaxes(joint.reshape((HEADS, images) + joint.shape[2:]), 0, 1)]


def per_device(
    images,
    image_sides,
    labels,
    timesteps,
    cotangent,
    first_gain,
    first_bias,
    conv_one,
    time_proj,
    time_bias,
    second_gain,
    second_bias,
    conv_two,
    conv_bias,
    third_gain,
    third_bias,
    proj_in,
    proj_in_bias,
    attn_gain,
    attn_bias,
    qkv_proj,
    attn_out,
    attn_out_bias,
    class_table,
    cross_value,
    cross_out,
    feed_gain,
    feed_bias,
    geglu_proj,
    geglu_bias,
    feed_out,
    feed_out_bias,
    proj_out,
    proj_out_bias,
):
    image_count, band_rows, width, channels = images.shape
    tokens = band_rows * width
    head_dim = channels // HEADS
    score_scale = head_dim ** (-0.5)
    bands = lax.axis_size("rows")
    groups = lax.axis_size("heads")
    halving = bands == 8 and groups == 4 and channels == 512
    me = lax.axis_index("rows")
    first_image = lax.axis_index("heads") * image_count
    sides = lax.dynamic_slice_in_dim(image_sides, first_image, image_count)
    place = jnp.stack([me * band_rows, me]).astype(jnp.int32)

    field = images.reshape(image_count, tokens, channels)
    cot = cotangent.reshape(image_count, tokens, channels)

    hot = rounded(
        (labels[:, None] == jnp.arange(class_table.shape[0], dtype=jnp.int32)[None, :]).astype(F32)
    )
    context = jnp.dot(hot, class_table, preferred_element_type=F32)
    value = rounded(jnp.dot(rounded(context), cross_value, preferred_element_type=F32))
    cross = jnp.dot(value, cross_out, preferred_element_type=F32)
    cross = pad_rows(lax.dynamic_slice_in_dim(cross, first_image, image_count))
    embed = rounded(jax.nn.silu(time_features(timesteps, time_proj.shape[0])))
    shift = jnp.dot(embed, time_proj, preferred_element_type=F32) + time_bias.astype(F32)
    shift = pad_rows(lax.dynamic_slice_in_dim(shift, first_image, image_count))

    avg_one, halo_images = begin(place, sides, field, width, bands)
    hidden, avg_two, halo_hidden = conv_forward(
        place, sides, field, halo_images, avg_one, first_gain, first_bias, conv_one,
        shift, None, width, bands,
    )
    residual, avg_three, halo_residual = conv_forward(
        place, sides, hidden, halo_hidden, avg_two, second_gain, second_bias, conv_two,
        jnp.broadcast_to(conv_bias.astype(F32), (8, channels)), field, width, bands,
    )
    stream, *sent = entry(
        residual, avg_three, third_gain, third_bias, proj_in, proj_in_bias,
        attn_gain, attn_bias, qkv_proj, bands,
    )
    chunks = to_items(sent, bands)
    first_item = me * len(chunks)
    item_sides = [
        lax.dynamic_slice_in_dim(sides, lax.rem(first_item + at, image_count), 1)
        for at in range(len(chunks))
    ]
    attended = [attend(side, chunk, width, score_scale) for side, chunk in zip(item_sides, chunks)]
    mixed = [pairs for pairs, _, _ in attended]
    (
        output, three, grad_chunks, halo_cot, *feed_grads, feed_sums, cross_sum, pair_sums,
    ) = feed(
        place, sides, mixed, stream, residual, cot, cross, attn_out, attn_out_bias,
        feed_gain, feed_bias, geglu_proj, geglu_bias, feed_out,
        feed_out_bias, proj_out, proj_out_bias, width, bands, halving,
    )
    halved = (feed_grads[0:2], feed_grads[2:4]) if halving else None
    results = []
    for spot, (side, chunk, (_, norms, kept)) in enumerate(zip(item_sides, chunks, attended)):
        if halving and spot in (1, 2):
            halved = [
                halve_rows(kept, given, spot if at == 0 else 3 - spot) for at, (kept, given) in enumerate(halved)
            ]
            *halved, norms = lax.optimization_barrier((*halved, norms))
            halved = [(part[0], part[1]) for part in halved] if spot == 1 else halved
        results.append(attend_back(side, chunk, grad_chunks, spot, norms, kept, width, score_scale))
    grad_qkv = from_items(results, image_count, bands)
    if halving:
        early = halved
    else:
        early = feed_grads[0].reshape((bands,) + feed_grads[0].shape[-2:])
        early = lax.psum_scatter(early, "rows", scatter_dimension=0, tiled=True)[0]
        early = lax.psum(early, "heads")
    moved, back_three, halo_moved, third_sums, leave_sums, grad_qkv_proj, grad_proj_in = leave(
        place, sides, grad_qkv, stream, three, residual, avg_three, third_gain,
        third_bias, proj_in, attn_gain, attn_bias, qkv_proj, width, bands,
    )
    if halving:
        *early, back_three = lax.optimization_barrier((*early, back_three))
        early = sum_groups(early, 0, groups)
    *folded, grad_residual, moved, back_two, second_sums, residual_sums, grad_conv_two, halo_moved = conv_backward(
        place, sides, moved, halo_moved, residual, halo_residual, avg_three, back_three,
        third_gain, cot, halo_cot, conv_two, hidden, avg_two, second_gain,
        second_bias, (grad_qkv_proj, grad_proj_in) if halving else (), (), width, bands,
    )
    if halving:
        early, back_two = lax.optimization_barrier((early, back_two))
        early = sum_groups(early, 1, groups)
    *folded, moved, back_one, first_sums, hidden_sums, grad_conv_one = conv_backward(
        place, sides, moved, halo_moved, hidden, halo_hidden, avg_two, back_two, second_gain,
        None, None, conv_one, field, avg_one, first_gain, first_bias,
        (grad_conv_two,) if halving else (), folded, width, bands,
    )
    if halving:
        early, back_one = lax.optimization_barrier((early, back_one))
    grad_images, output = finish(
        place, sides, grad_residual, moved, field, avg_one, back_one, first_gain, output, width
    )
    grad_images = grad_images.reshape(images.shape)

    def own(whole, axis=0):
        size = whole.shape[axis] // bands
        return lax.dynamic_slice_in_dim(whole, me * size, size, axis)

    def reduced(part):
        part = lax.psum_scatter(part, "rows", scatter_dimension=0, tiled=True)
        return lax.psum(part, "heads").astype(F32)

    used = 2 * image_count
    pieces = feed_pieces(channels, geglu_proj.shape[1], feed_out.shape[0], bands)
    if halving:
        grad_images, first_sums = lax.optimization_barrier((grad_images, first_sums))
        rows_two, rows_qkv, rows_in = folded
        rows_one, rows_two, table, other = reduce_parts(
            grad_conv_one, (rows_two,), early, bands, groups,
            (cross_sum, hidden_sums, first_sums, second_sums, third_sums, residual_sums, leave_sums, feed_sums,
             pair_sums),
        )
        late = (rows_two, rows_one, rows_qkv, rows_in)
        odd = jnp.stack([lax.rem(lax.axis_index("heads"), 2), me]).astype(jnp.int32)
        (
            rows_conv_two, rows_conv_one, rows_qkv, rows_proj_in, rows_geglu, rows_feed, rows_proj_out,
            rows_attn_out, grad_class_table, grad_cross_value, grad_cross_out, grad_time_proj,
        ) = finals(
            odd, late, early, other, table, value, context, hot, embed, cross_out, cross_value,
            pieces,
        )
    else:
        table = jnp.concatenate(
            [
                cross_sum[:image_count],
                hidden_sums[:image_count],
                jnp.stack(
                    [
                        jnp.sum(first_sums[1:used:2], axis=0),
                        jnp.sum(first_sums[0:used:2], axis=0),
                        jnp.sum(second_sums[1:used:2], axis=0),
                        jnp.sum(second_sums[0:used:2], axis=0),
                        jnp.sum(third_sums[1:used:2], axis=0),
                        jnp.sum(third_sums[0:used:2], axis=0),
                        jnp.sum(residual_sums[:image_count], axis=0),
                    ]
                ),
                leave_sums[:3],
                feed_sums[:4],
                pair_sums.reshape(-1, channels),
            ]
        )
        table = jnp.pad(table, ((0, -table.shape[0] % 8), (0, 0)))
        table = lax.all_gather(lax.psum(table, "rows"), "heads")
        rows_conv_two, rows_qkv, rows_proj_in, rows_conv_one = (
            reduced(part) for part in (grad_conv_two, grad_qkv_proj, grad_proj_in, grad_conv_one)
        )
        keys_values = rows_qkv[:, : 2 * channels].reshape(-1, HEADS, 2, head_dim)
        rows_qkv = jnp.concatenate(
            [
                rows_qkv[:, 2 * channels :],
                keys_values[:, :, 0].reshape(-1, channels),
                keys_values[:, :, 1].reshape(-1, channels),
            ],
            axis=1,
        )
        early = early.astype(F32)
        rows_geglu = jnp.concatenate([early[first : first + size] for first, size in pieces[0]], axis=1)
        rows_feed, rows_proj_out, rows_attn_out = (
            early[first : first + size] for ((first, size),) in pieces[1:]
        )
    all_cross = table[:, :image_count].reshape(-1, channels)
    all_shift = table[:, image_count : 2 * image_count].reshape(-1, channels)
    if not halving:
        own_value, own_context = own(value.astype(F32), 1), own(context, 1)
        own_embed, own_cross = own(embed.astype(F32), 1), own(cross_value)
        hot = hot.astype(F32)
        grad_cross_out = jnp.dot(own_value.T, all_cross, precision=HIGH)
        grad_value = jnp.dot(all_cross, cross_out.astype(F32).T, precision=HIGH)
        grad_cross_value = jnp.dot(own_context.T, grad_value, precision=HIGH)
        grad_context = jnp.dot(grad_value, own_cross.astype(F32).T, precision=HIGH)
        grad_class_table = jnp.dot(hot.T, grad_context, precision=HIGH)
        grad_time_proj = jnp.dot(own_embed.T, all_shift, precision=HIGH)
    joint = jnp.concatenate(
        [jnp.sum(table[:, 2 * image_count :], axis=0), jnp.sum(all_cross, axis=0)[None],
         jnp.sum(all_shift, axis=0)[None]]
    )
    mine = own(joint, 1)
    singles = [mine[at] for at in range(14)]
    grad_geglu_bias = own(joint[14 : 14 + geglu_bias.shape[0] // channels].reshape(-1))
    return (
        output.reshape(images.shape),
        grad_images,
        singles[0],
        singles[1],
        rows_conv_one,
        grad_time_proj,
        mine[-1],
        singles[2],
        singles[3],
        rows_conv_two,
        singles[6],
        singles[4],
        singles[5],
        rows_proj_in,
        singles[9],
        singles[7],
        singles[8],
        rows_qkv,
        rows_attn_out,
        mine[-2],
        grad_class_table,
        grad_cross_value,
        grad_cross_out,
        singles[12],
        singles[13],
        rows_geglu,
        grad_geglu_bias,
        rows_feed,
        singles[11],
        rows_proj_out,
        singles[10],
    )


def solution(mesh):
    return jax.shard_map(
        per_device,
        mesh=mesh,
        in_specs=(
            P("heads", "rows", None, None),
            P(),
            P(),
            P(),
            P("heads", "rows", None, None),
            P(),
            P(),
            P(),
            P(),
            P(),
            P(),
            P(),
            P(),
            P(),
            P(),
            P(),
            P(),
            P(),
            P(),
            P(),
            P(),
            P(),
            P(),
            P(),
            P(),
            P(),
            P(),
            P(),
            P(),
            P(),
            P(),
            P(),
            P(),
            P(),
        ),
        out_specs=(
            P("heads", "rows", None, None),
            P("heads", "rows", None, None),
            P("rows"),
            P("rows"),
            P("rows", None),
            P("rows", None),
            P("rows"),
            P("rows"),
            P("rows"),
            P("rows", None),
            P("rows"),
            P("rows"),
            P("rows"),
            P("rows", None),
            P("rows"),
            P("rows"),
            P("rows"),
            P("rows", None),
            P("rows", None),
            P("rows"),
            P(None, "rows"),
            P("rows", None),
            P("rows", None),
            P("rows"),
            P("rows"),
            P("rows", None),
            P("rows"),
            P("rows", None),
            P("rows"),
            P("rows", None),
            P("rows"),
        ),
        check_vma=False,
    )
```

```python
from functools import partial
import math

import jax
import jax.numpy as jnp
from jax import lax
from jax.experimental import pallas as pl
from jax.experimental.pallas import tpu as pltpu
from jax.sharding import PartitionSpec as P

HEADS = 8
GROUPS = 32
GN_EPS = 1e-06
LN_EPS = 1e-05
HIGH = lax.Precision.HIGHEST
LOG2E = math.log2(math.e)
BF = jnp.bfloat16
F32 = jnp.float32
KEPT = 256
APART = 80

def dot_nt(lhs, rhs):
    return lax.dot_general(lhs, rhs, (((1,), (1,)), ((), ())), preferred_element_type=F32)


def dot_nn(lhs, rhs):
    return lax.dot_general(lhs, rhs, (((1,), (0,)), ((), ())), preferred_element_type=F32)


def lane_ids(rows):
    return lax.broadcasted_iota(jnp.int32, (rows, 128), 1)


def swap_halves(field):
    return pltpu.roll(field, 64, 1)


def pieces_of(column):
    top = column.astype(BF).astype(F32)
    rest = column - top
    mid = rest.astype(BF).astype(F32)
    return (top, mid, rest - mid)


def extras(column, lanes, first):
    top, mid, low = pieces_of(column)
    return jnp.where(
        lanes == first, top, jnp.where(lanes == first + 1, mid, jnp.where(lanes == first + 2, low, 0.0))
    )


def block_of(count, pref):
    for size in pref:
        if count % size == 0:
            return size
    return count


def crop(field, width, side):
    rows = field.shape[0] // width
    if side == width:
        return field
    return field.reshape(rows, width, 128)[:, :side].reshape(rows * side, 128)


def uncrop(field, width, side):
    if side == width:
        return field
    rows = field.shape[0] // side
    spread = field.reshape(rows, side, 128)
    return jnp.concatenate(
        [spread, jnp.zeros((rows, width - side, 128), field.dtype)], axis=1
    ).reshape(rows * width, 128)


def unpack_pairs(pairs):
    return jnp.concatenate([pairs, swap_halves(pairs)], axis=0)


def pack_pairs(field, lanes):
    half = field.shape[0] // 2
    return jnp.where(lanes[:half] < 64, field[:half], swap_halves(field[half:]))


def attend_kernel(width, scale, side_ref, qkv_ref, out_ref, norm_ref, kept_ref, q_s, k_s, v_s, vt_s, top_s, stage_s, sems):
    bands, packed, _ = qkv_ref.shape
    band_tokens = packed * 2 // 3
    band_rows = band_tokens // width
    side_now = side_ref[0]

    def variant(side):
        tokens = side * side
        used = side // band_rows
        own = band_rows * side
        lanes = lane_ids(own)
        low = lanes < 64
        row_ids = lax.broadcasted_iota(jnp.int32, (128, 128), 0)
        col_ids = lax.broadcasted_iota(jnp.int32, (128, 128), 1)
        picks = jnp.where((row_ids < 64) == (col_ids < 64), 1.0, 0.0).astype(BF)

        def gather_band(band, norms):
            pairs = crop(qkv_ref[band, band_tokens:, :].astype(F32), width, side)
            keys = crop(qkv_ref[band, :band_tokens, :].astype(F32), width, side)
            queries = unpack_pairs(pairs) * (scale * LOG2E)
            head = queries.astype(BF).astype(F32)
            turned = swap_halves(keys)
            rows = pl.ds(pl.multiple_of(band * own, 16), own)
            q_s[rows, :] = jnp.where(low, head, swap_halves(queries - head)).astype(BF)
            k_s[rows, :] = jnp.where(low, keys, turned).astype(BF)
            v_s[rows, :] = jnp.where(low, turned, jnp.where(lanes == 64, 1.0, 0.0)).astype(BF)
            joint = jnp.where(low, queries, turned)
            sums = dot_nn((joint * joint).astype(BF), picks)
            return jnp.maximum(norms, jnp.max(sums, axis=0, keepdims=True))

        norms = lax.fori_loop(0, used, gather_band, jnp.zeros((1, 128), F32))
        step = block_of(tokens, (512, 256))
        for first in range(0, tokens, step):
            vt_s[:, first : first + step] = v_s[first : first + step, :].T
        first_lanes = lane_ids(1) < 64
        query_top = jnp.max(jnp.where(first_lanes, norms, 0.0))
        key_top = jnp.max(jnp.where(first_lanes, 0.0, norms))
        safe = query_top * key_top * 1.05 <= 100.0 * 100.0
        bq = block_of(tokens, (1024, 768, 256))
        bk = block_of(tokens, (1024, 768, 256))

        @pl.when(safe)
        def _():
            top_s[...] = jnp.zeros_like(top_s)

        @pl.when(jnp.logical_not(safe))
        def _():
            def tops(qi, _):
                cols = pl.ds(pl.multiple_of(qi * bq, 256), bq)
                queries = q_s[cols, :]

                def more(ki, top):
                    scores = dot_nt(k_s[pl.ds(pl.multiple_of(ki * bk, 256), bk), :], queries)
                    return jnp.maximum(top, jnp.max(scores, axis=0, keepdims=True))

                top = lax.fori_loop(0, tokens // bk, more, jnp.full((1, bq), -jnp.inf, F32))
                top_s[:, cols] = jnp.broadcast_to(top, (8, bq))
                return 0

            lax.fori_loop(0, tokens // bq, tops, 0)

        parts = bq // KEPT
        steps = tokens // bq
        slots = min(steps, stage_s.shape[0] // tokens, 3)

        def stores(qi, first=0, rows=tokens):
            slot = lax.rem(qi, slots)
            return [
                pltpu.make_async_copy(
                    stage_s.at[pl.ds(pl.multiple_of(slot * tokens + first, 128), rows), pl.ds(part * KEPT, KEPT)],
                    kept_ref.at[pl.ds(pl.multiple_of((qi * parts + part) * (tokens + APART) + first, 16), rows)],
                    sems.at[slot, part],
                )
                for part in range(parts)
            ]

        def main(qi, _):
            cols = pl.ds(pl.multiple_of(qi * bq, 256), bq)
            queries = q_s[cols, :]
            top = top_s[0:1, cols]
            slot = lax.rem(qi, slots)

            @pl.when(qi >= slots)
            def _():
                for item in stores(qi - slots):
                    item.wait()

            total = jnp.zeros((80, bq), F32)
            for first in range(0, tokens, bk):
                scores = dot_nt(k_s[first : first + bk, :], queries)
                weights = jnp.exp2(scores - top).astype(BF)
                stage_s[pl.ds(pl.multiple_of(slot * tokens + first, 128), bk), :bq] = weights
                total = total + dot_nn(vt_s[0:80, first : first + bk], weights)
                for item in stores(qi, first, bk):
                    item.start()
            row_total = total[64:65]
            mixed = total[:64] / row_total
            extra = jnp.broadcast_to(1.0 / row_total, (64, bq))
            norm_ref[cols, :] = jnp.concatenate([mixed, extra], axis=0).T
            return 0

        lax.fori_loop(0, steps, main, 0)
        for qi in range(steps - slots, steps):
            for item in stores(qi):
                item.wait()

        def spread_band(band, _):
            rows = pl.ds(pl.multiple_of(band * own, 16), own)
            pairs = pack_pairs(norm_ref[rows, :], lanes)
            out_ref[band] = uncrop(pairs, width, side).astype(BF)
            return 0

        lax.fori_loop(0, used, spread_band, 0)
        if used < bands:
            out_ref[used:] = jnp.zeros((bands - used,) + out_ref.shape[1:], BF)

    for side in (width, width * 3 // 4, width // 2):
        pl.when(side_now == side)(partial(variant, side))


def attend(side, qkv, width, scale):
    bands, packed, _ = qkv.shape
    tokens = bands * packed * 2 // 3
    vm = pl.BlockSpec(memory_space=pltpu.VMEM)
    return pl.pallas_call(
        partial(attend_kernel, width, scale),
        out_shape=(
            jax.ShapeDtypeStruct((bands, packed // 3, 128), BF),
            jax.ShapeDtypeStruct((tokens, 128), F32),
            jax.ShapeDtypeStruct((tokens // KEPT * (tokens + APART), KEPT), BF),
        ),
        in_specs=[pl.BlockSpec(memory_space=pltpu.SMEM), vm],
        out_specs=(vm, vm, pl.BlockSpec(memory_space=pl.ANY)),
        scratch_shapes=[
            pltpu.VMEM((tokens, 128), BF),
            pltpu.VMEM((tokens, 128), BF),
            pltpu.VMEM((tokens, 128), BF),
            pltpu.VMEM((128, tokens), BF),
            pltpu.VMEM((8, tokens), F32),
            pltpu.VMEM((2 * tokens, 1024), BF),
            pltpu.SemaphoreType.DMA((3, 4)),
        ],
        compiler_params=pltpu.CompilerParams(vmem_limit_bytes=62 << 20),
        cost_estimate=pl.CostEstimate(
            flops=4 * 256 * tokens * tokens, bytes_accessed=8 << 20, transcendentals=tokens * tokens
        ),
        name="attend",
    )(side, qkv)


def attend_back_kernel(width, scale, side_ref, qkv_ref, grad_ref, norm_ref, kept_ref, out_ref,
                       k_s, g_s, gn_s, v_s, q_s, kt_s, dq_s, dkv_s, recip_s, stage_s, sems):
    bands, packed, _ = qkv_ref.shape
    band_tokens = packed * 2 // 3
    band_rows = band_tokens // width
    side_now = side_ref[0]

    def variant(side):
        tokens = side * side
        used = side // band_rows
        own = band_rows * side
        lanes = lane_ids(own)
        low = lanes < 64
        ones_high = jnp.where((lanes >= 64) & (lanes < 67), 1.0, 0.0)
        bq = block_of(tokens, (1024, 768, 256))
        bk = block_of(tokens, (512, 768, 256))
        parts = bq // KEPT
        steps = tokens // bq
        slots = min(steps, stage_s.shape[0] // tokens, 3)

        def loads(qi):
            slot = lax.rem(qi, slots)
            return [
                pltpu.make_async_copy(
                    kept_ref.at[pl.ds(pl.multiple_of((qi * parts + part) * (tokens + APART), 16), tokens)],
                    stage_s.at[pl.ds(pl.multiple_of(slot * tokens, 128), tokens), pl.ds(part * KEPT, KEPT)],
                    sems.at[slot, part],
                )
                for part in range(parts)
            ]

        ahead = steps if slots == steps else slots - 1
        for qi in range(ahead):
            for item in loads(qi):
                item.start()

        def gather_band(band, _):
            queries = unpack_pairs(crop(qkv_ref[band, band_tokens:, :].astype(F32), width, side))
            keys = crop(qkv_ref[band, :band_tokens, :].astype(F32), width, side)
            grads = unpack_pairs(crop(grad_ref[0, band].astype(F32), width, side))
            rows = pl.ds(pl.multiple_of(band * own, 16), own)
            mixed = norm_ref[rows, :]
            delta = jnp.sum(jnp.where(low, grads * mixed, 0.0), axis=1, keepdims=True)
            turned = swap_halves(keys)
            q_s[rows, :] = jnp.where(low, 0.0, swap_halves(queries)).astype(BF)
            gn_s[rows, :] = jnp.where(low, grads, 0.0).astype(BF)
            g_s[rows, :] = jnp.where(low, grads, extras(-delta, lanes, 64)).astype(BF)
            v_s[rows, :] = jnp.where(low, turned, ones_high).astype(BF)
            k_s[rows, :] = jnp.where(low, keys, 0.0).astype(BF)
            return 0

        lax.fori_loop(0, used, gather_band, 0)
        step = block_of(tokens, (512, 256))
        for first in range(0, tokens, step):
            kt_s[:, first : first + step] = k_s[first : first + step, :].T[:64]
            recip_s[:, first : first + step] = norm_ref[first : first + step, :].T[64:72]
        dkv_s[...] = jnp.zeros_like(dkv_s)

        def main(qi, _):
            cols = pl.ds(pl.multiple_of(qi * bq, 256), bq)
            slot = lax.rem(qi, slots)
            for item in loads(qi):
                item.wait()

            @pl.when(qi + ahead < steps)
            def _():
                for item in loads(qi + ahead):
                    item.start()

            grads = g_s[cols, :]
            plain = gn_s[cols, :]
            queries = q_s[cols, :]
            recip = recip_s[0:1, cols]
            total = jnp.zeros((64, bq), F32)
            for first in range(0, tokens, bk):
                lines = pl.ds(pl.multiple_of(slot * tokens + first, 128), bk)
                probs = stage_s[lines, :bq].astype(F32) * recip
                slopes = dot_nt(v_s[first : first + bk, :], grads)
                grad_scores = (probs * slopes).astype(BF)
                dkv_s[first : first + bk, :] += dot_nn(probs.astype(BF), plain) + dot_nn(grad_scores, queries)
                total = total + dot_nn(kt_s[:, first : first + bk], grad_scores)
            dq_s[:, cols] = total
            return 0

        lax.fori_loop(0, steps, main, 0)
        for first in range(0, tokens, step):
            turned = dq_s[:, first : first + step]
            v_s[first : first + step, :] = (
                jnp.concatenate([turned, turned], axis=0).T * scale
            ).astype(BF)

        def spread_band(band, _):
            rows = pl.ds(pl.multiple_of(band * own, 16), own)
            joint = swap_halves(dkv_s[rows, :])
            out_ref[band, :band_tokens] = uncrop(jnp.where(low, joint * scale, joint), width, side).astype(BF)
            pairs = pack_pairs(v_s[rows, :].astype(F32), lanes)
            out_ref[band, band_tokens:] = uncrop(pairs, width, side).astype(BF)
            return 0

        lax.fori_loop(0, used, spread_band, 0)
        if used < bands:
            out_ref[used:] = jnp.zeros((bands - used,) + out_ref.shape[1:], BF)

    for side in (width, width * 3 // 4, width // 2):
        pl.when(side_now == side)(partial(variant, side))


def attend_back(side, qkv, grads, spot, norms, kept, width, scale):
    bands, packed, _ = qkv.shape
    tokens = bands * packed * 2 // 3
    vm = pl.BlockSpec(memory_space=pltpu.VMEM)
    rows = pltpu.VMEM((tokens, 128), BF)
    return pl.pallas_call(
        partial(attend_back_kernel, width, scale),
        out_shape=jax.ShapeDtypeStruct((bands, packed, 128), BF),
        grid=(1,),
        in_specs=[
            pl.BlockSpec(memory_space=pltpu.SMEM),
            vm,
            pl.BlockSpec((1,) + grads.shape[1:], lambda at: (spot, 0, 0, 0)),
            vm,
            pl.BlockSpec(memory_space=pl.ANY),
        ],
        out_specs=vm,
        scratch_shapes=[rows] * 5
        + [
            pltpu.VMEM((64, tokens), BF),
            pltpu.VMEM((64, tokens), F32),
            pltpu.VMEM((tokens, 128), F32),
            pltpu.VMEM((8, tokens), F32),
            pltpu.VMEM((2 * tokens, 1024), BF),
            pltpu.SemaphoreType.DMA((3, 4)),
        ],
        compiler_params=pltpu.CompilerParams(vmem_limit_bytes=62 << 20),
        cost_estimate=pl.CostEstimate(
            flops=8 * 256 * tokens * tokens, bytes_accessed=40 << 20, transcendentals=0
        ),
        name="attend_back",
    )(side, qkv, grads, norms, kept)


def dot_tn(lhs, rhs):
    return lax.dot_general(lhs, rhs, (((0,), (0,)), ((), ())), preferred_element_type=F32)


def row_of(table, at):
    ids = lax.broadcasted_iota(jnp.int32, table.shape, 0)
    return jnp.sum(jnp.where(ids == at, table, 0.0), axis=0, keepdims=True)


def put_row(table_ref, at, row):
    ids = lax.broadcasted_iota(jnp.int32, table_ref.shape, 0)
    table_ref[...] = jnp.where(ids == at, row, table_ref[...])


def col_sum(field):
    return jnp.sum(field, axis=0, keepdims=True)


def vec(ref):
    return ref[...].astype(F32).reshape(1, -1)


def spread_lanes(tile, channels):
    return jnp.concatenate([tile] * (channels // 128), axis=1)


def token_ids(shape):
    return lax.broadcasted_iota(jnp.int32, (shape[0], 128), 0)


def pixel_inside(shape, first_row, side, width):
    token = token_ids(shape)
    row = first_row + lax.shift_right_logical(token, int(math.log2(width)))
    return spread_lanes((row >= 0) & (row < side) & ((token & (width - 1)) < side), shape[1])


def sigmoid(field):
    return 0.5 * jnp.tanh(0.5 * field) + 0.5


def moments(avg_ref, at):
    table = avg_ref[...]
    mean = row_of(table, 2 * at)
    return mean, lax.rsqrt(row_of(table, 2 * at + 1) - mean * mean + GN_EPS)


def put_taps(taps_s, first, field, width, flipped):
    channels = field.shape[1]
    column = token_ids(field.shape) & (width - 1)
    count = field.shape[0]
    left = jnp.where(spread_lanes(column == 0, channels), 0.0, pltpu.roll(field, 1, 0))
    right = jnp.where(spread_lanes(column == width - 1, channels), 0.0, pltpu.roll(field, count - 1, 0))
    order = (right, field, left) if flipped else (left, field, right)
    for at, part in enumerate(order):
        taps_s[first : first + count, at * channels : (at + 1) * channels] = part.astype(BF)


VMEM_WHOLE = pl.BlockSpec(memory_space=pltpu.VMEM)
SMEM_WHOLE = pl.BlockSpec(memory_space=pltpu.SMEM)


def image_block(tokens, channels):
    return pl.BlockSpec((1, tokens, channels), lambda at: (at, 0, 0))


def edge_block(width, channels):
    return pl.BlockSpec((2, 1, width, channels), lambda at: (0, at, 0, 0))


def table_block(channels, rows=8):
    return pl.BlockSpec((rows, channels), lambda at: (0, 0))


def vector_block(channels):
    return pl.BlockSpec((channels,), lambda at: (0,))


def fixed_block(shape):
    return pl.BlockSpec(shape, lambda at: (0,) * len(shape), pipeline_mode=pl.Buffered(1))


def greet_rows(me, bands):
    barrier = pltpu.get_barrier_semaphore()
    for away in range(1, bands):
        pl.semaphore_signal(
            barrier, inc=1, device_id={"rows": lax.rem(me + away, bands)},
            device_id_type=pl.DeviceIdType.MESH,
        )


def meet_rows(bands):
    pl.semaphore_wait(pltpu.get_barrier_semaphore(), bands - 1)


def row_copy(src, dst, send, recv, target):
    return pltpu.make_async_remote_copy(
        src_ref=src, dst_ref=dst, send_sem=send, recv_sem=recv, device_id={"rows": target},
        device_id_type=pl.DeviceIdType.MESH,
    )


def edge_copies(top, bottom, halo, at, send, recv, me, bands):
    return [
        row_copy(top, halo.at[1, at], send.at[0, at], recv.at[1, at], lax.rem(me + bands - 1, bands)),
        row_copy(bottom, halo.at[0, at], send.at[1, at], recv.at[0, at], lax.rem(me + 1, bands)),
    ]


def group_average(sums, weight_ref, sides, slots, send, recv, me, bands):
    slots[me] = sums
    copies = [
        row_copy(slots.at[me], slots.at[me], send.at[away], recv.at[me], lax.rem(me + away, bands))
        for away in range(1, bands)
    ]
    for item in copies:
        item.start()
    for away in range(1, bands):
        source = lax.rem(me + away, bands)
        row_copy(slots.at[source], slots.at[source], send.at[away], recv.at[source], source).wait_recv()
    total = slots[0]
    for at in range(1, bands):
        total = total + slots[at]
    for item in copies:
        item.wait_send()
    if weight_ref is not None:
        total = total * vec(weight_ref)
    image = lax.shift_right_logical(lax.broadcasted_iota(jnp.int32, total.shape, 0), 1)
    side = jnp.ones(total.shape, jnp.int32)
    for at in range(sides.shape[0]):
        side = jnp.where(image == at, sides[at], side)
    side = side.astype(F32)
    channels = total.shape[1]
    size = channels // GROUPS
    lane = lax.broadcasted_iota(jnp.int32, total.shape, 1)
    step = 1
    while step < size:
        total = total + jnp.where(
            (lane & step) == 0, pltpu.roll(total, channels - step, 1), pltpu.roll(total, step, 1)
        )
        step *= 2
    return total / (side * side * size)


def exchange_scratch(images, width, channels, bands):
    return [
        pltpu.VMEM((2, images, width, channels), BF),
        pltpu.VMEM((bands, 8, channels), F32),
        pltpu.SemaphoreType.DMA((2, images)),
        pltpu.SemaphoreType.DMA((2, images)),
        pltpu.SemaphoreType.DMA((bands,)),
        pltpu.SemaphoreType.DMA((bands,)),
    ]


def share_edges(grads, at, width, halo_ref, scratch, me, bands, met=False):
    edge_s, _, send, recv = scratch[:4]
    tokens = grads.shape[0]
    edge_s[0, at] = grads[:width].astype(BF)
    edge_s[1, at] = grads[tokens - width :].astype(BF)
    if not met:
        pl.when(at == 0)(partial(meet_rows, bands))
    for item in edge_copies(edge_s.at[0, at], edge_s.at[1, at], halo_ref, at, send, recv, me, bands):
        item.start()


def close_exchange(sums, weight_ref, sides, avg_ref, halo_ref, scratch, me, bands):
    edge_s, slots, send, recv, sum_send, sum_recv = scratch
    avg_ref[...] = group_average(sums, weight_ref, sides, slots, sum_send, sum_recv, me, bands)
    for at in range(edge_s.shape[1]):
        for item in edge_copies(
            edge_s.at[0, at], edge_s.at[1, at], halo_ref, at, send, recv, me, bands
        ):
            item.wait_send()
        for end in range(2):
            edge = halo_ref.at[end, at]
            row_copy(
                edge, edge, send.at[end, at], recv.at[end, at], lax.rem(me + 1, bands)
            ).wait_recv()


def begin_kernel(width, bands, place, sides, field_ref, whole_ref, avg_ref, halo_ref, sums_s, slots, send, recv, sum_send, sum_recv):
    at = pl.program_id(0)
    last = pl.num_programs(0) - 1
    me = lax.axis_index("rows")
    images, tokens, _ = whole_ref.shape

    def edges():
        return [
            edge_copies(
                whole_ref.at[image, pl.ds(0, width)], whole_ref.at[image, pl.ds(tokens - width, width)],
                halo_ref, image, send, recv, me, bands,
            )
            for image in range(images)
        ]

    @pl.when(at == 0)
    def _():
        greet_rows(me, bands)
        sums_s[...] = jnp.zeros_like(sums_s)

    @pl.when(at == 1)
    def _():
        meet_rows(bands)
        for pair in edges():
            for item in pair:
                item.start()

    field = field_ref[0].astype(F32)
    field = jnp.where(pixel_inside(field.shape, place[0], sides[at], width), field, 0.0)
    put_row(sums_s, 2 * at, col_sum(field))
    put_row(sums_s, 2 * at + 1, col_sum(field * field))

    @pl.when(at == last)
    def _():
        avg_ref[...] = group_average(
            sums_s[...], None, sides, slots, sum_send, sum_recv, me, bands
        )
        for image, pair in enumerate(edges()):
            for item in pair:
                item.wait_send()
            for end in range(2):
                edge = halo_ref.at[end, image]
                row_copy(
                    edge, edge, send.at[end, image], recv.at[end, image], lax.rem(me + 1, bands)
                ).wait_recv()


def begin(place, sides, field, width, bands):
    images, tokens, channels = field.shape
    anywhere = pl.BlockSpec(memory_space=pl.ANY)
    return pl.pallas_call(
        partial(begin_kernel, width, bands),
        grid=(images,),
        out_shape=(
            jax.ShapeDtypeStruct((8, channels), F32),
            jax.ShapeDtypeStruct((2, images, width, channels), BF),
        ),
        in_specs=[
            SMEM_WHOLE,
            SMEM_WHOLE,
            image_block(tokens, channels),
            anywhere,
        ],
        out_specs=(table_block(channels), anywhere),
        scratch_shapes=[pltpu.VMEM((8, channels), F32)]
        + exchange_scratch(images, width, channels, bands)[1:],
        compiler_params=pltpu.CompilerParams(collective_id=1, has_side_effects=True),
        name="begin",
    )(place, sides, field, field)


def conv_forward_kernel(width, bands, base_given, *refs):
    place, sides, field_ref, halo_ref, avg_ref, gain_ref, bias_ref, weight_ref, shift_ref = refs[:9]
    refs = refs[9:]
    if base_given:
        base_ref, refs = refs[0], refs[1:]
    out_ref, next_avg, next_halo = refs[:3]
    refs = refs[3:]
    taps_s, stats_ref = refs[:2]
    scratch = refs[2:]
    me = lax.axis_index("rows")
    at = pl.program_id(0)
    last = pl.num_programs(0) - 1

    @pl.when(at == 0)
    def _():
        greet_rows(me, bands)
        stats_ref[...] = jnp.zeros_like(stats_ref)

    _, tokens, channels = field_ref.shape
    first_row = place[0]
    side = sides[at]
    mean, inv_std = moments(avg_ref, at)
    slope = inv_std * vec(gain_ref)
    offset = vec(bias_ref) - mean * slope

    def active(field, row):
        normed = field.astype(F32) * slope + offset
        inside = pixel_inside(normed.shape, row, side, width)
        return jnp.where(inside, normed * sigmoid(normed), 0.0)

    rows = tokens // width
    put_taps(taps_s, 0, active(halo_ref[0, 0], first_row - 1), width, False)
    put_taps(taps_s, width, active(field_ref[0], first_row), width, False)
    put_taps(taps_s, width + tokens, active(halo_ref[1, 0], first_row + rows), width, False)
    deep = 3 * channels
    total = dot_nn(taps_s[:tokens], weight_ref[:deep])
    for tap in (1, 2):
        total = total + dot_nn(
            taps_s[tap * width : tap * width + tokens], weight_ref[tap * deep : (tap + 1) * deep]
        )
    total = total + row_of(shift_ref[...], at)
    inside = pixel_inside(total.shape, first_row, side, width)
    if base_given:
        total = total + jnp.where(inside, base_ref[0].astype(F32), 0.0)
    out_ref[0] = total
    share_edges(total, at, width, next_halo, scratch, me, bands)
    masked = jnp.where(inside, total, 0.0)
    put_row(stats_ref, 2 * at, col_sum(masked))
    put_row(stats_ref, 2 * at + 1, col_sum(masked * masked))

    @pl.when(at == last)
    def _():
        close_exchange(stats_ref[...], None, sides, next_avg, next_halo, scratch, me, bands)


def conv_forward(place, sides, field, halo, avg, gain, bias, weight, shift, base, width, bands):
    images, tokens, channels = field.shape
    added = base is not None
    tok = image_block(tokens, channels)
    return pl.pallas_call(
        partial(conv_forward_kernel, width, bands, added),
        grid=(images,),
        out_shape=(
            jax.ShapeDtypeStruct(field.shape, F32),
            jax.ShapeDtypeStruct((8, channels), F32),
            jax.ShapeDtypeStruct((2, images, width, channels), BF),
        ),
        in_specs=[
            SMEM_WHOLE,
            SMEM_WHOLE,
            tok,
            edge_block(width, channels),
            table_block(channels),
            vector_block(channels),
            vector_block(channels),
            fixed_block(weight.shape),
            table_block(channels),
        ]
        + ([tok] if added else []),
        out_specs=(tok, table_block(channels), pl.BlockSpec(memory_space=pl.ANY)),
        scratch_shapes=[
            pltpu.VMEM((tokens + 2 * width, 3 * channels), BF),
            pltpu.VMEM((8, channels), F32),
        ]
        + exchange_scratch(images, width, channels, bands),
        compiler_params=pltpu.CompilerParams(
            vmem_limit_bytes=62 << 20, collective_id=2 if added else 3, has_side_effects=True
        ),
        name="conv_forward",
    )(place, sides, field, halo, avg, gain, bias, weight, shift, *([base] if added else []))


class BandFold:
    def __init__(self, parts, scratch, me):
        self.parts, self.me = parts, me
        count = len(parts)
        self.own, self.pair, self.first, self.second_s = (
            scratch[at * count : (at + 1) * count] for at in range(4)
        )
        self.load, self.pair_send, self.pair_recv, self.hop_send, self.hop_recv = scratch[4 * count :]
        self.core, self.chip = lax.rem(me, 2), me // 2
        self.chunks = fold_chunks([part.shape for part in parts])

    def loads(self, which):
        size = self.parts[which].shape[0] // 8
        return [
            pltpu.make_async_copy(
                self.parts[which].at[pl.ds(pl.multiple_of((2 * spot + self.core) * size, 16), size)],
                self.own[which].at[spot],
                self.load.at[which, spot],
            )
            for spot in range(4)
        ]

    def pairs(self, which):
        size = self.parts[which].shape[0] // 8
        return [
            row_copy(
                self.parts[which].at[pl.ds(pl.multiple_of((2 * spot + 1 - self.core) * size, 16), size)],
                self.pair[which].at[spot],
                self.pair_send.at[which, spot],
                self.pair_recv.at[which, spot],
                self.me + 1 - 2 * self.core,
            )
            for spot in range(4)
        ]

    def hops(self, at):
        which, first, wide, one, two = self.chunks[at]
        cols = pl.ds(first, wide)
        near, far = jnp.bitwise_xor(self.chip, one), jnp.bitwise_xor(self.chip, two)

        def hop(spot, dst, step, chip):
            return row_copy(
                self.own[which].at[spot, :, cols], dst, self.hop_send.at[at, step], self.hop_recv.at[at, step],
                2 * chip + self.core,
            )

        return [
            hop(near, self.first[which].at[0, :, cols], 0, near),
            hop(jnp.bitwise_xor(near, two), self.first[which].at[1, :, cols], 1, near),
            hop(far, self.second_s[which].at[:, cols], 2, far),
        ]

    def start(self):
        for which in range(len(self.parts)):
            for item in self.loads(which) + self.pairs(which):
                item.start()

    def spread(self):
        for which in range(len(self.parts)):
            for item in self.loads(which):
                item.wait()
            for item in self.pairs(which):
                item.wait_recv()
            for spot in range(4):
                self.own[which][spot] = self.own[which][spot] + self.pair[which][spot]
        for at in range(len(self.chunks)):
            for item in self.hops(at)[:2]:
                item.start()

    def second(self):
        for at, (which, first, wide, _, two) in enumerate(self.chunks):
            cols = pl.ds(first, wide)
            for step, item in enumerate(self.hops(at)[:2]):
                item.wait()
                spot = jnp.bitwise_xor(self.chip, two) if step else self.chip
                self.own[which][spot, :, cols] = (
                    self.own[which][spot, :, cols] + self.first[which][step, :, cols]
                )
            self.hops(at)[2].start()

    def finish(self, outs):
        for at, (which, first, wide, _, _) in enumerate(self.chunks):
            cols = pl.ds(first, wide)
            self.hops(at)[2].wait()
            outs[which][:, cols] = self.own[which][self.chip, :, cols] + self.second_s[which][:, cols]
        for which in range(len(self.parts)):
            for item in self.pairs(which):
                item.wait_send()


def fold_chunks(shapes):
    total = sum(rows * cols for rows, cols in shapes)
    rows, cols = shapes[0]
    wide = (total // 2 // rows + 64) // 128 * 128
    chunks = [(0, 0, wide, 1, 2), (0, wide, cols - wide, 2, 1)]
    return chunks + [(at, 0, shape[1], 2, 1) for at, shape in enumerate(shapes) if at]


def fold_scratch(shapes):
    def bufs(lead):
        return [pltpu.VMEM(lead + (rows // 8, cols), BF) for rows, cols in shapes]

    chunks = len(fold_chunks(shapes))
    return (
        bufs((4,)) + bufs((4,)) + bufs((2,)) + bufs(())
        + [pltpu.SemaphoreType.DMA((len(shapes), 4))] * 3
        + [pltpu.SemaphoreType.DMA((chunks, 3))] * 2
    )


class GroupTree:
    def __init__(self, fields, outs, scratch, group):
        self.fields, self.outs, self.group = fields, outs, group
        count = len(fields)
        self.near_s, self.far_s = scratch[:count], scratch[count : 2 * count]
        self.send, self.recv = scratch[2 * count :]
        self.odd = lax.rem(group, 2)

    def half(self, which, odd):
        size = self.fields[which].shape[0] // 2
        return pl.ds(pl.multiple_of(odd * size, 16), size)

    def copies(self, which, step):
        mine, theirs = self.half(which, self.odd), self.half(which, 1 - self.odd)
        out = self.outs[which].at[mine]
        src, dst, bit = (
            (self.fields[which].at[theirs], self.near_s[which], 1),
            (self.fields[which].at[mine], self.far_s[which], 2),
            (out, out, 1),
        )[step]
        return pltpu.make_async_remote_copy(
            src_ref=src, dst_ref=dst, send_sem=self.send.at[which, step], recv_sem=self.recv.at[which, step],
            device_id={"heads": jnp.bitwise_xor(self.group, bit)}, device_id_type=pl.DeviceIdType.MESH,
        )

    def near(self):
        for which in range(len(self.fields)):
            self.copies(which, 0).start()

    def far(self):
        for which in range(len(self.fields)):
            mine = self.half(which, self.odd)
            self.copies(which, 0).wait()
            self.fields[which][mine] = (
                self.fields[which][mine].astype(F32) + self.near_s[which][...].astype(F32)
            ).astype(BF)
            self.copies(which, 1).start()

    def back(self):
        for which in range(len(self.fields)):
            mine = self.half(which, self.odd)
            self.copies(which, 1).wait()
            self.outs[which][mine] = (
                self.fields[which][mine].astype(F32) + self.far_s[which][...].astype(F32)
            ).astype(BF)
            self.copies(which, 2).start()

    def end(self):
        for which in range(len(self.fields)):
            self.copies(which, 2).wait_send()
            theirs = self.outs[which].at[self.half(which, 1 - self.odd)]
            pltpu.make_async_remote_copy(
                src_ref=theirs, dst_ref=theirs, send_sem=self.send.at[which, 2],
                recv_sem=self.recv.at[which, 2], device_id={"heads": jnp.bitwise_xor(self.group, 1)},
                device_id_type=pl.DeviceIdType.MESH,
            ).wait_recv()


def tree_scratch(shapes):
    return [pltpu.VMEM((rows // 2, cols), BF) for rows, cols in shapes] * 2 + [
        pltpu.SemaphoreType.DMA((len(shapes), 3))
    ] * 2


def conv_backward_kernel(width, bands, added, late, summed, *refs):
    refs = list(refs)
    late_refs, refs = refs[:late], refs[late:]
    summed_refs, refs = refs[:summed], refs[summed:]
    me = lax.axis_index("rows")
    (place, sides, grad_ref, grad_halo, field_ref, field_halo, avg_ref, back_avg, gain_ref) = refs[:9]
    refs = refs[9:]
    if added:
        add_ref, add_halo = refs[:2]
        refs = refs[2:]
    (weight_ref, prior_ref, prior_avg, prior_gain, prior_bias) = refs[:5]
    refs = refs[5:]
    late_outs, refs = refs[:late], refs[late:]
    summed_outs, refs = refs[:summed], refs[summed:]
    if added:
        kept_ref = refs[0]
        refs = refs[1:]
    out_ref, next_avg, stats_ref, sums_ref, weight_grad = refs[:5]
    next_halo = None
    if added:
        next_halo = refs[5]
        refs = refs[1:]
    taps_s, act_s, total_s = refs[5:8]
    scratch = refs[8:]
    if late:
        base = 6 if added else 3
        after = base + 4 * late + 5
        fold = BandFold(late_refs, scratch[base:after], me)
        if summed:
            fields, made = scratch[after : after + summed], scratch[after + summed : after + 2 * summed]
            group = lax.axis_index("heads")
            tree = GroupTree(fields, made, scratch[after + 2 * summed :], group)
        scratch = scratch[:base]
    at = pl.program_id(0)
    last = pl.num_programs(0) - 1
    _, tokens, channels = grad_ref.shape
    first_row = place[0]
    side = sides[at]
    mean, inv_std = moments(avg_ref, at)
    back = back_avg[...]
    back_mean, back_cross = row_of(back, 2 * at), row_of(back, 2 * at + 1)
    gain = vec(gain_ref)
    grad_slope = inv_std * gain
    field_slope = inv_std * inv_std * back_cross
    offset = inv_std * back_mean - mean * field_slope

    def through(grads, field, extra, row):
        moved = grads.astype(F32) * grad_slope - field.astype(F32) * field_slope - offset
        if extra is not None:
            moved = moved + extra.astype(F32)
        return jnp.where(pixel_inside(moved.shape, row, side, width), moved, 0.0)

    rows = tokens // width
    own = through(grad_ref[0], field_ref[0], add_ref[0] if added else None, first_row)
    put_taps(taps_s, width, own, width, True)
    for end, row, first in ((0, first_row - 1, 0), (1, first_row + rows, width + tokens)):
        put_taps(
            taps_s,
            first,
            through(grad_halo[end, 0], field_halo[end, 0], add_halo[end, 0] if added else None, row),
            width,
            True,
        )
    if added:
        kept_ref[0] = own

    @pl.when(at == 0)
    def _():
        greet_rows(me, bands)
        stats_ref[...] = jnp.zeros_like(stats_ref)
        sums_ref[...] = jnp.zeros_like(sums_ref)
        if summed:
            for bit in (1, 2):
                pl.semaphore_signal(
                    pltpu.get_barrier_semaphore(), inc=1, device_id={"heads": jnp.bitwise_xor(group, bit)},
                    device_id_type=pl.DeviceIdType.MESH,
                )
            for field, ref in zip(fields, summed_refs):
                field[...] = ref[...]
        if late:
            meet_rows(bands + 2 if summed else bands)
            fold.start()
        if summed:
            tree.near()
        total_s[...] = jnp.zeros_like(total_s)

    put_row(sums_ref, at, col_sum(own))
    prior_mean, prior_std = moments(prior_avg, at)
    centred = (prior_ref[0].astype(F32) - prior_mean) * prior_std
    normed = centred * vec(prior_gain) + vec(prior_bias)
    gate = sigmoid(normed)
    inside = pixel_inside(normed.shape, first_row, side, width)
    act_s[...] = jnp.where(inside, normed * gate, 0.0).astype(BF).T
    act_t = act_s[...]
    moved = None
    for down in range(3):
        lines = pl.ds((2 - down) * width, tokens)
        for across in range(3):
            tap = 3 * down + across
            low = taps_s[lines, across * channels : (across + 1) * channels]
            part = slice(tap * channels, (tap + 1) * channels)
            term = dot_nt(low, weight_ref[part])
            moved = term if moved is None else moved + term
            total_s[part] += dot_nn(act_t, low)
    if late:
        pl.when(at == 0)(fold.spread)
        pl.when(at == 2)(fold.second)
    if summed:
        pl.when(at == 1)(tree.far)
        pl.when(at == 2)(tree.back)
    grads = jnp.where(inside, moved * (gate + normed * gate * (1.0 - gate)), 0.0)
    out_ref[0] = grads
    if added:
        share_edges(grads, at, width, next_halo, scratch, me, bands, late > 0)
    put_row(stats_ref, 2 * at, col_sum(grads))
    put_row(stats_ref, 2 * at + 1, col_sum(grads * centred))

    @pl.when(at == last)
    def _():
        if late:
            fold.finish(late_outs)
        if summed:
            tree.end()
            for out, field in zip(summed_outs, made):
                out[...] = field[...]
        if added:
            close_exchange(stats_ref[...], prior_gain, sides, next_avg, next_halo, scratch, me, bands)
        else:
            if not late:
                meet_rows(bands)
            next_avg[...] = group_average(stats_ref[...], prior_gain, sides, *scratch, me, bands)
        weight_grad[...] = total_s[...].astype(BF)


def conv_backward(place, sides, grads, grad_halo, field, field_halo, avg, back_avg, gain, extra,
                  extra_halo, weight, prior, prior_avg, prior_gain, prior_bias, late, summed, width, bands):
    images, tokens, channels = grads.shape
    added = extra is not None
    tok = image_block(tokens, channels)
    edge = edge_block(width, channels)
    table = table_block(channels)
    vector = vector_block(channels)
    anywhere = pl.BlockSpec(memory_space=pl.ANY)
    ins = [*late, *summed, place, sides, grads, grad_halo, field, field_halo, avg, back_avg, gain]
    specs = [anywhere] * len(late) + [fixed_block(part.shape) for part in summed] + [SMEM_WHOLE, SMEM_WHOLE, tok, edge, tok, edge, table, table, vector]
    if added:
        ins += [extra, extra_halo]
        specs += [tok, edge]
    ins += [weight, prior, prior_avg, prior_gain, prior_bias]
    specs += [fixed_block(weight.shape), tok, table, vector, vector]
    outs = [
        jax.ShapeDtypeStruct(grads.shape, F32),
        jax.ShapeDtypeStruct((8, channels), F32),
        jax.ShapeDtypeStruct((8, channels), F32),
        jax.ShapeDtypeStruct((8, channels), F32),
        jax.ShapeDtypeStruct(weight.shape, BF),
    ]
    out_specs = [tok, table, table, table, fixed_block(weight.shape)]
    if added:
        outs.append(jax.ShapeDtypeStruct((2, images, width, channels), BF))
        out_specs.append(pl.BlockSpec(memory_space=pl.ANY))
        outs.insert(0, jax.ShapeDtypeStruct(grads.shape, F32))
        out_specs.insert(0, tok)
    shapes = [(part.shape[0] // 8, part.shape[1]) for part in late] + [part.shape for part in summed]
    outs = [jax.ShapeDtypeStruct(shape, BF) for shape in shapes] + outs
    out_specs = [fixed_block(shape) for shape in shapes] + out_specs
    return pl.pallas_call(
        partial(conv_backward_kernel, width, bands, added, len(late), len(summed)),
        grid=(images,),
        out_shape=outs,
        in_specs=specs,
        out_specs=out_specs,
        scratch_shapes=[
            pltpu.VMEM((tokens + 2 * width, 3 * channels), BF),
            pltpu.VMEM((channels, tokens), BF),
            pltpu.VMEM(weight.shape, F32),
        ]
        + (
            exchange_scratch(images, width, channels, bands)
            if added
            else [
                pltpu.VMEM((bands, 8, channels), F32),
                pltpu.SemaphoreType.DMA((bands,)),
                pltpu.SemaphoreType.DMA((bands,)),
            ]
        )
        + (fold_scratch([part.shape for part in late]) if late else [])
        + [pltpu.VMEM(part.shape, BF) for part in (*summed, *summed)]
        + (tree_scratch([part.shape for part in summed]) if summed else []),
        compiler_params=pltpu.CompilerParams(
            vmem_limit_bytes=62 << 20, collective_id=4 if added else 6, has_side_effects=True
        ),
        name="conv_backward",
    )(*ins)


def layer_stats(field):
    centre = jnp.mean(field, axis=-1, keepdims=True)
    centred = field - centre
    inv_std = lax.rsqrt(jnp.mean(centred * centred, axis=-1, keepdims=True) + LN_EPS)
    return centred * inv_std, inv_std


def layer_back(grads, gain, centred, inv_std):
    scaled = grads * gain
    return inv_std * (
        scaled
        - jnp.mean(scaled, axis=-1, keepdims=True)
        - centred * jnp.mean(scaled * centred, axis=-1, keepdims=True)
    )


def turn_qkv(weight_ref, turned_s):
    rows, channels = weight_ref.shape[0], weight_ref.shape[1] // 3
    low = lane_ids(rows) < 64
    for head in range(HEADS):
        first = (head // 2) * 128
        keys = weight_ref[:, channels + first : channels + first + 128].astype(F32)
        values = weight_ref[:, 2 * channels + first : 2 * channels + first + 128].astype(F32)
        if head % 2 == 0:
            joint = jnp.where(low, keys, swap_halves(values))
        else:
            joint = jnp.where(low, swap_halves(keys), values)
        turned_s[:, head * 128 : head * 128 + 128] = joint.astype(BF)
    turned_s[:, 2 * channels :] = weight_ref[:, :channels]


def entry_kernel(bands, direct, field_ref, avg_ref, gain_ref, bias_ref, proj_ref, proj_bias, ln_gain,
                 ln_bias, qkv_ref, stream_ref, *refs):
    images = pl.num_programs(0)
    at = pl.program_id(0)
    if direct:
        count = len(refs) - 4
        sent_refs, (turned_s, first_s, send, recv) = refs[:count], refs[count:]
        me = lax.axis_index("rows")
    else:
        sent_refs, turned_s = refs[:-1], refs[-1]
    _, tokens, channels = field_ref.shape
    half = tokens // 2

    @pl.when(at == 0)
    def _():
        if direct:
            greet_rows(me, bands)
        turn_qkv(qkv_ref, turned_s)

    mean, inv_std = moments(avg_ref, at)
    slope = inv_std * vec(gain_ref)
    flat = (field_ref[0] * slope + (vec(bias_ref) - mean * slope)).astype(BF)
    stream = dot_nn(flat, proj_ref[...]) + vec(proj_bias)
    stream_ref[0] = stream
    centred, _ = layer_stats(stream)
    joint = dot_nn((centred * vec(ln_gain) + vec(ln_bias)).astype(BF), turned_s[...])
    low = lane_ids(half) < 64

    def put(out):
        for head in range(HEADS):
            out[head, :tokens] = joint[:, head * 128 : head * 128 + 128].astype(BF)
            first = 2 * channels + (head // 2) * 128
            upper, lower = joint[:half, first : first + 128], joint[half:, first : first + 128]
            if head % 2 == 0:
                pairs = jnp.where(low, upper, swap_halves(lower))
            else:
                pairs = jnp.where(low, swap_halves(upper), lower)
            out[head, tokens:] = pairs.astype(BF)

    for image, out in enumerate(sent_refs):
        pl.when(at == image)(partial(put, first_s if direct and image == 0 else out))
    if not direct:
        return
    copies = [
        row_copy(
            first_s.at[lax.rem(me + away, bands)], sent_refs[0].at[me], send.at[away], recv.at[me],
            lax.rem(me + away, bands),
        )
        for away in range(1, bands)
    ]
    own = pltpu.make_async_copy(first_s.at[me], sent_refs[0].at[me], recv.at[me])

    @pl.when(at == 0)
    def _():
        meet_rows(bands)
        for item in copies:
            item.start()
        own.start()

    @pl.when(at == images - 1)
    def _():
        own.wait()
        for away, item in enumerate(copies):
            item.wait_send()
            source = lax.rem(me + away + 1, bands)
            row_copy(
                sent_refs[0].at[source], sent_refs[0].at[source], send.at[away + 1], recv.at[source], source
            ).wait_recv()


def entry(field, avg, gain, bias, proj, proj_bias, ln_gain, ln_bias, qkv, bands):
    images, tokens, channels = field.shape
    vector = vector_block(channels)
    direct = bands == HEADS
    packed = (HEADS, tokens * 3 // 2, 128)
    anywhere = pl.BlockSpec(memory_space=pl.ANY)
    params = {"collective_id": 9, "has_side_effects": True} if direct else {}
    return pl.pallas_call(
        partial(entry_kernel, bands, direct),
        grid=(images,),
        out_shape=(jax.ShapeDtypeStruct(field.shape, F32),)
        + (jax.ShapeDtypeStruct(packed, BF),) * images,
        in_specs=[
            image_block(tokens, channels),
            table_block(channels),
            vector,
            vector,
            fixed_block(proj.shape),
            vector,
            vector,
            vector,
            fixed_block(qkv.shape),
        ],
        out_specs=(image_block(tokens, channels),)
        + ((anywhere,) if direct else (fixed_block(packed),))
        + (fixed_block(packed),) * (images - 1),
        scratch_shapes=[pltpu.VMEM(qkv.shape, BF)]
        + (
            [
                pltpu.VMEM(packed, BF),
                pltpu.SemaphoreType.DMA((bands,)),
                pltpu.SemaphoreType.DMA((bands,)),
            ]
            if direct
            else []
        ),
        compiler_params=pltpu.CompilerParams(vmem_limit_bytes=62 << 20, **params),
        name="entry",
    )(field, avg, gain, bias, proj, proj_bias, ln_gain, ln_bias, qkv)


def join_heads(pairs_ref, at):
    half = pairs_ref.shape[-2]
    low = lane_ids(half) < 64
    upper, lower = [], []
    for head in range(0, HEADS, 2):
        one, two = pairs_ref[at, head].astype(F32), pairs_ref[at, head + 1].astype(F32)
        upper.append(jnp.where(low, one, swap_halves(two)))
        lower.append(jnp.where(low, swap_halves(one), two))
    return jnp.concatenate(
        [jnp.concatenate(upper, axis=1), jnp.concatenate(lower, axis=1)], axis=0
    ).astype(BF)


def split_heads(field, out_ref, at):
    half = field.shape[0] // 2
    low = lane_ids(half) < 64
    for head in range(HEADS):
        first = (head // 2) * 128
        upper, lower = field[:half, first : first + 128], field[half:, first : first + 128]
        if head % 2 == 0:
            pairs = jnp.where(low, upper, swap_halves(lower))
        else:
            pairs = jnp.where(low, swap_halves(upper), lower)
        out_ref[at, head] = pairs.astype(BF)


def feed_pieces(channels, wide, hidden, bands):
    size = channels // bands
    geglu = [(at * size, size) for at in range(wide // channels)]
    first = wide // bands
    return (
        geglu,
        [(first, hidden // bands)],
        [(first + hidden // bands, size)],
        [(first + hidden // bands + size, size)],
    )


def feed_kernel(width, bands, per_band, halving, place, sides, *refs):
    given, refs = refs[:per_band], refs[per_band:]
    cot_hbm, refs = refs[0], refs[1:]
    count = 4 if halving else 1
    grads_ref, refs = refs[18 : 18 + count], refs[:18] + refs[18 + count :]
    (stream_ref, residual_ref, cot_ref, cross_ref, attn_ref, attn_bias, ln_gain, ln_bias,
     geglu_hbm, geglu_bias, feed_hbm, feed_bias, proj_ref, proj_bias,
     out_ref, three_ref, back_ref, ride_halo, sums_ref, cross_sum, pair_sums, geglu_s, feed_s, proj_s, attn_s,
     geglu_ref, feed_ref, weight_sems, ride_send, ride_recv, turned_s, mixed_s, sent_s, out_send, out_recv, back_send, back_recv, *more) = refs
    if halving:
        given_s, taken_s, pair_sems = more
    at = pl.program_id(0)
    images = pl.num_programs(0)
    last = images - 1
    me = lax.axis_index("rows")

    def move(src, dst, send, recv, target):
        @pl.when(target != me)
        def _():
            pltpu.make_async_remote_copy(
                src_ref=src, dst_ref=dst, send_sem=send, recv_sem=recv, device_id={"rows": target},
                device_id_type=pl.DeviceIdType.MESH,
            ).start()

        @pl.when(target == me)
        def _():
            pltpu.make_async_copy(src, dst, recv).start()

    def arrived(dst, send, recv, source):
        @pl.when(source != me)
        def _():
            pltpu.make_async_remote_copy(
                src_ref=dst, dst_ref=dst, send_sem=send, recv_sem=recv, device_id={"rows": source},
                device_id_type=pl.DeviceIdType.MESH,
            ).wait_recv()

        @pl.when(source == me)
        def _():
            pltpu.make_async_copy(dst, dst, recv).wait()

    def left(src, send, recv, target):
        @pl.when(target != me)
        def _():
            pltpu.make_async_remote_copy(
                src_ref=src, dst_ref=src, send_sem=send, recv_sem=recv, device_id={"rows": target},
                device_id_type=pl.DeviceIdType.MESH,
            ).wait_send()

    def send_spot(spot):
        item = me * per_band + spot
        head, image = item // images, lax.rem(item, images)
        for away in range(bands):
            band = lax.rem(me + away, bands)
            move(
                given[spot].at[band], mixed_s.at[image, head], out_send.at[spot, away],
                out_recv.at[image, head], band,
            )

    loads = [
        pltpu.make_async_copy(src, dst, weight_sems.at[spot])
        for spot, (src, dst) in enumerate(((geglu_hbm, geglu_ref), (feed_hbm, feed_ref)))
    ]

    @pl.when(at == 0)
    def _():
        greet_rows(me, bands)
        meet_rows(bands)
        send_spot(0)
        for item in loads:
            item.start()

    for head in range(HEADS):
        arrived(
            mixed_s.at[at, head], out_send.at[0, 0], out_recv.at[at, head], (head * images + at) // per_band
        )
    @pl.when(at == 0)
    def _():
        for item in loads:
            item.wait()

    def ride(image):
        below = cot_hbm.shape[1] - width
        return edge_copies(
            cot_hbm.at[image, pl.ds(0, width)], cot_hbm.at[image, pl.ds(below, width)], ride_halo, image,
            ride_send, ride_recv, me, bands,
        )

    @pl.when(at == images - 1)
    def _():
        for image in range(sent_s.shape[0]):
            for item in ride(image):
                item.start()

    for spot in range(1, per_band):
        pl.when(at == spot - 1)(partial(send_spot, spot))
    _, tokens, channels = stream_ref.shape
    hidden = feed_ref.shape[0]
    side = sides[at]
    inside = pixel_inside((tokens, channels), place[0], side, width)

    @pl.when(at == 0)
    def _():
        for ref in (sums_ref, cross_sum, pair_sums, geglu_s, feed_s, proj_s, attn_s):
            ref[...] = jnp.zeros_like(ref)

    mixed = join_heads(mixed_s, at)
    three = stream_ref[0] + dot_nn(mixed, attn_ref[...]) + (vec(attn_bias) + row_of(cross_ref[...], at))
    centred, inv_std = layer_stats(three)
    feed_in = (centred * vec(ln_gain) + vec(ln_bias)).astype(BF)
    grad_out = jnp.where(inside, cot_ref[0].astype(F32), 0.0)
    branch = grad_out.astype(BF)
    grad_four = dot_nt(branch, proj_ref[...])
    low_feed = grad_four.astype(BF)
    low_feed_t = low_feed.T
    feed_in_t = feed_in.T
    four = three + vec(feed_bias)
    grad_in = jnp.zeros((tokens, channels), F32)
    step = 512

    pair_bias = vec(geglu_bias)

    def products(first):
        own = slice(first, first + step)
        gates = slice(hidden + first, hidden + first + step)
        value = dot_nn(feed_in, geglu_ref[:, own]) + pair_bias[:, own]
        gate = dot_nn(feed_in, geglu_ref[:, gates]) + pair_bias[:, gates]
        return value, gate, dot_nt(low_feed, feed_ref[own])

    ahead = products(0)
    for first in range(0, hidden, step):
        own = slice(first, first + step)
        gates = slice(hidden + first, hidden + first + step)
        value, gate, back = ahead
        if first + step < hidden:
            ahead = products(first + step)
        below = 0.5 + 0.5 * lax.erf(gate * math.sqrt(0.5))
        bell = jnp.exp(gate * gate * -0.5) * (1.0 / math.sqrt(2.0 * math.pi))
        act = gate * below
        gated = (value * act).astype(BF)
        four = four + dot_nn(gated, feed_ref[own])
        feed_s[:, own] += dot_nn(low_feed_t, gated)
        grad_value = back * act
        grad_gate = back * value * (below + gate * bell)
        pair_sums[:, own] += col_sum(grad_value)
        pair_sums[:, gates] += col_sum(grad_gate)
        low_value, low_gate = grad_value.astype(BF), grad_gate.astype(BF)
        geglu_s[:, own] += dot_nn(feed_in_t, low_value)
        geglu_s[:, gates] += dot_nn(feed_in_t, low_gate)
        grad_in = grad_in + dot_nt(low_value, geglu_ref[:, own]) + dot_nt(low_gate, geglu_ref[:, gates])
    last_in = four.astype(BF)
    proj_s[...] += dot_tn(last_in, branch)
    output = residual_ref[0] + dot_nn(last_in, proj_ref[...]) + vec(proj_bias)
    out_ref[0] = jnp.where(inside, output, 0.0).astype(BF)
    grad_three = grad_four + layer_back(grad_in, vec(ln_gain), centred, inv_std)
    three_ref[0] = grad_three
    low_attn = grad_three.astype(BF)
    attn_s[...] += dot_tn(mixed, low_attn)
    split_heads(dot_nt(low_attn, attn_ref[...]), sent_s, at)
    for head in range(HEADS):
        item = head * images + at
        move(
            sent_s.at[at, head], back_ref.at[lax.rem(item, per_band), me], back_send.at[at, head],
            back_recv.at[lax.rem(item, per_band), me], item // per_band,
        )
    put_row(cross_sum, at, col_sum(grad_three))
    ids = lax.broadcasted_iota(jnp.int32, sums_ref.shape, 0)
    for row, total in enumerate(
        (col_sum(grad_out), col_sum(grad_four), col_sum(grad_in * centred), col_sum(grad_in))
    ):
        sums_ref[...] += jnp.where(ids == row, total, 0.0)

    @pl.when(at == last)
    def _():
        def settle():
            for image in range(sent_s.shape[0]):
                for item in ride(image):
                    item.wait_send()
                for end in range(2):
                    edge = ride_halo.at[end, image]
                    row_copy(
                        edge, edge, ride_send.at[end, image], ride_recv.at[end, image],
                        lax.rem(me + 1, bands),
                    ).wait_recv()
            for spot in range(per_band):
                for away in range(bands):
                    band = lax.rem(me + away, bands)
                    left(given[spot].at[band], out_send.at[spot, away], out_recv.at[0, 0], band)
                    arrived(back_ref.at[spot, band], back_send.at[0, 0], back_recv.at[spot, band], band)
            for image in range(sent_s.shape[0]):
                for head in range(HEADS):
                    left(
                        sent_s.at[image, head], back_send.at[image, head], back_recv.at[0, 0],
                        (head * sent_s.shape[0] + image) // per_band,
                    )

        pieces = feed_pieces(channels, 2 * hidden, hidden, bands)

        def put(place_of, band):
            for total, parts in zip((geglu_s, feed_s, proj_s, attn_s), pieces):
                for at_col, (first, size) in enumerate(parts):
                    if total is feed_s:
                        part = turned_s[pl.ds(pl.multiple_of(band * size, 16), size)]
                    else:
                        part = total[
                            pl.ds(pl.multiple_of(band * size, 16), size),
                            at_col * channels : (at_col + 1) * channels,
                        ]
                    ref, own, skip = place_of(first)
                    ref[own + (pl.ds(first - skip, size),)] = part.astype(BF)

        for first in range(0, hidden, step):
            turned_s[first : first + step, :] = feed_s[:, first : first + step].T.astype(BF)

        if not halving:
            for band in range(bands):
                put(lambda first, band=band: (grads_ref[0], (band,), 0), band)
            settle()
            return
        rows = given_s.shape[-2] // 2
        for apart in range(bands // 2):
            own = (apart & 1, apart >> 1)
            put(lambda first, own=own: (given_s, own, 0), jnp.bitwise_xor(me, 2 * apart + 1))
        item = row_copy(given_s, taken_s, pair_sems.at[0], pair_sems.at[1], jnp.bitwise_xor(me, 1))
        item.start()
        for apart in range(bands // 2):
            over_x, over_y = apart & 1, apart >> 1

            def half(first, over_x=over_x, over_y=over_y):
                return (
                    (grads_ref[over_x], (over_y,), 0)
                    if first < rows
                    else (grads_ref[2 + over_y], (over_x,), rows)
                )

            put(half, jnp.bitwise_xor(me, 2 * apart))
        item.wait()
        for apart in range(bands // 2):
            over_x, over_y = apart & 1, apart >> 1
            for ref, spot, lines in (
                (grads_ref[over_x], over_y, slice(0, rows)),
                (grads_ref[2 + over_y], over_x, slice(rows, 2 * rows)),
            ):
                ref[spot] = (ref[spot].astype(F32) + taken_s[over_x, over_y, lines].astype(F32)).astype(BF)
        settle()


def feed(place, sides, mixed, stream, residual, cot, cross, attn, attn_bias, ln_gain, ln_bias, geglu,
         geglu_bias, feed_out, feed_bias, proj, proj_bias, width, bands, halving):
    images, tokens, channels = stream.shape
    tok = image_block(tokens, channels)
    vector = vector_block(channels)
    table = table_block(channels)
    half = tokens // 2
    per_band = len(mixed)
    anywhere = pl.BlockSpec(memory_space=pl.ANY)
    wide = geglu.shape[1]
    weights = (geglu, feed_out, proj, attn)
    rows = sum(w.size for w in weights) // channels // bands
    lead = (2, 2) if halving else (bands,)
    grads = lead + (rows, channels)
    given = [(2, rows // 2, channels)] * 4 if halving else [grads]
    return pl.pallas_call(
        partial(feed_kernel, width, bands, per_band, halving),
        grid=(images,),
        out_shape=(
            jax.ShapeDtypeStruct(stream.shape, BF),
            jax.ShapeDtypeStruct(stream.shape, F32),
            jax.ShapeDtypeStruct((per_band, bands, half, 128), BF),
            jax.ShapeDtypeStruct((2, images, width, channels), BF),
        )
        + tuple(jax.ShapeDtypeStruct(shape, BF) for shape in given)
        + (
            jax.ShapeDtypeStruct((8, channels), F32),
            jax.ShapeDtypeStruct((8, channels), F32),
            jax.ShapeDtypeStruct((1, wide), F32),
        ),
        in_specs=[
            SMEM_WHOLE,
            SMEM_WHOLE,
        ]
        + [anywhere] * (per_band + 1)
        + [
            tok,
            tok,
            tok,
            table,
            fixed_block(attn.shape),
            vector,
            vector,
            vector,
            anywhere,
            vector_block(wide),
            anywhere,
            vector,
            fixed_block(proj.shape),
            vector,
        ],
        out_specs=(tok, tok, anywhere, anywhere)
        + tuple(fixed_block(shape) for shape in given)
        + (table, table, table_block(wide, 1)),
        scratch_shapes=[
            pltpu.VMEM(geglu.shape, F32),
            pltpu.VMEM(feed_out.shape[::-1], F32),
            pltpu.VMEM(proj.shape, F32),
            pltpu.VMEM(attn.shape, F32),
            pltpu.VMEM(geglu.shape, BF),
            pltpu.VMEM(feed_out.shape, BF),
            pltpu.SemaphoreType.DMA((2,)),
            pltpu.SemaphoreType.DMA((2, images)),
            pltpu.SemaphoreType.DMA((2, images)),
            pltpu.VMEM(feed_out.shape, BF),
        ]
        + [pltpu.VMEM((images, HEADS, half, 128), BF)] * 2
        + [
            pltpu.SemaphoreType.DMA((per_band, bands)),
            pltpu.SemaphoreType.DMA((images, HEADS)),
            pltpu.SemaphoreType.DMA((images, HEADS)),
            pltpu.SemaphoreType.DMA((per_band, bands)),
        ]
        + ([pltpu.VMEM(grads, BF)] * 2 + [pltpu.SemaphoreType.DMA((2,))] if halving else []),
        compiler_params=pltpu.CompilerParams(
            vmem_limit_bytes=62 << 20, collective_id=5, has_side_effects=True
        ),
        name="feed",
    )(place, sides, *mixed, cot, stream, residual, cot, cross, attn, attn_bias, ln_gain, ln_bias, geglu,
      geglu_bias, feed_out, feed_bias, proj, proj_bias)


def leave_kernel(width, bands, images, place, sides, *refs):
    direct = bands == HEADS
    if direct:
        *arrays, raw_ref = refs[:images]
        refs = refs[images:]
    else:
        packed_ref, refs = refs[0], refs[1:]
    (stream_ref, three_ref, field_ref, avg_ref, gain_ref, bias_ref, proj_ref, ln_gain, ln_bias,
     qkv_ref, out_ref, next_avg, next_halo, stats_ref, sums_ref, grad_qkv, grad_proj, qkv_s,
     proj_s, turned_s) = refs[:20]
    scratch = refs[20:26]
    me = lax.axis_index("rows")
    at = pl.program_id(0)
    last = pl.num_programs(0) - 1
    _, tokens, channels = stream_ref.shape
    inside = pixel_inside((tokens, channels), place[0], sides[at], width)

    @pl.when(at == 0)
    def _():
        greet_rows(me, bands)
        for ref in (stats_ref, sums_ref, qkv_s, proj_s):
            ref[...] = jnp.zeros_like(ref)
        turn_qkv(qkv_ref, turned_s)

    if direct:
        item_s, last_s, item_sems, last_send, last_recv = refs[26:]
        fetch = [
            pltpu.make_async_copy(array, item_s.at[image % 2], item_sems.at[image % 2])
            for image, array in enumerate(arrays)
        ]
        send_last = [
            row_copy(
                raw_ref.at[lax.rem(me + away, bands)], last_s.at[me], last_send.at[away], last_recv.at[me],
                lax.rem(me + away, bands),
            )
            for away in range(1, bands)
        ]
        keep_last = pltpu.make_async_copy(raw_ref.at[me], last_s.at[me], last_recv.at[me])

        @pl.when(at == 0)
        def _():
            fetch[0].start()
            meet_rows(bands)
            for item in send_last:
                item.start()
            keep_last.start()

        for image in range(len(fetch)):

            @pl.when(at == image)
            def _(image=image):
                if image + 1 < len(fetch):
                    fetch[image + 1].start()
                fetch[image].wait()

        @pl.when(at == last)
        def _():
            keep_last.wait()
            for away in range(1, bands):
                source = lax.rem(me + away, bands)
                row_copy(
                    last_s.at[source], last_s.at[source], last_send.at[away], last_recv.at[source], source
                ).wait_recv()
            item_s[(images - 1) % 2] = last_s[...]
            for item in send_last:
                item.wait_send()

        packed_ref, spot = item_s, lax.rem(at, 2)
    else:
        spot = 0
    queries = join_heads(packed_ref.at[:, :, tokens:, :], spot)
    joint = jnp.concatenate([packed_ref[spot, head, :tokens] for head in range(HEADS)] + [queries], axis=1)
    centred, inv_std = layer_stats(stream_ref[0])
    attn_in = (centred * vec(ln_gain) + vec(ln_bias)).astype(BF)
    qkv_s[...] += dot_tn(attn_in, joint)
    grads = dot_nt(joint, turned_s[...])
    grad_stream = three_ref[0] + layer_back(grads, vec(ln_gain), centred, inv_std)
    low_in = grad_stream.astype(BF)
    mean, deviation = moments(avg_ref, at)
    normed = (field_ref[0] - mean) * deviation
    flat = (normed * vec(gain_ref) + vec(bias_ref)).astype(BF)
    proj_s[...] += dot_tn(flat, low_in)
    moved = jnp.where(inside, dot_nt(low_in, proj_ref[...]), 0.0)
    out_ref[0] = moved
    share_edges(moved, at, width, next_halo, scratch, me, bands, direct)
    put_row(stats_ref, 2 * at, col_sum(moved))
    put_row(stats_ref, 2 * at + 1, col_sum(moved * normed))
    ids = lax.broadcasted_iota(jnp.int32, sums_ref.shape, 0)
    for row, total in enumerate((col_sum(grads * centred), col_sum(grads), col_sum(grad_stream))):
        sums_ref[...] += jnp.where(ids == row, total, 0.0)

    @pl.when(at == last)
    def _():
        close_exchange(stats_ref[...], gain_ref, sides, next_avg, next_halo, scratch, me, bands)
        grad_qkv[...] = qkv_s[...].astype(BF)
        grad_proj[...] = proj_s[...].astype(BF)


def leave(place, sides, packed, stream, three, field, avg, gain, bias, proj, ln_gain, ln_bias, qkv, width,
          bands):
    images, tokens, channels = stream.shape
    direct = bands == HEADS
    tok = image_block(tokens, channels)
    vector = vector_block(channels)
    table = table_block(channels)
    return pl.pallas_call(
        partial(leave_kernel, width, bands, images),
        grid=(images,),
        out_shape=(
            jax.ShapeDtypeStruct(stream.shape, F32),
            jax.ShapeDtypeStruct((8, channels), F32),
            jax.ShapeDtypeStruct((2, images, width, channels), BF),
            jax.ShapeDtypeStruct((8, channels), F32),
            jax.ShapeDtypeStruct((8, channels), F32),
            jax.ShapeDtypeStruct(qkv.shape, BF),
            jax.ShapeDtypeStruct(proj.shape, BF),
        ),
        in_specs=[
            SMEM_WHOLE,
            SMEM_WHOLE,
        ]
        + (
            [pl.BlockSpec(memory_space=pl.ANY)] * images
            if direct
            else [pl.BlockSpec((1,) + packed[0].shape[1:], lambda at: (at, 0, 0, 0))]
        )
        + [
            tok,
            tok,
            tok,
            table,
            vector,
            vector,
            fixed_block(proj.shape),
            vector,
            vector,
            fixed_block(qkv.shape),
        ],
        out_specs=(
            tok,
            table,
            pl.BlockSpec(memory_space=pl.ANY),
            table,
            table,
            fixed_block(qkv.shape),
            fixed_block(proj.shape),
        ),
        scratch_shapes=[
            pltpu.VMEM(qkv.shape, F32), pltpu.VMEM(proj.shape, F32), pltpu.VMEM(qkv.shape, BF)
        ]
        + exchange_scratch(images, width, channels, bands)
        + (
            [
                pltpu.VMEM((2,) + packed[0].shape, BF),
                pltpu.VMEM(packed[0].shape, BF),
                pltpu.SemaphoreType.DMA((2,)),
                pltpu.SemaphoreType.DMA((bands,)),
                pltpu.SemaphoreType.DMA((bands,)),
            ]
            if direct
            else []
        ),
        compiler_params=pltpu.CompilerParams(
            vmem_limit_bytes=62 << 20, collective_id=7, has_side_effects=True
        ),
        name="leave",
    )(place, sides, *packed, stream, three, field, avg, gain, bias, proj, ln_gain, ln_bias, qkv)

def rounded(field):
    return field.astype(BF)


def join_sums(table_ref, cross, hidden, first, second, third, residual, leaves, feeds, pairs):
    images = cross.shape[0] // 2
    channels = cross.shape[1]
    ids = lax.broadcasted_iota(jnp.int32, cross.shape, 0)

    def total(ref, step, offset, count):
        return col_sum(jnp.where((ids < count) & (lax.rem(ids, step) == offset), ref[...], 0.0))

    rows = [row_of(cross[...], at) for at in range(images)] + [row_of(hidden[...], at) for at in range(images)]
    for ref in (first, second, third):
        rows += [total(ref, 2, 1, 2 * images), total(ref, 2, 0, 2 * images)]
    rows.append(total(residual, 1, 0, images))
    rows += [row_of(leaves[...], at) for at in range(3)] + [row_of(feeds[...], at) for at in range(4)]
    rows += [pairs[:, first : first + channels] for first in range(0, pairs.shape[1], channels)]
    table_ref[...] = jnp.zeros_like(table_ref)
    for at, row in enumerate(rows):
        put_row(table_ref.at[pl.ds(at // 8 * 8, 8)], at % 8, row)


def reduce_kernel(count, bands, groups, *refs):
    last_ref, bands_refs = refs[0], refs[1 : 1 + count]
    half_ref, tables = refs[1 + count], refs[2 + count : 11 + count]
    refs = refs[11 + count :]
    last_out, bands_outs, (gathered, other_ref) = refs[0], refs[1 : 1 + count], refs[1 + count : 3 + count]
    refs = refs[3 + count :]
    table_ref, slots, table_send, table_recv, far_send, far_recv, half_sems = refs[:7]
    sum_s, fields = refs[7], refs[8 : 8 + count]
    refs = refs[8 + count :]
    me, group = lax.axis_index("rows"), lax.axis_index("heads")
    fold = BandFold([last_ref], refs[:9], me)
    tree = GroupTree(fields, bands_outs, refs[9 : 11 + 2 * count], group)
    last_tree = GroupTree([sum_s], [last_out], refs[11 + 2 * count :], group)
    row_peers = [lax.rem(me + away, bands) for away in range(1, bands)]
    far_peers = [lax.rem(group + away, groups) for away in range(1, groups)]
    barrier = pltpu.get_barrier_semaphore()
    for axis, peers in (("rows", row_peers), ("heads", far_peers)):
        for peer in peers:
            pl.semaphore_signal(
                barrier, inc=1, device_id={axis: peer}, device_id_type=pl.DeviceIdType.MESH
            )
    for field, ref in zip(fields, bands_refs):
        field[...] = ref[...]
    join_sums(table_ref, *tables)
    pl.semaphore_wait(barrier, bands + groups - 2)

    def copy(src, dst, send, recv, axis, peer):
        return pltpu.make_async_remote_copy(
            src_ref=src,
            dst_ref=dst,
            send_sem=send,
            recv_sem=recv,
            device_id={axis: peer},
            device_id_type=pl.DeviceIdType.MESH,
        )

    near = [
        copy(table_ref, slots.at[away], table_send.at[away], table_recv.at[away], "rows", peer)
        for away, peer in enumerate(row_peers)
    ]
    for item in near:
        item.start()
    fold.start()
    tree.near()
    half = copy(half_ref, other_ref, half_sems.at[0], half_sems.at[1], "heads", jnp.bitwise_xor(group, 1))
    half.start()
    fold.spread()
    for item in near:
        item.wait_recv()
    total = table_ref[...]
    for away in range(bands - 1):
        total = total + slots[away]
    gathered[group] = total
    far = [
        copy(gathered.at[group], gathered.at[group], far_send.at[away], far_recv.at[away], "heads", peer)
        for away, peer in enumerate(far_peers)
    ]
    for item in far:
        item.start()
    tree.far()
    fold.second()
    tree.back()
    fold.finish([sum_s])
    last_tree.near()
    last_tree.far()
    last_tree.back()
    for away in range(groups - 1):
        source = lax.rem(group - (away + 1) + groups, groups)
        copy(
            gathered.at[source], gathered.at[source], far_send.at[away], far_recv.at[away], "heads", source
        ).wait_recv()
    tree.end()
    last_tree.end()
    half.wait_recv()
    for item in [half] + near + far:
        item.wait_send()


def reduce_parts(last, parts, half, bands, groups, sums):
    shapes = [part.shape for part in parts]
    own = (last.shape[0] // bands, last.shape[1])
    rows = 2 * (sums[0].shape[0] // 2) + 14 + sums[-1].shape[1] // last.shape[1]
    table = (-(-rows // 8) * 8, last.shape[1])
    return pl.pallas_call(
        partial(reduce_kernel, len(parts), bands, groups),
        out_shape=(jax.ShapeDtypeStruct(own, BF),)
        + tuple(jax.ShapeDtypeStruct(shape, BF) for shape in shapes)
        + (
            jax.ShapeDtypeStruct((groups,) + table, F32),
            jax.ShapeDtypeStruct(half.shape, BF),
        ),
        in_specs=[pl.BlockSpec(memory_space=pl.ANY)] + [VMEM_WHOLE] * (len(parts) + 1 + len(sums)),
        out_specs=(VMEM_WHOLE,) * (len(parts) + 3),
        scratch_shapes=[pltpu.VMEM(table, F32), pltpu.VMEM((bands - 1,) + table, F32)]
        + [pltpu.SemaphoreType.DMA((bands - 1,))] * 2
        + [pltpu.SemaphoreType.DMA((groups - 1,))] * 2
        + [pltpu.SemaphoreType.DMA((2,)), pltpu.VMEM(own, BF)]
        + [pltpu.VMEM(shape, BF) for shape in shapes]
        + fold_scratch([last.shape])
        + tree_scratch(shapes)
        + tree_scratch([own]),
        compiler_params=pltpu.CompilerParams(
            vmem_limit_bytes=62 << 20, collective_id=8, has_side_effects=True
        ),
        name="reduce_parts",
    )(last, *parts, half, *sums)


def halve_rows(kept, given, step):
    pairs = [(band, band ^ (1 << step)) for band in range(8)]
    return rounded(kept.astype(F32) + lax.ppermute(given, "rows", pairs).astype(F32))


def sum_groups(part, step, groups):
    odd = lax.rem(lax.axis_index("heads"), 2)
    near = [(at, at ^ 1) for at in range(groups)]
    far = [(at, at ^ 2) for at in range(groups)]
    if step == 0:
        one, two = part
        kept, sent = jnp.where(odd == 0, one, two), jnp.where(odd == 0, two, one)
        return rounded(kept.astype(F32) + lax.ppermute(sent, "heads", near).astype(F32))
    if step == 1:
        return rounded(part.astype(F32) + lax.ppermute(part, "heads", far).astype(F32))
    other = lax.ppermute(part, "heads", near)
    return jnp.where(odd == 0, jnp.concatenate([part, other]), jnp.concatenate([other, part]))


def finals_kernel(pieces, *refs):
    (odd, conv_two, conv_one, qkv, proj_in, kept, other, table, value, context, hot, embed, cross_out,
     cross_value, out_conv_two, out_conv_one, out_qkv, out_proj_in, out_geglu, out_feed, out_proj_out,
     out_attn_out, out_class, out_cross_value, out_cross_out, out_time, rows_s) = refs
    out_conv_two[...] = conv_two[...].astype(F32)
    out_conv_one[...] = conv_one[...].astype(F32)
    out_proj_in[...] = proj_in[...].astype(F32)
    rows, channels = out_proj_in.shape
    low = lane_ids(rows) < 64
    out_qkv[:, :channels] = qkv[:, 2 * channels :].astype(F32)
    for first in range(0, channels, 128):
        one = qkv[:, 2 * first : 2 * first + 128].astype(F32)
        two = qkv[:, 2 * first + 128 : 2 * first + 256].astype(F32)
        out_qkv[:, channels + first : channels + first + 128] = jnp.where(low, one, swap_halves(two))
        out_qkv[:, 2 * channels + first : 2 * channels + first + 128] = jnp.where(
            low, swap_halves(one), two
        )
    flag = jnp.full((1, channels), odd[0], jnp.int32) == 0
    one, two = kept[...].astype(F32), other[...].astype(F32)
    early = jnp.concatenate([jnp.where(flag, one, two), jnp.where(flag, two, one)], axis=0)
    for at, (first, size) in enumerate(pieces[0]):
        out_geglu[:, at * channels : (at + 1) * channels] = early[first : first + size]
    for out, ((first, size),) in zip((out_feed, out_proj_out, out_attn_out), pieces[1:]):
        out[...] = early[first : first + size]
    per_group = value.shape[0] // table.shape[0]

    def joined(first):
        return jnp.concatenate(
            [table[group, first : first + per_group] for group in range(table.shape[0])], axis=0
        )

    def exact(lhs, rhs, dims):
        return lax.dot_general(lhs, rhs, (dims, ((), ())), precision=HIGH, preferred_element_type=F32)

    crossed, shifted = joined(0), joined(per_group)
    own = pl.ds(pl.multiple_of(odd[1] * rows, 16), rows)
    tile = pl.ds(pl.multiple_of(odd[1] * rows // 128 * 128, 128), 128)
    inner = pl.ds(pl.multiple_of(lax.rem(odd[1] * rows, 128), 16), rows)
    rows_s[...] = exact(value[:, tile].astype(F32), crossed, ((0,), (0,)))
    out_cross_out[...] = rows_s[inner]
    grad_value = exact(crossed, cross_out[...].astype(F32), ((1,), (1,)))
    rows_s[...] = exact(context[:, tile], grad_value, ((0,), (0,)))
    out_cross_value[...] = rows_s[inner]
    grad_context = exact(grad_value, cross_value[own].astype(F32), ((1,), (1,)))
    out_class[...] = exact(hot[...].astype(F32), grad_context, ((0,), (0,)))
    times = out_time.shape[0]
    columns = pl.ds(pl.multiple_of(odd[1] * times, 128), times)
    out_time[...] = exact(embed[:, columns].astype(F32), shifted, ((0,), (0,)))


def finals(odd, parts, kept, other, table, value, context, hot, embed, cross_out, cross_value, pieces):
    conv_two, conv_one, qkv, proj_in = parts
    rows, channels = proj_in.shape
    shapes = [part.shape for part in parts] + [
        (rows, len(pieces[0]) * channels),
        (pieces[1][0][1], channels),
        (rows, channels),
        (rows, channels),
        (hot.shape[1], rows),
        (rows, channels),
        (rows, channels),
        (embed.shape[1] * rows // channels, channels),
    ]
    return pl.pallas_call(
        partial(finals_kernel, pieces),
        out_shape=tuple(jax.ShapeDtypeStruct(shape, F32) for shape in shapes),
        in_specs=[SMEM_WHOLE] + [VMEM_WHOLE] * 13,
        out_specs=(VMEM_WHOLE,) * len(shapes),
        scratch_shapes=[pltpu.VMEM((128, channels), F32)],
        compiler_params=pltpu.CompilerParams(vmem_limit_bytes=62 << 20),
        name="finals",
    )(odd, *parts, kept, other, table, value, context, hot, embed, cross_out, cross_value)


def finish_kernel(width, place, sides, kept_ref, grad_ref, field_ref, avg_ref, back_avg, gain_ref, made_ref,
                  out_ref, pass_ref):
    pass_ref[...] = made_ref[...]
    at = pl.program_id(0)
    mean, inv_std = moments(avg_ref, at)
    back = back_avg[...]
    field_slope = inv_std * inv_std * row_of(back, 2 * at + 1)
    offset = inv_std * row_of(back, 2 * at) - mean * field_slope
    moved = grad_ref[0] * (inv_std * vec(gain_ref)) - field_ref[0].astype(F32) * field_slope - offset
    inside = pixel_inside(moved.shape, place[0], sides[at], width)
    out_ref[0] = jnp.where(inside, kept_ref[0] + moved, 0.0)


def finish(place, sides, kept, grads, field, avg, back_avg, gain, made, width):
    images, tokens, channels = kept.shape
    tok = image_block(tokens, channels)
    table = table_block(channels)
    return pl.pallas_call(
        partial(finish_kernel, width),
        grid=(images,),
        out_shape=(jax.ShapeDtypeStruct(kept.shape, F32), jax.ShapeDtypeStruct(made.shape, BF)),
        in_specs=[SMEM_WHOLE, SMEM_WHOLE, tok, tok, tok, table, table, vector_block(channels), tok],
        out_specs=(tok, tok),
        compiler_params=pltpu.CompilerParams(vmem_limit_bytes=62 << 20),
        name="finish",
    )(place, sides, kept, grads, field, avg, back_avg, gain, made)


def time_features(time_steps, dims):
    half_dim = dims // 2
    frequency = jnp.exp(-math.log(10000.0) * jnp.arange(half_dim, dtype=jnp.float32) / half_dim)
    angles = time_steps.astype(jnp.float32)[:, None] * frequency[None, :]
    return jnp.concatenate([jnp.cos(angles), jnp.sin(angles)], axis=-1)


def pad_rows(table):
    return jnp.pad(table, ((0, 8 - table.shape[0]), (0, 0)))


def to_items(sent, bands):
    images, heads = len(sent), sent[0].shape[0]
    per_band = heads * images // bands
    if bands == heads:
        first, *parts = sent
    else:
        items = jnp.stack(sent, axis=1).reshape((bands, per_band) + sent[0].shape[1:])
        parts = [items[:, at] for at in range(per_band)]
    parts = [lax.all_to_all(part, "rows", split_axis=0, concat_axis=0, tiled=True) for part in parts]
    return [first] + parts if bands == heads else parts


def from_items(results, images, bands):
    if bands == HEADS:
        return [
            lax.all_to_all(result, "rows", split_axis=0, concat_axis=0, tiled=True)
            for result in results[:-1]
        ] + results[-1:]
    back = [
        lax.all_to_all(result, "rows", split_axis=0, concat_axis=0, tiled=True)
        for result in results
    ]
    joint = jnp.stack(back, axis=1)
    return [jnp.swapaxes(joint.reshape((HEADS, images) + joint.shape[2:]), 0, 1)]


def per_device(
    images,
    image_sides,
    labels,
    timesteps,
    cotangent,
    first_gain,
    first_bias,
    conv_one,
    time_proj,
    time_bias,
    second_gain,
    second_bias,
    conv_two,
    conv_bias,
    third_gain,
    third_bias,
    proj_in,
    proj_in_bias,
    attn_gain,
    attn_bias,
    qkv_proj,
    attn_out,
    attn_out_bias,
    class_table,
    cross_value,
    cross_out,
    feed_gain,
    feed_bias,
    geglu_proj,
    geglu_bias,
    feed_out,
    feed_out_bias,
    proj_out,
    proj_out_bias,
):
    image_count, band_rows, width, channels = images.shape
    tokens = band_rows * width
    head_dim = channels // HEADS
    score_scale = head_dim ** (-0.5)
    bands = lax.axis_size("rows")
    groups = lax.axis_size("heads")
    halving = bands == 8 and groups == 4 and channels == 512
    me = lax.axis_index("rows")
    first_image = lax.axis_index("heads") * image_count
    sides = lax.dynamic_slice_in_dim(image_sides, first_image, image_count)
    place = jnp.stack([me * band_rows, me]).astype(jnp.int32)

    field = images.reshape(image_count, tokens, channels)
    cot = cotangent.reshape(image_count, tokens, channels)

    hot = rounded(
        (labels[:, None] == jnp.arange(class_table.shape[0], dtype=jnp.int32)[None, :]).astype(F32)
    )
    context = jnp.dot(hot, class_table, preferred_element_type=F32)
    value = rounded(jnp.dot(rounded(context), cross_value, preferred_element_type=F32))
    cross = jnp.dot(value, cross_out, preferred_element_type=F32)
    cross = pad_rows(lax.dynamic_slice_in_dim(cross, first_image, image_count))
    embed = rounded(jax.nn.silu(time_features(timesteps, time_proj.shape[0])))
    shift = jnp.dot(embed, time_proj, preferred_element_type=F32) + time_bias.astype(F32)
    shift = pad_rows(lax.dynamic_slice_in_dim(shift, first_image, image_count))

    avg_one, halo_images = begin(place, sides, field, width, bands)
    hidden, avg_two, halo_hidden = conv_forward(
        place, sides, field, halo_images, avg_one, first_gain, first_bias, conv_one,
        shift, None, width, bands,
    )
    residual, avg_three, halo_residual = conv_forward(
        place, sides, hidden, halo_hidden, avg_two, second_gain, second_bias, conv_two,
        jnp.broadcast_to(conv_bias.astype(F32), (8, channels)), field, width, bands,
    )
    stream, *sent = entry(
        residual, avg_three, third_gain, third_bias, proj_in, proj_in_bias,
        attn_gain, attn_bias, qkv_proj, bands,
    )
    chunks = to_items(sent, bands)
    first_item = me * len(chunks)
    item_sides = [
        lax.dynamic_slice_in_dim(sides, lax.rem(first_item + at, image_count), 1)
        for at in range(len(chunks))
    ]
    attended = [attend(side, chunk, width, score_scale) for side, chunk in zip(item_sides, chunks)]
    mixed = [pairs for pairs, _, _ in attended]
    (
        output, three, grad_chunks, halo_cot, *feed_grads, feed_sums, cross_sum, pair_sums,
    ) = feed(
        place, sides, mixed, stream, residual, cot, cross, attn_out, attn_out_bias,
        feed_gain, feed_bias, geglu_proj, geglu_bias, feed_out,
        feed_out_bias, proj_out, proj_out_bias, width, bands, halving,
    )
    halved = (feed_grads[0:2], feed_grads[2:4]) if halving else None
    results = []
    for spot, (side, chunk, (_, norms, kept)) in enumerate(zip(item_sides, chunks, attended)):
        if halving and spot in (1, 2):
            halved = [
                halve_rows(kept, given, spot if at == 0 else 3 - spot) for at, (kept, given) in enumerate(halved)
            ]
            *halved, norms = lax.optimization_barrier((*halved, norms))
            halved = [(part[0], part[1]) for part in halved] if spot == 1 else halved
        results.append(attend_back(side, chunk, grad_chunks, spot, norms, kept, width, score_scale))
    grad_qkv = from_items(results, image_count, bands)
    if halving:
        early = halved
    else:
        early = feed_grads[0].reshape((bands,) + feed_grads[0].shape[-2:])
        early = lax.psum_scatter(early, "rows", scatter_dimension=0, tiled=True)[0]
        early = lax.psum(early, "heads")
    moved, back_three, halo_moved, third_sums, leave_sums, grad_qkv_proj, grad_proj_in = leave(
        place, sides, grad_qkv, stream, three, residual, avg_three, third_gain,
        third_bias, proj_in, attn_gain, attn_bias, qkv_proj, width, bands,
    )
    if halving:
        *early, back_three = lax.optimization_barrier((*early, back_three))
        early = sum_groups(early, 0, groups)
    *folded, grad_residual, moved, back_two, second_sums, residual_sums, grad_conv_two, halo_moved = conv_backward(
        place, sides, moved, halo_moved, residual, halo_residual, avg_three, back_three,
        third_gain, cot, halo_cot, conv_two, hidden, avg_two, second_gain,
        second_bias, (grad_qkv_proj, grad_proj_in) if halving else (), (), width, bands,
    )
    if halving:
        early, back_two = lax.optimization_barrier((early, back_two))
        early = sum_groups(early, 1, groups)
    *folded, moved, back_one, first_sums, hidden_sums, grad_conv_one = conv_backward(
        place, sides, moved, halo_moved, hidden, halo_hidden, avg_two, back_two, second_gain,
        None, None, conv_one, field, avg_one, first_gain, first_bias,
        (grad_conv_two,) if halving else (), folded, width, bands,
    )
    if halving:
        early, back_one = lax.optimization_barrier((early, back_one))
    grad_images, output = finish(
        place, sides, grad_residual, moved, field, avg_one, back_one, first_gain, output, width
    )
    grad_images = grad_images.reshape(images.shape)

    def own(whole, axis=0):
        size = whole.shape[axis] // bands
        return lax.dynamic_slice_in_dim(whole, me * size, size, axis)

    def reduced(part):
        part = lax.psum_scatter(part, "rows", scatter_dimension=0, tiled=True)
        return lax.psum(part, "heads").astype(F32)

    used = 2 * image_count
    pieces = feed_pieces(channels, geglu_proj.shape[1], feed_out.shape[0], bands)
    if halving:
        grad_images, first_sums = lax.optimization_barrier((grad_images, first_sums))
        rows_two, rows_qkv, rows_in = folded
        rows_one, rows_two, table, other = reduce_parts(
            grad_conv_one, (rows_two,), early, bands, groups,
            (cross_sum, hidden_sums, first_sums, second_sums, third_sums, residual_sums, leave_sums, feed_sums,
             pair_sums),
        )
        late = (rows_two, rows_one, rows_qkv, rows_in)
        odd = jnp.stack([lax.rem(lax.axis_index("heads"), 2), me]).astype(jnp.int32)
        (
            rows_conv_two, rows_conv_one, rows_qkv, rows_proj_in, rows_geglu, rows_feed, rows_proj_out,
            rows_attn_out, grad_class_table, grad_cross_value, grad_cross_out, grad_time_proj,
        ) = finals(
            odd, late, early, other, table, value, context, hot, embed, cross_out, cross_value,
            pieces,
        )
    else:
        table = jnp.concatenate(
            [
                cross_sum[:image_count],
                hidden_sums[:image_count],
                jnp.stack(
                    [
                        jnp.sum(first_sums[1:used:2], axis=0),
                        jnp.sum(first_sums[0:used:2], axis=0),
                        jnp.sum(second_sums[1:used:2], axis=0),
                        jnp.sum(second_sums[0:used:2], axis=0),
                        jnp.sum(third_sums[1:used:2], axis=0),
                        jnp.sum(third_sums[0:used:2], axis=0),
                        jnp.sum(residual_sums[:image_count], axis=0),
                    ]
                ),
                leave_sums[:3],
                feed_sums[:4],
                pair_sums.reshape(-1, channels),
            ]
        )
        table = jnp.pad(table, ((0, -table.shape[0] % 8), (0, 0)))
        table = lax.all_gather(lax.psum(table, "rows"), "heads")
        rows_conv_two, rows_qkv, rows_proj_in, rows_conv_one = (
            reduced(part) for part in (grad_conv_two, grad_qkv_proj, grad_proj_in, grad_conv_one)
        )
        keys_values = rows_qkv[:, : 2 * channels].reshape(-1, HEADS, 2, head_dim)
        rows_qkv = jnp.concatenate(
            [
                rows_qkv[:, 2 * channels :],
                keys_values[:, :, 0].reshape(-1, channels),
                keys_values[:, :, 1].reshape(-1, channels),
            ],
            axis=1,
        )
        early = early.astype(F32)
        rows_geglu = jnp.concatenate([early[first : first + size] for first, size in pieces[0]], axis=1)
        rows_feed, rows_proj_out, rows_attn_out = (
            early[first : first + size] for ((first, size),) in pieces[1:]
        )
    all_cross = table[:, :image_count].reshape(-1, channels)
    all_shift = table[:, image_count : 2 * image_count].reshape(-1, channels)
    if not halving:
        own_value, own_context = own(value.astype(F32), 1), own(context, 1)
        own_embed, own_cross = own(embed.astype(F32), 1), own(cross_value)
        hot = hot.astype(F32)
        grad_cross_out = jnp.dot(own_value.T, all_cross, precision=HIGH)
        grad_value = jnp.dot(all_cross, cross_out.astype(F32).T, precision=HIGH)
        grad_cross_value = jnp.dot(own_context.T, grad_value, precision=HIGH)
        grad_context = jnp.dot(grad_value, own_cross.astype(F32).T, precision=HIGH)
        grad_class_table = jnp.dot(hot.T, grad_context, precision=HIGH)
        grad_time_proj = jnp.dot(own_embed.T, all_shift, precision=HIGH)
    joint = jnp.concatenate(
        [jnp.sum(table[:, 2 * image_count :], axis=0), jnp.sum(all_cross, axis=0)[None],
         jnp.sum(all_shift, axis=0)[None]]
    )
    mine = own(joint, 1)
    singles = [mine[at] for at in range(14)]
    grad_geglu_bias = own(joint[14 : 14 + geglu_bias.shape[0] // channels].reshape(-1))
    return (
        output.reshape(images.shape),
        grad_images,
        singles[0],
        singles[1],
        rows_conv_one,
        grad_time_proj,
        mine[-1],
        singles[2],
        singles[3],
        rows_conv_two,
        singles[6],
        singles[4],
        singles[5],
        rows_proj_in,
        singles[9],
        singles[7],
        singles[8],
        rows_qkv,
        rows_attn_out,
        mine[-2],
        grad_class_table,
        grad_cross_value,
        grad_cross_out,
        singles[12],
        singles[13],
        rows_geglu,
        grad_geglu_bias,
        rows_feed,
        singles[11],
        rows_proj_out,
        singles[10],
    )


def solution(mesh):
    return jax.shard_map(
        per_device,
        mesh=mesh,
        in_specs=(
            P("heads", "rows", None, None),
            P(),
            P(),
            P(),
            P("heads", "rows", None, None),
            P(),
            P(),
            P(),
            P(),
            P(),
            P(),
            P(),
            P(),
            P(),
            P(),
            P(),
            P(),
            P(),
            P(),
            P(),
            P(),
            P(),
            P(),
            P(),
            P(),
            P(),
            P(),
            P(),
            P(),
            P(),
            P(),
            P(),
            P(),
            P(),
        ),
        out_specs=(
            P("heads", "rows", None, None),
            P("heads", "rows", None, None),
            P("rows"),
            P("rows"),
            P("rows", None),
            P("rows", None),
            P("rows"),
            P("rows"),
            P("rows"),
            P("rows", None),
            P("rows"),
            P("rows"),
            P("rows"),
            P("rows", None),
            P("rows"),
            P("rows"),
            P("rows"),
            P("rows", None),
            P("rows", None),
            P("rows"),
            P(None, "rows"),
            P("rows", None),
            P("rows", None),
            P("rows"),
            P("rows"),
            P("rows", None),
            P("rows"),
            P("rows", None),
            P("rows"),
            P("rows", None),
            P("rows"),
        ),
        check_vma=False,
    )
```
